32 devices in a mesh: section: 4 (over y, core), dp: 8 (over z, x).
Axes of the slice: x: 2, y: 2, z: 4, core: 2. Of those that a mesh axis runs over, the one named last changes fastest.
Arguments:
- inputs: bfloat16 [2, 8, 512, 1024], P(None, 'dp'), may hold values from -6 to 6
- cotangent: bfloat16 [2, 8, 512, 1024], P(None, 'dp'), may hold values from -6 to 6
- lengths: int32 [2, 8], P(None, 'dp'), may hold values from 32 to 512, as said below
- attn_gain: bfloat16 [4, 1024], P('section'), may hold values from 0.5 to 1.5
- qkv_weight: bfloat16 [4, 1024, 3, 1024], P('section'), may hold values from -0.1875 to 0.1875
- conv_weight: bfloat16 [4, 4, 3, 1024], P('section'), may hold values from -3 to 3
- beta_weight: bfloat16 [4, 1024, 8], P('section'), may hold values from -0.1875 to 0.1875
- head_gain: bfloat16 [4, 128], P('section'), may hold values from 0.5 to 1.5
- out_weight: bfloat16 [4, 1024, 1024], P('section'), may hold values from -0.1875 to 0.1875
- mlp_gain: bfloat16 [4, 1024], P('section'), may hold values from 0.5 to 1.5
- gate_up_weight: bfloat16 [4, 1024, 2, 2816], P('section'), may hold values from -0.1875 to 0.1875
- down_weight: bfloat16 [4, 2816, 1024], P('section'), may hold values from -0.109375 to 0.109375
Outputs:
- section_outputs: bfloat16 [4, 2, 8, 512, 1024], P('section', None, 'dp')
- section_input_grads: bfloat16 [4, 2, 8, 512, 1024], P('section', None, 'dp')
- grad_attn_gain: float32 [4, 1024], P('section', 'dp')
- grad_qkv_weight: float32 [4, 1024, 3, 1024], P('section', 'dp')
- grad_conv_weight: float32 [4, 4, 3, 1024], P('section', None, None, 'dp')
- grad_beta_weight: float32 [4, 1024, 8], P('section', 'dp')
- grad_head_gain: float32 [4, 128], P('section', 'dp')
- grad_out_weight: float32 [4, 1024, 1024], P('section', 'dp')
- grad_mlp_gain: float32 [4, 1024], P('section', 'dp')
- grad_gate_up_weight: float32 [4, 1024, 2, 2816], P('section', 'dp')
- grad_down_weight: float32 [4, 2816, 1024], P('section', 'dp')
The draws below stay inside these ranges and needn't reach their ends.
Inputs may be any that keep to these rules, and one draw needn't show every extreme that they name: `lengths`: in every micro-batch some sequence has exactly 512 tokens.
All inputs are finite; a program needn't handle non-finite values.
Results may differ from the reference program's by a relative error of at most 0.022.
Values may be sent and summed in bfloat16 or wider, within the bound.
A program may use at most 448 MiB of HBM per device.

```python
import jax
import jax.numpy as jnp
from jax import lax

D = 1024
HEADS = 8
HEAD = 128
FF = 2816
CONV = 4
SPAN = 64
LEN = 512
MICRO = 2
SECTIONS = 4
BATCH = 8


def draw_lengths(key, part):
    key = jax.random.fold_in(key, 17)
    key_list = jax.random.split(key, 3)
    base_len = jax.random.randint(key_list[0], (MICRO, BATCH), LEN // 4, LEN + 1)
    shrink = jax.random.randint(key_list[1], (MICRO, BATCH), 0, 3)
    shorter = jnp.right_shift(base_len, shrink)
    longest = jax.random.randint(key_list[2], (MICRO, 1), 0, BATCH)
    columns = jnp.arange(BATCH)[None, :]
    return jnp.where(columns == longest, LEN, shorter).astype(jnp.int32)


def steps_of(stream_key, extent, cuts, least, largest):
    level = 1.0
    for dim, blocks in cuts:
        steps = jax.random.uniform(jax.random.fold_in(jax.random.fold_in(stream_key, 6), dim), (blocks,), jnp.float32, least / len(cuts), largest / len(cuts))
        level = level * jnp.repeat(jnp.exp(steps), extent[dim] // blocks).reshape((-1,) + (1,) * (len(extent) - 1 - dim))
    return level


def noise(own_key, shape, width, reach, cuts=(), kind=jnp.bfloat16):
    result = width * jax.random.normal(own_key, shape, jnp.float32)
    if cuts:
        result = result * steps_of(own_key, shape, cuts, -0.22, 0.18)
    return jnp.clip(result, -reach, reach).astype(kind)


def setup_inputs(seed: int = 0) -> dict:
    splits = jax.random.split(jax.random.key(seed), 13)
    return {
        "inputs": noise(splits[0], (MICRO, BATCH, LEN, D), 1.0, 6.0, ((1, 8),)),
        "cotangent": noise(splits[1], (MICRO, BATCH, LEN, D), 1.0, 6.0, ((1, 8),)),
        "lengths": draw_lengths(jax.random.fold_in(splits[12], 71), 0),
        "attn_gain": jnp.clip(1.0 + 0.1 * jax.random.normal(splits[3], (SECTIONS, D), jnp.float32), 0.5, 1.5).astype(jnp.bfloat16),
        "qkv_weight": noise(splits[4], (SECTIONS, D, 3, D), D ** -0.5, 0.1875, ((0, 4),)),
        "conv_weight": noise(splits[5], (SECTIONS, CONV, 3, D), CONV ** -0.5, 3.0, ((0, 4),)),
        "beta_weight": noise(splits[6], (SECTIONS, D, HEADS), D ** -0.5, 0.1875, ((0, 4),)),
        "head_gain": jnp.clip(1.0 + 0.1 * jax.random.normal(splits[7], (SECTIONS, HEAD), jnp.float32), 0.5, 1.5).astype(jnp.bfloat16),
        "out_weight": noise(splits[8], (SECTIONS, D, D), D ** -0.5, 0.1875, ((0, 4),)),
        "mlp_gain": jnp.clip(1.0 + 0.1 * jax.random.normal(splits[9], (SECTIONS, D), jnp.float32), 0.5, 1.5).astype(jnp.bfloat16),
        "gate_up_weight": noise(splits[10], (SECTIONS, D, 2, FF), D ** -0.5, 0.1875, ((0, 4),)),
        "down_weight": noise(splits[11], (SECTIONS, FF, D), FF ** -0.5, 0.109375, ((0, 4),)),
    }


highest = lax.Precision.HIGHEST

@jax.custom_vjp
def low(v):
    return lax.optimization_barrier(v.astype(jnp.bfloat16)).astype(jnp.float32)

@jax.custom_vjp
def low_back(v):
    return v

def low_keep(v):
    return (low(v), None)

def low_pass(kept, grad):
    return (grad,)

def back_keep(v):
    return (v, None)

def back_low(kept, grad):
    return (low(grad),)
low.defvjp(low_keep, low_pass)
low_back.defvjp(back_keep, back_low)

def delta_rule(query_vec, key_vec, value_vec, beta_rate):
    seq_len, head_count, head_size = query_vec.shape
    blocks = seq_len // SPAN

    def to_blocks(tensor):
        return tensor.reshape(blocks, SPAN, head_count, -1).transpose(0, 2, 1, 3)
    row_ids = jnp.arange(SPAN)
    strict = (row_ids[:, None] > row_ids[None, :]).astype(query_vec.dtype)
    causal = (row_ids[:, None] >= row_ids[None, :]).astype(query_vec.dtype)
    identity = jnp.eye(SPAN, dtype=query_vec.dtype)

    def span_step(state_mat, block_in):
        query_blk, key_blk, value_blk, beta_blk = block_in
        weighted = key_blk * beta_blk[..., None]
        inner_kk = jnp.einsum('hce,hse->hcs', weighted, key_blk, precision=highest) * strict
        right_side = jnp.concatenate([weighted, value_blk * beta_blk[..., None]], -1)
        solved = jax.scipy.linalg.solve_triangular(identity + inner_kk, right_side, lower=True, unit_diagonal=True)
        w_factor = solved[..., :head_size]
        u_factor = solved[..., head_size:]
        new_values = u_factor - jnp.einsum('hce,hef->hcf', w_factor, state_mat, precision=highest)
        scores = jnp.einsum('hce,hse->hcs', query_blk, key_blk, precision=highest) * causal
        block_out = jnp.einsum('hce,hef->hcf', query_blk, state_mat, precision=highest)
        block_out = block_out + jnp.einsum('hcs,hsf->hcf', scores, new_values, precision=highest)
        state_mat = state_mat + jnp.einsum('hce,hcf->hef', key_blk, new_values, precision=highest)
        return (state_mat, block_out)
    beta_blocks = beta_rate.reshape(blocks, SPAN, head_count).transpose(0, 2, 1)
    start_state = jnp.zeros((head_count, head_size, head_size), query_vec.dtype)
    final_state, outputs = lax.scan(jax.checkpoint(span_step), start_state, (to_blocks(query_vec), to_blocks(key_vec), to_blocks(value_vec), beta_blocks))
    return outputs.transpose(0, 2, 1, 3).reshape(seq_len, head_count, head_size)

def core(projected, logits, conv_taps, head_scale, token_mask):
    seq_len, triple = projected.shape
    model_width = triple // 3
    head_count = logits.shape[1]
    head_size = model_width // head_count
    grouped = projected.reshape(seq_len, 3, model_width)
    tap_count = conv_taps.shape[0]
    padded = jnp.concatenate([jnp.zeros((tap_count - 1, 3, model_width), projected.dtype), grouped], 0)
    mixed_sum = conv_taps[0] * padded[0:seq_len]
    for tap_index in range(1, tap_count):
        mixed_sum = mixed_sum + conv_taps[tap_index] * padded[tap_index:tap_index + seq_len]
    activated = jax.nn.silu(mixed_sum)
    query_vec = activated[:, 0].reshape(seq_len, head_count, head_size)
    key_vec = activated[:, 1].reshape(seq_len, head_count, head_size)
    value_vec = activated[:, 2].reshape(seq_len, head_count, head_size)
    query_vec = query_vec * lax.rsqrt(lax.optimization_barrier(jnp.sum(query_vec * query_vec, -1, keepdims=True)) + 1e-06)
    key_vec = key_vec * lax.rsqrt(lax.optimization_barrier(jnp.sum(key_vec * key_vec, -1, keepdims=True)) + 1e-06)
    beta_rate = jax.nn.sigmoid(logits) * token_mask[:, None]
    attended = delta_rule(query_vec, key_vec, value_vec, beta_rate)
    normed_out = attended * lax.rsqrt(lax.optimization_barrier(jnp.mean(attended * attended, -1, keepdims=True)) + 1e-05) * head_scale
    return normed_out.reshape(seq_len, model_width)

def mixer_layer(residual, norm_gain, weight_qkv, conv_taps, weight_beta, head_scale, weight_out, token_mask):
    residual = low_back(residual)
    model_width = residual.shape[1]
    normed = low(residual * lax.rsqrt(lax.optimization_barrier(jnp.mean(residual * residual, -1, keepdims=True)) + 1e-06) * norm_gain)
    projected = low_back(jnp.dot(normed, weight_qkv.reshape(model_width, -1), precision=highest))
    logits = jnp.dot(normed, weight_beta, precision=highest)
    mixed_out = low(core(projected, logits, conv_taps, head_scale, token_mask))
    return low(residual + jnp.dot(mixed_out, weight_out, precision=highest))

def mlp_layer(residual, norm_gain, weight_gate_up, weight_down):
    residual = low_back(residual)
    seq_len, model_width = residual.shape
    normed = low(residual * lax.rsqrt(lax.optimization_barrier(jnp.mean(residual * residual, -1, keepdims=True)) + 1e-06) * norm_gain)
    gate_both = low_back(jnp.dot(normed, weight_gate_up.reshape(model_width, -1), precision=highest))
    gate_both = gate_both.reshape(seq_len, 2, -1)
    hidden = low(jax.nn.silu(gate_both[:, 0]) * gate_both[:, 1])
    return low(residual + jnp.dot(hidden, weight_down, precision=highest))

def reference(inputs, cotangent, lengths, attn_gain, qkv_weight, conv_weight, beta_weight, head_gain, out_weight, mlp_gain, gate_up_weight, down_weight):
    params = tuple((tensor.astype(jnp.float32) for tensor in (attn_gain, qkv_weight, conv_weight, beta_weight, head_gain, out_weight, mlp_gain, gate_up_weight, down_weight)))
    seq_count = MICRO * BATCH
    flat_inputs = inputs.astype(jnp.float32).reshape(seq_count, LEN, D)
    flat_cot = cotangent.astype(jnp.float32).reshape(seq_count, LEN, D)
    flat_lengths = lengths.reshape(seq_count)

    def one_sequence(totals, record):
        sequence, seq_cot, seq_length = record
        token_mask = (jnp.arange(LEN) < seq_length).astype(jnp.float32)
        current = sequence
        outputs = []
        pullbacks = []
        for position in range(SECTIONS):
            if position % 2 == 0:

                def section_fn(cur, *tensors, position=position):
                    return mixer_layer(cur, *(tensor[position] for tensor in tensors), token_mask)
                current, pullback = jax.vjp(section_fn, current, *params[:6])
            else:

                def section_fn(cur, *tensors, position=position):
                    return mlp_layer(cur, *(tensor[position] for tensor in tensors))
                current, pullback = jax.vjp(section_fn, current, *params[6:])
            outputs.append(current)
            pullbacks.append(pullback)
        upstream = seq_cot
        input_grads = [None] * SECTIONS
        totals = list(totals)
        for position in reversed(range(SECTIONS)):
            pieces = pullbacks[position](upstream)
            upstream = pieces[0]
            input_grads[position] = upstream
            offset = 0 if position % 2 == 0 else 6
            for member, piece in enumerate(pieces[1:]):
                totals[offset + member] = totals[offset + member] + piece
        return (tuple(totals), (jnp.stack(outputs), jnp.stack(input_grads)))
    zero_totals = tuple((jnp.zeros(tensor.shape, jnp.float32) for tensor in params))
    totals, stacked = lax.scan(one_sequence, zero_totals, (flat_inputs, flat_cot, flat_lengths))
    section_out = stacked[0].transpose(1, 0, 2, 3).reshape(SECTIONS, MICRO, BATCH, LEN, D)
    section_grad = stacked[1].transpose(1, 0, 2, 3).reshape(SECTIONS, MICRO, BATCH, LEN, D)
    return (section_out.astype(jnp.bfloat16), section_grad.astype(jnp.bfloat16), totals[0], totals[1], totals[2], totals[3], totals[4], totals[5], totals[6], totals[7], totals[8])
```

```python
import functools

import jax, jax.numpy as jnp
from jax import lax
from jax.experimental import pallas as pl
from jax.experimental.pallas import tpu as pltpu
from jax.sharding import PartitionSpec as P

CHUNK = 128
bf16, f32 = jnp.bfloat16, jnp.float32


def nn(a, b):
    return lax.dot_general(a.astype(bf16), b.astype(bf16), (((1,), (0,)), ((), ())), preferred_element_type=f32)


def nt(a, b):
    return lax.dot_general(a.astype(bf16), b.astype(bf16), (((1,), (1,)), ((), ())), preferred_element_type=f32)


def tn(a, b):
    return lax.dot_general(a.astype(bf16), b.astype(bf16), (((0,), (0,)), ((), ())), preferred_element_type=f32)


def shifted_rows(x, steps):
    rows = lax.broadcasted_iota(jnp.int32, x.shape, 0)
    count = x.shape[0]
    if steps > 0:
        return jnp.where(rows >= steps, pltpu.roll(x, steps, 0), 0.0)
    return jnp.where(rows < count + steps, pltpu.roll(x, count + steps, 0), 0.0)


def convolved(x, taps):
    total = x * taps[3:4]
    for back in range(1, 4):
        total = total + shifted_rows(x, back) * taps[3 - back : 4 - back]
    return total


def chunk_masks():
    row = lax.broadcasted_iota(jnp.int32, (CHUNK, CHUNK), 0)
    col = lax.broadcasted_iota(jnp.int32, (CHUNK, CHUNK), 1)
    return row, col


def level_mask(row, col, size):
    shift = size.bit_length() - 1
    same = (row >> (shift + 1)) == (col >> (shift + 1))
    return same & (((row >> shift) & 1) == 1) & (((col >> shift) & 1) == 0)


def triangular_inverse(a_list, row, col):
    mask = level_mask(row, col, 1)
    xs = [jnp.where(mask, -a, 0.0) for a in a_list]
    size = 2
    while size < CHUNK:
        mask = level_mask(row, col, size)
        parts = [jnp.where(mask, a, 0.0) for a in a_list]
        ys = [p + nn(p, x) for p, x in zip(parts, xs)]
        xs = [x - (y + nn(x, y)) for x, y in zip(xs, ys)]
        size *= 2
    return xs


def head_column(block, head):
    lanes = lax.broadcasted_iota(jnp.int32, block.shape, 1)
    return jnp.sum(jnp.where(lanes == head, block, 0.0), axis=1, keepdims=True)


def mixer_fwd_kernel(per, q_ref, k_ref, v_ref, beta_ref, taps_q, taps_k, taps_v, gain_ref, mixed_ref, t_ref, n_ref, s_ref, o_ref):
    row, col = chunk_masks()
    strict, causal = row > col, row >= col
    chunks = q_ref.shape[0] // CHUNK
    beta_all = beta_ref[...]
    for j in range(per):
        lane = slice(j * 128, (j + 1) * 128)
        head = pl.program_id(0) * per + j
        beta = head_column(beta_all, head)

        def activated(ref, taps):
            c = convolved(ref[:, lane], taps[:, lane])
            return c * jax.nn.sigmoid(c)

        q, k, v = activated(q_ref, taps_q), activated(k_ref, taps_k), activated(v_ref, taps_v)
        q = q * lax.rsqrt(jnp.sum(q * q, 1, keepdims=True) + 1e-6)
        k = k * lax.rsqrt(jnp.sum(k * k, 1, keepdims=True) + 1e-6)
        cut = lambda x: [x[i * CHUNK : (i + 1) * CHUNK] for i in range(chunks)]
        qs, ks, vs, bs = cut(q), cut(k), cut(v), cut(beta)
        a_list = [jnp.where(strict, nt(kc, kc) * bc, 0.0) for kc, bc in zip(ks, bs)]
        ps = [jnp.where(causal, nt(qc, kc), 0.0) for qc, kc in zip(qs, ks)]
        ts = triangular_inverse(a_list, row, col)
        wu = []
        for kc, vc, bc, t in zip(ks, vs, bs, ts):
            both = jnp.concatenate([kc * bc, vc * bc], 1)
            wu.append(both + nn(t, both))
        state = jnp.zeros((128, 128), f32)
        outs = []
        for i in range(chunks):
            n = wu[i][:, 128:] - nn(wu[i][:, :128], state)
            o = nn(jnp.concatenate([qs[i], ps[i]], 1), jnp.concatenate([state, n], 0))
            span = pl.ds(i * CHUNK, CHUNK)
            s_ref[j, span, :] = state.astype(bf16)
            n_ref[j, span, :] = n.astype(bf16)
            t_ref[j, span, :] = ts[i].astype(bf16)
            o_ref[span, lane] = o
            mixed_ref[span, lane] = (o * lax.rsqrt(jnp.mean(o * o, 1, keepdims=True) + 1e-5) * gain_ref[...]).astype(bf16)
            if i + 1 < chunks:
                state = state + tn(ks[i], n)


def mixer_fwd(proj, beta, taps, gain, per=2):
    rows, width = proj[0].shape
    heads = width // 128
    steps = heads // per
    wide = 128 * per
    part = pl.BlockSpec((rows, wide), lambda h: (0, h))
    tap = lambda p: pl.BlockSpec((4, wide), lambda h, p=p: (0, p * steps + h))
    whole = lambda a: pl.BlockSpec(a.shape, lambda h: (0,) * a.ndim)
    saved = pl.BlockSpec((per, rows, 128), lambda h: (h, 0, 0))
    return pl.pallas_call(
        functools.partial(mixer_fwd_kernel, per),
        grid=(steps,),
        in_specs=[part, part, part, whole(beta), tap(0), tap(1), tap(2), whole(gain)],
        out_specs=[part, saved, saved, saved, part],
        out_shape=[
            jax.ShapeDtypeStruct((rows, width), bf16),
            jax.ShapeDtypeStruct((heads, rows, 128), bf16),
            jax.ShapeDtypeStruct((heads, rows, 128), bf16),
            jax.ShapeDtypeStruct((heads, rows, 128), bf16),
            jax.ShapeDtypeStruct((rows, width), f32),
        ],
        compiler_params=pltpu.CompilerParams(vmem_limit_bytes=48 * 1024 * 1024),
        name="mixer_forward",
    )(*proj, beta, taps, taps, taps, gain)


def mixer_bwd_kernel(per, q_ref, k_ref, v_ref, beta_ref, taps_q, taps_k, taps_v, gain_ref, t_ref, n_ref, s_ref, o_ref, dm_ref,
                     dq_ref, dk_ref, dv_ref, dbeta_ref, dtq_ref, dtk_ref, dtv_ref, dgain_ref):
    row, col = chunk_masks()
    strict, causal_t = row > col, row <= col
    causal = row >= col
    chunks = q_ref.shape[0] // CHUNK
    beta_all = beta_ref[...]
    step = pl.program_id(0)

    @pl.when(step == 0)
    def _():
        dbeta_ref[...] = jnp.zeros_like(dbeta_ref)
        dgain_ref[...] = jnp.zeros_like(dgain_ref)

    for j in range(per):
        lane = slice(j * 128, (j + 1) * 128)
        head = step * per + j
        beta = head_column(beta_all, head)

        def activated(ref, taps):
            c = convolved(ref[:, lane], taps[:, lane])
            sig = jax.nn.sigmoid(c)
            return c * sig, sig * (1.0 + c * (1.0 - sig))

        q_act, q_slope = activated(q_ref, taps_q)
        k_act, k_slope = activated(k_ref, taps_k)
        v, v_slope = activated(v_ref, taps_v)
        q_scale = lax.rsqrt(jnp.sum(q_act * q_act, 1, keepdims=True) + 1e-6)
        k_scale = lax.rsqrt(jnp.sum(k_act * k_act, 1, keepdims=True) + 1e-6)
        q, k = q_act * q_scale, k_act * k_scale
        o, dm, gain = o_ref[:, lane], dm_ref[:, lane], gain_ref[...]
        o_scale = lax.rsqrt(jnp.mean(o * o, 1, keepdims=True) + 1e-5)
        o_hat = o * o_scale
        dgain_ref[...] += jnp.sum(dm * o_hat, 0, keepdims=True)
        dmg = dm * gain
        do = o_scale * (dmg - o_hat * jnp.mean(dmg * o_hat, 1, keepdims=True))
        cut = lambda x: [x[i * CHUNK : (i + 1) * CHUNK] for i in range(chunks)]
        qs, ks, vs, bs, dos = cut(q), cut(k), cut(v), cut(beta), cut(do)
        dstate = jnp.zeros((128, 128), f32)
        dqs, dks, dvs, dbs = [], [], [], []
        for i in reversed(range(chunks)):
            span = pl.ds(i * CHUNK, CHUNK)
            qc, kc, vc, bc, doc = qs[i], ks[i], vs[i], bs[i], dos[i]
            n, s, t = n_ref[j, span, :], s_ref[j, span, :], t_ref[j, span, :]
            gp = nt(kc, jnp.concatenate([kc, qc], 0))
            g = jnp.where(strict, gp[:, :128], 0.0)
            p_t = jnp.where(causal_t, gp[:, 128:], 0.0)
            dn = nn(jnp.concatenate([p_t, kc], 1), jnp.concatenate([doc, dstate], 0))
            dr = dn + tn(t, dn)
            de = dr * bc
            both = nt(doc, jnp.concatenate([n, s], 0))
            dp = jnp.where(causal, both[:, :128], 0.0)
            dqs.append(both[:, 128:] + nn(dp, kc))
            e = vc - nn(kc, s)
            da = jnp.where(strict, -nt(dr, n), 0.0)
            dbs.append(jnp.sum(dr * e, 1, keepdims=True) + jnp.sum(da * g, 1, keepdims=True))
            dg = da * bc
            dk = tn(dp, qc) + nt(jnp.concatenate([n, -de], 1), jnp.concatenate([dstate, s.astype(f32)], 1)) + nn(dg, kc) + tn(dg, kc)
            dks.append(dk)
            dvs.append(de)
            if i:
                dstate = dstate + tn(qc, doc) - tn(kc, de)
        join = lambda xs: jnp.concatenate(xs[::-1], 0)
        dq, dk, dv, db = join(dqs), join(dks), join(dvs), join(dbs)
        dq = q_scale * (dq - q * jnp.sum(dq * q, 1, keepdims=True))
        dk = k_scale * (dk - k * jnp.sum(dk * k, 1, keepdims=True))
        lanes = lax.broadcasted_iota(jnp.int32, dbeta_ref.shape, 1)
        dbeta_ref[...] += jnp.where(lanes == head, db, 0.0)
        for grad, slope, ref, taps, out, dtaps in (
            (dq, q_slope, q_ref, taps_q, dq_ref, dtq_ref),
            (dk, k_slope, k_ref, taps_k, dk_ref, dtk_ref),
            (dv, v_slope, v_ref, taps_v, dv_ref, dtv_ref),
        ):
            dc = grad * slope
            x = ref[:, lane]
            w = taps[:, lane]
            dx = dc * w[3:4]
            rows = [None] * 4
            rows[3] = jnp.sum(dc * x, 0, keepdims=True)
            for back in range(1, 4):
                moved = shifted_rows(dc, -back)
                dx = dx + moved * w[3 - back : 4 - back]
                rows[3 - back] = jnp.sum(moved * x, 0, keepdims=True)
            out[:, lane] = dx.astype(bf16)
            dtaps[:, lane] = jnp.concatenate(rows, 0)


def mixer_bwd(proj, beta, taps, gain, saved, dmixed, per=2):
    t, n, s, o = saved
    rows, width = proj[0].shape
    heads = width // 128
    steps = heads // per
    wide = 128 * per
    part = pl.BlockSpec((rows, wide), lambda h: (0, h))
    tap = lambda p: pl.BlockSpec((4, wide), lambda h, p=p: (0, p * steps + h))
    whole = lambda a: pl.BlockSpec(a.shape, lambda h: (0,) * len(a.shape))
    kept = pl.BlockSpec((per, rows, 128), lambda h: (h, 0, 0))
    dproj = jax.ShapeDtypeStruct((rows, width), bf16)
    dtap = jax.ShapeDtypeStruct((4, width), f32)
    return pl.pallas_call(
        functools.partial(mixer_bwd_kernel, per),
        grid=(steps,),
        in_specs=[part, part, part, whole(beta), tap(0), tap(1), tap(2), whole(gain), kept, kept, kept, part, part],
        out_specs=[part] * 3 + [whole(beta)] + [tap(0)] * 3 + [whole(gain)],
        out_shape=[dproj] * 3 + [jax.ShapeDtypeStruct(beta.shape, f32)] + [dtap] * 3 + [jax.ShapeDtypeStruct(gain.shape, f32)],
        compiler_params=pltpu.CompilerParams(vmem_limit_bytes=48 * 1024 * 1024),
        name="mixer_backward",
    )(*proj, beta, taps, taps, taps, gain, t, n, s, o, dmixed)


def rms_forward(x, gain):
    scale = lax.rsqrt(jnp.mean(x * x, -1, keepdims=True) + 1e-06)
    return (x * scale * gain).astype(bf16), scale


def rms_backward(x, scale, gain, grad):
    gain_grad = jnp.sum(grad * x * scale, 0)
    inner = jnp.mean(grad * gain * x, -1, keepdims=True)
    return scale * gain * grad - x * scale**3 * inner, gain_grad


def matmul(a, b):
    return jnp.dot(a, b, preferred_element_type=f32)


def matmul_nt(a, b):
    return lax.dot_general(a, b, (((1,), (1,)), ((), ())), preferred_element_type=f32)


def matmul_tn(a, b):
    return lax.dot_general(a, b, (((0,), (0,)), ((), ())), preferred_element_type=f32)


def mixer_forward(u, w, token_mask):
    x = u.astype(f32)
    normed, scale = rms_forward(x, w["attn_gain"])
    proj = [matmul(normed, w["qkv"][p]) for p in range(3)]
    rate = jax.nn.sigmoid(matmul(normed, w["beta"]))
    beta = rate * token_mask
    mixed, *saved = mixer_fwd(proj, beta, w["conv"], w["head_gain"])
    result = (x + matmul(mixed, w["out"])).astype(bf16)
    return result, (u, normed, scale, proj, rate, beta, mixed, saved)


def mixer_input_grad(kept, dy, w, token_mask):
    u, normed, scale, proj, rate, beta, mixed, saved = kept
    dmixed = matmul_nt(dy, w["out"])
    *dproj, dbeta, dtq, dtk, dtv, dhead = mixer_bwd(proj, beta, w["conv"], w["head_gain"], saved, dmixed)
    dlogits = dbeta * token_mask * rate * (1.0 - rate)
    dnormed = sum(matmul_nt(d, w["qkv"][p]) for p, d in enumerate(dproj))
    dnormed = dnormed + matmul_nt(dlogits.astype(bf16), w["beta"])
    dx, dgain = rms_backward(u.astype(f32), scale, w["attn_gain"], dnormed)
    g = (dy.astype(f32) + dx).astype(bf16)
    return g, (dproj, dlogits, jnp.stack([dtq, dtk, dtv], 1), dhead[0], dgain)


def mlp_forward(u, w):
    x = u.astype(f32)
    normed, scale = rms_forward(x, w["mlp_gain"])
    gate, up = matmul(normed, w["gate"]), matmul(normed, w["up"])
    hidden = (jax.nn.silu(gate) * up).astype(bf16)
    result = (x + matmul(hidden, w["down"])).astype(bf16)
    return result, (u, normed, scale, gate, up, hidden)


def mlp_input_grad(kept, dy, w):
    u, normed, scale, gate, up, hidden = kept
    dhidden = matmul_nt(dy, w["down"])
    sig = jax.nn.sigmoid(gate)
    dgate = (dhidden * up * (sig * (1.0 + gate * (1.0 - sig)))).astype(bf16)
    dup = (dhidden * (gate * sig)).astype(bf16)
    dnormed = matmul_nt(dgate, w["gate"]) + matmul_nt(dup, w["up"])
    dx, dgain = rms_backward(u.astype(f32), scale, w["mlp_gain"], dnormed)
    g = (dy.astype(f32) + dx).astype(bf16)
    return g, (dgate, dup, dgain)


def pick(x, index, axis):
    return lax.dynamic_index_in_dim(x, index, axis, keepdims=False)


def shards(inputs, cotangent, lengths, attn_gain, qkv_weight, conv_weight, beta_weight, head_gain, out_weight, mlp_gain, gate_up_weight, down_weight):
    section, sections = lax.axis_index("section"), lax.axis_size("section")
    me, group = lax.axis_index("dp"), lax.axis_size("dp")
    core, stage = section % 2, section // 2
    swap = [(i, i ^ 1) for i in range(sections)]
    to_odd = [(i, i + 1) for i in range(0, sections, 2)]
    to_even = [(i + 1, i) for i in range(0, sections, 2)]
    rows = inputs.shape[2]
    width = inputs.shape[3]

    def from_even(x):
        return jnp.where(core == 0, x, lax.ppermute(x, "section", to_odd))

    def from_odd(x):
        return jnp.where(core == 1, x, lax.ppermute(x, "section", to_even))

    qkv = jnp.moveaxis(qkv_weight[0], 1, 0)
    w = {
        "attn_gain": from_even(attn_gain)[0].astype(f32),
        "conv": from_even(jnp.moveaxis(conv_weight[0], 1, 0)).astype(f32),
        "beta": from_even(beta_weight[0]),
        "head_gain": from_even(head_gain).astype(f32),
        "qkv": [from_even(qkv[p]) for p in range(3)],
        "out": from_even(out_weight[0]),
        "mlp_gain": from_odd(mlp_gain)[0].astype(f32),
        "gate": from_odd(gate_up_weight[0, :, 0]),
        "up": from_odd(gate_up_weight[0, :, 1]),
        "down": from_odd(down_weight[0]),
    }
    w["conv"] = jnp.moveaxis(w["conv"], 0, 1).reshape(-1, 3 * width)

    first = pick(inputs[:, 0], core, 0)
    seed = pick(cotangent[:, 0], core, 0)
    length = pick(lengths[:, 0], core, 0)
    token_mask = (jnp.arange(rows) < length).astype(f32)[:, None]
    up_stage = [(i, i + 2) for i in range(sections - 2)]
    down_stage = [(i + 2, i) for i in range(sections - 2)]

    u0 = first
    for step in range(sections // 2):
        u1, kept_mixer = mixer_forward(u0, w, token_mask)
        u2, kept_mlp = mlp_forward(u1, w)
        if step + 1 < sections // 2:
            u0 = jnp.where(stage == 0, first, lax.ppermute(u2, "section", up_stage))
    last_stage = sections // 2 - 1
    dy = seed
    for step in range(sections // 2):
        g1, mlp_parts = mlp_input_grad(kept_mlp, dy, w)
        g0, mixer_parts = mixer_input_grad(kept_mixer, g1, w, token_mask)
        if step + 1 < sections // 2:
            dy = jnp.where(stage == last_stage, seed, lax.ppermute(g0, "section", down_stage))

    _, normed1, _, _, _, _, mixed, _ = kept_mixer
    _, normed2, _, _, _, hidden = kept_mlp
    dgate, dup, d_mlp_gain = mlp_parts
    dproj, dlogits, dtaps, dhead, d_attn_gain = mixer_parts

    def halve(x):
        kept = pick(x, core, 1).astype(f32)
        x = (kept + lax.ppermute(pick(x, 1 - core, 1), "section", swap).astype(f32)).astype(bf16)
        return scatter(x)

    def scatter(x):
        kind = x.dtype
        bit = 1
        while bit < group:
            pairs = [(i, i ^ bit) for i in range(group)]
            mine = (me // bit) % 2
            x = x.reshape((x.shape[0] // 2, 2) + x.shape[1:])
            other = lax.ppermute(pick(x, 1 - mine, 1), "dp", pairs)
            x = pick(x, mine, 1).astype(f32) + other.astype(f32)
            bit *= 2
            if bit < group:
                x = x.astype(kind)
        return x[0]

    def share(grad):
        count, cols = grad.shape
        return halve(grad.astype(bf16).reshape(group, 2, count // group // 2, cols))

    down_share = share(matmul_tn(hidden, dy))
    gate_share = share(matmul_tn(normed2, dgate))
    up_share = share(matmul_tn(normed2, dup))
    out_share = share(matmul_tn(mixed, g1))
    qkv_share = [share(matmul_tn(normed1, d)) for d in dproj]
    dbeta = lax.dot_general(normed1.astype(f32), dlogits, (((0,), (0,)), ((), ())), precision=lax.Precision.HIGHEST)
    taps_rows = jnp.moveaxis(dtaps.reshape(-1, 3, group, width // group), 2, 0).reshape(group, -1)
    small = [d_attn_gain.reshape(group, -1), taps_rows, dbeta.reshape(group, -1), dhead.reshape(group, -1), d_mlp_gain.reshape(group, -1)]
    sizes = [a.shape[1] for a in small]
    joined = jnp.concatenate(small, 1)
    small = scatter(joined + lax.ppermute(joined, "section", swap))
    offsets = [sum(sizes[:i]) for i in range(len(sizes) + 1)]
    s_attn, s_taps, s_beta, s_head, s_mlp = [small[a:b] for a, b in zip(offsets, offsets[1:])]

    def to_core(x, target):
        other = lax.ppermute(x, "section", to_even if target == 0 else to_odd)
        both = jnp.concatenate([x, other] if target == 0 else [other, x], 0)
        return jnp.where(core == target, both, 0.0)

    on_even = lambda x: jnp.where(core == 0, x, 0.0)
    on_odd = lambda x: jnp.where(core == 1, x, 0.0)
    grad_qkv = jnp.stack([to_core(x, 0) for x in qkv_share], 1)
    grad_out = to_core(out_share, 0)
    grad_gate_up = jnp.stack([to_core(gate_share, 1), to_core(up_share, 1)], 1)
    grad_down = to_core(down_share, 1)

    def both_micro(mixer_side, mlp_side):
        own = jnp.where(core == 0, mixer_side, mlp_side)
        other = lax.ppermute(jnp.where(core == 0, mlp_side, mixer_side), "section", swap)
        return jnp.where(core == 0, jnp.stack([own, other]), jnp.stack([other, own]))[None, :, None]

    return (
        both_micro(u1, u2),
        both_micro(g0, g1),
        on_even(s_attn)[None],
        grad_qkv[None],
        on_even(s_taps).reshape(1, -1, 3, width // group),
        on_even(s_beta).reshape(1, -1, dbeta.shape[1]),
        on_even(s_head)[None],
        grad_out[None],
        on_odd(s_mlp)[None],
        grad_gate_up[None],
        grad_down[None],
    )


def solution(mesh):
    in_specs = (
        P(None, "dp", None, None),
        P(None, "dp", None, None),
        P(None, "dp"),
        P("section", None),
        P("section", None, None, None),
        P("section", None, None, None),
        P("section", None, None),
        P("section", None),
        P("section", None, None),
        P("section", None),
        P("section", None, None, None),
        P("section", None, None),
    )
    out_specs = (
        P("section", None, "dp", None, None),
        P("section", None, "dp", None, None),
        P("section", "dp"),
        P("section", "dp", None, None),
        P("section", None, None, "dp"),
        P("section", "dp", None),
        P("section", "dp"),
        P("section", "dp", None),
        P("section", "dp"),
        P("section", "dp", None, None),
        P("section", "dp", None),
    )
    return jax.shard_map(shards, mesh=mesh, in_specs=in_specs, out_specs=out_specs, check_vma=False)
```

```python
import functools

import jax, jax.numpy as jnp
from jax import lax
from jax.experimental import pallas as pl
from jax.experimental.pallas import tpu as pltpu
from jax.sharding import PartitionSpec as P

CHUNK = 128
bf16, f32 = jnp.bfloat16, jnp.float32


def nn(a, b):
    return lax.dot_general(a.astype(bf16), b.astype(bf16), (((1,), (0,)), ((), ())), preferred_element_type=f32)


def nt(a, b):
    return lax.dot_general(a.astype(bf16), b.astype(bf16), (((1,), (1,)), ((), ())), preferred_element_type=f32)


def tn(a, b):
    return lax.dot_general(a.astype(bf16), b.astype(bf16), (((0,), (0,)), ((), ())), preferred_element_type=f32)


def shifted_rows(x, steps):
    rows = lax.broadcasted_iota(jnp.int32, x.shape, 0)
    count = x.shape[0]
    if steps > 0:
        return jnp.where(rows >= steps, pltpu.roll(x, steps, 0), 0.0)
    return jnp.where(rows < count + steps, pltpu.roll(x, count + steps, 0), 0.0)


def convolved(x, taps):
    total = x * taps[3:4]
    for back in range(1, 4):
        total = total + shifted_rows(x, back) * taps[3 - back : 4 - back]
    return total


def chunk_masks():
    row = lax.broadcasted_iota(jnp.int32, (CHUNK, CHUNK), 0)
    col = lax.broadcasted_iota(jnp.int32, (CHUNK, CHUNK), 1)
    return row, col


def level_mask(row, col, size):
    shift = size.bit_length() - 1
    same = (row >> (shift + 1)) == (col >> (shift + 1))
    return same & (((row >> shift) & 1) == 1) & (((col >> shift) & 1) == 0)


def triangular_inverse(a_list, row, col):
    mask = level_mask(row, col, 1)
    xs = [jnp.where(mask, -a, 0.0) for a in a_list]
    size = 2
    while size < CHUNK:
        mask = level_mask(row, col, size)
        parts = [jnp.where(mask, a, 0.0) for a in a_list]
        ys = [p + nn(p, x) for p, x in zip(parts, xs)]
        xs = [x - (y + nn(x, y)) for x, y in zip(xs, ys)]
        size *= 2
    return xs


def head_column(block, head):
    lanes = lax.broadcasted_iota(jnp.int32, block.shape, 1)
    return jnp.sum(jnp.where(lanes == head, block, 0.0), axis=1, keepdims=True)


def mixer_fwd_kernel(per, q_ref, k_ref, v_ref, beta_ref, taps_q, taps_k, taps_v, gain_ref, mixed_ref, t_ref, n_ref, s_ref, o_ref):
    row, col = chunk_masks()
    strict, causal = row > col, row >= col
    chunks = q_ref.shape[0] // CHUNK
    beta_all = beta_ref[...]
    for j in range(per):
        lane = slice(j * 128, (j + 1) * 128)
        head = pl.program_id(0) * per + j
        beta = head_column(beta_all, head)

        def activated(ref, taps):
            c = convolved(ref[:, lane], taps[:, lane])
            return c * jax.nn.sigmoid(c)

        q, k, v = activated(q_ref, taps_q), activated(k_ref, taps_k), activated(v_ref, taps_v)
        q = q * lax.rsqrt(jnp.sum(q * q, 1, keepdims=True) + 1e-6)
        k = k * lax.rsqrt(jnp.sum(k * k, 1, keepdims=True) + 1e-6)
        cut = lambda x: [x[i * CHUNK : (i + 1) * CHUNK] for i in range(chunks)]
        qs, ks, vs, bs = cut(q), cut(k), cut(v), cut(beta)
        a_list = [jnp.where(strict, nt(kc, kc) * bc, 0.0) for kc, bc in zip(ks, bs)]
        ps = [jnp.where(causal, nt(qc, kc), 0.0) for qc, kc in zip(qs, ks)]
        ts = triangular_inverse(a_list, row, col)
        wu = []
        for kc, vc, bc, t in zip(ks, vs, bs, ts):
            both = jnp.concatenate([kc * bc, vc * bc], 1)
            wu.append(both + nn(t, both))
        state = jnp.zeros((128, 128), f32)
        outs = []
        for i in range(chunks):
            n = wu[i][:, 128:] - nn(wu[i][:, :128], state)
            o = nn(jnp.concatenate([qs[i], ps[i]], 1), jnp.concatenate([state, n], 0))
            span = pl.ds(i * CHUNK, CHUNK)
            s_ref[j, span, :] = state.astype(bf16)
            n_ref[j, span, :] = n.astype(bf16)
            t_ref[j, span, :] = ts[i].astype(bf16)
            o_ref[span, lane] = o
            mixed_ref[span, lane] = (o * lax.rsqrt(jnp.mean(o * o, 1, keepdims=True) + 1e-5) * gain_ref[...]).astype(bf16)
            if i + 1 < chunks:
                state = state + tn(ks[i], n)


def mixer_fwd(proj, beta, taps, gain, per=2):
    rows, width = proj[0].shape
    heads = width // 128
    steps = heads // per
    wide = 128 * per
    part = pl.BlockSpec((rows, wide), lambda h: (0, h))
    tap = lambda p: pl.BlockSpec((4, wide), lambda h, p=p: (0, p * steps + h))
    whole = lambda a: pl.BlockSpec(a.shape, lambda h: (0,) * a.ndim)
    saved = pl.BlockSpec((per, rows, 128), lambda h: (h, 0, 0))
    return pl.pallas_call(
        functools.partial(mixer_fwd_kernel, per),
        grid=(steps,),
        in_specs=[part, part, part, whole(beta), tap(0), tap(1), tap(2), whole(gain)],
        out_specs=[part, saved, saved, saved, part],
        out_shape=[
            jax.ShapeDtypeStruct((rows, width), bf16),
            jax.ShapeDtypeStruct((heads, rows, 128), bf16),
            jax.ShapeDtypeStruct((heads, rows, 128), bf16),
            jax.ShapeDtypeStruct((heads, rows, 128), bf16),
            jax.ShapeDtypeStruct((rows, width), f32),
        ],
        compiler_params=pltpu.CompilerParams(vmem_limit_bytes=48 * 1024 * 1024),
        name="mixer_forward",
    )(*proj, beta, taps, taps, taps, gain)


def mixer_bwd_kernel(per, q_ref, k_ref, v_ref, beta_ref, taps_q, taps_k, taps_v, gain_ref, t_ref, n_ref, s_ref, o_ref, dm_ref,
                     dq_ref, dk_ref, dv_ref, dbeta_ref, dtq_ref, dtk_ref, dtv_ref, dgain_ref):
    row, col = chunk_masks()
    strict, causal_t = row > col, row <= col
    causal = row >= col
    chunks = q_ref.shape[0] // CHUNK
    beta_all = beta_ref[...]
    step = pl.program_id(0)

    @pl.when(step == 0)
    def _():
        dbeta_ref[...] = jnp.zeros_like(dbeta_ref)
        dgain_ref[...] = jnp.zeros_like(dgain_ref)

    for j in range(per):
        lane = slice(j * 128, (j + 1) * 128)
        head = step * per + j
        beta = head_column(beta_all, head)

        def activated(ref, taps):
            c = convolved(ref[:, lane], taps[:, lane])
            sig = jax.nn.sigmoid(c)
            return c * sig, sig * (1.0 + c * (1.0 - sig))

        q_act, q_slope = activated(q_ref, taps_q)
        k_act, k_slope = activated(k_ref, taps_k)
        v, v_slope = activated(v_ref, taps_v)
        q_scale = lax.rsqrt(jnp.sum(q_act * q_act, 1, keepdims=True) + 1e-6)
        k_scale = lax.rsqrt(jnp.sum(k_act * k_act, 1, keepdims=True) + 1e-6)
        q, k = q_act * q_scale, k_act * k_scale
        o, dm, gain = o_ref[:, lane], dm_ref[:, lane], gain_ref[...]
        o_scale = lax.rsqrt(jnp.mean(o * o, 1, keepdims=True) + 1e-5)
        o_hat = o * o_scale
        dgain_ref[...] += jnp.sum(dm * o_hat, 0, keepdims=True)
        dmg = dm * gain
        do = o_scale * (dmg - o_hat * jnp.mean(dmg * o_hat, 1, keepdims=True))
        cut = lambda x: [x[i * CHUNK : (i + 1) * CHUNK] for i in range(chunks)]
        qs, ks, vs, bs, dos = cut(q), cut(k), cut(v), cut(beta), cut(do)
        dstate = jnp.zeros((128, 128), f32)
        dqs, dks, dvs, dbs = [], [], [], []
        for i in reversed(range(chunks)):
            span = pl.ds(i * CHUNK, CHUNK)
            qc, kc, vc, bc, doc = qs[i], ks[i], vs[i], bs[i], dos[i]
            n, s, t = n_ref[j, span, :], s_ref[j, span, :], t_ref[j, span, :]
            gp = nt(kc, jnp.concatenate([kc, qc], 0))
            g = jnp.where(strict, gp[:, :128], 0.0)
            p_t = jnp.where(causal_t, gp[:, 128:], 0.0)
            dn = nn(jnp.concatenate([p_t, kc], 1), jnp.concatenate([doc, dstate], 0))
            dr = dn + tn(t, dn)
            de = dr * bc
            both = nt(doc, jnp.concatenate([n, s], 0))
            dp = jnp.where(causal, both[:, :128], 0.0)
            dqs.append(both[:, 128:] + nn(dp, kc))
            e = vc - nn(kc, s)
            da = jnp.where(strict, -nt(dr, n), 0.0)
            dbs.append(jnp.sum(dr * e, 1, keepdims=True) + jnp.sum(da * g, 1, keepdims=True))
            dg = da * bc
            dk = tn(dp, qc) + nt(jnp.concatenate([n, -de], 1), jnp.concatenate([dstate, s.astype(f32)], 1)) + nn(dg, kc) + tn(dg, kc)
            dks.append(dk)
            dvs.append(de)
            if i:
                dstate = dstate + tn(qc, doc) - tn(kc, de)
        join = lambda xs: jnp.concatenate(xs[::-1], 0)
        dq, dk, dv, db = join(dqs), join(dks), join(dvs), join(dbs)
        dq = q_scale * (dq - q * jnp.sum(dq * q, 1, keepdims=True))
        dk = k_scale * (dk - k * jnp.sum(dk * k, 1, keepdims=True))
        lanes = lax.broadcasted_iota(jnp.int32, dbeta_ref.shape, 1)
        dbeta_ref[...] += jnp.where(lanes == head, db, 0.0)
        for grad, slope, ref, taps, out, dtaps in (
            (dq, q_slope, q_ref, taps_q, dq_ref, dtq_ref),
            (dk, k_slope, k_ref, taps_k, dk_ref, dtk_ref),
            (dv, v_slope, v_ref, taps_v, dv_ref, dtv_ref),
        ):
            dc = grad * slope
            x = ref[:, lane]
            w = taps[:, lane]
            dx = dc * w[3:4]
            rows = [None] * 4
            rows[3] = jnp.sum(dc * x, 0, keepdims=True)
            for back in range(1, 4):
                moved = shifted_rows(dc, -back)
                dx = dx + moved * w[3 - back : 4 - back]
                rows[3 - back] = jnp.sum(moved * x, 0, keepdims=True)
            out[:, lane] = dx.astype(bf16)
            dtaps[:, lane] = jnp.concatenate(rows, 0)


def mixer_bwd(proj, beta, taps, gain, saved, dmixed, per=2):
    t, n, s, o = saved
    rows, width = proj[0].shape
    heads = width // 128
    steps = heads // per
    wide = 128 * per
    part = pl.BlockSpec((rows, wide), lambda h: (0, h))
    tap = lambda p: pl.BlockSpec((4, wide), lambda h, p=p: (0, p * steps + h))
    whole = lambda a: pl.BlockSpec(a.shape, lambda h: (0,) * len(a.shape))
    kept = pl.BlockSpec((per, rows, 128), lambda h: (h, 0, 0))
    dproj = jax.ShapeDtypeStruct((rows, width), bf16)
    dtap = jax.ShapeDtypeStruct((4, width), f32)
    return pl.pallas_call(
        functools.partial(mixer_bwd_kernel, per),
        grid=(steps,),
        in_specs=[part, part, part, whole(beta), tap(0), tap(1), tap(2), whole(gain), kept, kept, kept, part, part],
        out_specs=[part] * 3 + [whole(beta)] + [tap(0)] * 3 + [whole(gain)],
        out_shape=[dproj] * 3 + [jax.ShapeDtypeStruct(beta.shape, f32)] + [dtap] * 3 + [jax.ShapeDtypeStruct(gain.shape, f32)],
        compiler_params=pltpu.CompilerParams(vmem_limit_bytes=48 * 1024 * 1024),
        name="mixer_backward",
    )(*proj, beta, taps, taps, taps, gain, t, n, s, o, dmixed)


PIECE = (64, 256)
SLOTS = 4
MESH = pl.DeviceIdType.MESH


def sum_kernel(total, n2_ref, n1_ref, m_ref, h_ref, dgate, dup, dy, dq, dk, dv, g1, small, out,
               own, send, rc, rx, ry, rz, send_sem, xs_sem, ys_sem, zs_sem, rc_sem, rx_sem, ry_sem, rz_sem):
    section, me = lax.axis_index("section"), lax.axis_index("dp")
    core, x, low, high = lax.rem(section, 2), lax.rem(me, 2), lax.rem(me // 2, 2), me // 4
    far_core = {"section": section + 1 - 2 * core}
    far_x, far_low, far_high = {"dp": me + 1 - 2 * x}, {"dp": me + 2 - 4 * low}, {"dp": me + 4 - 8 * high}
    barrier = pltpu.get_barrier_semaphore()
    for other in (far_core, far_x, far_low, far_high):
        pl.semaphore_signal(barrier, inc=1, device_id=other, device_id_type=MESH)
    pl.semaphore_wait(barrier, 4)

    def remote(src, dst, sent, got, other):
        return pltpu.make_async_remote_copy(src_ref=src, dst_ref=dst, send_sem=sent, recv_sem=got, device_id=other, device_id_type=MESH)

    def slot(t):
        return lax.rem(t, SLOTS)

    def core_copy(t):
        return remote(send.at[slot(t)], rc.at[t], send_sem.at[slot(t)], rc_sem.at[t], far_core)

    def x_copy(t):
        return remote(rc.at[t, :, :, 1 - x], rx.at[t], xs_sem.at[slot(t)], rx_sem.at[t], far_x)

    def low_copy(t):
        return remote(rx.at[t, :, 1 - low], ry.at[t], ys_sem.at[slot(t)], ry_sem.at[t], far_low)

    def high_copy(t):
        return remote(ry.at[t, 1 - high], rz.at[t], zs_sem.at[slot(t)], rz_sem.at[t], far_high)

    def begin(copy, t):
        @pl.when(t >= SLOTS)
        def _():
            copy(t - SLOTS).wait_send()

        copy(t).start()

    def after_core(t):
        core_copy(t).wait_recv()
        rc[t] = rc[t] + own[slot(t)]
        begin(x_copy, t)

    def after_x(t):
        x_copy(t).wait_recv()
        rx[t] = rx[t] + rc[t, :, :, x]
        begin(low_copy, t)

    def after_low(t):
        low_copy(t).wait_recv()
        ry[t] = ry[t] + rx[t, :, low]
        begin(high_copy, t)

    def after_high(t):
        high_copy(t).wait_recv()
        out[t] = rz[t].astype(f32) + ry[t, high].astype(f32)

    def later(t):
        for step, lag in ((after_core, 1), (after_x, 3), (after_low, 5), (after_high, 7)):
            @pl.when((t >= lag) & (t < total + lag))
            def _():
                step(t - lag)

    def span(t, base):
        return pl.ds(pl.multiple_of((t - base) * PIECE[1], PIECE[1]), PIECE[1])

    def by_columns(lhs, rhs, base):
        def fill(t):
            block = rhs[:, span(t, base)]
            for which, into in ((1 - core, send), (core, own)):
                part = nn(lhs[which], block).astype(bf16)
                into[slot(t)] = part.reshape(own.shape[1:])
        return fill

    def by_rows(base):
        def fill(t):
            for which, into in ((1 - core, send), (core, own)):
                part = nn(h_ref[t - base, which], dy[...]).astype(bf16)
                count = part.shape[0] // 8
                for d in range(8):
                    for c in range(PIECE[0] // count):
                        into[slot(t), d // 4, d // 2 % 2, d % 2, c * count : (c + 1) * count, :] = part[d * count : (d + 1) * count, c * PIECE[1] : (c + 1) * PIECE[1]]
        return fill

    def given(t):
        send[slot(t)] = small[1 - core]
        own[slot(t)] = small[core]

    base = 0
    for make, refs, count in (
        (by_columns, (n2_ref, dgate), dgate.shape[1] // PIECE[1]),
        (by_columns, (n2_ref, dup), dup.shape[1] // PIECE[1]),
        (by_rows, (), h_ref.shape[0]),
        (by_columns, (n1_ref, dq), dq.shape[1] // PIECE[1]),
        (by_columns, (n1_ref, dk), dk.shape[1] // PIECE[1]),
        (by_columns, (n1_ref, dv), dv.shape[1] // PIECE[1]),
        (by_columns, (m_ref, g1), g1.shape[1] // PIECE[1]),
        (None, (), 1),
    ):
        fill = make(*refs, base) if make else given

        def body(t, carry, fill=fill):
            @pl.when(t >= SLOTS)
            def _():
                core_copy(t - SLOTS).wait_send()

            fill(t)
            core_copy(t).start()
            later(t)
            return carry

        lax.fori_loop(base, base + count, body, 0)
        base += count

    def drain(t, carry):
        later(t)
        return carry

    lax.fori_loop(total, total + 7, drain, 0)
    for copy in (core_copy, x_copy, low_copy, high_copy):
        for t in range(total - SLOTS, total):
            copy(jnp.int32(t)).wait_send()


def summed_gradients(n2, n1, m, h, dgate, dup, dy, dq, dk, dv, g1, small):
    total = (2 * dgate.shape[1] + 4 * dq.shape[1]) // PIECE[1] + h.shape[0] + 1
    piece = PIECE
    buffer = lambda *lead: pltpu.VMEM(lead + piece, bf16)
    dma = lambda n: pltpu.SemaphoreType.DMA((n,))
    operands = (n2, n1, m, h, dgate, dup, dy, dq, dk, dv, g1, small)
    return pl.pallas_call(
        functools.partial(sum_kernel, total),
        out_shape=jax.ShapeDtypeStruct((total,) + piece, f32),
        in_specs=[pl.BlockSpec(memory_space=pltpu.VMEM)] * len(operands),
        out_specs=pl.BlockSpec(memory_space=pltpu.VMEM),
        scratch_shapes=[
            buffer(SLOTS, 2, 2, 2), buffer(SLOTS, 2, 2, 2), buffer(total, 2, 2, 2), buffer(total, 2, 2), buffer(total, 2), buffer(total),
            dma(SLOTS), dma(SLOTS), dma(SLOTS), dma(SLOTS), dma(total), dma(total), dma(total), dma(total),
        ],
        compiler_params=pltpu.CompilerParams(collective_id=0, has_side_effects=True, vmem_limit_bytes=60 * 1024 * 1024),
        name="gradient_sums",
    )(*operands)


def rms_forward(x, gain):
    scale = lax.rsqrt(jnp.mean(x * x, -1, keepdims=True) + 1e-06)
    return (x * scale * gain).astype(bf16), scale


def rms_backward(x, scale, gain, grad):
    gain_grad = jnp.sum(grad * x * scale, 0)
    inner = jnp.mean(grad * gain * x, -1, keepdims=True)
    return scale * gain * grad - x * scale**3 * inner, gain_grad


def matmul(a, b):
    return jnp.dot(a, b, preferred_element_type=f32)


def matmul_nt(a, b):
    return lax.dot_general(a, b, (((1,), (1,)), ((), ())), preferred_element_type=f32)


def matmul_tn(a, b):
    return lax.dot_general(a, b, (((0,), (0,)), ((), ())), preferred_element_type=f32)


def mixer_forward(u, w, token_mask):
    x = u.astype(f32)
    normed, scale = rms_forward(x, w["attn_gain"])
    proj = [matmul(normed, w["qkv"][p]) for p in range(3)]
    rate = jax.nn.sigmoid(matmul(normed, w["beta"]))
    beta = rate * token_mask
    mixed, *saved = mixer_fwd(proj, beta, w["conv"], w["head_gain"])
    result = (x + matmul(mixed, w["out"])).astype(bf16)
    return result, (u, normed, scale, proj, rate, beta, mixed, saved)


def mixer_input_grad(kept, dy, w, token_mask):
    u, normed, scale, proj, rate, beta, mixed, saved = kept
    dmixed = matmul_nt(dy, w["out"])
    *dproj, dbeta, dtq, dtk, dtv, dhead = mixer_bwd(proj, beta, w["conv"], w["head_gain"], saved, dmixed)
    dlogits = dbeta * token_mask * rate * (1.0 - rate)
    dnormed = sum(matmul_nt(d, w["qkv"][p]) for p, d in enumerate(dproj))
    dnormed = dnormed + matmul_nt(dlogits.astype(bf16), w["beta"])
    dx, dgain = rms_backward(u.astype(f32), scale, w["attn_gain"], dnormed)
    g = (dy.astype(f32) + dx).astype(bf16)
    return g, (dproj, dlogits, jnp.stack([dtq, dtk, dtv], 1), dhead[0], dgain)


def mlp_forward(u, w):
    x = u.astype(f32)
    normed, scale = rms_forward(x, w["mlp_gain"])
    gate, up = matmul(normed, w["gate"]), matmul(normed, w["up"])
    hidden = (jax.nn.silu(gate) * up).astype(bf16)
    result = (x + matmul(hidden, w["down"])).astype(bf16)
    return result, (u, normed, scale, gate, up, hidden)


def mlp_input_grad(kept, dy, w):
    u, normed, scale, gate, up, hidden = kept
    dhidden = matmul_nt(dy, w["down"])
    sig = jax.nn.sigmoid(gate)
    dgate = (dhidden * up * (sig * (1.0 + gate * (1.0 - sig)))).astype(bf16)
    dup = (dhidden * (gate * sig)).astype(bf16)
    dnormed = matmul_nt(dgate, w["gate"]) + matmul_nt(dup, w["up"])
    dx, dgain = rms_backward(u.astype(f32), scale, w["mlp_gain"], dnormed)
    g = (dy.astype(f32) + dx).astype(bf16)
    return g, (dgate, dup, dgain)


def pick(x, index, axis):
    return lax.dynamic_index_in_dim(x, index, axis, keepdims=False)


def shards(inputs, cotangent, lengths, attn_gain, qkv_weight, conv_weight, beta_weight, head_gain, out_weight, mlp_gain, gate_up_weight, down_weight):
    section, sections = lax.axis_index("section"), lax.axis_size("section")
    me, group = lax.axis_index("dp"), lax.axis_size("dp")
    core, stage = section % 2, section // 2
    swap = [(i, i ^ 1) for i in range(sections)]
    to_odd = [(i, i + 1) for i in range(0, sections, 2)]
    to_even = [(i + 1, i) for i in range(0, sections, 2)]
    rows = inputs.shape[2]
    width = inputs.shape[3]

    def from_even(x):
        return jnp.where(core == 0, x, lax.ppermute(x, "section", to_odd))

    def from_odd(x):
        return jnp.where(core == 1, x, lax.ppermute(x, "section", to_even))

    qkv = jnp.moveaxis(qkv_weight[0], 1, 0)
    w = {
        "attn_gain": from_even(attn_gain)[0].astype(f32),
        "conv": from_even(jnp.moveaxis(conv_weight[0], 1, 0)).astype(f32),
        "beta": from_even(beta_weight[0]),
        "head_gain": from_even(head_gain).astype(f32),
        "qkv": [from_even(qkv[p]) for p in range(3)],
        "out": from_even(out_weight[0]),
        "mlp_gain": from_odd(mlp_gain)[0].astype(f32),
        "gate": from_odd(gate_up_weight[0, :, 0]),
        "up": from_odd(gate_up_weight[0, :, 1]),
        "down": from_odd(down_weight[0]),
    }
    w["conv"] = jnp.moveaxis(w["conv"], 0, 1).reshape(-1, 3 * width)

    first = pick(inputs[:, 0], core, 0)
    seed = pick(cotangent[:, 0], core, 0)
    length = pick(lengths[:, 0], core, 0)
    token_mask = (jnp.arange(rows) < length).astype(f32)[:, None]
    up_stage = [(i, i + 2) for i in range(sections - 2)]
    down_stage = [(i + 2, i) for i in range(sections - 2)]

    u0 = first
    for step in range(sections // 2):
        u1, kept_mixer = mixer_forward(u0, w, token_mask)
        u2, kept_mlp = mlp_forward(u1, w)
        if step + 1 < sections // 2:
            u0 = jnp.where(stage == 0, first, lax.ppermute(u2, "section", up_stage))
    last_stage = sections // 2 - 1
    dy = seed
    for step in range(sections // 2):
        g1, mlp_parts = mlp_input_grad(kept_mlp, dy, w)
        g0, mixer_parts = mixer_input_grad(kept_mixer, g1, w, token_mask)
        if step + 1 < sections // 2:
            dy = jnp.where(stage == last_stage, seed, lax.ppermute(g0, "section", down_stage))

    _, normed1, _, _, _, _, mixed, _ = kept_mixer
    _, normed2, _, _, _, hidden = kept_mlp
    dgate, dup, d_mlp_gain = mlp_parts
    dproj, dlogits, dtaps, dhead, d_attn_gain = mixer_parts

    def halve(x):
        kept = pick(x, core, 1).astype(f32)
        x = (kept + lax.ppermute(pick(x, 1 - core, 1), "section", swap).astype(f32)).astype(bf16)
        return scatter(x)

    def scatter(x):
        kind = x.dtype
        bit = 1
        while bit < group:
            pairs = [(i, i ^ bit) for i in range(group)]
            mine = (me // bit) % 2
            x = x.reshape((x.shape[0] // 2, 2) + x.shape[1:])
            other = lax.ppermute(pick(x, 1 - mine, 1), "dp", pairs)
            x = pick(x, mine, 1).astype(f32) + other.astype(f32)
            bit *= 2
            if bit < group:
                x = x.astype(kind)
        return x[0]

    def share(grad):
        count, cols = grad.shape
        return halve(grad.astype(bf16).reshape(group, 2, count // group // 2, cols))

    dbeta = lax.dot_general(normed1.astype(f32), dlogits, (((0,), (0,)), ((), ())), precision=lax.Precision.HIGHEST)
    taps_rows = jnp.moveaxis(dtaps.reshape(-1, 3, group, width // group), 2, 0).reshape(group, -1)
    small = [d_attn_gain.reshape(group, -1), taps_rows, dbeta.reshape(group, -1), dhead.reshape(group, -1), d_mlp_gain.reshape(group, -1)]
    sizes = [a.shape[1] for a in small]
    joined = jnp.concatenate(small, 1)
    ff = dgate.shape[1]
    if group == 8 and width == 1024 and ff % 256 == 0:
        by_owner = lambda a: a.reshape(rows, group, 2, 64).transpose(2, 1, 3, 0).reshape(2, group * 64, rows)
        down_rows = hidden.reshape(rows, group, 2, ff // 256, 16).transpose(3, 2, 1, 4, 0).reshape(ff // 256, 2, group * 16, rows)
        per = PIECE[0] * PIECE[1]
        low_small = jnp.pad(joined, ((0, 0), (0, per - joined.shape[1]))).astype(bf16).reshape(1, 2, 2, 2, *PIECE)
        low_small = jnp.concatenate([low_small, jnp.zeros_like(low_small)], 0)
        sums = summed_gradients(by_owner(normed2), by_owner(normed1), by_owner(mixed), down_rows, dgate, dup, dy, *dproj, g1, low_small)
        cuts = [0]
        for count in (ff // 256, ff // 256, ff // 256, 4, 4, 4, 4, 1):
            cuts.append(cuts[-1] + count)
        parts = [sums[a:b] for a, b in zip(cuts, cuts[1:])]
        wide = lambda a: a.transpose(1, 0, 2).reshape(PIECE[0], -1)
        gate_share, up_share = wide(parts[0]), wide(parts[1])
        down_share = parts[2].reshape(-1, 4, 16, 256).transpose(0, 2, 1, 3).reshape(-1, width)
        qkv_share = [wide(a) for a in parts[3:6]]
        out_share = wide(parts[6])
        flat = parts[7].reshape(-1)
        flat = jnp.where(core == 0, flat, lax.ppermute(flat, "section", to_odd))
        small = flat[: joined.shape[1]]
    else:
        down_share = share(matmul_tn(hidden, dy))
        gate_share = share(matmul_tn(normed2, dgate))
        up_share = share(matmul_tn(normed2, dup))
        out_share = share(matmul_tn(mixed, g1))
        qkv_share = [share(matmul_tn(normed1, d)) for d in dproj]
        small = scatter(joined + lax.ppermute(joined, "section", swap))
    offsets = [sum(sizes[:i]) for i in range(len(sizes) + 1)]
    s_attn, s_taps, s_beta, s_head, s_mlp = [small[a:b] for a, b in zip(offsets, offsets[1:])]

    def to_core(x, target):
        other = lax.ppermute(x, "section", to_even if target == 0 else to_odd)
        both = jnp.concatenate([x, other] if target == 0 else [other, x], 0)
        return jnp.where(core == target, both, 0.0)

    on_even = lambda x: jnp.where(core == 0, x, 0.0)
    on_odd = lambda x: jnp.where(core == 1, x, 0.0)
    grad_qkv = jnp.stack([to_core(x, 0) for x in qkv_share], 1)
    grad_out = to_core(out_share, 0)
    grad_gate_up = jnp.stack([to_core(gate_share, 1), to_core(up_share, 1)], 1)
    grad_down = to_core(down_share, 1)

    def both_micro(mixer_side, mlp_side):
        own = jnp.where(core == 0, mixer_side, mlp_side)
        other = lax.ppermute(jnp.where(core == 0, mlp_side, mixer_side), "section", swap)
        return jnp.where(core == 0, jnp.stack([own, other]), jnp.stack([other, own]))[None, :, None]

    return (
        both_micro(u1, u2),
        both_micro(g0, g1),
        on_even(s_attn)[None],
        grad_qkv[None],
        on_even(s_taps).reshape(1, -1, 3, width // group),
        on_even(s_beta).reshape(1, -1, dbeta.shape[1]),
        on_even(s_head)[None],
        grad_out[None],
        on_odd(s_mlp)[None],
        grad_gate_up[None],
        grad_down[None],
    )


def solution(mesh):
    in_specs = (
        P(None, "dp", None, None),
        P(None, "dp", None, None),
        P(None, "dp"),
        P("section", None),
        P("section", None, None, None),
        P("section", None, None, None),
        P("section", None, None),
        P("section", None),
        P("section", None, None),
        P("section", None),
        P("section", None, None, None),
        P("section", None, None),
    )
    out_specs = (
        P("section", None, "dp", None, None),
        P("section", None, "dp", None, None),
        P("section", "dp"),
        P("section", "dp", None, None),
        P("section", None, None, "dp"),
        P("section", "dp", None),
        P("section", "dp"),
        P("section", "dp", None),
        P("section", "dp"),
        P("section", "dp", None, None),
        P("section", "dp", None),
    )
    return jax.shard_map(shards, mesh=mesh, in_specs=in_specs, out_specs=out_specs, check_vma=False)
```

```python
import functools

import jax, jax.numpy as jnp
from jax import lax
from jax.experimental import pallas as pl
from jax.experimental.pallas import tpu as pltpu
from jax.sharding import PartitionSpec as P

CHUNK = 128
MESH = pl.DeviceIdType.MESH
bf16, f32 = jnp.bfloat16, jnp.float32


def nn(a, b):
    return lax.dot_general(a.astype(bf16), b.astype(bf16), (((1,), (0,)), ((), ())), preferred_element_type=f32)


def nt(a, b):
    return lax.dot_general(a.astype(bf16), b.astype(bf16), (((1,), (1,)), ((), ())), preferred_element_type=f32)


def tn(a, b):
    return lax.dot_general(a.astype(bf16), b.astype(bf16), (((0,), (0,)), ((), ())), preferred_element_type=f32)


def shifted_rows(x, steps):
    rows = lax.broadcasted_iota(jnp.int32, x.shape, 0)
    count = x.shape[0]
    if steps > 0:
        return jnp.where(rows >= steps, pltpu.roll(x, steps, 0), 0.0)
    return jnp.where(rows < count + steps, pltpu.roll(x, count + steps, 0), 0.0)


def convolved(x, taps):
    total = x * taps[3:4]
    for back in range(1, 4):
        total = total + shifted_rows(x, back) * taps[3 - back : 4 - back]
    return total


def chunk_masks():
    row = lax.broadcasted_iota(jnp.int32, (CHUNK, CHUNK), 0)
    col = lax.broadcasted_iota(jnp.int32, (CHUNK, CHUNK), 1)
    return row, col


def level_mask(row, col, size):
    shift = size.bit_length() - 1
    same = (row >> (shift + 1)) == (col >> (shift + 1))
    return same & (((row >> shift) & 1) == 1) & (((col >> shift) & 1) == 0)


def triangular_inverse(a_list, row, col):
    mask = level_mask(row, col, 1)
    xs = [jnp.where(mask, -a, 0.0) for a in a_list]
    size = 2
    while size < CHUNK:
        mask = level_mask(row, col, size)
        parts = [jnp.where(mask, a, 0.0) for a in a_list]
        ys = [p + nn(p, x) for p, x in zip(parts, xs)]
        xs = [x - (y + nn(x, y)) for x, y in zip(xs, ys)]
        size *= 2
    return xs


def head_column(block, head):
    lanes = lax.broadcasted_iota(jnp.int32, block.shape, 1)
    return jnp.sum(jnp.where(lanes == head, block, 0.0), axis=1, keepdims=True)


def greet_far_core(section):
    far = {"section": section + 1 - 2 * lax.rem(section, 2)}
    barrier = pltpu.get_barrier_semaphore()
    pl.semaphore_signal(barrier, inc=1, device_id=far, device_id_type=MESH)
    pl.semaphore_wait(barrier, 1)
    return far


def give_weights(step, steps, from_even, from_odd, send_sem, recv_sem):
    section = lax.axis_index("section")
    core = lax.rem(section, 2)
    far = {"section": section + 1 - 2 * core}
    pairs = [(0, *p) for p in from_even] + [(1, *p) for p in from_odd]

    def give(i):
        return pltpu.make_async_remote_copy(
            src_ref=pairs[i][1], dst_ref=pairs[i][2], send_sem=send_sem.at[i], recv_sem=recv_sem.at[i], device_id=far, device_id_type=MESH
        )

    @pl.when(step == 0)
    def _():
        greet_far_core(section)
        for i, (owner, _, _) in enumerate(pairs):
            @pl.when(core == owner)
            def _():
                give(i).start()

    @pl.when(step == steps - 1)
    def _():
        for i, (owner, _, _) in enumerate(pairs):
            @pl.when(core == owner)
            def _():
                give(i).wait_send()

            @pl.when(core != owner)
            def _():
                give(i).wait_recv()


def first_kernel(qkv, out, down, conv, beta, attn_gain, head_gain, mlp_gain, both, qkv_part, out_part, down_part, qkv_full, out_full, down_full, conv_full, beta_full, attn_full, head_full, mlp_full, gate, up,
                 mine, theirs, local_sem, send_sem, recv_sem, small_sems):
    step, steps = pl.program_id(0), pl.num_programs(0)
    section = lax.axis_index("section")
    core = lax.rem(section, 2)
    give_weights(step, steps, [(qkv, qkv_full), (out, out_full)], [(down, down_full)], send_sem, recv_sem)
    small = pltpu.make_async_remote_copy(
        src_ref=mine, dst_ref=theirs, send_sem=small_sems.at[0], recv_sem=small_sems.at[1],
        device_id={"section": section + 1 - 2 * core}, device_id_type=MESH,
    )

    @pl.when(step == 0)
    def _():
        mine[...] = jnp.zeros_like(mine)
        for p in range(3):
            mine[8 * p : 8 * p + 4, :] = conv[p].astype(f32)
        mine[4:5, :] = attn_gain[...].astype(f32)
        mine[5:6, : head_gain.shape[1]] = head_gain[...].astype(f32)
        mine[6:7, :] = mlp_gain[...].astype(f32)
        mine[24:32, :] = beta[...].astype(f32)
        small.start()

    count, down_count = out_part.shape[0], down_part.shape[0]
    block, down_block = pl.ds(step * count, count), pl.ds(step * down_count, down_count)
    own = [
        (0, pltpu.make_async_copy(qkv_part, qkv_full.at[:, block], local_sem.at[0])),
        (0, pltpu.make_async_copy(out_part, out_full.at[block], local_sem.at[1])),
        (1, pltpu.make_async_copy(down_part, down_full.at[down_block], local_sem.at[2])),
    ]
    for owner, copy in own:
        @pl.when(core == owner)
        def _():
            copy.start()

    apart = jnp.swapaxes(both[...], 0, 1)
    gate[...] = apart[0]
    up[...] = apart[1]
    for owner, copy in own:
        @pl.when(core == owner)
        def _():
            copy.wait()

    @pl.when(step == steps - 1)
    def _():
        small.wait()
        mixer = jnp.where(core == 0, mine[...], theirs[...])
        for p in range(3):
            conv_full[p] = mixer[8 * p : 8 * p + 4]
        attn_full[...] = mixer[4:5]
        head_full[...] = mixer[5:6, : head_full.shape[1]]
        beta_full[...] = mixer[24:32].astype(bf16)
        mlp_full[...] = jnp.where(core == 1, mine[6:7, :], theirs[6:7, :])


def first_exchange(qkv, out, down, conv, beta, attn_gain, head_gain, mlp_gain, both):
    rows, _, ff = both.shape
    width = out.shape[1]
    count = 128
    anywhere = pl.BlockSpec(memory_space=pl.ANY)
    whole = lambda a: pl.BlockSpec(a.shape, lambda i: (0,) * len(a.shape))
    like = lambda a, kind: jax.ShapeDtypeStruct(a.shape, kind)
    smalls = (conv, beta, attn_gain, head_gain, mlp_gain)
    return pl.pallas_call(
        first_kernel,
        grid=(rows // count,),
        in_specs=[anywhere] * 3 + [whole(a) for a in smalls] + [
            pl.BlockSpec((count, 2, ff), lambda i: (i, 0, 0)),
            pl.BlockSpec((3, count, width), lambda i: (0, i, 0)),
            pl.BlockSpec((count, width), lambda i: (i, 0)),
            pl.BlockSpec((ff * count // rows, width), lambda i: (i, 0)),
        ],
        out_specs=[anywhere] * 3 + [whole(a) for a in smalls] + [pl.BlockSpec((count, ff), lambda i: (i, 0))] * 2,
        out_shape=[like(qkv, bf16), like(out, bf16), like(down, bf16), like(conv, f32), like(beta, bf16), like(attn_gain, f32), like(head_gain, f32), like(mlp_gain, f32)]
        + [jax.ShapeDtypeStruct((rows, ff), bf16)] * 2,
        scratch_shapes=[pltpu.VMEM((32, width), f32)] * 2 + [pltpu.SemaphoreType.DMA((3,))] * 3 + [pltpu.SemaphoreType.DMA((2,))],
        compiler_params=pltpu.CompilerParams(collective_id=1, has_side_effects=True, vmem_limit_bytes=48 * 1024 * 1024),
        name="first_exchange",
    )(qkv, out, down, *smalls, both, qkv, out, down)


def mixer_fwd_kernel(per, trade, q_ref, k_ref, v_ref, beta_ref, taps_q, taps_k, taps_v, gain_ref, *refs):
    if trade:
        own = refs[:trade]
        mixed_ref, t_ref, n_ref, s_ref, o_ref = refs[trade : trade + 5]
        full = refs[trade + 5 : 2 * trade + 5]
        give_weights(pl.program_id(0), pl.num_programs(0), [], list(zip(own, full)), *refs[2 * trade + 5 :])
    else:
        mixed_ref, t_ref, n_ref, s_ref, o_ref = refs
    row, col = chunk_masks()
    strict, causal = row > col, row >= col
    chunks = q_ref.shape[0] // CHUNK
    beta_all = beta_ref[...]
    for j in range(per):
        lane = slice(j * 128, (j + 1) * 128)
        head = pl.program_id(0) * per + j
        beta = head_column(beta_all, head)

        def activated(ref, taps):
            c = convolved(ref[:, lane], taps[:, lane])
            return c * jax.nn.sigmoid(c)

        q, k, v = activated(q_ref, taps_q), activated(k_ref, taps_k), activated(v_ref, taps_v)
        q = q * lax.rsqrt(jnp.sum(q * q, 1, keepdims=True) + 1e-6)
        k = k * lax.rsqrt(jnp.sum(k * k, 1, keepdims=True) + 1e-6)
        cut = lambda x: [x[i * CHUNK : (i + 1) * CHUNK] for i in range(chunks)]
        qs, ks, vs, bs = cut(q), cut(k), cut(v), cut(beta)
        a_list = [jnp.where(strict, nt(kc, kc) * bc, 0.0) for kc, bc in zip(ks, bs)]
        ps = [jnp.where(causal, nt(qc, kc), 0.0) for qc, kc in zip(qs, ks)]
        ts = triangular_inverse(a_list, row, col)
        wu = []
        for kc, vc, bc, t in zip(ks, vs, bs, ts):
            both = jnp.concatenate([kc * bc, vc * bc], 1)
            wu.append(both + nn(t, both))
        state = jnp.zeros((128, 128), f32)
        outs = []
        for i in range(chunks):
            n = wu[i][:, 128:] - nn(wu[i][:, :128], state)
            o = nn(jnp.concatenate([qs[i], ps[i]], 1), jnp.concatenate([state, n], 0))
            span = pl.ds(i * CHUNK, CHUNK)
            s_ref[j, span, :] = state.astype(bf16)
            n_ref[j, span, :] = n.astype(bf16)
            t_ref[j, span, :] = ts[i].astype(bf16)
            o_ref[span, lane] = o
            mixed_ref[span, lane] = (o * lax.rsqrt(jnp.mean(o * o, 1, keepdims=True) + 1e-5) * gain_ref[...]).astype(bf16)
            if i + 1 < chunks:
                state = state + tn(ks[i], n)


def mixer_fwd(proj, beta, taps, gain, own=(), per=2):
    rows, width = proj[0].shape
    heads = width // 128
    steps = heads // per
    wide = 128 * per
    part = pl.BlockSpec((rows, wide), lambda h: (0, h))
    tap = lambda p: pl.BlockSpec((None, 4, wide), lambda h, p=p: (p, 0, h))
    whole = lambda a: pl.BlockSpec(a.shape, lambda h: (0,) * a.ndim)
    saved = pl.BlockSpec((per, rows, 128), lambda h: (h, 0, 0))
    anywhere = [pl.BlockSpec(memory_space=pl.ANY)] * len(own)
    dma = pltpu.SemaphoreType.DMA((max(1, len(own)),))
    return pl.pallas_call(
        functools.partial(mixer_fwd_kernel, per, len(own)),
        grid=(steps,),
        in_specs=[part, part, part, whole(beta), tap(0), tap(1), tap(2), whole(gain)] + anywhere,
        out_specs=[part, saved, saved, saved, part] + anywhere,
        out_shape=[
            jax.ShapeDtypeStruct((rows, width), bf16),
            jax.ShapeDtypeStruct((heads, rows, 128), bf16),
            jax.ShapeDtypeStruct((heads, rows, 128), bf16),
            jax.ShapeDtypeStruct((heads, rows, 128), bf16),
            jax.ShapeDtypeStruct((rows, width), f32),
        ]
        + [jax.ShapeDtypeStruct(a.shape, a.dtype) for a in own],
        scratch_shapes=[dma, dma] if own else [],
        input_output_aliases={8 + i: 5 + i for i in range(len(own))},
        compiler_params=pltpu.CompilerParams(vmem_limit_bytes=48 * 1024 * 1024, **({"collective_id": 2, "has_side_effects": True} if own else {})),
        name="mixer_forward",
    )(*proj, beta, taps, taps, taps, gain, *own)


def mixer_bwd_kernel(per, q_ref, k_ref, v_ref, beta_ref, taps_q, taps_k, taps_v, gain_ref, t_ref, n_ref, s_ref, o_ref, dm_ref,
                     dq_ref, dk_ref, dv_ref, dbeta_ref, dtq_ref, dtk_ref, dtv_ref, dgain_ref):
    row, col = chunk_masks()
    strict, causal_t = row > col, row <= col
    causal = row >= col
    chunks = q_ref.shape[0] // CHUNK
    beta_all = beta_ref[...]
    step = pl.program_id(0)

    @pl.when(step == 0)
    def _():
        dbeta_ref[...] = jnp.zeros_like(dbeta_ref)
        dgain_ref[...] = jnp.zeros_like(dgain_ref)

    for j in range(per):
        lane = slice(j * 128, (j + 1) * 128)
        head = step * per + j
        beta = head_column(beta_all, head)

        def activated(ref, taps):
            c = convolved(ref[:, lane], taps[:, lane])
            sig = jax.nn.sigmoid(c)
            return c * sig, sig * (1.0 + c * (1.0 - sig))

        q_act, q_slope = activated(q_ref, taps_q)
        k_act, k_slope = activated(k_ref, taps_k)
        v, v_slope = activated(v_ref, taps_v)
        q_scale = lax.rsqrt(jnp.sum(q_act * q_act, 1, keepdims=True) + 1e-6)
        k_scale = lax.rsqrt(jnp.sum(k_act * k_act, 1, keepdims=True) + 1e-6)
        q, k = q_act * q_scale, k_act * k_scale
        o, dm, gain = o_ref[:, lane], dm_ref[:, lane], gain_ref[...]
        o_scale = lax.rsqrt(jnp.mean(o * o, 1, keepdims=True) + 1e-5)
        o_hat = o * o_scale
        dgain_ref[...] += jnp.sum(dm * o_hat, 0, keepdims=True)
        dmg = dm * gain
        do = o_scale * (dmg - o_hat * jnp.mean(dmg * o_hat, 1, keepdims=True))
        cut = lambda x: [x[i * CHUNK : (i + 1) * CHUNK] for i in range(chunks)]
        qs, ks, vs, bs, dos = cut(q), cut(k), cut(v), cut(beta), cut(do)
        dstate = jnp.zeros((128, 128), f32)
        dqs, dks, dvs, dbs = [], [], [], []
        for i in reversed(range(chunks)):
            span = pl.ds(i * CHUNK, CHUNK)
            qc, kc, vc, bc, doc = qs[i], ks[i], vs[i], bs[i], dos[i]
            n, s, t = n_ref[j, span, :], s_ref[j, span, :], t_ref[j, span, :]
            gp = nt(kc, jnp.concatenate([kc, qc], 0))
            g = jnp.where(strict, gp[:, :128], 0.0)
            p_t = jnp.where(causal_t, gp[:, 128:], 0.0)
            dn = nn(jnp.concatenate([p_t, kc], 1), jnp.concatenate([doc, dstate], 0))
            dr = dn + tn(t, dn)
            de = dr * bc
            both = nt(doc, jnp.concatenate([n, s], 0))
            dp = jnp.where(causal, both[:, :128], 0.0)
            dqs.append(both[:, 128:] + nn(dp, kc))
            e = vc - nn(kc, s)
            da = jnp.where(strict, -nt(dr, n), 0.0)
            dbs.append(jnp.sum(dr * e, 1, keepdims=True) + jnp.sum(da * g, 1, keepdims=True))
            dg = da * bc
            dk = tn(dp, qc) + nt(jnp.concatenate([n, -de], 1), jnp.concatenate([dstate, s.astype(f32)], 1)) + nn(dg, kc) + tn(dg, kc)
            dks.append(dk)
            dvs.append(de)
            if i:
                dstate = dstate + tn(qc, doc) - tn(kc, de)
        join = lambda xs: jnp.concatenate(xs[::-1], 0)
        dq, dk, dv, db = join(dqs), join(dks), join(dvs), join(dbs)
        dq = q_scale * (dq - q * jnp.sum(dq * q, 1, keepdims=True))
        dk = k_scale * (dk - k * jnp.sum(dk * k, 1, keepdims=True))
        lanes = lax.broadcasted_iota(jnp.int32, dbeta_ref.shape, 1)
        dbeta_ref[...] += jnp.where(lanes == head, db, 0.0)
        for grad, slope, ref, taps, out, dtaps in (
            (dq, q_slope, q_ref, taps_q, dq_ref, dtq_ref),
            (dk, k_slope, k_ref, taps_k, dk_ref, dtk_ref),
            (dv, v_slope, v_ref, taps_v, dv_ref, dtv_ref),
        ):
            dc = grad * slope
            x = ref[:, lane]
            w = taps[:, lane]
            dx = dc * w[3:4]
            rows = [None] * 4
            rows[3] = jnp.sum(dc * x, 0, keepdims=True)
            for back in range(1, 4):
                moved = shifted_rows(dc, -back)
                dx = dx + moved * w[3 - back : 4 - back]
                rows[3 - back] = jnp.sum(moved * x, 0, keepdims=True)
            out[:, lane] = dx.astype(bf16)
            dtaps[:, lane] = jnp.concatenate(rows, 0)


def mixer_bwd(proj, beta, taps, gain, saved, dmixed, per=2):
    t, n, s, o = saved
    rows, width = proj[0].shape
    heads = width // 128
    steps = heads // per
    wide = 128 * per
    part = pl.BlockSpec((rows, wide), lambda h: (0, h))
    tap = lambda p: pl.BlockSpec((None, 4, wide), lambda h, p=p: (p, 0, h))
    whole = lambda a: pl.BlockSpec(a.shape, lambda h: (0,) * len(a.shape))
    kept = pl.BlockSpec((per, rows, 128), lambda h: (h, 0, 0))
    dproj = jax.ShapeDtypeStruct((rows, width), bf16)
    dtap = jax.ShapeDtypeStruct((4, width), f32)
    return pl.pallas_call(
        functools.partial(mixer_bwd_kernel, per),
        grid=(steps,),
        in_specs=[part, part, part, whole(beta), tap(0), tap(1), tap(2), whole(gain), kept, kept, kept, part, part],
        out_specs=[part] * 3 + [whole(beta)] + [pl.BlockSpec((4, wide), lambda h: (0, h))] * 3 + [whole(gain)],
        out_shape=[dproj] * 3 + [jax.ShapeDtypeStruct(beta.shape, f32)] + [dtap] * 3 + [jax.ShapeDtypeStruct(gain.shape, f32)],
        compiler_params=pltpu.CompilerParams(vmem_limit_bytes=48 * 1024 * 1024),
        name="mixer_backward",
    )(*proj, beta, taps, taps, taps, gain, t, n, s, o, dmixed)


PIECE = (64, 256)
SLOTS = 4


def sum_kernel(total, n2_ref, n1_ref, m_ref, h_ref, dgate, dup, dy, dq, dk, dv, g1, small, u1, u2, g0, g1_all,
               qkv_out, out_out, gate_out, up_out, down_out, small_out, u_out, g_out,
               fin, far_fin, keep_sem, give_sem, take_sem, fin_sem, far_sem, own, send, rc, rx, ry, rz, send_sem, xs_sem, ys_sem, zs_sem, rc_sem, rx_sem, ry_sem, rz_sem):
    section, me = lax.axis_index("section"), lax.axis_index("dp")
    core, x, low, high = lax.rem(section, 2), lax.rem(me, 2), lax.rem(me // 2, 2), me // 4
    far_core = {"section": section + 1 - 2 * core}
    far_x, far_low, far_high = {"dp": me + 1 - 2 * x}, {"dp": me + 2 - 4 * low}, {"dp": me + 4 - 8 * high}
    barrier = pltpu.get_barrier_semaphore()
    for other in (far_core, far_x, far_low, far_high):
        pl.semaphore_signal(barrier, inc=1, device_id=other, device_id_type=MESH)
    pl.semaphore_wait(barrier, 4)

    def remote(src, dst, sent, got, other):
        return pltpu.make_async_remote_copy(src_ref=src, dst_ref=dst, send_sem=sent, recv_sem=got, device_id=other, device_id_type=MESH)

    def micro(which, mixer_side, mlp_side, into):
        return (
            pltpu.make_async_copy(mixer_side if which == 0 else mlp_side, into.at[core], keep_sem.at[0 if into is u_out else 1]),
            remote(mlp_side if which == 0 else mixer_side, into.at[core], give_sem.at[0 if into is u_out else 1], take_sem.at[0 if into is u_out else 1], far_core),
        )

    for which in range(2):
        @pl.when(core == which)
        def _():
            for pair in (micro(which, u1, u2, u_out), micro(which, g0, g1_all, g_out)):
                for copy in pair:
                    copy.start()

    @pl.when(core != 0)
    def _():
        qkv_out[...] = jnp.zeros_like(qkv_out)
        out_out[...] = jnp.zeros_like(out_out)

    @pl.when(core != 1)
    def _():
        for ref in (gate_out, up_out, down_out):
            ref[...] = jnp.zeros_like(ref)

    def slot(t):
        return lax.rem(t, SLOTS)

    def core_copy(t):
        return remote(send.at[slot(t)], rc.at[t], send_sem.at[slot(t)], rc_sem.at[t], far_core)

    def x_copy(t):
        return remote(rc.at[t, :, :, 1 - x], rx.at[t], xs_sem.at[slot(t)], rx_sem.at[t], far_x)

    def low_copy(t):
        return remote(rx.at[t, :, 1 - low], ry.at[t], ys_sem.at[slot(t)], ry_sem.at[t], far_low)

    def high_copy(t):
        return remote(ry.at[t, 1 - high], rz.at[t], zs_sem.at[slot(t)], rz_sem.at[t], far_high)

    def begin(copy, t):
        @pl.when(t >= SLOTS)
        def _():
            copy(t - SLOTS).wait_send()

        copy(t).start()

    def after_core(t):
        core_copy(t).wait_recv()
        rc[t] = rc[t] + own[slot(t)]
        begin(x_copy, t)

    def after_x(t):
        x_copy(t).wait_recv()
        rx[t] = rx[t] + rc[t, :, :, x]
        begin(low_copy, t)

    def after_low(t):
        low_copy(t).wait_recv()
        ry[t] = ry[t] + rx[t, :, low]
        begin(high_copy, t)

    def far_copy(t):
        return remote(fin.at[slot(t)], far_fin.at[t], fin_sem.at[slot(t)], far_sem.at[t], far_core)

    def place_columns(into, base):
        def place(t, half, value):
            into[pl.ds(pl.multiple_of(half * PIECE[0], PIECE[0]), PIECE[0]), span(t, base)] = value
        return place

    def place_rows(base):
        def place(t, half, value):
            count = h_ref.shape[2] // 8
            begin_row = pl.multiple_of(half * (down_out.shape[0] // 2) + (t - base) * count, 16)
            for c in range(PIECE[0] // count):
                down_out[pl.ds(begin_row, count), c * PIECE[1] : (c + 1) * PIECE[1]] = value[c * count : (c + 1) * count]
        return place

    def after_high(t):
        high_copy(t).wait_recv()
        value = rz[t].astype(f32) + ry[t, high].astype(f32)
        for base, count, target, _, place in segments:
            @pl.when((t >= base) & (t < base + count))
            def _():
                if target is None:
                    small_out[...] = value
                    return

                @pl.when(core == target)
                def _():
                    place(t, core, value)

                @pl.when(core != target)
                def _():
                    @pl.when(t - SLOTS >= first_of[target])
                    def _():
                        far_copy(t - SLOTS).wait_send()

                    fin[slot(t)] = value
                    far_copy(t).start()

    def after_far(t):
        for base, count, target, _, place in segments:
            if target is not None:
                @pl.when((t >= base) & (t < base + count) & (core == target))
                def _():
                    far_copy(t).wait_recv()
                    place(t, 1 - core, far_fin[t])

    def later(t):
        for step, lag in ((after_core, 1), (after_x, 3), (after_low, 5), (after_high, 7), (after_far, 8)):
            @pl.when((t >= lag) & (t < total + lag))
            def _():
                step(t - lag)

    def span(t, base):
        return pl.ds(pl.multiple_of((t - base) * PIECE[1], PIECE[1]), PIECE[1])

    def by_columns(lhs, rhs, base):
        def fill(t):
            block = rhs[:, span(t, base)]
            for which, into in ((1 - core, send), (core, own)):
                part = nn(lhs[which], block).astype(bf16)
                into[slot(t)] = part.reshape(own.shape[1:])
        return fill

    def by_rows(base):
        def fill(t):
            for which, into in ((1 - core, send), (core, own)):
                part = nn(h_ref[t - base, which], dy[...]).astype(bf16)
                count = part.shape[0] // 8
                for d in range(8):
                    for c in range(PIECE[0] // count):
                        into[slot(t), d // 4, d // 2 % 2, d % 2, c * count : (c + 1) * count, :] = part[d * count : (d + 1) * count, c * PIECE[1] : (c + 1) * PIECE[1]]
        return fill

    def given(t):
        send[slot(t)] = small[1 - core]
        own[slot(t)] = small[core]

    segments, base = [], 0
    for target, columns, lhs, rhs, into in (
        (1, True, n2_ref, dgate, gate_out),
        (1, True, n2_ref, dup, up_out),
        (1, False, h_ref, dy, down_out),
        (0, True, n1_ref, dq, qkv_out.at[0]),
        (0, True, n1_ref, dk, qkv_out.at[1]),
        (0, True, n1_ref, dv, qkv_out.at[2]),
        (0, True, m_ref, g1, out_out),
    ):
        count = rhs.shape[1] // PIECE[1] if columns else lhs.shape[0]
        fill = by_columns(lhs, rhs, base) if columns else by_rows(base)
        place = place_columns(into, base) if columns else place_rows(base)
        segments.append((base, count, target, fill, place))
        base += count
    first_of = {c: min(s[0] for s in segments if s[2] == c) for c in range(2)}
    last_of = {c: max(s[0] + s[1] for s in segments if s[2] == c) for c in range(2)}
    segments.append((base, 1, None, given, None))
    for base, count, _, fill, _ in segments:
        def body(t, carry, fill=fill):
            @pl.when(t >= SLOTS)
            def _():
                core_copy(t - SLOTS).wait_send()

            fill(t)
            core_copy(t).start()
            later(t)
            return carry

        lax.fori_loop(base, base + count, body, 0)

    def drain(t, carry):
        later(t)
        return carry

    lax.fori_loop(total, total + 8, drain, 0)
    for copy in (core_copy, x_copy, low_copy, high_copy):
        for t in range(total - SLOTS, total):
            copy(jnp.int32(t)).wait_send()
    for target in range(2):
        @pl.when(core != target)
        def _():
            for t in range(last_of[target] - SLOTS, last_of[target]):
                far_copy(jnp.int32(t)).wait_send()

    for which in range(2):
        @pl.when(core == which)
        def _():
            for keep, give in (micro(which, u1, u2, u_out), micro(which, g0, g1_all, g_out)):
                keep.wait()
                give.wait_send()
                give.wait_recv()


def summed_gradients(n2, n1, m, h, dgate, dup, dy, dq, dk, dv, g1, small, u1, u2, g0):
    total = (2 * dgate.shape[1] + 4 * dq.shape[1]) // PIECE[1] + h.shape[0] + 1
    buffer = lambda *lead: pltpu.VMEM(lead + PIECE, bf16)
    dma = lambda n: pltpu.SemaphoreType.DMA((n,))
    vmem, anywhere = pl.BlockSpec(memory_space=pltpu.VMEM), pl.BlockSpec(memory_space=pl.ANY)
    operands = (n2, n1, m, h, dgate, dup, dy, dq, dk, dv, g1, small)
    ff, width, rows = dgate.shape[1], dq.shape[1], 2 * PIECE[0]
    result = lambda *shape: jax.ShapeDtypeStruct(shape, f32)
    pair = jax.ShapeDtypeStruct((2,) + u1.shape, bf16)
    return pl.pallas_call(
        functools.partial(sum_kernel, total),
        out_shape=[result(3, rows, width), result(rows, width), result(rows, ff), result(rows, ff), result(ff // 8, width), result(*PIECE), pair, pair],
        in_specs=[vmem] * len(operands) + [anywhere] * 4,
        out_specs=[vmem] * 6 + [anywhere] * 2,
        scratch_shapes=[
            pltpu.VMEM((SLOTS,) + PIECE, f32), pltpu.VMEM((total,) + PIECE, f32), dma(2), dma(2), dma(2), dma(SLOTS), dma(total),
            buffer(SLOTS, 2, 2, 2), buffer(SLOTS, 2, 2, 2), buffer(total, 2, 2, 2), buffer(total, 2, 2), buffer(total, 2), buffer(total),
            dma(SLOTS), dma(SLOTS), dma(SLOTS), dma(SLOTS), dma(total), dma(total), dma(total), dma(total),
        ],
        compiler_params=pltpu.CompilerParams(collective_id=0, has_side_effects=True, vmem_limit_bytes=62 * 1024 * 1024),
        name="gradient_sums",
    )(*operands, u1, u2, g0, g1)


def rms_forward(x, gain):
    scale = lax.rsqrt(jnp.mean(x * x, -1, keepdims=True) + 1e-06)
    return (x * scale * gain).astype(bf16), scale


def rms_backward(x, scale, gain, grad):
    gain_grad = jnp.sum(grad * x * scale, 0)
    inner = jnp.mean(grad * gain * x, -1, keepdims=True)
    return scale * gain * grad - x * scale**3 * inner, gain_grad


def matmul(a, b):
    return jnp.dot(a, b, preferred_element_type=f32)


def matmul_nt(a, b):
    return lax.dot_general(a, b, (((1,), (1,)), ((), ())), preferred_element_type=f32)


def matmul_tn(a, b):
    return lax.dot_general(a, b, (((0,), (0,)), ((), ())), preferred_element_type=f32)


def mixer_forward(u, w, token_mask, own=()):
    x = u.astype(f32)
    normed, scale = rms_forward(x, w["attn_gain"])
    proj = [matmul(normed, w["qkv"][p]) for p in range(3)]
    rate = jax.nn.sigmoid(matmul_nt(normed, w["beta"]))
    beta = rate * token_mask
    mixed, *saved = mixer_fwd(proj, beta, w["conv"], w["head_gain"], own)
    saved, given = saved[:4], saved[4:]
    result = (x + matmul(mixed, w["out"])).astype(bf16)
    return result, (u, normed, scale, proj, rate, beta, mixed, saved), given


def mixer_input_grad(kept, dy, w, token_mask):
    u, normed, scale, proj, rate, beta, mixed, saved = kept
    dmixed = matmul_nt(dy, w["out"])
    *dproj, dbeta, dtq, dtk, dtv, dhead = mixer_bwd(proj, beta, w["conv"], w["head_gain"], saved, dmixed)
    dlogits = dbeta * token_mask * rate * (1.0 - rate)
    dnormed = sum(matmul_nt(d, w["qkv"][p]) for p, d in enumerate(dproj))
    dnormed = dnormed + matmul(dlogits.astype(bf16), w["beta"])
    dx, dgain = rms_backward(u.astype(f32), scale, w["attn_gain"], dnormed)
    g = (dy.astype(f32) + dx).astype(bf16)
    return g, (dproj, dlogits, jnp.stack([dtq, dtk, dtv], 1), dhead[0], dgain)


def mlp_forward(u, w):
    x = u.astype(f32)
    normed, scale = rms_forward(x, w["mlp_gain"])
    gate, up = matmul(normed, w["gate"]), matmul(normed, w["up"])
    hidden = (jax.nn.silu(gate) * up).astype(bf16)
    result = (x + matmul(hidden, w["down"])).astype(bf16)
    return result, (u, normed, scale, gate, up, hidden)


def mlp_input_grad(kept, dy, w):
    u, normed, scale, gate, up, hidden = kept
    dhidden = matmul_nt(dy, w["down"])
    sig = jax.nn.sigmoid(gate)
    dgate = (dhidden * up * (sig * (1.0 + gate * (1.0 - sig)))).astype(bf16)
    dup = (dhidden * (gate * sig)).astype(bf16)
    dnormed = matmul_nt(dgate, w["gate"]) + matmul_nt(dup, w["up"])
    dx, dgain = rms_backward(u.astype(f32), scale, w["mlp_gain"], dnormed)
    g = (dy.astype(f32) + dx).astype(bf16)
    return g, (dgate, dup, dgain)


def pick(x, index, axis):
    return lax.dynamic_index_in_dim(x, index, axis, keepdims=False)


def shards(inputs, cotangent, lengths, attn_gain, qkv_weight, conv_weight, beta_weight, head_gain, out_weight, mlp_gain, gate_up_weight, down_weight):
    section, sections = lax.axis_index("section"), lax.axis_size("section")
    me, group = lax.axis_index("dp"), lax.axis_size("dp")
    core, stage = section % 2, section // 2
    swap = [(i, i ^ 1) for i in range(sections)]
    to_odd = [(i, i + 1) for i in range(0, sections, 2)]
    to_even = [(i + 1, i) for i in range(0, sections, 2)]
    rows = inputs.shape[2]
    width = inputs.shape[3]

    qkv, out_w, down, conv, beta_w, attn, head, mlp, own_gate, own_up = first_exchange(
        jnp.moveaxis(qkv_weight[0], 1, 0),
        out_weight[0],
        down_weight[0],
        jnp.moveaxis(conv_weight[0], 1, 0),
        beta_weight[0].T,
        attn_gain,
        head_gain,
        mlp_gain,
        gate_up_weight[0],
    )
    w = {"attn_gain": attn, "conv": conv, "beta": beta_w, "head_gain": head, "qkv": qkv, "out": out_w, "mlp_gain": mlp, "down": down}

    first = pick(inputs[:, 0], core, 0)
    seed = pick(cotangent[:, 0], core, 0)
    length = pick(lengths[:, 0], core, 0)
    token_mask = (jnp.arange(rows) < length).astype(f32)[:, None]
    up_stage = [(i, i + 2) for i in range(sections - 2)]
    down_stage = [(i + 2, i) for i in range(sections - 2)]

    u0 = first
    for step in range(sections // 2):
        if step == 0:
            u1, kept_mixer, (w["gate"], w["up"]) = mixer_forward(u0, w, token_mask, (own_gate, own_up))
        else:
            u1, kept_mixer, _ = mixer_forward(u0, w, token_mask)
        u2, kept_mlp = mlp_forward(u1, w)
        if step + 1 < sections // 2:
            u0 = jnp.where(stage == 0, first, lax.ppermute(u2, "section", up_stage))
    last_stage = sections // 2 - 1
    dy = seed
    for step in range(sections // 2):
        g1, mlp_parts = mlp_input_grad(kept_mlp, dy, w)
        g0, mixer_parts = mixer_input_grad(kept_mixer, g1, w, token_mask)
        if step + 1 < sections // 2:
            dy = jnp.where(stage == last_stage, seed, lax.ppermute(g0, "section", down_stage))

    _, normed1, _, _, _, _, mixed, _ = kept_mixer
    _, normed2, _, _, _, hidden = kept_mlp
    dgate, dup, d_mlp_gain = mlp_parts
    dproj, dlogits, dtaps, dhead, d_attn_gain = mixer_parts

    def halve(x):
        kept = pick(x, core, 1).astype(f32)
        x = (kept + lax.ppermute(pick(x, 1 - core, 1), "section", swap).astype(f32)).astype(bf16)
        return scatter(x)

    def scatter(x):
        kind = x.dtype
        bit = 1
        while bit < group:
            pairs = [(i, i ^ bit) for i in range(group)]
            mine = (me // bit) % 2
            x = x.reshape((x.shape[0] // 2, 2) + x.shape[1:])
            other = lax.ppermute(pick(x, 1 - mine, 1), "dp", pairs)
            x = pick(x, mine, 1).astype(f32) + other.astype(f32)
            bit *= 2
            if bit < group:
                x = x.astype(kind)
        return x[0]

    def share(grad):
        count, cols = grad.shape
        return halve(grad.astype(bf16).reshape(group, 2, count // group // 2, cols))

    dbeta = lax.dot_general(normed1.astype(f32), dlogits, (((0,), (0,)), ((), ())), precision=lax.Precision.HIGHEST)
    taps_rows = jnp.moveaxis(dtaps.reshape(-1, 3, group, width // group), 2, 0).reshape(group, -1)
    small = [d_attn_gain.reshape(group, -1), taps_rows, dbeta.reshape(group, -1), dhead.reshape(group, -1), d_mlp_gain.reshape(group, -1)]
    sizes = [a.shape[1] for a in small]
    joined = jnp.concatenate(small, 1)
    ff = dgate.shape[1]
    mixer_size = sum(sizes[:4])
    on_even = lambda x: jnp.where(core == 0, x, 0.0)
    on_odd = lambda x: jnp.where(core == 1, x, 0.0)
    if group == 8 and width == 1024 and ff % 256 == 0:
        by_owner = lambda a: a.reshape(rows, group, 2, 64).transpose(2, 1, 3, 0).reshape(2, group * 64, rows)
        down_rows = hidden.reshape(rows, group, 2, ff // 256, 16).transpose(3, 2, 1, 4, 0).reshape(ff // 256, 2, group * 16, rows)
        per = PIECE[0] * PIECE[1]
        one = lambda a: jnp.pad(a, ((0, 0), (0, per - a.shape[1]))).astype(bf16).reshape(2, 2, 2, *PIECE)
        low_small = jnp.stack([one(joined[:, :mixer_size]), one(joined[:, mixer_size:])])
        grad_qkv, grad_out, grad_gate, grad_up, grad_down, small, sec_out, sec_grad = summed_gradients(
            by_owner(normed2), by_owner(normed1), by_owner(mixed), down_rows, dgate, dup, dy, *dproj, g1, low_small, u1, u2, g0
        )
        grad_qkv = jnp.moveaxis(grad_qkv, 0, 1)
        grad_gate_up = jnp.stack([grad_gate, grad_up], 1)
        small = small.reshape(-1)
        small = jnp.concatenate([small[:mixer_size], small[: sizes[4]]])
        sec_out, sec_grad = sec_out[None, :, None], sec_grad[None, :, None]
    else:
        down_share = share(matmul_tn(hidden, dy))
        gate_share = share(matmul_tn(normed2, dgate))
        up_share = share(matmul_tn(normed2, dup))
        out_share = share(matmul_tn(mixed, g1))
        qkv_share = [share(matmul_tn(normed1, d)) for d in dproj]
        small = scatter(joined + lax.ppermute(joined, "section", swap))
        def to_core(x, target):
            other = lax.ppermute(x, "section", to_even if target == 0 else to_odd)
            both = jnp.concatenate([x, other] if target == 0 else [other, x], 0)
            return jnp.where(core == target, both, 0.0)

        grad_qkv = jnp.stack([to_core(x, 0) for x in qkv_share], 1)
        grad_out = to_core(out_share, 0)
        grad_gate_up = jnp.stack([to_core(gate_share, 1), to_core(up_share, 1)], 1)
        grad_down = to_core(down_share, 1)

        def both_micro(mixer_side, mlp_side):
            own = jnp.where(core == 0, mixer_side, mlp_side)
            other = lax.ppermute(jnp.where(core == 0, mlp_side, mixer_side), "section", swap)
            return jnp.where(core == 0, jnp.stack([own, other]), jnp.stack([other, own]))[None, :, None]

        sec_out, sec_grad = both_micro(u1, u2), both_micro(g0, g1)

    offsets = [sum(sizes[:i]) for i in range(len(sizes) + 1)]
    s_attn, s_taps, s_beta, s_head, s_mlp = [small[a:b] for a, b in zip(offsets, offsets[1:])]

    return (
        sec_out,
        sec_grad,
        on_even(s_attn)[None],
        grad_qkv[None],
        on_even(s_taps).reshape(1, -1, 3, width // group),
        on_even(s_beta).reshape(1, -1, dbeta.shape[1]),
        on_even(s_head)[None],
        grad_out[None],
        on_odd(s_mlp)[None],
        grad_gate_up[None],
        grad_down[None],
    )


def solution(mesh):
    in_specs = (
        P(None, "dp", None, None),
        P(None, "dp", None, None),
        P(None, "dp"),
        P("section", None),
        P("section", None, None, None),
        P("section", None, None, None),
        P("section", None, None),
        P("section", None),
        P("section", None, None),
        P("section", None),
        P("section", None, None, None),
        P("section", None, None),
    )
    out_specs = (
        P("section", None, "dp", None, None),
        P("section", None, "dp", None, None),
        P("section", "dp"),
        P("section", "dp", None, None),
        P("section", None, None, "dp"),
        P("section", "dp", None),
        P("section", "dp"),
        P("section", "dp", None),
        P("section", "dp"),
        P("section", "dp", None, None),
        P("section", "dp", None),
    )
    return jax.shard_map(shards, mesh=mesh, in_specs=in_specs, out_specs=out_specs, check_vma=False)
```

```python
import functools

import jax, jax.numpy as jnp
from jax import lax
from jax.experimental import pallas as pl
from jax.experimental.pallas import tpu as pltpu
from jax.sharding import PartitionSpec as P

CHUNK = 128
MESH = pl.DeviceIdType.MESH
bf16, f32 = jnp.bfloat16, jnp.float32


def nn(a, b):
    return lax.dot_general(a.astype(bf16), b.astype(bf16), (((1,), (0,)), ((), ())), preferred_element_type=f32)


def nt(a, b):
    return lax.dot_general(a.astype(bf16), b.astype(bf16), (((1,), (1,)), ((), ())), preferred_element_type=f32)


def tn(a, b):
    return lax.dot_general(a.astype(bf16), b.astype(bf16), (((0,), (0,)), ((), ())), preferred_element_type=f32)


def shifted_rows(x, steps):
    count = x.shape[0]
    rows = lax.broadcasted_iota(jnp.int32, (8, x.shape[1]), 0)
    moved = pltpu.roll(x, steps % count, 0)
    if steps > 0:
        return jnp.concatenate([jnp.where(rows >= steps, moved[:8], 0.0), moved[8:]], 0)
    return jnp.concatenate([moved[:-8], jnp.where(rows < 8 + steps, moved[-8:], 0.0)], 0)


def convolved(x, taps):
    total = x * taps[3:4]
    for back in range(1, 4):
        total = total + shifted_rows(x, back) * taps[3 - back : 4 - back]
    return total


def chunk_masks():
    row = lax.broadcasted_iota(jnp.int32, (CHUNK, CHUNK), 0)
    col = lax.broadcasted_iota(jnp.int32, (CHUNK, CHUNK), 1)
    return row, col


def level_mask(row, col, size):
    shift = size.bit_length() - 1
    same = (row >> (shift + 1)) == (col >> (shift + 1))
    return same & (((row >> shift) & 1) == 1) & (((col >> shift) & 1) == 0)


def triangular_inverse(a_list, row, col):
    mask = level_mask(row, col, 1)
    xs = [jnp.where(mask, -a, 0.0) for a in a_list]
    size = 2
    while size < CHUNK:
        mask = level_mask(row, col, size)
        parts = [jnp.where(mask, a, 0.0) for a in a_list]
        ys = [p + nn(p, x) for p, x in zip(parts, xs)]
        xs = [x - (y + nn(x, y)) for x, y in zip(xs, ys)]
        size *= 2
    return xs


def head_column(block, head):
    lanes = lax.broadcasted_iota(jnp.int32, block.shape, 1)
    return jnp.sum(jnp.where(lanes == head, block, 0.0), axis=1, keepdims=True)


def greet_far_core(section):
    far = {"section": section + 1 - 2 * lax.rem(section, 2)}
    barrier = pltpu.get_barrier_semaphore()
    pl.semaphore_signal(barrier, inc=1, device_id=far, device_id_type=MESH)
    pl.semaphore_wait(barrier, 1)
    return far


def give_weights(step, steps, from_even, from_odd, send_sem, recv_sem):
    section = lax.axis_index("section")
    core = lax.rem(section, 2)
    far = {"section": section + 1 - 2 * core}
    pairs = [(0, *p) for p in from_even] + [(1, *p) for p in from_odd]

    def give(i):
        return pltpu.make_async_remote_copy(
            src_ref=pairs[i][1], dst_ref=pairs[i][2], send_sem=send_sem.at[i], recv_sem=recv_sem.at[i], device_id=far, device_id_type=MESH
        )

    @pl.when(step == 0)
    def _():
        greet_far_core(section)
        for i, (owner, _, _) in enumerate(pairs):
            @pl.when(core == owner)
            def _():
                give(i).start()

    @pl.when(step == steps - 1)
    def _():
        for i, (owner, _, _) in enumerate(pairs):
            @pl.when(core == owner)
            def _():
                give(i).wait_send()

            @pl.when(core != owner)
            def _():
                give(i).wait_recv()


def first_kernel(qkv, out, down, conv, beta, attn_gain, head_gain, mlp_gain, both, qkv_part, out_part, down_part, qkv_full, out_full, down_full, conv_full, beta_full, attn_full, head_full, mlp_full, gate, up,
                 mine, theirs, local_sem, send_sem, recv_sem, small_sems):
    step, steps = pl.program_id(0), pl.num_programs(0)
    section = lax.axis_index("section")
    core = lax.rem(section, 2)
    give_weights(step, steps, [(qkv, qkv_full), (out, out_full)], [(down, down_full)], send_sem, recv_sem)
    small = pltpu.make_async_remote_copy(
        src_ref=mine, dst_ref=theirs, send_sem=small_sems.at[0], recv_sem=small_sems.at[1],
        device_id={"section": section + 1 - 2 * core}, device_id_type=MESH,
    )

    @pl.when(step == 0)
    def _():
        mine[...] = jnp.zeros_like(mine)
        for p in range(3):
            mine[8 * p : 8 * p + 4, :] = conv[p].astype(f32)
        mine[4:5, :] = attn_gain[...].astype(f32)
        mine[5:6, : head_gain.shape[1]] = head_gain[...].astype(f32)
        mine[6:7, :] = mlp_gain[...].astype(f32)
        mine[24:32, :] = beta[...].astype(f32)
        small.start()

    count, down_count = out_part.shape[0], down_part.shape[0]
    block, down_block = pl.ds(step * count, count), pl.ds(step * down_count, down_count)
    own = [
        (0, pltpu.make_async_copy(qkv_part, qkv_full.at[:, block], local_sem.at[0])),
        (0, pltpu.make_async_copy(out_part, out_full.at[block], local_sem.at[1])),
        (1, pltpu.make_async_copy(down_part, down_full.at[down_block], local_sem.at[2])),
    ]
    for owner, copy in own:
        @pl.when(core == owner)
        def _():
            copy.start()

    apart = jnp.swapaxes(both[...], 0, 1)
    gate[...] = apart[0]
    up[...] = apart[1]
    for owner, copy in own:
        @pl.when(core == owner)
        def _():
            copy.wait()

    @pl.when(step == steps - 1)
    def _():
        small.wait()
        mixer = jnp.where(core == 0, mine[...], theirs[...])
        for p in range(3):
            conv_full[p] = mixer[8 * p : 8 * p + 4]
        attn_full[...] = mixer[4:5]
        head_full[...] = mixer[5:6, : head_full.shape[1]]
        beta_full[...] = mixer[24:32].astype(bf16)
        mlp_full[...] = jnp.where(core == 1, mine[6:7, :], theirs[6:7, :])


def first_exchange(qkv, out, down, conv, beta, attn_gain, head_gain, mlp_gain, both):
    rows, _, ff = both.shape
    width = out.shape[1]
    count = 128
    anywhere = pl.BlockSpec(memory_space=pl.ANY)
    whole = lambda a: pl.BlockSpec(a.shape, lambda i: (0,) * len(a.shape))
    like = lambda a, kind: jax.ShapeDtypeStruct(a.shape, kind)
    smalls = (conv, beta, attn_gain, head_gain, mlp_gain)
    return pl.pallas_call(
        first_kernel,
        grid=(rows // count,),
        in_specs=[anywhere] * 3 + [whole(a) for a in smalls] + [
            pl.BlockSpec((count, 2, ff), lambda i: (i, 0, 0)),
            pl.BlockSpec((3, count, width), lambda i: (0, i, 0)),
            pl.BlockSpec((count, width), lambda i: (i, 0)),
            pl.BlockSpec((ff * count // rows, width), lambda i: (i, 0)),
        ],
        out_specs=[anywhere] * 3 + [whole(a) for a in smalls] + [pl.BlockSpec((count, ff), lambda i: (i, 0))] * 2,
        out_shape=[like(qkv, bf16), like(out, bf16), like(down, bf16), like(conv, f32), like(beta, bf16), like(attn_gain, f32), like(head_gain, f32), like(mlp_gain, f32)]
        + [jax.ShapeDtypeStruct((rows, ff), bf16)] * 2,
        scratch_shapes=[pltpu.VMEM((32, width), f32)] * 2 + [pltpu.SemaphoreType.DMA((3,))] * 3 + [pltpu.SemaphoreType.DMA((2,))],
        compiler_params=pltpu.CompilerParams(collective_id=1, has_side_effects=True, vmem_limit_bytes=48 * 1024 * 1024),
        name="first_exchange",
    )(qkv, out, down, *smalls, both, qkv, out, down)


def mixer_fwd_kernel(per, trade, q_ref, k_ref, v_ref, beta_ref, taps_q, taps_k, taps_v, gain_ref, *refs):
    if trade:
        own = refs[:trade]
        mixed_ref, t_ref, n_ref, s_ref, o_ref = refs[trade : trade + 5]
        full = refs[trade + 5 : 2 * trade + 5]
        give_weights(pl.program_id(0), pl.num_programs(0), [], list(zip(own, full)), *refs[2 * trade + 5 :])
    else:
        mixed_ref, t_ref, n_ref, s_ref, o_ref = refs
    row, col = chunk_masks()
    strict, causal = row > col, row >= col
    chunks = q_ref.shape[0] // CHUNK
    beta_all = beta_ref[...]
    cut = lambda x: [x[i * CHUNK : (i + 1) * CHUNK] for i in range(chunks)]
    lanes = [slice(j * 128, (j + 1) * 128) for j in range(per)]
    qs, ks, vs, bs = [], [], [], []
    for j, lane in enumerate(lanes):

        def activated(ref, taps):
            c = convolved(ref[:, lane], taps[:, lane])
            return c * jax.nn.sigmoid(c)

        q, k, v = activated(q_ref, taps_q), activated(k_ref, taps_k), activated(v_ref, taps_v)
        q = q * lax.rsqrt(jnp.sum(q * q, 1, keepdims=True) + 1e-6)
        k = k * lax.rsqrt(jnp.sum(k * k, 1, keepdims=True) + 1e-6)
        qs.append(cut(q))
        ks.append(cut(k))
        vs.append(cut(v))
        bs.append(cut(head_column(beta_all, pl.program_id(0) * per + j)))
    each = [(j, i) for j in range(per) for i in range(chunks)]
    a_list = [jnp.where(strict, nt(ks[j][i], ks[j][i]) * bs[j][i], 0.0) for j, i in each]
    ps = {(j, i): jnp.where(causal, nt(qs[j][i], ks[j][i]), 0.0) for j, i in each}
    ts = dict(zip(each, triangular_inverse(a_list, row, col)))
    wu = {}
    for j, i in each:
        both = jnp.concatenate([ks[j][i] * bs[j][i], vs[j][i] * bs[j][i]], 1)
        wu[j, i] = both + nn(ts[j, i], both)
    states = [jnp.zeros((128, 128), f32)] * per
    for i in range(chunks):
        span = pl.ds(i * CHUNK, CHUNK)
        news = [wu[j, i][:, 128:] - nn(wu[j, i][:, :128], states[j]) for j in range(per)]
        outs = [nn(jnp.concatenate([qs[j][i], ps[j, i]], 1), jnp.concatenate([states[j], news[j]], 0)) for j in range(per)]
        for j, lane in enumerate(lanes):
            o = outs[j]
            s_ref[j, span, :] = states[j].astype(bf16)
            n_ref[j, span, :] = news[j].astype(bf16)
            t_ref[j, span, :] = ts[j, i].astype(bf16)
            o_ref[span, lane] = o
            mixed_ref[span, lane] = (o * lax.rsqrt(jnp.mean(o * o, 1, keepdims=True) + 1e-5) * gain_ref[...]).astype(bf16)
        if i + 1 < chunks:
            states = [states[j] + tn(ks[j][i], news[j]) for j in range(per)]


def mixer_fwd(proj, beta, taps, gain, own=(), per=4):
    rows, width = proj[0].shape
    heads = width // 128
    steps = heads // per
    wide = 128 * per
    part = pl.BlockSpec((rows, wide), lambda h: (0, h))
    tap = lambda p: pl.BlockSpec((None, 4, wide), lambda h, p=p: (p, 0, h))
    whole = lambda a: pl.BlockSpec(a.shape, lambda h: (0,) * a.ndim)
    saved = pl.BlockSpec((per, rows, 128), lambda h: (h, 0, 0))
    anywhere = [pl.BlockSpec(memory_space=pl.ANY)] * len(own)
    dma = pltpu.SemaphoreType.DMA((max(1, len(own)),))
    return pl.pallas_call(
        functools.partial(mixer_fwd_kernel, per, len(own)),
        grid=(steps,),
        in_specs=[part, part, part, whole(beta), tap(0), tap(1), tap(2), whole(gain)] + anywhere,
        out_specs=[part, saved, saved, saved, part] + anywhere,
        out_shape=[
            jax.ShapeDtypeStruct((rows, width), bf16),
            jax.ShapeDtypeStruct((heads, rows, 128), bf16),
            jax.ShapeDtypeStruct((heads, rows, 128), bf16),
            jax.ShapeDtypeStruct((heads, rows, 128), bf16),
            jax.ShapeDtypeStruct((rows, width), f32),
        ]
        + [jax.ShapeDtypeStruct(a.shape, a.dtype) for a in own],
        scratch_shapes=[dma, dma] if own else [],
        input_output_aliases={8 + i: 5 + i for i in range(len(own))},
        compiler_params=pltpu.CompilerParams(vmem_limit_bytes=48 * 1024 * 1024, **({"collective_id": 2, "has_side_effects": True} if own else {})),
        name="mixer_forward",
    )(*proj, beta, taps, taps, taps, gain, *own)


def mixer_bwd_kernel(per, q_ref, k_ref, v_ref, beta_ref, taps_q, taps_k, taps_v, gain_ref, t_ref, n_ref, s_ref, o_ref, dm_ref,
                     dq_ref, dk_ref, dv_ref, dbeta_ref, dtq_ref, dtk_ref, dtv_ref, dgain_ref):
    row, col = chunk_masks()
    strict, causal_t = row > col, row <= col
    causal = row >= col
    chunks = q_ref.shape[0] // CHUNK
    beta_all = beta_ref[...]
    step = pl.program_id(0)

    @pl.when(step == 0)
    def _():
        dbeta_ref[...] = jnp.zeros_like(dbeta_ref)
        dgain_ref[...] = jnp.zeros_like(dgain_ref)

    cut = lambda x: [x[i * CHUNK : (i + 1) * CHUNK] for i in range(chunks)]
    heads = range(per)
    lanes = [slice(j * 128, (j + 1) * 128) for j in heads]
    kept, qs, ks, vs, bs, dos = [], [], [], [], [], []
    for j, lane in enumerate(lanes):

        def activated(ref, taps):
            c = convolved(ref[:, lane], taps[:, lane])
            sig = jax.nn.sigmoid(c)
            return c * sig, sig * (1.0 + c * (1.0 - sig))

        q_act, q_slope = activated(q_ref, taps_q)
        k_act, k_slope = activated(k_ref, taps_k)
        v, v_slope = activated(v_ref, taps_v)
        q_scale = lax.rsqrt(jnp.sum(q_act * q_act, 1, keepdims=True) + 1e-6)
        k_scale = lax.rsqrt(jnp.sum(k_act * k_act, 1, keepdims=True) + 1e-6)
        q, k = q_act * q_scale, k_act * k_scale
        o, dm, gain = o_ref[:, lane], dm_ref[:, lane], gain_ref[...]
        o_scale = lax.rsqrt(jnp.mean(o * o, 1, keepdims=True) + 1e-5)
        o_hat = o * o_scale
        dgain_ref[...] += jnp.sum(dm * o_hat, 0, keepdims=True)
        dmg = dm * gain
        do = o_scale * (dmg - o_hat * jnp.mean(dmg * o_hat, 1, keepdims=True))
        kept.append((q, k, q_scale, k_scale, q_slope, k_slope, v_slope))
        qs.append(cut(q))
        ks.append(cut(k))
        vs.append(cut(v))
        bs.append(cut(head_column(beta_all, step * per + j)))
        dos.append(cut(do))
    dstates = [jnp.zeros((128, 128), f32)] * per
    dqs, dks, dvs, dbs = [[[] for _ in heads] for _ in range(4)]
    for i in reversed(range(chunks)):
        span = pl.ds(i * CHUNK, CHUNK)
        qc, kc, vc, bc, doc = [[x[j][i] for j in heads] for x in (qs, ks, vs, bs, dos)]
        n, s, t = [[ref[j, span, :] for j in heads] for ref in (n_ref, s_ref, t_ref)]
        gp = [nt(kc[j], jnp.concatenate([kc[j], qc[j]], 0)) for j in heads]
        p_t = [jnp.where(causal_t, gp[j][:, 128:], 0.0) for j in heads]
        dn = [nn(jnp.concatenate([p_t[j], kc[j]], 1), jnp.concatenate([doc[j], dstates[j]], 0)) for j in heads]
        dr = [dn[j] + tn(t[j], dn[j]) for j in heads]
        de = [dr[j] * bc[j] for j in heads]
        both = [nt(doc[j], jnp.concatenate([n[j], s[j]], 0)) for j in heads]
        e = [vc[j] - nn(kc[j], s[j]) for j in heads]
        da = [jnp.where(strict, -nt(dr[j], n[j]), 0.0) for j in heads]
        dp = [jnp.where(causal, both[j][:, :128], 0.0) for j in heads]
        dg = [da[j] * bc[j] for j in heads]
        for j in heads:
            dqs[j].append(both[j][:, 128:] + nn(dp[j], kc[j]))
            dbs[j].append(jnp.sum(dr[j] * e[j], 1, keepdims=True) + jnp.sum(da[j] * gp[j][:, :128], 1, keepdims=True))
            dks[j].append(
                tn(dp[j], qc[j])
                + nt(jnp.concatenate([n[j], -de[j].astype(bf16)], 1), jnp.concatenate([dstates[j].astype(bf16), s[j]], 1))
                + nn(dg[j], kc[j])
                + tn(dg[j], kc[j])
            )
            dvs[j].append(de[j])
        if i:
            dstates = [dstates[j] + tn(qc[j], doc[j]) - tn(kc[j], de[j]) for j in heads]
    join = lambda xs: jnp.concatenate(xs[::-1], 0)
    lane_ids = lax.broadcasted_iota(jnp.int32, dbeta_ref.shape, 1)
    for j, lane in enumerate(lanes):
        q, k, q_scale, k_scale, q_slope, k_slope, v_slope = kept[j]
        dq, dk, dv, db = join(dqs[j]), join(dks[j]), join(dvs[j]), join(dbs[j])
        dq = q_scale * (dq - q * jnp.sum(dq * q, 1, keepdims=True))
        dk = k_scale * (dk - k * jnp.sum(dk * k, 1, keepdims=True))
        dbeta_ref[...] += jnp.where(lane_ids == step * per + j, db, 0.0)
        for grad, slope, ref, taps, out, dtaps in (
            (dq, q_slope, q_ref, taps_q, dq_ref, dtq_ref),
            (dk, k_slope, k_ref, taps_k, dk_ref, dtk_ref),
            (dv, v_slope, v_ref, taps_v, dv_ref, dtv_ref),
        ):
            dc = grad * slope
            x = ref[:, lane]
            w = taps[:, lane]
            dx = dc * w[3:4]
            rows = [None] * 4
            rows[3] = jnp.sum(dc * x, 0, keepdims=True)
            for back in range(1, 4):
                moved = shifted_rows(dc, -back)
                dx = dx + moved * w[3 - back : 4 - back]
                rows[3 - back] = jnp.sum(moved * x, 0, keepdims=True)
            out[:, lane] = dx.astype(bf16)
            dtaps[:, lane] = jnp.concatenate(rows, 0)


def mixer_bwd(proj, beta, taps, gain, saved, dmixed, per=4):
    t, n, s, o = saved
    rows, width = proj[0].shape
    heads = width // 128
    steps = heads // per
    wide = 128 * per
    part = pl.BlockSpec((rows, wide), lambda h: (0, h))
    tap = lambda p: pl.BlockSpec((None, 4, wide), lambda h, p=p: (p, 0, h))
    whole = lambda a: pl.BlockSpec(a.shape, lambda h: (0,) * len(a.shape))
    kept = pl.BlockSpec((per, rows, 128), lambda h: (h, 0, 0))
    dproj = jax.ShapeDtypeStruct((rows, width), bf16)
    dtap = jax.ShapeDtypeStruct((4, width), f32)
    return pl.pallas_call(
        functools.partial(mixer_bwd_kernel, per),
        grid=(steps,),
        in_specs=[part, part, part, whole(beta), tap(0), tap(1), tap(2), whole(gain), kept, kept, kept, part, part],
        out_specs=[part] * 3 + [whole(beta)] + [pl.BlockSpec((4, wide), lambda h: (0, h))] * 3 + [whole(gain)],
        out_shape=[dproj] * 3 + [jax.ShapeDtypeStruct(beta.shape, f32)] + [dtap] * 3 + [jax.ShapeDtypeStruct(gain.shape, f32)],
        compiler_params=pltpu.CompilerParams(vmem_limit_bytes=48 * 1024 * 1024),
        name="mixer_backward",
    )(*proj, beta, taps, taps, taps, gain, t, n, s, o, dmixed)


PIECE = (64, 256)
SLOTS = 4
LAGS = (1, 4, 7, 10, 11)


def sum_kernel(total, n2_ref, n1_ref, m_ref, h_ref, dgate, dup, dy, dq, dk, dv, g1, small, u1, u2, g0, g1_all,
               qkv_out, out_out, gate_out, up_out, down_out, small_out, u_out, g_out,
               fin, far_fin, keep_sem, give_sem, take_sem, fin_sem, far_sem, own, send, rc, rx, ry, rz, send_sem, xs_sem, ys_sem, zs_sem, rc_sem, rx_sem, ry_sem, rz_sem):
    section, me = lax.axis_index("section"), lax.axis_index("dp")
    core, x, low, high = lax.rem(section, 2), lax.rem(me, 2), lax.rem(me // 2, 2), me // 4
    far_core = {"section": section + 1 - 2 * core}
    far_x, far_low, far_high = {"dp": me + 1 - 2 * x}, {"dp": me + 2 - 4 * low}, {"dp": me + 4 - 8 * high}
    barrier = pltpu.get_barrier_semaphore()
    for other in (far_core, far_x, far_low, far_high):
        pl.semaphore_signal(barrier, inc=1, device_id=other, device_id_type=MESH)
    pl.semaphore_wait(barrier, 4)

    def remote(src, dst, sent, got, other):
        return pltpu.make_async_remote_copy(src_ref=src, dst_ref=dst, send_sem=sent, recv_sem=got, device_id=other, device_id_type=MESH)

    def micro(which, mixer_side, mlp_side, into):
        return (
            pltpu.make_async_copy(mixer_side if which == 0 else mlp_side, into.at[core], keep_sem.at[0 if into is u_out else 1]),
            remote(mlp_side if which == 0 else mixer_side, into.at[core], give_sem.at[0 if into is u_out else 1], take_sem.at[0 if into is u_out else 1], far_core),
        )

    for which in range(2):
        @pl.when(core == which)
        def _():
            for pair in (micro(which, u1, u2, u_out), micro(which, g0, g1_all, g_out)):
                for copy in pair:
                    copy.start()

    @pl.when(core != 0)
    def _():
        qkv_out[...] = jnp.zeros_like(qkv_out)
        out_out[...] = jnp.zeros_like(out_out)

    @pl.when(core != 1)
    def _():
        for ref in (gate_out, up_out, down_out):
            ref[...] = jnp.zeros_like(ref)

    def slot(t):
        return lax.rem(t, SLOTS)

    def core_copy(t):
        return remote(send.at[slot(t)], rc.at[t], send_sem.at[slot(t)], rc_sem.at[t], far_core)

    def turned(t):
        return lax.rem(t, 4) // 3

    def first_copy(t, z_first):
        src = rc.at[t, :, 1 - low] if z_first else rc.at[t, :, :, 1 - x]
        return remote(src, rx.at[t], xs_sem.at[slot(t)], rx_sem.at[t], far_low if z_first else far_x)

    def second_copy(t):
        way = turned(t)
        other = {"dp": me + way * (1 - 2 * x) + (1 - way) * (2 - 4 * low)}
        mine = way * x + (1 - way) * low
        return remote(rx.at[t, :, 1 - mine], ry.at[t], ys_sem.at[slot(t)], ry_sem.at[t], other)

    def high_copy(t):
        return remote(ry.at[t, 1 - high], rz.at[t], zs_sem.at[slot(t)], rz_sem.at[t], far_high)

    def free(copy, t):
        @pl.when(t >= SLOTS)
        def _():
            copy(t - SLOTS).wait_send()

    def either(t, act):
        for z_first in (False, True):
            @pl.when(turned(t) == int(z_first))
            def _():
                act(z_first)

    def after_core(t):
        core_copy(t).wait_recv()
        rc[t] = rc[t] + own[slot(t)]
        free(lambda u: first_copy(u, False), t)
        either(t, lambda z_first: first_copy(t, z_first).start())

    def after_first(t):
        first_copy(t, False).wait_recv()

        def add(z_first):
            rx[t] = rx[t] + (rc[t, :, low] if z_first else rc[t, :, :, x])

        either(t, add)
        free(second_copy, t)
        second_copy(t).start()

    def after_second(t):
        second_copy(t).wait_recv()
        way = turned(t)
        ry[t] = ry[t] + rx[t, :, way * x + (1 - way) * low]
        free(high_copy, t)
        high_copy(t).start()

    def far_copy(t):
        return remote(fin.at[slot(t)], far_fin.at[t], fin_sem.at[slot(t)], far_sem.at[t], far_core)

    def place_columns(into, base):
        def place(t, half, value):
            into[pl.ds(pl.multiple_of(half * PIECE[0], PIECE[0]), PIECE[0]), span(t, base)] = value
        return place

    def place_rows(base):
        def place(t, half, value):
            count = h_ref.shape[2] // 8
            begin_row = pl.multiple_of(half * (down_out.shape[0] // 2) + (t - base) * count, 16)
            for c in range(PIECE[0] // count):
                down_out[pl.ds(begin_row, count), c * PIECE[1] : (c + 1) * PIECE[1]] = value[c * count : (c + 1) * count]
        return place

    def after_high(t):
        high_copy(t).wait_recv()
        value = rz[t].astype(f32) + ry[t, high].astype(f32)
        for base, count, target, _, place in segments:
            @pl.when((t >= base) & (t < base + count))
            def _():
                if target is None:
                    small_out[...] = value
                    return

                @pl.when(core == target)
                def _():
                    place(t, core, value)

                @pl.when(core != target)
                def _():
                    @pl.when(t - SLOTS >= first_of[target])
                    def _():
                        far_copy(t - SLOTS).wait_send()

                    fin[slot(t)] = value
                    far_copy(t).start()

    def after_far(t):
        for base, count, target, _, place in segments:
            if target is not None:
                @pl.when((t >= base) & (t < base + count) & (core == target))
                def _():
                    far_copy(t).wait_recv()
                    place(t, 1 - core, far_fin[t])

    def later(t):
        for step, lag in zip((after_core, after_first, after_second, after_high, after_far), LAGS):
            @pl.when((t >= lag) & (t < total + lag))
            def _():
                step(t - lag)

    def span(t, base):
        return pl.ds(pl.multiple_of((t - base) * PIECE[1], PIECE[1]), PIECE[1])

    def by_columns(lhs, rhs, base):
        def fill(t):
            block = rhs[:, span(t, base)]
            for which, into in ((1 - core, send), (core, own)):
                part = nn(lhs[which], block).astype(bf16)
                into[slot(t)] = part.reshape(own.shape[1:])
        return fill

    def by_rows(base):
        def fill(t):
            for which, into in ((1 - core, send), (core, own)):
                part = nn(h_ref[t - base, which], dy[...]).astype(bf16)
                count = part.shape[0] // 8
                for d in range(8):
                    for c in range(PIECE[0] // count):
                        into[slot(t), d // 4, d // 2 % 2, d % 2, c * count : (c + 1) * count, :] = part[d * count : (d + 1) * count, c * PIECE[1] : (c + 1) * PIECE[1]]
        return fill

    def given(t):
        send[slot(t)] = small[1 - core]
        own[slot(t)] = small[core]

    segments, base = [], 0
    for target, columns, lhs, rhs, into in (
        (1, True, n2_ref, dgate, gate_out),
        (1, True, n2_ref, dup, up_out),
        (1, False, h_ref, dy, down_out),
        (0, True, n1_ref, dq, qkv_out.at[0]),
        (0, True, n1_ref, dk, qkv_out.at[1]),
        (0, True, n1_ref, dv, qkv_out.at[2]),
        (0, True, m_ref, g1, out_out),
    ):
        count = rhs.shape[1] // PIECE[1] if columns else lhs.shape[0]
        fill = by_columns(lhs, rhs, base) if columns else by_rows(base)
        place = place_columns(into, base) if columns else place_rows(base)
        segments.append((base, count, target, fill, place))
        base += count
    first_of = {c: min(s[0] for s in segments if s[2] == c) for c in range(2)}
    last_of = {c: max(s[0] + s[1] for s in segments if s[2] == c) for c in range(2)}
    segments.append((base, 1, None, given, None))
    for base, count, _, fill, _ in segments:
        def body(t, carry, fill=fill):
            @pl.when(t >= SLOTS)
            def _():
                core_copy(t - SLOTS).wait_send()

            fill(t)
            core_copy(t).start()
            later(t)
            return carry

        lax.fori_loop(base, base + count, body, 0)

    def drain(t, carry):
        later(t)
        return carry

    lax.fori_loop(total, total + LAGS[-1], drain, 0)
    for copy in (core_copy, lambda t: first_copy(t, False), second_copy, high_copy):
        for t in range(total - SLOTS, total):
            copy(jnp.int32(t)).wait_send()
    for target in range(2):
        @pl.when(core != target)
        def _():
            for t in range(last_of[target] - SLOTS, last_of[target]):
                far_copy(jnp.int32(t)).wait_send()

    for which in range(2):
        @pl.when(core == which)
        def _():
            for keep, give in (micro(which, u1, u2, u_out), micro(which, g0, g1_all, g_out)):
                keep.wait()
                give.wait_send()
                give.wait_recv()


def summed_gradients(n2, n1, m, h, dgate, dup, dy, dq, dk, dv, g1, small, u1, u2, g0):
    total = (2 * dgate.shape[1] + 4 * dq.shape[1]) // PIECE[1] + h.shape[0] + 1
    buffer = lambda *lead: pltpu.VMEM(lead + PIECE, bf16)
    dma = lambda n: pltpu.SemaphoreType.DMA((n,))
    vmem, anywhere = pl.BlockSpec(memory_space=pltpu.VMEM), pl.BlockSpec(memory_space=pl.ANY)
    operands = (n2, n1, m, h, dgate, dup, dy, dq, dk, dv, g1, small)
    ff, width, rows = dgate.shape[1], dq.shape[1], 2 * PIECE[0]
    result = lambda *shape: jax.ShapeDtypeStruct(shape, f32)
    pair = jax.ShapeDtypeStruct((2,) + u1.shape, bf16)
    return pl.pallas_call(
        functools.partial(sum_kernel, total),
        out_shape=[result(3, rows, width), result(rows, width), result(rows, ff), result(rows, ff), result(ff // 8, width), result(*PIECE), pair, pair],
        in_specs=[vmem] * len(operands) + [anywhere] * 4,
        out_specs=[vmem] * 6 + [anywhere] * 2,
        scratch_shapes=[
            pltpu.VMEM((SLOTS,) + PIECE, f32), pltpu.VMEM((total,) + PIECE, f32), dma(2), dma(2), dma(2), dma(SLOTS), dma(total),
            buffer(SLOTS, 2, 2, 2), buffer(SLOTS, 2, 2, 2), buffer(total, 2, 2, 2), buffer(total, 2, 2), buffer(total, 2), buffer(total),
            dma(SLOTS), dma(SLOTS), dma(SLOTS), dma(SLOTS), dma(total), dma(total), dma(total), dma(total),
        ],
        compiler_params=pltpu.CompilerParams(collective_id=0, has_side_effects=True, vmem_limit_bytes=62 * 1024 * 1024),
        name="gradient_sums",
    )(*operands, u1, u2, g0, g1)


def rms_forward(x, gain):
    scale = lax.rsqrt(jnp.mean(x * x, -1, keepdims=True) + 1e-06)
    return (x * scale * gain).astype(bf16), scale


def rms_backward(x, scale, gain, grad):
    gain_grad = jnp.sum(grad * x * scale, 0)
    inner = jnp.mean(grad * gain * x, -1, keepdims=True)
    return scale * gain * grad - x * scale**3 * inner, gain_grad


def matmul(a, b):
    return jnp.dot(a, b, preferred_element_type=f32)


def matmul_nt(a, b):
    return lax.dot_general(a, b, (((1,), (1,)), ((), ())), preferred_element_type=f32)


def matmul_tn(a, b):
    return lax.dot_general(a, b, (((0,), (0,)), ((), ())), preferred_element_type=f32)


def mixer_forward(u, w, token_mask, own=()):
    x = u.astype(f32)
    normed, scale = rms_forward(x, w["attn_gain"])
    proj = [matmul(normed, w["qkv"][p]) for p in range(3)]
    rate = jax.nn.sigmoid(matmul_nt(normed, w["beta"]))
    beta = rate * token_mask
    mixed, *saved = mixer_fwd(proj, beta, w["conv"], w["head_gain"], own)
    saved, given = saved[:4], saved[4:]
    result = (x + matmul(mixed, w["out"])).astype(bf16)
    return result, (u, normed, scale, proj, rate, beta, mixed, saved), given


def mixer_input_grad(kept, dy, w, token_mask):
    u, normed, scale, proj, rate, beta, mixed, saved = kept
    dmixed = matmul_nt(dy, w["out"])
    *dproj, dbeta, dtq, dtk, dtv, dhead = mixer_bwd(proj, beta, w["conv"], w["head_gain"], saved, dmixed)
    dlogits = dbeta * token_mask * rate * (1.0 - rate)
    dnormed = sum(matmul_nt(d, w["qkv"][p]) for p, d in enumerate(dproj))
    dnormed = dnormed + matmul(dlogits.astype(bf16), w["beta"])
    dx, dgain = rms_backward(u.astype(f32), scale, w["attn_gain"], dnormed)
    g = (dy.astype(f32) + dx).astype(bf16)
    return g, (dproj, dlogits, jnp.stack([dtq, dtk, dtv], 1), dhead[0], dgain)


def mlp_forward(u, w):
    x = u.astype(f32)
    normed, scale = rms_forward(x, w["mlp_gain"])
    gate, up = matmul(normed, w["gate"]), matmul(normed, w["up"])
    hidden = (jax.nn.silu(gate) * up).astype(bf16)
    result = (x + matmul(hidden, w["down"])).astype(bf16)
    return result, (u, normed, scale, gate, up, hidden)


def mlp_input_grad(kept, dy, w):
    u, normed, scale, gate, up, hidden = kept
    dhidden = matmul_nt(dy, w["down"])
    sig = jax.nn.sigmoid(gate)
    dgate = (dhidden * up * (sig * (1.0 + gate * (1.0 - sig)))).astype(bf16)
    dup = (dhidden * (gate * sig)).astype(bf16)
    dnormed = matmul_nt(dgate, w["gate"]) + matmul_nt(dup, w["up"])
    dx, dgain = rms_backward(u.astype(f32), scale, w["mlp_gain"], dnormed)
    g = (dy.astype(f32) + dx).astype(bf16)
    return g, (dgate, dup, dgain)


def pick(x, index, axis):
    return lax.dynamic_index_in_dim(x, index, axis, keepdims=False)


def shards(inputs, cotangent, lengths, attn_gain, qkv_weight, conv_weight, beta_weight, head_gain, out_weight, mlp_gain, gate_up_weight, down_weight):
    section, sections = lax.axis_index("section"), lax.axis_size("section")
    me, group = lax.axis_index("dp"), lax.axis_size("dp")
    core, stage = section % 2, section // 2
    swap = [(i, i ^ 1) for i in range(sections)]
    to_odd = [(i, i + 1) for i in range(0, sections, 2)]
    to_even = [(i + 1, i) for i in range(0, sections, 2)]
    rows = inputs.shape[2]
    width = inputs.shape[3]

    qkv, out_w, down, conv, beta_w, attn, head, mlp, own_gate, own_up = first_exchange(
        jnp.moveaxis(qkv_weight[0], 1, 0),
        out_weight[0],
        down_weight[0],
        jnp.moveaxis(conv_weight[0], 1, 0),
        beta_weight[0].T,
        attn_gain,
        head_gain,
        mlp_gain,
        gate_up_weight[0],
    )
    w = {"attn_gain": attn, "conv": conv, "beta": beta_w, "head_gain": head, "qkv": qkv, "out": out_w, "mlp_gain": mlp, "down": down}

    first = pick(inputs[:, 0], core, 0)
    seed = pick(cotangent[:, 0], core, 0)
    length = pick(lengths[:, 0], core, 0)
    token_mask = (jnp.arange(rows) < length).astype(f32)[:, None]
    up_stage = [(i, i + 2) for i in range(sections - 2)]
    down_stage = [(i + 2, i) for i in range(sections - 2)]

    u0 = first
    for step in range(sections // 2):
        if step == 0:
            u1, kept_mixer, (w["gate"], w["up"]) = mixer_forward(u0, w, token_mask, (own_gate, own_up))
        else:
            u1, kept_mixer, _ = mixer_forward(u0, w, token_mask)
        u2, kept_mlp = mlp_forward(u1, w)
        if step + 1 < sections // 2:
            u0 = jnp.where(stage == 0, first, lax.ppermute(u2, "section", up_stage))
    last_stage = sections // 2 - 1
    _, normed1, _, _, _, _, mixed, _ = kept_mixer
    _, normed2, _, _, _, hidden = kept_mlp
    ff = hidden.shape[1]
    fused = group == 8 and width == 1024 and ff % 256 == 0
    for_sums = ()
    if fused:
        by_owner = lambda a: a.reshape(rows, group, 2, 64).transpose(2, 1, 3, 0).reshape(2, group * 64, rows)
        down_rows = hidden.reshape(rows, group, 2, ff // 256, 16).transpose(3, 2, 1, 4, 0).reshape(ff // 256, 2, group * 16, rows)
        for_sums = (by_owner(normed2), by_owner(normed1), by_owner(mixed), down_rows)
    dy = seed
    for step in range(sections // 2):
        g1, mlp_parts = mlp_input_grad(kept_mlp, dy, w)
        g0, mixer_parts = mixer_input_grad(kept_mixer, g1, w, token_mask)
        if step + 1 < sections // 2:
            dy = jnp.where(stage == last_stage, seed, lax.ppermute(g0, "section", down_stage))
            dy, u2, for_sums = lax.optimization_barrier((dy, u2, for_sums))

    dgate, dup, d_mlp_gain = mlp_parts
    dproj, dlogits, dtaps, dhead, d_attn_gain = mixer_parts

    def halve(x):
        kept = pick(x, core, 1).astype(f32)
        x = (kept + lax.ppermute(pick(x, 1 - core, 1), "section", swap).astype(f32)).astype(bf16)
        return scatter(x)

    def scatter(x):
        kind = x.dtype
        bit = 1
        while bit < group:
            pairs = [(i, i ^ bit) for i in range(group)]
            mine = (me // bit) % 2
            x = x.reshape((x.shape[0] // 2, 2) + x.shape[1:])
            other = lax.ppermute(pick(x, 1 - mine, 1), "dp", pairs)
            x = pick(x, mine, 1).astype(f32) + other.astype(f32)
            bit *= 2
            if bit < group:
                x = x.astype(kind)
        return x[0]

    def share(grad):
        count, cols = grad.shape
        return halve(grad.astype(bf16).reshape(group, 2, count // group // 2, cols))

    dbeta = lax.dot_general(normed1.astype(f32), dlogits, (((0,), (0,)), ((), ())), precision=lax.Precision.HIGHEST)
    taps_rows = jnp.moveaxis(dtaps.reshape(-1, 3, group, width // group), 2, 0).reshape(group, -1)
    small = [d_attn_gain.reshape(group, -1), taps_rows, dbeta.reshape(group, -1), dhead.reshape(group, -1), d_mlp_gain.reshape(group, -1)]
    sizes = [a.shape[1] for a in small]
    joined = jnp.concatenate(small, 1)
    mixer_size = sum(sizes[:4])
    on_even = lambda x: jnp.where(core == 0, x, 0.0)
    on_odd = lambda x: jnp.where(core == 1, x, 0.0)
    if fused:
        per = PIECE[0] * PIECE[1]
        one = lambda a: jnp.pad(a, ((0, 0), (0, per - a.shape[1]))).astype(bf16).reshape(2, 2, 2, *PIECE)
        low_small = jnp.stack([one(joined[:, :mixer_size]), one(joined[:, mixer_size:])])
        grad_qkv, grad_out, grad_gate, grad_up, grad_down, small, sec_out, sec_grad = summed_gradients(
            *for_sums, dgate, dup, dy, *dproj, g1, low_small, u1, u2, g0
        )
        grad_qkv = jnp.moveaxis(grad_qkv, 0, 1)
        grad_gate_up = jnp.stack([grad_gate, grad_up], 1)
        small = small.reshape(-1)
        small = jnp.concatenate([small[:mixer_size], small[: sizes[4]]])
        sec_out, sec_grad = sec_out[None, :, None], sec_grad[None, :, None]
    else:
        down_share = share(matmul_tn(hidden, dy))
        gate_share = share(matmul_tn(normed2, dgate))
        up_share = share(matmul_tn(normed2, dup))
        out_share = share(matmul_tn(mixed, g1))
        qkv_share = [share(matmul_tn(normed1, d)) for d in dproj]
        small = scatter(joined + lax.ppermute(joined, "section", swap))
        def to_core(x, target):
            other = lax.ppermute(x, "section", to_even if target == 0 else to_odd)
            both = jnp.concatenate([x, other] if target == 0 else [other, x], 0)
            return jnp.where(core == target, both, 0.0)

        grad_qkv = jnp.stack([to_core(x, 0) for x in qkv_share], 1)
        grad_out = to_core(out_share, 0)
        grad_gate_up = jnp.stack([to_core(gate_share, 1), to_core(up_share, 1)], 1)
        grad_down = to_core(down_share, 1)

        def both_micro(mixer_side, mlp_side):
            own = jnp.where(core == 0, mixer_side, mlp_side)
            other = lax.ppermute(jnp.where(core == 0, mlp_side, mixer_side), "section", swap)
            return jnp.where(core == 0, jnp.stack([own, other]), jnp.stack([other, own]))[None, :, None]

        sec_out, sec_grad = both_micro(u1, u2), both_micro(g0, g1)

    offsets = [sum(sizes[:i]) for i in range(len(sizes) + 1)]
    s_attn, s_taps, s_beta, s_head, s_mlp = [small[a:b] for a, b in zip(offsets, offsets[1:])]

    return (
        sec_out,
        sec_grad,
        on_even(s_attn)[None],
        grad_qkv[None],
        on_even(s_taps).reshape(1, -1, 3, width // group),
        on_even(s_beta).reshape(1, -1, dbeta.shape[1]),
        on_even(s_head)[None],
        grad_out[None],
        on_odd(s_mlp)[None],
        grad_gate_up[None],
        grad_down[None],
    )


def solution(mesh):
    in_specs = (
        P(None, "dp", None, None),
        P(None, "dp", None, None),
        P(None, "dp"),
        P("section", None),
        P("section", None, None, None),
        P("section", None, None, None),
        P("section", None, None),
        P("section", None),
        P("section", None, None),
        P("section", None),
        P("section", None, None, None),
        P("section", None, None),
    )
    out_specs = (
        P("section", None, "dp", None, None),
        P("section", None, "dp", None, None),
        P("section", "dp"),
        P("section", "dp", None, None),
        P("section", None, None, "dp"),
        P("section", "dp", None),
        P("section", "dp"),
        P("section", "dp", None),
        P("section", "dp"),
        P("section", "dp", None, None),
        P("section", "dp", None),
    )
    return jax.shard_map(shards, mesh=mesh, in_specs=in_specs, out_specs=out_specs, check_vma=False)
```

```python
import functools

import jax, jax.numpy as jnp
from jax import lax
from jax.experimental import pallas as pl
from jax.experimental.pallas import tpu as pltpu
from jax.sharding import PartitionSpec as P

CHUNK = 128
MESH = pl.DeviceIdType.MESH
bf16, f32 = jnp.bfloat16, jnp.float32


def nn(a, b):
    return lax.dot_general(a.astype(bf16), b.astype(bf16), (((1,), (0,)), ((), ())), preferred_element_type=f32)


def nt(a, b):
    return lax.dot_general(a.astype(bf16), b.astype(bf16), (((1,), (1,)), ((), ())), preferred_element_type=f32)


def tn(a, b):
    return lax.dot_general(a.astype(bf16), b.astype(bf16), (((0,), (0,)), ((), ())), preferred_element_type=f32)


def shifted_rows(x, steps):
    count = x.shape[0]
    rows = lax.broadcasted_iota(jnp.int32, (8, x.shape[1]), 0)
    moved = pltpu.roll(x, steps % count, 0)
    if steps > 0:
        return jnp.concatenate([jnp.where(rows >= steps, moved[:8], 0.0), moved[8:]], 0)
    return jnp.concatenate([moved[:-8], jnp.where(rows < 8 + steps, moved[-8:], 0.0)], 0)


def convolved(x, taps):
    total = x * taps[3:4]
    for back in range(1, 4):
        total = total + shifted_rows(x, back) * taps[3 - back : 4 - back]
    return total


def chunk_masks():
    row = lax.broadcasted_iota(jnp.int32, (CHUNK, CHUNK), 0)
    col = lax.broadcasted_iota(jnp.int32, (CHUNK, CHUNK), 1)
    return row, col


def level_mask(row, col, size):
    shift = size.bit_length() - 1
    same = (row >> (shift + 1)) == (col >> (shift + 1))
    return same & (((row >> shift) & 1) == 1) & (((col >> shift) & 1) == 0)


def triangular_inverse(a_list, row, col):
    mask = level_mask(row, col, 1)
    xs = [jnp.where(mask, -a, 0.0) for a in a_list]
    size = 2
    while size < CHUNK:
        mask = level_mask(row, col, size)
        parts = [jnp.where(mask, a, 0.0) for a in a_list]
        ys = [p + nn(p, x) for p, x in zip(parts, xs)]
        xs = [x - (y + nn(x, y)) for x, y in zip(xs, ys)]
        size *= 2
    return xs


def head_column(block, head):
    lanes = lax.broadcasted_iota(jnp.int32, block.shape, 1)
    return jnp.sum(jnp.where(lanes == head, block, 0.0), axis=1, keepdims=True)


def greet_far_core(section):
    far = {"section": section + 1 - 2 * lax.rem(section, 2)}
    barrier = pltpu.get_barrier_semaphore()
    pl.semaphore_signal(barrier, inc=1, device_id=far, device_id_type=MESH)
    pl.semaphore_wait(barrier, 1)
    return far


def give_weights(step, steps, from_even, from_odd, send_sem, recv_sem):
    section = lax.axis_index("section")
    core = lax.rem(section, 2)
    far = {"section": section + 1 - 2 * core}
    pairs = [(0, *p) for p in from_even] + [(1, *p) for p in from_odd]

    def give(i):
        return pltpu.make_async_remote_copy(
            src_ref=pairs[i][1], dst_ref=pairs[i][2], send_sem=send_sem.at[i], recv_sem=recv_sem.at[i], device_id=far, device_id_type=MESH
        )

    @pl.when(step == 0)
    def _():
        greet_far_core(section)
        for i, (owner, _, _) in enumerate(pairs):
            @pl.when(core == owner)
            def _():
                give(i).start()

    @pl.when(step == steps - 1)
    def _():
        for i, (owner, _, _) in enumerate(pairs):
            @pl.when(core == owner)
            def _():
                give(i).wait_send()

            @pl.when(core != owner)
            def _():
                give(i).wait_recv()


def first_kernel(qkv, out, down, conv, beta, attn_gain, head_gain, mlp_gain, both, qkv_part, out_part, down_part, qkv_full, out_full, down_full, conv_full, beta_full, attn_full, head_full, mlp_full, gate, up,
                 mine, theirs, local_sem, send_sem, recv_sem, small_sems):
    step, steps = pl.program_id(0), pl.num_programs(0)
    section = lax.axis_index("section")
    core = lax.rem(section, 2)
    give_weights(step, steps, [(qkv, qkv_full), (out, out_full)], [(down, down_full)], send_sem, recv_sem)
    small = pltpu.make_async_remote_copy(
        src_ref=mine, dst_ref=theirs, send_sem=small_sems.at[0], recv_sem=small_sems.at[1],
        device_id={"section": section + 1 - 2 * core}, device_id_type=MESH,
    )

    @pl.when(step == 0)
    def _():
        mine[...] = jnp.zeros_like(mine)
        for p in range(3):
            mine[8 * p : 8 * p + 4, :] = conv[p].astype(f32)
        mine[4:5, :] = attn_gain[...].astype(f32)
        mine[5:6, : head_gain.shape[1]] = head_gain[...].astype(f32)
        mine[6:7, :] = mlp_gain[...].astype(f32)
        mine[24:32, :] = beta[...].astype(f32)
        small.start()

    count, down_count = out_part.shape[0], down_part.shape[0]
    block, down_block = pl.ds(step * count, count), pl.ds(step * down_count, down_count)
    own = [
        (0, pltpu.make_async_copy(qkv_part, qkv_full.at[:, block], local_sem.at[0])),
        (0, pltpu.make_async_copy(out_part, out_full.at[block], local_sem.at[1])),
        (1, pltpu.make_async_copy(down_part, down_full.at[down_block], local_sem.at[2])),
    ]
    for owner, copy in own:
        @pl.when(core == owner)
        def _():
            copy.start()

    apart = jnp.swapaxes(both[...], 0, 1)
    gate[...] = apart[0]
    up[...] = apart[1]
    for owner, copy in own:
        @pl.when(core == owner)
        def _():
            copy.wait()

    @pl.when(step == steps - 1)
    def _():
        small.wait()
        mixer = jnp.where(core == 0, mine[...], theirs[...])
        for p in range(3):
            conv_full[p] = mixer[8 * p : 8 * p + 4]
        attn_full[...] = mixer[4:5]
        head_full[...] = mixer[5:6, : head_full.shape[1]]
        beta_full[...] = mixer[24:32].astype(bf16)
        mlp_full[...] = jnp.where(core == 1, mine[6:7, :], theirs[6:7, :])


def first_exchange(qkv, out, down, conv, beta, attn_gain, head_gain, mlp_gain, both):
    rows, _, ff = both.shape
    width = out.shape[1]
    count = 128
    anywhere = pl.BlockSpec(memory_space=pl.ANY)
    whole = lambda a: pl.BlockSpec(a.shape, lambda i: (0,) * len(a.shape))
    like = lambda a, kind: jax.ShapeDtypeStruct(a.shape, kind)
    smalls = (conv, beta, attn_gain, head_gain, mlp_gain)
    return pl.pallas_call(
        first_kernel,
        grid=(rows // count,),
        in_specs=[anywhere] * 3 + [whole(a) for a in smalls] + [
            pl.BlockSpec((count, 2, ff), lambda i: (i, 0, 0)),
            pl.BlockSpec((3, count, width), lambda i: (0, i, 0)),
            pl.BlockSpec((count, width), lambda i: (i, 0)),
            pl.BlockSpec((ff * count // rows, width), lambda i: (i, 0)),
        ],
        out_specs=[anywhere] * 3 + [whole(a) for a in smalls] + [pl.BlockSpec((count, ff), lambda i: (i, 0))] * 2,
        out_shape=[like(qkv, bf16), like(out, bf16), like(down, bf16), like(conv, f32), like(beta, bf16), like(attn_gain, f32), like(head_gain, f32), like(mlp_gain, f32)]
        + [jax.ShapeDtypeStruct((rows, ff), bf16)] * 2,
        scratch_shapes=[pltpu.VMEM((32, width), f32)] * 2 + [pltpu.SemaphoreType.DMA((3,))] * 3 + [pltpu.SemaphoreType.DMA((2,))],
        compiler_params=pltpu.CompilerParams(collective_id=1, has_side_effects=True, vmem_limit_bytes=48 * 1024 * 1024),
        name="first_exchange",
    )(qkv, out, down, *smalls, both, qkv, out, down)


def mixer_fwd_kernel(per, trade, u_ref, gain_in, w_ref, w_beta, mask_ref, taps_q, taps_k, taps_v, gain_ref, *refs):
    own, refs = refs[:trade], refs[trade:]
    normed_ref, rate_ref, beta_ref, q_ref, k_ref, v_ref, mixed_ref, t_ref, n_ref, s_ref, o_ref = refs[:11]
    if trade:
        give_weights(pl.program_id(0), pl.num_programs(0), [], list(zip(own, refs[11 : 11 + trade])), *refs[11 + trade :])

    @pl.when(pl.program_id(0) == 0)
    def _():
        x = u_ref[...].astype(f32)
        normed = (x * lax.rsqrt(jnp.mean(x * x, 1, keepdims=True) + 1e-6) * gain_in[...]).astype(bf16)
        normed_ref[...] = normed
        rate = jax.nn.sigmoid(nt(normed, w_beta[...]))
        rate_ref[...] = rate
        beta_ref[...] = rate * mask_ref[...]

    for p, ref in enumerate((q_ref, k_ref, v_ref)):
        ref[...] = nn(normed_ref[...], w_ref[p])
    row, col = chunk_masks()
    strict, causal = row > col, row >= col
    chunks = q_ref.shape[0] // CHUNK
    beta_all = beta_ref[...]
    cut = lambda x: [x[i * CHUNK : (i + 1) * CHUNK] for i in range(chunks)]
    lanes = [slice(j * 128, (j + 1) * 128) for j in range(per)]
    qs, ks, vs, bs = [], [], [], []
    for j, lane in enumerate(lanes):

        def activated(ref, taps):
            c = convolved(ref[:, lane], taps[:, lane])
            return c * jax.nn.sigmoid(c)

        q, k, v = activated(q_ref, taps_q), activated(k_ref, taps_k), activated(v_ref, taps_v)
        q = q * lax.rsqrt(jnp.sum(q * q, 1, keepdims=True) + 1e-6)
        k = k * lax.rsqrt(jnp.sum(k * k, 1, keepdims=True) + 1e-6)
        qs.append(cut(q))
        ks.append(cut(k))
        vs.append(cut(v))
        bs.append(cut(head_column(beta_all, pl.program_id(0) * per + j)))
    each = [(j, i) for j in range(per) for i in range(chunks)]
    a_list = [jnp.where(strict, nt(ks[j][i], ks[j][i]) * bs[j][i], 0.0) for j, i in each]
    ps = {(j, i): jnp.where(causal, nt(qs[j][i], ks[j][i]), 0.0) for j, i in each}
    ts = dict(zip(each, triangular_inverse(a_list, row, col)))
    wu = {}
    for j, i in each:
        both = jnp.concatenate([ks[j][i] * bs[j][i], vs[j][i] * bs[j][i]], 1)
        wu[j, i] = both + nn(ts[j, i], both)
    states = [jnp.zeros((128, 128), f32)] * per
    for i in range(chunks):
        span = pl.ds(i * CHUNK, CHUNK)
        news = [wu[j, i][:, 128:] - nn(wu[j, i][:, :128], states[j]) for j in range(per)]
        outs = [nn(jnp.concatenate([qs[j][i], ps[j, i]], 1), jnp.concatenate([states[j], news[j]], 0)) for j in range(per)]
        for j, lane in enumerate(lanes):
            o = outs[j]
            s_ref[j, span, :] = states[j].astype(bf16)
            n_ref[j, span, :] = news[j].astype(bf16)
            t_ref[j, span, :] = ts[j, i].astype(bf16)
            o_ref[span, lane] = o
            mixed_ref[span, lane] = (o * lax.rsqrt(jnp.mean(o * o, 1, keepdims=True) + 1e-5) * gain_ref[...]).astype(bf16)
        if i + 1 < chunks:
            states = [states[j] + tn(ks[j][i], news[j]) for j in range(per)]


def mixer_fwd(u, w, mask, own=(), per=4):
    rows, width = u.shape
    heads = width // 128
    steps = heads // per
    wide = 128 * per
    part = pl.BlockSpec((rows, wide), lambda h: (0, h))
    tap = lambda p: pl.BlockSpec((None, 4, wide), lambda h, p=p: (p, 0, h))
    whole = lambda *shape: pl.BlockSpec(shape, lambda h: (0,) * len(shape))
    saved = pl.BlockSpec((per, rows, 128), lambda h: (h, 0, 0))
    anywhere = [pl.BlockSpec(memory_space=pl.ANY)] * len(own)
    dma = pltpu.SemaphoreType.DMA((max(1, len(own)),))
    shape = lambda kind, *dims: jax.ShapeDtypeStruct(dims, kind)
    return pl.pallas_call(
        functools.partial(mixer_fwd_kernel, per, len(own)),
        grid=(steps,),
        in_specs=[whole(rows, width), whole(1, width), pl.BlockSpec((3, width, wide), lambda h: (0, 0, h)), whole(heads, width), whole(rows, 1)]
        + [tap(0), tap(1), tap(2), whole(1, 128)] + anywhere,
        out_specs=[whole(rows, width), whole(rows, heads), whole(rows, heads), part, part, part, part, saved, saved, saved, part] + anywhere,
        out_shape=[shape(bf16, rows, width), shape(f32, rows, heads), shape(f32, rows, heads)]
        + [shape(f32, rows, width)] * 3
        + [shape(bf16, rows, width)]
        + [shape(bf16, heads, rows, 128)] * 3
        + [shape(f32, rows, width)]
        + [jax.ShapeDtypeStruct(a.shape, a.dtype) for a in own],
        scratch_shapes=[dma, dma] if own else [],
        input_output_aliases={9 + i: 11 + i for i in range(len(own))},
        compiler_params=pltpu.CompilerParams(vmem_limit_bytes=60 * 1024 * 1024, **({"collective_id": 2, "has_side_effects": True} if own else {})),
        name="mixer_forward",
    )(u, w["attn_gain"], w["qkv"], w["beta"], mask, w["conv"], w["conv"], w["conv"], w["head_gain"], *own)


def mixer_back_step(per, step, q_ref, k_ref, v_ref, beta_ref, taps_q, taps_k, taps_v, gain_ref, t_ref, n_ref, s_ref, o_ref, dm_ref, w_ref,
                    dq_ref, dk_ref, dv_ref, dtq_ref, dtk_ref, dtv_ref, dgain_ref, dbeta_ref, dnormed):
    row, col = chunk_masks()
    strict, causal_t = row > col, row <= col
    causal = row >= col
    chunks = q_ref.shape[0] // CHUNK
    beta_all = beta_ref[...]

    @pl.when(step == 0)
    def _():
        dbeta_ref[...] = jnp.zeros_like(dbeta_ref)
        dgain_ref[...] = jnp.zeros_like(dgain_ref)
        dnormed[...] = jnp.zeros_like(dnormed)

    cut = lambda x: [x[i * CHUNK : (i + 1) * CHUNK] for i in range(chunks)]
    heads = range(per)
    lanes = [slice(j * 128, (j + 1) * 128) for j in heads]
    kept, qs, ks, vs, bs, dos = [], [], [], [], [], []
    for j, lane in enumerate(lanes):

        def activated(ref, taps):
            c = convolved(ref[:, lane], taps[:, lane])
            sig = jax.nn.sigmoid(c)
            return c * sig, sig * (1.0 + c * (1.0 - sig))

        q_act, q_slope = activated(q_ref, taps_q)
        k_act, k_slope = activated(k_ref, taps_k)
        v, v_slope = activated(v_ref, taps_v)
        q_scale = lax.rsqrt(jnp.sum(q_act * q_act, 1, keepdims=True) + 1e-6)
        k_scale = lax.rsqrt(jnp.sum(k_act * k_act, 1, keepdims=True) + 1e-6)
        q, k = q_act * q_scale, k_act * k_scale
        o, dm, gain = o_ref[:, lane], dm_ref[:, lane], gain_ref[...]
        o_scale = lax.rsqrt(jnp.mean(o * o, 1, keepdims=True) + 1e-5)
        o_hat = o * o_scale
        dgain_ref[...] += jnp.sum(dm * o_hat, 0, keepdims=True)
        dmg = dm * gain
        do = o_scale * (dmg - o_hat * jnp.mean(dmg * o_hat, 1, keepdims=True))
        kept.append((q, k, q_scale, k_scale, q_slope, k_slope, v_slope))
        qs.append(cut(q))
        ks.append(cut(k))
        vs.append(cut(v))
        bs.append(cut(head_column(beta_all, step * per + j)))
        dos.append(cut(do))
    dstates = [jnp.zeros((128, 128), f32)] * per
    dqs, dks, dvs, dbs = [[[] for _ in heads] for _ in range(4)]
    for i in reversed(range(chunks)):
        span = pl.ds(i * CHUNK, CHUNK)
        qc, kc, vc, bc, doc = [[x[j][i] for j in heads] for x in (qs, ks, vs, bs, dos)]
        n, s, t = [[ref[j, span, :] for j in heads] for ref in (n_ref, s_ref, t_ref)]
        gp = [nt(kc[j], jnp.concatenate([kc[j], qc[j]], 0)) for j in heads]
        p_t = [jnp.where(causal_t, gp[j][:, 128:], 0.0) for j in heads]
        dn = [nn(jnp.concatenate([p_t[j], kc[j]], 1), jnp.concatenate([doc[j], dstates[j]], 0)) for j in heads]
        dr = [dn[j] + tn(t[j], dn[j]) for j in heads]
        de = [dr[j] * bc[j] for j in heads]
        both = [nt(doc[j], jnp.concatenate([n[j], s[j]], 0)) for j in heads]
        e = [vc[j] - nn(kc[j], s[j]) for j in heads]
        da = [jnp.where(strict, -nt(dr[j], n[j]), 0.0) for j in heads]
        dp = [jnp.where(causal, both[j][:, :128], 0.0) for j in heads]
        dg = [da[j] * bc[j] for j in heads]
        for j in heads:
            dqs[j].append(both[j][:, 128:] + nn(dp[j], kc[j]))
            dbs[j].append(jnp.sum(dr[j] * e[j], 1, keepdims=True) + jnp.sum(da[j] * gp[j][:, :128], 1, keepdims=True))
            dks[j].append(
                tn(dp[j], qc[j])
                + nt(jnp.concatenate([n[j], -de[j].astype(bf16)], 1), jnp.concatenate([dstates[j].astype(bf16), s[j]], 1))
                + nn(dg[j], kc[j])
                + tn(dg[j], kc[j])
            )
            dvs[j].append(de[j])
        if i:
            dstates = [dstates[j] + tn(qc[j], doc[j]) - tn(kc[j], de[j]) for j in heads]
    join = lambda xs: jnp.concatenate(xs[::-1], 0)
    lane_ids = lax.broadcasted_iota(jnp.int32, dbeta_ref.shape, 1)
    for j, lane in enumerate(lanes):
        q, k, q_scale, k_scale, q_slope, k_slope, v_slope = kept[j]
        dq, dk, dv, db = join(dqs[j]), join(dks[j]), join(dvs[j]), join(dbs[j])
        dq = q_scale * (dq - q * jnp.sum(dq * q, 1, keepdims=True))
        dk = k_scale * (dk - k * jnp.sum(dk * k, 1, keepdims=True))
        dbeta_ref[...] += jnp.where(lane_ids == step * per + j, db, 0.0)
        for grad, slope, ref, taps, out, dtaps in (
            (dq, q_slope, q_ref, taps_q, dq_ref, dtq_ref),
            (dk, k_slope, k_ref, taps_k, dk_ref, dtk_ref),
            (dv, v_slope, v_ref, taps_v, dv_ref, dtv_ref),
        ):
            dc = grad * slope
            x = ref[:, lane]
            w = taps[:, lane]
            dx = dc * w[3:4]
            rows = [None] * 4
            rows[3] = jnp.sum(dc * x, 0, keepdims=True)
            for back in range(1, 4):
                moved = shifted_rows(dc, -back)
                dx = dx + moved * w[3 - back : 4 - back]
                rows[3 - back] = jnp.sum(moved * x, 0, keepdims=True)
            out[:, lane] = dx.astype(bf16)
            dtaps[:, lane] = jnp.concatenate(rows, 0)

    dnormed[...] += sum(nt(ref[...], w_ref[p]) for p, ref in enumerate((dq_ref, dk_ref, dv_ref)))


def mixer_back_end(beta_ref, rate_ref, u_ref, normed_ref, gain_in, w_beta, dy_ref, dbeta_ref, dnormed, g_ref, dgain_in, dw_beta):
    dlogits = dbeta_ref[...] * beta_ref[...] * (1.0 - rate_ref[...])
    high = dlogits.astype(bf16)
    low = (dlogits - high.astype(f32)).astype(bf16)
    dw_beta[...] = tn(high, normed_ref[...]) + tn(low, normed_ref[...])
    x = u_ref[...].astype(f32)
    scale = lax.rsqrt(jnp.mean(x * x, 1, keepdims=True) + 1e-6)
    hat = x * scale
    grad = dnormed[...] + nn(high, w_beta[...])
    dgain_in[...] = jnp.sum(grad * hat, 0, keepdims=True)
    grad = grad * gain_in[...]
    dx = scale * (grad - hat * jnp.mean(grad * hat, 1, keepdims=True))
    g_ref[...] = (dy_ref[...].astype(f32) + dx).astype(bf16)


def mixer_bwd_kernel(per, q_ref, k_ref, v_ref, beta_ref, taps_q, taps_k, taps_v, gain_ref, t_ref, n_ref, s_ref, o_ref, dm_ref,
                     u_ref, normed_ref, rate_ref, gain_in, w_ref, w_beta, dy_ref,
                     dq_ref, dk_ref, dv_ref, dtq_ref, dtk_ref, dtv_ref, dgain_ref, g_ref, dgain_in, dw_beta, dbeta_ref, dnormed):
    step = pl.program_id(0)
    mixer_back_step(per, step, q_ref, k_ref, v_ref, beta_ref, taps_q, taps_k, taps_v, gain_ref, t_ref, n_ref, s_ref, o_ref, dm_ref, w_ref,
                    dq_ref, dk_ref, dv_ref, dtq_ref, dtk_ref, dtv_ref, dgain_ref, dbeta_ref, dnormed)

    @pl.when(step == pl.num_programs(0) - 1)
    def _():
        mixer_back_end(beta_ref, rate_ref, u_ref, normed_ref, gain_in, w_beta, dy_ref, dbeta_ref, dnormed, g_ref, dgain_in, dw_beta)


def mixer_bwd(kept, w, dmixed, dy, per=4):
    u, normed, rate, beta, q, k, v, t, n, s, o = kept
    rows, width = u.shape
    heads = width // 128
    steps = heads // per
    wide = 128 * per
    part = pl.BlockSpec((rows, wide), lambda h: (0, h))
    tap = lambda p: pl.BlockSpec((None, 4, wide), lambda h, p=p: (p, 0, h))
    taps_out = pl.BlockSpec((4, wide), lambda h: (0, h))
    whole = lambda *shape: pl.BlockSpec(shape, lambda h: (0,) * len(shape))
    saved = pl.BlockSpec((per, rows, 128), lambda h: (h, 0, 0))
    shape = lambda kind, *dims: jax.ShapeDtypeStruct(dims, kind)
    stream = whole(rows, width)
    return pl.pallas_call(
        functools.partial(mixer_bwd_kernel, per),
        grid=(steps,),
        in_specs=[part, part, part, whole(rows, heads), tap(0), tap(1), tap(2), whole(1, 128), saved, saved, saved, part, part]
        + [stream, stream, whole(rows, heads), whole(1, width), pl.BlockSpec((3, width, wide), lambda h: (0, 0, h)), whole(heads, width), stream],
        out_specs=[part] * 3 + [taps_out] * 3 + [whole(1, 128), stream, whole(1, width), whole(heads, width)],
        out_shape=[shape(bf16, rows, width)] * 3 + [shape(f32, 4, width)] * 3
        + [shape(f32, 1, 128), shape(bf16, rows, width), shape(f32, 1, width), shape(f32, heads, width)],
        scratch_shapes=[pltpu.VMEM((rows, heads), f32), pltpu.VMEM((rows, width), f32)],
        compiler_params=pltpu.CompilerParams(vmem_limit_bytes=60 * 1024 * 1024),
        name="mixer_backward",
    )(q, k, v, beta, w["conv"], w["conv"], w["conv"], w["head_gain"], t, n, s, o, dmixed, u, normed, rate, w["attn_gain"], w["qkv"], w["beta"], dy)


AHEAD = 2


def ff_blocks(ff):
    cuts = [0, 256]
    while cuts[-1] < ff:
        cuts.append(min(ff, cuts[-1] + 512))
    return list(zip(cuts, cuts[1:]))


def mlp_kernel(forward, keep, down, backward, *refs):
    refs = list(refs)
    take = lambda n: [refs.pop(0) for _ in range(n)]
    gain_ref, w_out_hbm, w_gate_hbm, w_up_hbm, w_down_hbm = take(5)
    if forward:
        u0_ref, mixed_ref = take(2)
    else:
        u1_ref, gate_hbm, up_hbm = take(3)
    if backward:
        (dy_ref,) = take(1)
    if forward:
        u1_ref, normed_ref = take(2)
    if keep:
        kept_hbm = take(3)
    if down:
        (u2_ref,) = take(1)
    if backward:
        if not forward:
            (grads_hbm,) = take(1)
        g1_ref, dm_ref, dgain_ref = take(3)
    w_out, w_gate, w_up, w_down, sems, out_sems, out_sem = take(7)
    if keep or not forward:
        gate_all, up_all = take(2)
    if keep:
        (hidden_all,) = take(1)
    if backward and not forward:
        dgate_all, dup_all = take(2)
    blocks = ff_blocks(w_down.shape[0])
    out_copy = pltpu.make_async_copy(w_out_hbm, w_out, out_sem)

    def loads(i):
        a, b = blocks[i]
        pairs = [(w_gate_hbm.at[:, a:b], w_gate.at[:, a:b]), (w_up_hbm.at[:, a:b], w_up.at[:, a:b]), (w_down_hbm.at[a:b], w_down.at[a:b])]
        if not forward:
            pairs += [(gate_hbm.at[:, a:b], gate_all.at[:, a:b]), (up_hbm.at[:, a:b], up_all.at[:, a:b])]
        return [pltpu.make_async_copy(s, d, sems.at[i, n]) for n, (s, d) in enumerate(pairs)]

    def stores(i):
        a, b = blocks[i]
        pairs = []
        if keep:
            pairs = list(zip((gate_all, up_all, hidden_all), kept_hbm))
        pairs = [(s.at[:, a:b], d.at[:, a:b]) for s, d in pairs]
        if backward and not forward:
            ff = blocks[-1][1]
            pairs = [(dgate_all.at[:, a:b], grads_hbm.at[:, a:b]), (dup_all.at[:, a:b], grads_hbm.at[:, ff + a : ff + b])]
        return [pltpu.make_async_copy(s, d, out_sems.at[i, n]) for n, (s, d) in enumerate(pairs)]

    if forward:
        out_copy.start()
    for i in range(AHEAD):
        for copy in loads(i):
            copy.start()
    if forward:
        out_copy.wait()
        u1 = (u0_ref[...].astype(f32) + nn(mixed_ref[...], w_out[...])).astype(bf16)
        u1_ref[...] = u1
        x = u1.astype(f32)
        normed = (x * lax.rsqrt(jnp.mean(x * x, 1, keepdims=True) + 1e-6) * gain_ref[...]).astype(bf16)
        normed_ref[...] = normed
    total = dnormed = None
    for i, (a, b) in enumerate(blocks):
        for copy in loads(i):
            copy.wait()
        if i + AHEAD < len(blocks):
            for copy in loads(i + AHEAD):
                copy.start()
        elif not forward and i + AHEAD == len(blocks):
            out_copy.start()
        if forward:
            gate, up = nn(normed_ref[...], w_gate[:, a:b]), nn(normed_ref[...], w_up[:, a:b])
        else:
            gate, up = gate_all[:, a:b], up_all[:, a:b]
        sig = jax.nn.sigmoid(gate)
        silu = gate * sig
        if forward:
            hidden = (silu * up).astype(bf16)
        if keep:
            gate_all[:, a:b], up_all[:, a:b], hidden_all[:, a:b] = gate, up, hidden
        if down:
            part = nn(hidden, w_down[a:b])
            total = part if total is None else total + part
        if backward:
            dhidden = nt(dy_ref[...], w_down[a:b])
            dgate = (dhidden * up * (sig + silu * (1.0 - sig))).astype(bf16)
            dup = (dhidden * silu).astype(bf16)
            if not forward:
                dgate_all[:, a:b], dup_all[:, a:b] = dgate, dup
            part = nt(jnp.concatenate([dgate, dup], 1), jnp.concatenate([w_gate[:, a:b], w_up[:, a:b]], 1))
            dnormed = part if dnormed is None else dnormed + part
        for copy in stores(i):
            copy.start()
    x = u1_ref[...].astype(f32)
    if down:
        u2_ref[...] = (x + total).astype(bf16)
    if backward:
        if not forward:
            out_copy.wait()
        scale = lax.rsqrt(jnp.mean(x * x, 1, keepdims=True) + 1e-6)
        hat = x * scale
        dgain_ref[...] = jnp.sum(dnormed * hat, 0, keepdims=True)
        grad = dnormed * gain_ref[...]
        dx = scale * (grad - hat * jnp.mean(grad * hat, 1, keepdims=True))
        g1 = (dy_ref[...].astype(f32) + dx).astype(bf16)
        g1_ref[...] = g1
        dm_ref[...] = nt(g1, w_out[...])
    for i in range(len(blocks)):
        for copy in stores(i):
            copy.wait()


def mlp_call(w, rows, forward=None, backward=None, keep=False, down=False):
    width, ff = w["gate"].shape
    going = len(forward) == 2
    here, there = pl.BlockSpec(memory_space=pltpu.VMEM), pl.BlockSpec(memory_space=pl.ANY)
    shape = lambda kind, n=width: jax.ShapeDtypeStruct((rows, n), kind)
    ins = [here] + [there] * 4
    ins += [here, here] if going else [here, there, there]
    args = [w["mlp_gain"], w["out"], w["gate"], w["up"], w["down"], *forward]
    outs, shapes = [], []
    count = len(ff_blocks(ff))
    scratch = [pltpu.VMEM((width, width), bf16), pltpu.VMEM((width, ff), bf16), pltpu.VMEM((width, ff), bf16), pltpu.VMEM((ff, width), bf16)]
    scratch += [pltpu.SemaphoreType.DMA((count, 5)), pltpu.SemaphoreType.DMA((count, 3)), pltpu.SemaphoreType.DMA]
    if backward is not None:
        ins.append(here)
        args.append(backward)
    if going:
        outs += [here, here]
        shapes += [shape(bf16), shape(bf16)]
    if keep or not going:
        scratch += [pltpu.VMEM((rows, ff), f32)] * 2
    if keep:
        outs += [there] * 3
        shapes += [shape(f32, ff), shape(f32, ff), shape(bf16, ff)]
        scratch.append(pltpu.VMEM((rows, ff), bf16))
    if down:
        outs.append(here)
        shapes.append(shape(bf16))
    if backward is not None:
        if not going:
            outs.append(there)
            shapes.append(shape(bf16, 2 * ff))
            scratch += [pltpu.VMEM((rows, ff), bf16)] * 2
        outs += [here, here, here]
        shapes += [shape(bf16), shape(f32), jax.ShapeDtypeStruct((1, width), f32)]
    return pl.pallas_call(
        functools.partial(mlp_kernel, going, keep, down, backward is not None),
        in_specs=ins,
        out_specs=outs,
        out_shape=shapes,
        scratch_shapes=scratch,
        compiler_params=pltpu.CompilerParams(vmem_limit_bytes=62 * 1024 * 1024),
        name="feed_forward" + ("_keep" if keep else "") + ("_back" if backward is not None else ""),
    )(*args)


PIECE = (64, 256)
SLOTS = 4
LAGS = (1, 5, 9, 13, 14)
HELD = 24
PAIR = 2


def sum_kernel(total, n2_ref, n1_ref, m_ref, h_ref, dgu, dy, g1, beta_ref, rate_ref, conv_ref, head_ref, attn_ref, w_beta, u_ref, normed_ref, d_mlp_ref,
               q_hbm, k_hbm, v_hbm, o_hbm, dm_hbm, t_hbm, n_hbm, s_hbm, w_hbm, u1, u2,
               gu_out, down_out, out_out, qkv_out, small_out, u_out, g_out,
               q_blk, k_blk, v_blk, o_blk, dm_blk, t_blk, n_blk, s_blk, w_blk, load_sem, dqkv, dtaps, dhead, g0, dattn, dw_beta, dbeta, dnormed, small,
               fin, keep_sem, give_sem, take_sem, fin_sem, far_sem, own, send, rc, rx, ry, rz, send_sem, xs_sem, ys_sem, zs_sem, rc_sem, rx_sem, ry_sem, rz_sem):
    section, me = lax.axis_index("section"), lax.axis_index("dp")
    core, x, low, high = lax.rem(section, 2), lax.rem(me, 2), lax.rem(me // 2, 2), me // 4
    far_core = {"section": section + 1 - 2 * core}
    far_x, far_low, far_high = {"dp": me + 1 - 2 * x}, {"dp": me + 2 - 4 * low}, {"dp": me + 4 - 8 * high}
    barrier = pltpu.get_barrier_semaphore()
    for other in (far_core, far_x, far_low, far_high):
        pl.semaphore_signal(barrier, inc=1, device_id=other, device_id_type=MESH)
    pl.semaphore_wait(barrier, 4)

    def remote(src, dst, sent, got, other):
        return pltpu.make_async_remote_copy(src_ref=src, dst_ref=dst, send_sem=sent, recv_sem=got, device_id=other, device_id_type=MESH)

    def micro(which, mixer_side, mlp_side, into):
        return (
            pltpu.make_async_copy(mixer_side if which == 0 else mlp_side, into.at[core], keep_sem.at[0 if into is u_out else 1]),
            remote(mlp_side if which == 0 else mixer_side, into.at[core], give_sem.at[0 if into is u_out else 1], take_sem.at[0 if into is u_out else 1], far_core),
        )

    def each_core(act):
        for which in range(2):
            @pl.when(core == which)
            def _():
                act(which)

    def start_micro(*sides):
        def act(which):
            for copy in micro(which, *sides):
                copy.start()
        each_core(act)

    start_micro(u1, u2, u_out)

    def loads(s):
        cols = pl.ds(pl.multiple_of(s * PAIR * 128, PAIR * 128), PAIR * 128)
        pairs = [(src.at[:, cols], dst) for src, dst in ((q_hbm, q_blk), (k_hbm, k_blk), (v_hbm, v_blk), (o_hbm, o_blk), (dm_hbm, dm_blk))]
        pairs += [(src.at[pl.ds(s * PAIR, PAIR)], dst) for src, dst in ((t_hbm, t_blk), (n_hbm, n_blk), (s_hbm, s_blk))]
        pairs.append((w_hbm.at[:, :, cols], w_blk))
        return [pltpu.make_async_copy(src, dst, load_sem.at[i]) for i, (src, dst) in enumerate(pairs)]

    for copy in loads(0):
        copy.start()

    def mixer_step(s):
        for copy in loads(s):
            copy.wait()
        width = dattn.shape[1]
        cols = lambda p: pl.ds(pl.multiple_of(p * width + s * PAIR * 128, PAIR * 128), PAIR * 128)
        taps = [conv_ref.at[p, :, cols(0)] for p in range(3)]
        grads = [dqkv.at[:, cols(p)] for p in range(3)]
        dt = [dtaps.at[p, :, cols(0)] for p in range(3)]
        mixer_back_step(PAIR, s, q_blk, k_blk, v_blk, beta_ref, *taps, head_ref, t_blk, n_blk, s_blk, o_blk, dm_blk, w_blk, *grads, *dt, dhead, dbeta, dnormed)

        @pl.when(s + 1 < width // (PAIR * 128))
        def _():
            for copy in loads(s + 1):
                copy.start()

    def mixer_end():
        mixer_back_end(beta_ref, rate_ref, u_ref, normed_ref, attn_ref, w_beta, g1, dbeta, dnormed, g0, dattn, dw_beta)
        start_micro(g0, g1, g_out)
        zeros = lambda n: jnp.zeros((n, PIECE[1]), f32)
        for d in range(8):
            lane = slice(d * 128, (d + 1) * 128)
            wide = lambda a: jnp.concatenate([a, jnp.zeros_like(a)], 1)
            rows = [wide(dattn[:, lane]), zeros(7)]
            for p in range(3):
                rows += [wide(dtaps[p, :, lane])]
            rows += [zeros(4), wide(dhead[...]), zeros(7), wide(dw_beta[:, lane]), zeros(PIECE[0] - 40)]
            small[0, d // 4, d // 2 % 2, d % 2] = jnp.concatenate(rows, 0).astype(bf16)
            small[1, d // 4, d // 2 % 2, d % 2] = jnp.concatenate([wide(d_mlp_ref[:, lane]), zeros(PIECE[0] - 1)], 0).astype(bf16)

    def held(t):
        return lax.rem(t, HELD)

    def slot(t):
        return lax.rem(t, SLOTS)

    def core_copy(t):
        return remote(send.at[slot(t)], rc.at[held(t)], send_sem.at[slot(t)], rc_sem.at[t], far_core)

    def turned(t):
        return lax.rem(t, 4) // 3

    def first_copy(t, z_first):
        src = rc.at[held(t), :, 1 - low] if z_first else rc.at[held(t), :, :, 1 - x]
        return remote(src, rx.at[held(t)], xs_sem.at[slot(t)], rx_sem.at[t], far_low if z_first else far_x)

    def second_copy(t):
        way = turned(t)
        other = {"dp": me + way * (1 - 2 * x) + (1 - way) * (2 - 4 * low)}
        mine = way * x + (1 - way) * low
        return remote(rx.at[held(t), :, 1 - mine], ry.at[held(t)], ys_sem.at[slot(t)], ry_sem.at[t], other)

    def high_copy(t):
        return remote(ry.at[held(t), 1 - high], rz.at[held(t)], zs_sem.at[slot(t)], rz_sem.at[t], far_high)

    def free(copy, t):
        @pl.when(t >= SLOTS)
        def _():
            copy(t - SLOTS).wait_send()

    def either(t, act):
        for z_first in (False, True):
            @pl.when(turned(t) == int(z_first))
            def _():
                act(z_first)

    def after_core(t):
        core_copy(t).wait_recv()
        rc[held(t)] = rc[held(t)] + own[slot(t)]
        free(lambda u: first_copy(u, False), t)
        either(t, lambda z_first: first_copy(t, z_first).start())

    def after_first(t):
        first_copy(t, False).wait_recv()

        def add(z_first):
            rx[held(t)] = rx[held(t)] + (rc[held(t), :, low] if z_first else rc[held(t), :, :, x])

        either(t, add)
        free(second_copy, t)
        second_copy(t).start()

    def after_second(t):
        second_copy(t).wait_recv()
        way = turned(t)
        ry[held(t)] = ry[held(t)] + rx[held(t), :, way * x + (1 - way) * low]
        free(high_copy, t)
        high_copy(t).start()

    def rows_of(t, base, into):
        return into.at[pl.ds(pl.multiple_of(core * PIECE[0], PIECE[0]), PIECE[0]), span(t, base)]

    def slab_of(t, base, into):
        return into.at[core * (into.shape[0] // 2) + t - base]

    def part_of(t, base, into):
        per = into.shape[2] // PIECE[1]
        part = (t - base) // per
        return rows_of(t - part * per, base, into.at[part])

    def piece_here(t, where):
        return pltpu.make_async_copy(fin.at[slot(t)], where, fin_sem.at[slot(t)])

    def piece_there(t, where):
        return remote(fin.at[slot(t)], where, fin_sem.at[slot(t)], far_sem.at[t], far_core)

    def fin_wait(t):
        pltpu.make_async_copy(fin.at[slot(t)], fin.at[slot(t)], fin_sem.at[slot(t)]).wait()

    def after_high(t):
        high_copy(t).wait_recv()
        value = rz[held(t)].astype(f32) + ry[held(t), high].astype(f32)

        @pl.when(t == total - 1)
        def _():
            small_out[...] = value

        @pl.when(t < total - 1)
        def _():
            @pl.when(t >= SLOTS)
            def _():
                fin_wait(t)

            fin[slot(t)] = value
            for base, count, target, _, where, into in segments:
                @pl.when((t >= base) & (t < base + count))
                def _():
                    @pl.when(core == target)
                    def _():
                        piece_here(t, where(t, base, into)).start()

                    @pl.when(core != target)
                    def _():
                        piece_there(t, where(t, base, into)).start()

    def after_far(t):
        for base, count, target, _, where, into in segments:
            @pl.when((t >= base) & (t < base + count) & (core == target))
            def _():
                piece_there(t, where(t, base, into)).wait_recv()

    def later(t):
        for step, lag in zip((after_core, after_first, after_second, after_high, after_far), LAGS):
            @pl.when((t >= lag) & (t < total + lag))
            def _():
                step(t - lag)

    def span(t, base):
        return pl.ds(pl.multiple_of((t - base) * PIECE[1], PIECE[1]), PIECE[1])

    def by_columns(lhs, rhs, base):
        def fill(t):
            block = rhs[:, span(t, base)]
            for which, into in ((1 - core, send), (core, own)):
                part = nn(lhs[which], block).astype(bf16)
                into[slot(t)] = part.reshape(own.shape[1:])
        return fill

    def by_rows(base):
        def fill(t):
            for which, into in ((1 - core, send), (core, own)):
                part = nn(h_ref[t - base, which], dy[...]).astype(bf16)
                count = part.shape[0] // 8
                for d in range(8):
                    for c in range(PIECE[0] // count):
                        into[slot(t), d // 4, d // 2 % 2, d % 2, c * count : (c + 1) * count, :] = part[d * count : (d + 1) * count, c * PIECE[1] : (c + 1) * PIECE[1]]
        return fill

    def given(t):
        send[slot(t)] = small[1 - core]
        own[slot(t)] = small[core]

    segments, base = [], 0
    for target, columns, lhs, rhs, where, into in (
        (1, True, n2_ref, dgu, rows_of, gu_out),
        (1, False, h_ref, dy, slab_of, down_out),
        (0, True, m_ref, g1, rows_of, out_out),
        (0, True, n1_ref, dqkv, part_of, qkv_out),
    ):
        count = rhs.shape[1] // PIECE[1] if columns else lhs.shape[0]
        fill = by_columns(lhs, rhs, base) if columns else by_rows(base)
        segments.append((base, count, target, fill, where, into))
        base += count

    def block(t, fill):
        @pl.when(t >= SLOTS)
        def _():
            core_copy(t - SLOTS).wait_send()

        fill(t)
        core_copy(t).start()
        later(t)

    def run(begin, count, fill):
        def body(i, carry):
            block(begin + i, fill)
            return carry

        lax.fori_loop(0, count, body, 0)

    steps = dattn.shape[1] // (PAIR * 128)
    before = segments[0][1] // steps

    def mixer_turn(s, carry):
        run(s * before, before, segments[0][3])
        mixer_step(s)
        return carry

    lax.fori_loop(0, steps, mixer_turn, 0)
    mixer_end()
    done = steps * before
    for base, count, _, fill, _, _ in segments:
        run(max(base, done), base + count - max(base, done), fill)
    run(total - 1, 1, given)

    def drain(t, carry):
        later(t)
        return carry

    lax.fori_loop(total, total + LAGS[-1], drain, 0)
    for copy in (core_copy, lambda t: first_copy(t, False), second_copy, high_copy):
        for t in range(total - SLOTS, total):
            copy(jnp.int32(t)).wait_send()
    for t in range(SLOTS):
        fin_wait(jnp.int32(t))

    def end_micro(which):
        for keep, give in (micro(which, u1, u2, u_out), micro(which, g0, g1, g_out)):
            keep.wait()
            give.wait_send()
            give.wait_recv()

    each_core(end_micro)


def summed_gradients(n2, n1, m, h, dgu, dy, g1, kept, w, dm, d_mlp, u1, u2):
    u0, normed, rate, beta, q, k, v, t, n, s, o = kept
    rows, width = u0.shape
    ff = dgu.shape[1] // 2
    total = (2 * ff + 4 * width) // PIECE[1] + h.shape[0] + 1
    wide, heads = PAIR * 128, beta.shape[1]
    buffer = lambda *lead: pltpu.VMEM(lead + PIECE, bf16)
    dma = lambda n: pltpu.SemaphoreType.DMA((n,))
    vmem, anywhere = pl.BlockSpec(memory_space=pltpu.VMEM), pl.BlockSpec(memory_space=pl.ANY)
    near = (n2, n1, m, h, dgu, dy, g1, beta, rate, w["conv"], w["head_gain"], w["attn_gain"], w["beta"], u0, normed, d_mlp)
    far = (q, k, v, o, dm, t, n, s, w["qkv"], u1, u2)
    result = lambda *shape: jax.ShapeDtypeStruct(shape, f32)
    pair = jax.ShapeDtypeStruct((2,) + u1.shape, bf16)
    out_rows = 2 * PIECE[0]
    return pl.pallas_call(
        functools.partial(sum_kernel, total),
        out_shape=[result(out_rows, 2 * ff), result(2 * h.shape[0], *PIECE), result(out_rows, width), result(3, out_rows, width), result(*PIECE), pair, pair],
        in_specs=[vmem] * len(near) + [anywhere] * len(far),
        out_specs=[anywhere] * 4 + [vmem] + [anywhere] * 2,
        scratch_shapes=[pltpu.VMEM((rows, wide), f32)] * 5
        + [pltpu.VMEM((PAIR, rows, 128), bf16)] * 3
        + [pltpu.VMEM((3, width, wide), bf16), dma(9)]
        + [pltpu.VMEM((rows, 3 * width), bf16), pltpu.VMEM((3, 4, width), f32), pltpu.VMEM((1, 128), f32), pltpu.VMEM((rows, width), bf16)]
        + [pltpu.VMEM((1, width), f32), pltpu.VMEM((heads, width), f32), pltpu.VMEM((rows, heads), f32), pltpu.VMEM((rows, width), f32)]
        + [buffer(2, 2, 2, 2)]
        + [pltpu.VMEM((SLOTS,) + PIECE, f32), dma(2), dma(2), dma(2), dma(SLOTS), dma(total)]
        + [buffer(SLOTS, 2, 2, 2), buffer(SLOTS, 2, 2, 2), buffer(HELD, 2, 2, 2), buffer(HELD, 2, 2), buffer(HELD, 2), buffer(HELD)]
        + [dma(SLOTS)] * 4
        + [dma(total)] * 4,
        compiler_params=pltpu.CompilerParams(collective_id=0, has_side_effects=True, vmem_limit_bytes=63 * 1024 * 1024),
        name="gradient_sums",
    )(*near, *far)


def matmul(a, b):
    return jnp.dot(a, b, preferred_element_type=f32)


def matmul_tn(a, b):
    return lax.dot_general(a, b, (((0,), (0,)), ((), ())), preferred_element_type=f32)


def pick(x, index, axis):
    return lax.dynamic_index_in_dim(x, index, axis, keepdims=False)


def shards(inputs, cotangent, lengths, attn_gain, qkv_weight, conv_weight, beta_weight, head_gain, out_weight, mlp_gain, gate_up_weight, down_weight):
    section, sections = lax.axis_index("section"), lax.axis_size("section")
    me, group = lax.axis_index("dp"), lax.axis_size("dp")
    core, stage = section % 2, section // 2
    swap = [(i, i ^ 1) for i in range(sections)]
    to_odd = [(i, i + 1) for i in range(0, sections, 2)]
    to_even = [(i + 1, i) for i in range(0, sections, 2)]
    rows = inputs.shape[2]
    width = inputs.shape[3]

    qkv, out_w, down, conv, beta_w, attn, head, mlp, own_gate, own_up = first_exchange(
        jnp.moveaxis(qkv_weight[0], 1, 0),
        out_weight[0],
        down_weight[0],
        jnp.moveaxis(conv_weight[0], 1, 0),
        beta_weight[0].T,
        attn_gain,
        head_gain,
        mlp_gain,
        gate_up_weight[0],
    )
    w = {"attn_gain": attn, "conv": conv, "beta": beta_w, "head_gain": head, "qkv": qkv, "out": out_w, "mlp_gain": mlp, "down": down}

    first = pick(inputs[:, 0], core, 0)
    seed = pick(cotangent[:, 0], core, 0)
    length = pick(lengths[:, 0], core, 0)
    token_mask = (jnp.arange(rows) < length).astype(f32)[:, None]
    up_stage = [(i, i + 2) for i in range(sections - 2)]
    down_stage = [(i + 2, i) for i in range(sections - 2)]

    *passed, w["gate"], w["up"] = mixer_fwd(first, w, token_mask, (own_gate, own_up))
    mixed = passed[6]
    _, _, u2 = mlp_call(w, rows, (first, mixed), down=True)
    u0 = jnp.where(stage == 0, first, lax.ppermute(u2, "section", up_stage))
    normed1, rate, beta, q, k, v, mixed, *saved = mixer_fwd(u0, w, token_mask)
    kept = (u0, normed1, rate, beta, q, k, v, *saved)
    u1, normed2, gate, up, hidden, g1, dmixed, _ = mlp_call(w, rows, (u0, mixed), seed, keep=True)
    g0 = mixer_bwd(kept, w, dmixed, g1)[7]
    dy = jnp.where(stage == 1, seed, lax.ppermute(g0, "section", down_stage))
    u2 = (u1.astype(f32) + matmul(hidden, w["down"])).astype(bf16)
    ff = hidden.shape[1]
    fused = group == 8 and width == 1024 and ff % 256 == 0
    for_sums = ()
    if fused:
        by_owner = lambda a: a.reshape(rows, group, 2, 64).transpose(2, 1, 3, 0).reshape(2, group * 64, rows)
        down_rows = hidden.reshape(rows, group, 2, ff // 256, 16).transpose(3, 2, 1, 4, 0).reshape(ff // 256, 2, group * 16, rows)
        for_sums = (by_owner(normed2), by_owner(normed1), by_owner(mixed), down_rows)
    dy, u2, for_sums = lax.optimization_barrier((dy, u2, for_sums))
    dgate_up, g1, dmixed, d_mlp_gain = mlp_call(w, rows, (u1, gate, up), dy)
    on_even = lambda x: jnp.where(core == 0, x, 0.0)
    on_odd = lambda x: jnp.where(core == 1, x, 0.0)

    def halve(x):
        kept = pick(x, core, 1).astype(f32)
        x = (kept + lax.ppermute(pick(x, 1 - core, 1), "section", swap).astype(f32)).astype(bf16)
        return scatter(x)

    def scatter(x):
        kind = x.dtype
        bit = 1
        while bit < group:
            pairs = [(i, i ^ bit) for i in range(group)]
            mine = (me // bit) % 2
            x = x.reshape((x.shape[0] // 2, 2) + x.shape[1:])
            other = lax.ppermute(pick(x, 1 - mine, 1), "dp", pairs)
            x = pick(x, mine, 1).astype(f32) + other.astype(f32)
            bit *= 2
            if bit < group:
                x = x.astype(kind)
        return x[0]

    def share(grad):
        count, cols = grad.shape
        return halve(grad.astype(bf16).reshape(group, 2, count // group // 2, cols))

    if fused:
        grad_gate_up, grad_down, grad_out, grad_qkv, small, sec_out, sec_grad = summed_gradients(*for_sums, dgate_up, dy, g1, kept, w, dmixed, d_mlp_gain, u1, u2)
        grad_gate_up = on_odd(grad_gate_up).reshape(-1, 2, ff)
        grad_down = on_odd(grad_down.reshape(-1, 4, 16, 256).transpose(0, 2, 1, 3).reshape(-1, width))
        grad_out = on_even(grad_out)
        grad_qkv = jnp.moveaxis(on_even(grad_qkv), 0, 1)
        count = width // group
        s_attn, s_mlp = small[0, :count], small[0, :count]
        s_taps = jnp.moveaxis(small[8:20, :count].reshape(3, -1, count), 0, 1)
        s_head = pick(small[24, :128].reshape(group, -1), me, 0)
        s_beta = small[32:40, :count].T
        sec_out, sec_grad = sec_out[None, :, None], sec_grad[None, :, None]
    else:
        *dproj, dtq, dtk, dtv, dhead, g0, d_attn_gain, dbeta = mixer_bwd(kept, w, dmixed, g1)
        dtaps = jnp.stack([dtq, dtk, dtv], 1)
        dbeta = dbeta.T
        taps_rows = jnp.moveaxis(dtaps.reshape(-1, 3, group, width // group), 2, 0).reshape(group, -1)
        small = [d_attn_gain.reshape(group, -1), taps_rows, dbeta.reshape(group, -1), dhead.reshape(group, -1), d_mlp_gain.reshape(group, -1)]
        sizes = [a.shape[1] for a in small]
        joined = jnp.concatenate(small, 1)
        down_share = share(matmul_tn(hidden, dy))
        gate_share = share(matmul_tn(normed2, dgate_up[:, :ff]))
        up_share = share(matmul_tn(normed2, dgate_up[:, ff:]))
        out_share = share(matmul_tn(mixed, g1))
        qkv_share = [share(matmul_tn(normed1, d)) for d in dproj]
        small = scatter(joined + lax.ppermute(joined, "section", swap))
        def to_core(x, target):
            other = lax.ppermute(x, "section", to_even if target == 0 else to_odd)
            both = jnp.concatenate([x, other] if target == 0 else [other, x], 0)
            return jnp.where(core == target, both, 0.0)

        grad_qkv = jnp.stack([to_core(x, 0) for x in qkv_share], 1)
        grad_out = to_core(out_share, 0)
        grad_gate_up = jnp.stack([to_core(gate_share, 1), to_core(up_share, 1)], 1)
        grad_down = to_core(down_share, 1)

        def both_micro(mixer_side, mlp_side):
            own = jnp.where(core == 0, mixer_side, mlp_side)
            other = lax.ppermute(jnp.where(core == 0, mlp_side, mixer_side), "section", swap)
            return jnp.where(core == 0, jnp.stack([own, other]), jnp.stack([other, own]))[None, :, None]

        sec_out, sec_grad = both_micro(u1, u2), both_micro(g0, g1)
        offsets = [sum(sizes[:i]) for i in range(len(sizes) + 1)]
        s_attn, s_taps, s_beta, s_head, s_mlp = [small[a:b] for a, b in zip(offsets, offsets[1:])]

    return (
        sec_out,
        sec_grad,
        on_even(s_attn)[None],
        grad_qkv[None],
        on_even(s_taps).reshape(1, -1, 3, width // group),
        on_even(s_beta).reshape(1, -1, beta.shape[1]),
        on_even(s_head)[None],
        grad_out[None],
        on_odd(s_mlp)[None],
        grad_gate_up[None],
        grad_down[None],
    )


def solution(mesh):
    in_specs = (
        P(None, "dp", None, None),
        P(None, "dp", None, None),
        P(None, "dp"),
        P("section", None),
        P("section", None, None, None),
        P("section", None, None, None),
        P("section", None, None),
        P("section", None),
        P("section", None, None),
        P("section", None),
        P("section", None, None, None),
        P("section", None, None),
    )
    out_specs = (
        P("section", None, "dp", None, None),
        P("section", None, "dp", None, None),
        P("section", "dp"),
        P("section", "dp", None, None),
        P("section", None, None, "dp"),
        P("section", "dp", None),
        P("section", "dp"),
        P("section", "dp", None),
        P("section", "dp"),
        P("section", "dp", None, None),
        P("section", "dp", None),
    )
    return jax.shard_map(shards, mesh=mesh, in_specs=in_specs, out_specs=out_specs, check_vma=False)
```

```python
import functools

import jax, jax.numpy as jnp
from jax import lax
from jax.experimental import pallas as pl
from jax.experimental.pallas import tpu as pltpu
from jax.sharding import PartitionSpec as P

CHUNK = 128
VMEM = 63 * 1024 * 1024
MESH = pl.DeviceIdType.MESH
bf16, f32 = jnp.bfloat16, jnp.float32


def nn(a, b):
    return lax.dot_general(a.astype(bf16), b.astype(bf16), (((1,), (0,)), ((), ())), preferred_element_type=f32)


def nt(a, b):
    return lax.dot_general(a.astype(bf16), b.astype(bf16), (((1,), (1,)), ((), ())), preferred_element_type=f32)


def tn(a, b):
    return lax.dot_general(a.astype(bf16), b.astype(bf16), (((0,), (0,)), ((), ())), preferred_element_type=f32)


def shifted_rows(x, steps):
    count = x.shape[0]
    rows = lax.broadcasted_iota(jnp.int32, (8, x.shape[1]), 0)
    moved = pltpu.roll(x, steps % count, 0)
    if steps > 0:
        return jnp.concatenate([jnp.where(rows >= steps, moved[:8], 0.0), moved[8:]], 0)
    return jnp.concatenate([moved[:-8], jnp.where(rows < 8 + steps, moved[-8:], 0.0)], 0)


def convolved(x, taps):
    total = x * taps[3:4]
    for back in range(1, 4):
        total = total + shifted_rows(x, back) * taps[3 - back : 4 - back]
    return total


def chunk_masks():
    row = lax.broadcasted_iota(jnp.int32, (CHUNK, CHUNK), 0)
    col = lax.broadcasted_iota(jnp.int32, (CHUNK, CHUNK), 1)
    return row, col


def level_mask(row, col, size):
    shift = size.bit_length() - 1
    same = (row >> (shift + 1)) == (col >> (shift + 1))
    return same & (((row >> shift) & 1) == 1) & (((col >> shift) & 1) == 0)


def triangular_inverse(a_list, row, col):
    mask = level_mask(row, col, 1)
    xs = [jnp.where(mask, -a, 0.0) for a in a_list]
    size = 2
    while size < CHUNK:
        mask = level_mask(row, col, size)
        parts = [jnp.where(mask, a, 0.0) for a in a_list]
        ys = [p + nn(p, x) for p, x in zip(parts, xs)]
        xs = [x - (y + nn(x, y)) for x, y in zip(xs, ys)]
        size *= 2
    return xs


def head_column(block, head):
    lanes = lax.broadcasted_iota(jnp.int32, block.shape, 1)
    return jnp.sum(jnp.where(lanes == head, block, 0.0), axis=1, keepdims=True)


def greet_far_core(section):
    far = {"section": section + 1 - 2 * lax.rem(section, 2)}
    barrier = pltpu.get_barrier_semaphore()
    pl.semaphore_signal(barrier, inc=1, device_id=far, device_id_type=MESH)
    pl.semaphore_wait(barrier, 1)
    return far


def give_weights(step, steps, from_even, from_odd, send_sem, recv_sem):
    section = lax.axis_index("section")
    core = lax.rem(section, 2)
    far = {"section": section + 1 - 2 * core}
    pairs = [(0, *p) for p in from_even] + [(1, *p) for p in from_odd]

    def give(i):
        return pltpu.make_async_remote_copy(
            src_ref=pairs[i][1], dst_ref=pairs[i][2], send_sem=send_sem.at[i], recv_sem=recv_sem.at[i], device_id=far, device_id_type=MESH
        )

    @pl.when(step == 0)
    def _():
        greet_far_core(section)
        for i, (owner, _, _) in enumerate(pairs):
            @pl.when(core == owner)
            def _():
                give(i).start()

    @pl.when(step == steps - 1)
    def _():
        for i, (owner, _, _) in enumerate(pairs):
            @pl.when(core == owner)
            def _():
                give(i).wait_send()

            @pl.when(core != owner)
            def _():
                give(i).wait_recv()


def first_kernel(qkv, out, down, inputs, cotangent, lengths, conv, beta, attn_gain, head_gain, mlp_gain, both, qkv_part, out_part, down_part,
                 qkv_full, out_full, down_full, gate_full, first, seed, mask, conv_full, beta_full, attn_full, head_full, mlp_full, up,
                 gate, mine, theirs, local_sem, send_sem, recv_sem, small_sems, stream_sem, gate_local, gate_send, gate_recv):
    step, steps = pl.program_id(0), pl.num_programs(0)
    section = lax.axis_index("section")
    core = lax.rem(section, 2)
    far = {"section": section + 1 - 2 * core}
    give_weights(step, steps, [(qkv, qkv_full), (out, out_full)], [(down, down_full)], send_sem, recv_sem)
    small = pltpu.make_async_remote_copy(
        src_ref=mine, dst_ref=theirs, send_sem=small_sems.at[0], recv_sem=small_sems.at[1], device_id=far, device_id_type=MESH
    )
    streams = [
        pltpu.make_async_copy(inputs.at[core, 0], first, stream_sem.at[0]),
        pltpu.make_async_copy(cotangent.at[core, 0], seed, stream_sem.at[1]),
    ]

    @pl.when(step == 0)
    def _():
        for copy in streams:
            copy.start()
        mine[...] = jnp.zeros_like(mine)
        for p in range(3):
            mine[8 * p : 8 * p + 4, :] = conv[p].astype(f32)
        mine[4:5, :] = attn_gain[...].astype(f32)
        mine[5:6, : head_gain.shape[1]] = head_gain[...].astype(f32)
        mine[6:7, :] = mlp_gain[...].astype(f32)
        mine[24:32, :] = beta[...].astype(f32)
        small.start()
        length = jnp.where(core == 0, lengths[0:1, :], lengths[1:2, :])
        mask[...] = (lax.broadcasted_iota(jnp.int32, mask.shape, 0) < length).astype(f32)

    count, down_count = out_part.shape[0], down_part.shape[0]
    block, down_block = pl.ds(step * count, count), pl.ds(step * down_count, down_count)
    own = [
        (0, pltpu.make_async_copy(qkv_part, qkv_full.at[:, block], local_sem.at[0])),
        (0, pltpu.make_async_copy(out_part, out_full.at[block], local_sem.at[1])),
        (1, pltpu.make_async_copy(down_part, down_full.at[down_block], local_sem.at[2])),
    ]
    for owner, copy in own:
        @pl.when(core == owner)
        def _():
            copy.start()

    def gate_here(i):
        return pltpu.make_async_copy(gate.at[lax.rem(i, 2)], gate_full.at[pl.ds(i * count, count)], gate_local.at[i])

    def gate_there(i):
        return pltpu.make_async_remote_copy(
            src_ref=gate.at[lax.rem(i, 2)], dst_ref=gate_full.at[pl.ds(i * count, count)],
            send_sem=gate_send.at[i], recv_sem=gate_recv.at[i], device_id=far, device_id_type=MESH,
        )

    @pl.when((core == 1) & (step >= 2))
    def _():
        gate_here(step - 2).wait()
        gate_there(step - 2).wait_send()

    apart = jnp.swapaxes(both[...], 0, 1)
    gate[lax.rem(step, 2)] = apart[0]
    up[...] = apart[1]

    @pl.when(core == 1)
    def _():
        gate_here(step).start()
        gate_there(step).start()

    for owner, copy in own:
        @pl.when(core == owner)
        def _():
            copy.wait()

    @pl.when(step == steps - 1)
    def _():
        small.wait()
        mixer = jnp.where(core == 0, mine[...], theirs[...])
        for p in range(3):
            conv_full[p] = mixer[8 * p : 8 * p + 4]
        attn_full[...] = mixer[4:5]
        head_full[...] = mixer[5:6, : head_full.shape[1]]
        beta_full[...] = mixer[24:32].astype(bf16)
        mlp_full[...] = jnp.where(core == 1, mine[6:7, :], theirs[6:7, :])
        for copy in streams:
            copy.wait()

        @pl.when(core == 1)
        def _():
            for i in (step - 1, step):
                gate_here(i).wait()
                gate_there(i).wait_send()

        @pl.when(core == 0)
        def _():
            def arrived(i, carry):
                gate_there(i).wait_recv()
                return carry

            lax.fori_loop(0, steps, arrived, 0)


def first_exchange(qkv, out, down, inputs, cotangent, lengths, conv, beta, attn_gain, head_gain, mlp_gain, both):
    rows, _, ff = both.shape
    width = out.shape[1]
    length = inputs.shape[2]
    count = 128
    steps = rows // count
    anywhere = pl.BlockSpec(memory_space=pl.ANY)
    whole = lambda *shape: pl.BlockSpec(shape, lambda i: (0,) * len(shape))
    like = lambda a, kind: jax.ShapeDtypeStruct(a.shape, kind)
    shape = lambda kind, *dims: jax.ShapeDtypeStruct(dims, kind)
    smalls = (conv, beta, attn_gain, head_gain, mlp_gain)
    dma = lambda n: pltpu.SemaphoreType.DMA((n,))
    return pl.pallas_call(
        first_kernel,
        grid=(steps,),
        in_specs=[anywhere] * 5
        + [whole(*a.shape) for a in (lengths, *smalls)]
        + [
            pl.BlockSpec((count, 2, ff), lambda i: (i, 0, 0)),
            pl.BlockSpec((3, count, width), lambda i: (0, i, 0)),
            pl.BlockSpec((count, width), lambda i: (i, 0)),
            pl.BlockSpec((ff * count // rows, width), lambda i: (i, 0)),
        ],
        out_specs=[anywhere] * 4 + [whole(length, width)] * 2 + [whole(length, 1)] + [whole(*a.shape) for a in smalls] + [pl.BlockSpec((count, ff), lambda i: (i, 0))],
        out_shape=[like(qkv, bf16), like(out, bf16), like(down, bf16), shape(bf16, rows, ff), shape(bf16, length, width), shape(bf16, length, width), shape(f32, length, 1)]
        + [like(conv, f32), like(beta, bf16), like(attn_gain, f32), like(head_gain, f32), like(mlp_gain, f32), shape(bf16, rows, ff)],
        scratch_shapes=[pltpu.VMEM((2, count, ff), bf16)] + [pltpu.VMEM((32, width), f32)] * 2 + [dma(3)] * 3 + [dma(2)] * 2 + [dma(steps)] * 3,
        compiler_params=pltpu.CompilerParams(collective_id=1, has_side_effects=True, vmem_limit_bytes=VMEM),
        name="first_exchange",
    )(qkv, out, down, inputs, cotangent, lengths, *smalls, both, qkv, out, down)


def last_kernel(gate_up_in, down_in, out_in, qkv_in, small, sec_out_in, sec_grad_in, gate_up, down, out, qkv, attn, conv, head, beta, mlp, sec_out, sec_grad):
    core = lax.rem(lax.axis_index("section"), 2)
    me = lax.axis_index("dp")
    on = lambda which, x: jnp.where(core == which, x, 0.0)
    ff = gate_up.shape[2]
    both = on(1, gate_up_in[...])
    gate_up[...] = jnp.swapaxes(jnp.stack([both[:, :ff], both[:, ff:]], 0), 0, 1)
    count, wide = 16, small.shape[1]
    for j in range(down_in.shape[0]):
        for c in range(down.shape[1] // wide):
            down[j * count : (j + 1) * count, c * wide : (c + 1) * wide] = on(1, down_in[j, c * count : (c + 1) * count, :])
    out[...] = on(0, out_in[...])
    qkv[...] = on(0, qkv_in[...])
    sec_out[...] = sec_out_in[...]
    sec_grad[...] = sec_grad_in[...]
    lanes = attn.shape[1]
    attn[...] = on(0, small[0:1, :lanes])
    mlp[...] = on(1, small[0:1, :lanes])
    for p in range(3):
        conv[p] = on(0, small[8 + 4 * p : 12 + 4 * p, :lanes])
    beta[...] = on(0, small[32:40, :lanes])
    part = head.shape[1]
    turned = small[24:32, :lanes]
    shift = lax.rem(lanes - me * part, lanes)
    head[...] = on(0, pltpu.roll(turned, shift, 1)[0:1, :part])


def last_outputs(gate_up, down, out, qkv, small, sec_out, sec_grad, head_part):
    rows, width = out.shape
    ff = gate_up.shape[1] // 2
    half = rows // 2
    lanes = rows
    whole = lambda *shape: pl.BlockSpec(shape, lambda i: (0,) * len(shape))
    by_rows = lambda *shape: pl.BlockSpec(shape, lambda i: (i,) + (0,) * (len(shape) - 1))
    shape = lambda *dims: jax.ShapeDtypeStruct(dims, f32)
    qkv_spec = pl.BlockSpec((3, half, width), lambda i: (0, i, 0))
    stream = by_rows(1, *sec_out.shape[1:])
    tall = down.shape[0] // 2
    return pl.pallas_call(
        last_kernel,
        grid=(2,),
        in_specs=[by_rows(half, 2 * ff), by_rows(tall, *down.shape[1:]), by_rows(half, width), qkv_spec, whole(*small.shape), stream, stream],
        out_specs=[by_rows(half, 2, ff), by_rows(16 * tall, width), by_rows(half, width), qkv_spec]
        + [whole(1, lanes), whole(3, 4, lanes), whole(1, head_part), whole(8, lanes), whole(1, lanes), stream, stream],
        out_shape=[shape(rows, 2, ff), shape(32 * tall, width), shape(rows, width), shape(3, rows, width)]
        + [shape(1, lanes), shape(3, 4, lanes), shape(1, head_part), shape(8, lanes), shape(1, lanes)]
        + [jax.ShapeDtypeStruct(sec_out.shape, bf16)] * 2,
        compiler_params=pltpu.CompilerParams(vmem_limit_bytes=VMEM),
        name="last_outputs",
    )(gate_up, down, out, qkv, small, sec_out, sec_grad)


def mixer_fwd_kernel(per, trade, u_ref, gain_in, w_ref, w_beta, mask_ref, taps_q, taps_k, taps_v, gain_ref, *refs):
    own, refs = refs[:trade], refs[trade:]
    normed_ref, rate_ref, beta_ref, q_ref, k_ref, v_ref, mixed_ref, t_ref, n_ref, s_ref, o_ref = refs[:11]
    if trade:
        give_weights(pl.program_id(0), pl.num_programs(0), [], list(zip(own, refs[11 : 11 + trade])), *refs[11 + trade :])

    @pl.when(pl.program_id(0) == 0)
    def _():
        x = u_ref[...].astype(f32)
        normed = (x * lax.rsqrt(jnp.mean(x * x, 1, keepdims=True) + 1e-6) * gain_in[...]).astype(bf16)
        normed_ref[...] = normed
        rate = jax.nn.sigmoid(nt(normed, w_beta[...]))
        rate_ref[...] = rate
        beta_ref[...] = rate * mask_ref[...]

    for p, ref in enumerate((q_ref, k_ref, v_ref)):
        ref[...] = nn(normed_ref[...], w_ref[p])
    row, col = chunk_masks()
    strict, causal = row > col, row >= col
    chunks = q_ref.shape[0] // CHUNK
    beta_all = beta_ref[...]
    cut = lambda x: [x[i * CHUNK : (i + 1) * CHUNK] for i in range(chunks)]
    lanes = [slice(j * 128, (j + 1) * 128) for j in range(per)]
    qs, ks, vs, bs = [], [], [], []
    for j, lane in enumerate(lanes):

        def activated(ref, taps):
            c = convolved(ref[:, lane], taps[:, lane])
            return c * jax.nn.sigmoid(c)

        q, k, v = activated(q_ref, taps_q), activated(k_ref, taps_k), activated(v_ref, taps_v)
        q = q * lax.rsqrt(jnp.sum(q * q, 1, keepdims=True) + 1e-6)
        k = k * lax.rsqrt(jnp.sum(k * k, 1, keepdims=True) + 1e-6)
        qs.append(cut(q))
        ks.append(cut(k))
        vs.append(cut(v))
        bs.append(cut(head_column(beta_all, pl.program_id(0) * per + j)))
    each = [(j, i) for j in range(per) for i in range(chunks)]
    a_list = [jnp.where(strict, nt(ks[j][i], ks[j][i]) * bs[j][i], 0.0) for j, i in each]
    ps = {(j, i): jnp.where(causal, nt(qs[j][i], ks[j][i]), 0.0) for j, i in each}
    ts = dict(zip(each, triangular_inverse(a_list, row, col)))
    wu = {}
    for j, i in each:
        both = jnp.concatenate([ks[j][i] * bs[j][i], vs[j][i] * bs[j][i]], 1)
        wu[j, i] = both + nn(ts[j, i], both)
    states = [jnp.zeros((128, 128), f32)] * per
    for i in range(chunks):
        span = pl.ds(i * CHUNK, CHUNK)
        news = [wu[j, i][:, 128:] - nn(wu[j, i][:, :128], states[j]) for j in range(per)]
        outs = [nn(jnp.concatenate([qs[j][i], ps[j, i]], 1), jnp.concatenate([states[j], news[j]], 0)) for j in range(per)]
        for j, lane in enumerate(lanes):
            o = outs[j]
            s_ref[j, span, :] = states[j].astype(bf16)
            n_ref[j, span, :] = news[j].astype(bf16)
            t_ref[j, span, :] = ts[j, i].astype(bf16)
            o_ref[span, lane] = o
            mixed_ref[span, lane] = (o * lax.rsqrt(jnp.mean(o * o, 1, keepdims=True) + 1e-5) * gain_ref[...]).astype(bf16)
        if i + 1 < chunks:
            states = [states[j] + tn(ks[j][i], news[j]) for j in range(per)]


def mixer_fwd(u, w, mask, own=(), per=4):
    rows, width = u.shape
    heads = width // 128
    steps = heads // per
    wide = 128 * per
    part = pl.BlockSpec((rows, wide), lambda h: (0, h))
    tap = lambda p: pl.BlockSpec((None, 4, wide), lambda h, p=p: (p, 0, h))
    whole = lambda *shape: pl.BlockSpec(shape, lambda h: (0,) * len(shape))
    saved = pl.BlockSpec((per, rows, 128), lambda h: (h, 0, 0))
    anywhere = [pl.BlockSpec(memory_space=pl.ANY)] * len(own)
    dma = pltpu.SemaphoreType.DMA((max(1, len(own)),))
    shape = lambda kind, *dims: jax.ShapeDtypeStruct(dims, kind)
    return pl.pallas_call(
        functools.partial(mixer_fwd_kernel, per, len(own)),
        grid=(steps,),
        in_specs=[whole(rows, width), whole(1, width), pl.BlockSpec((3, width, wide), lambda h: (0, 0, h)), whole(heads, width), whole(rows, 1)]
        + [tap(0), tap(1), tap(2), whole(1, 128)] + anywhere,
        out_specs=[whole(rows, width), whole(rows, heads), whole(rows, heads), part, part, part, part, saved, saved, saved, part] + anywhere,
        out_shape=[shape(bf16, rows, width), shape(f32, rows, heads), shape(f32, rows, heads)]
        + [shape(f32, rows, width)] * 3
        + [shape(bf16, rows, width)]
        + [shape(bf16, heads, rows, 128)] * 3
        + [shape(f32, rows, width)]
        + [jax.ShapeDtypeStruct(a.shape, a.dtype) for a in own],
        scratch_shapes=[dma, dma] if own else [],
        input_output_aliases={9 + i: 11 + i for i in range(len(own))},
        compiler_params=pltpu.CompilerParams(vmem_limit_bytes=VMEM, **({"collective_id": 2, "has_side_effects": True} if own else {})),
        name="mixer_forward",
    )(u, w["attn_gain"], w["qkv"], w["beta"], mask, w["conv"], w["conv"], w["conv"], w["head_gain"], *own)


def mixer_back_step(per, step, q_ref, k_ref, v_ref, beta_ref, taps_q, taps_k, taps_v, gain_ref, t_ref, n_ref, s_ref, o_ref, dm_ref, w_ref,
                    dq_ref, dk_ref, dv_ref, dtq_ref, dtk_ref, dtv_ref, dgain_ref, dbeta_ref, dnormed):
    row, col = chunk_masks()
    strict, causal_t = row > col, row <= col
    causal = row >= col
    chunks = q_ref.shape[0] // CHUNK
    beta_all = beta_ref[...]

    @pl.when(step == 0)
    def _():
        dbeta_ref[...] = jnp.zeros_like(dbeta_ref)
        dgain_ref[...] = jnp.zeros_like(dgain_ref)
        dnormed[...] = jnp.zeros_like(dnormed)

    cut = lambda x: [x[i * CHUNK : (i + 1) * CHUNK] for i in range(chunks)]
    heads = range(per)
    lanes = [slice(j * 128, (j + 1) * 128) for j in heads]
    kept, qs, ks, vs, bs, dos = [], [], [], [], [], []
    for j, lane in enumerate(lanes):

        def activated(ref, taps):
            c = convolved(ref[:, lane], taps[:, lane])
            sig = jax.nn.sigmoid(c)
            return c * sig, sig * (1.0 + c * (1.0 - sig))

        q_act, q_slope = activated(q_ref, taps_q)
        k_act, k_slope = activated(k_ref, taps_k)
        v, v_slope = activated(v_ref, taps_v)
        q_scale = lax.rsqrt(jnp.sum(q_act * q_act, 1, keepdims=True) + 1e-6)
        k_scale = lax.rsqrt(jnp.sum(k_act * k_act, 1, keepdims=True) + 1e-6)
        q, k = q_act * q_scale, k_act * k_scale
        o, dm, gain = o_ref[:, lane], dm_ref[:, lane], gain_ref[...]
        o_scale = lax.rsqrt(jnp.mean(o * o, 1, keepdims=True) + 1e-5)
        o_hat = o * o_scale
        dgain_ref[...] += jnp.sum(dm * o_hat, 0, keepdims=True)
        dmg = dm * gain
        do = o_scale * (dmg - o_hat * jnp.mean(dmg * o_hat, 1, keepdims=True))
        kept.append((q, k, q_scale, k_scale, q_slope, k_slope, v_slope))
        qs.append(cut(q))
        ks.append(cut(k))
        vs.append(cut(v))
        bs.append(cut(head_column(beta_all, step * per + j)))
        dos.append(cut(do))
    dstates = [jnp.zeros((128, 128), f32)] * per
    dqs, dks, dvs, dbs = [[[] for _ in heads] for _ in range(4)]
    for i in reversed(range(chunks)):
        span = pl.ds(i * CHUNK, CHUNK)
        qc, kc, vc, bc, doc = [[x[j][i] for j in heads] for x in (qs, ks, vs, bs, dos)]
        n, s, t = [[ref[j, span, :] for j in heads] for ref in (n_ref, s_ref, t_ref)]
        gp = [nt(kc[j], jnp.concatenate([kc[j], qc[j]], 0)) for j in heads]
        p_t = [jnp.where(causal_t, gp[j][:, 128:], 0.0) for j in heads]
        dn = [nn(jnp.concatenate([p_t[j], kc[j]], 1), jnp.concatenate([doc[j], dstates[j]], 0)) for j in heads]
        dr = [dn[j] + tn(t[j], dn[j]) for j in heads]
        de = [dr[j] * bc[j] for j in heads]
        both = [nt(doc[j], jnp.concatenate([n[j], s[j]], 0)) for j in heads]
        e = [vc[j] - nn(kc[j], s[j]) for j in heads]
        da = [jnp.where(strict, -nt(dr[j], n[j]), 0.0) for j in heads]
        dp = [jnp.where(causal, both[j][:, :128], 0.0) for j in heads]
        dg = [da[j] * bc[j] for j in heads]
        for j in heads:
            dqs[j].append(both[j][:, 128:] + nn(dp[j], kc[j]))
            dbs[j].append(jnp.sum(dr[j] * e[j], 1, keepdims=True) + jnp.sum(da[j] * gp[j][:, :128], 1, keepdims=True))
            dks[j].append(
                tn(dp[j], qc[j])
                + nt(jnp.concatenate([n[j], -de[j].astype(bf16)], 1), jnp.concatenate([dstates[j].astype(bf16), s[j]], 1))
                + nn(dg[j], kc[j])
                + tn(dg[j], kc[j])
            )
            dvs[j].append(de[j])
        if i:
            dstates = [dstates[j] + tn(qc[j], doc[j]) - tn(kc[j], de[j]) for j in heads]
    join = lambda xs: jnp.concatenate(xs[::-1], 0)
    lane_ids = lax.broadcasted_iota(jnp.int32, dbeta_ref.shape, 1)
    for j, lane in enumerate(lanes):
        q, k, q_scale, k_scale, q_slope, k_slope, v_slope = kept[j]
        dq, dk, dv, db = join(dqs[j]), join(dks[j]), join(dvs[j]), join(dbs[j])
        dq = q_scale * (dq - q * jnp.sum(dq * q, 1, keepdims=True))
        dk = k_scale * (dk - k * jnp.sum(dk * k, 1, keepdims=True))
        dbeta_ref[...] += jnp.where(lane_ids == step * per + j, db, 0.0)
        for grad, slope, ref, taps, out, dtaps in (
            (dq, q_slope, q_ref, taps_q, dq_ref, dtq_ref),
            (dk, k_slope, k_ref, taps_k, dk_ref, dtk_ref),
            (dv, v_slope, v_ref, taps_v, dv_ref, dtv_ref),
        ):
            dc = grad * slope
            x = ref[:, lane]
            w = taps[:, lane]
            dx = dc * w[3:4]
            rows = [None] * 4
            rows[3] = jnp.sum(dc * x, 0, keepdims=True)
            for back in range(1, 4):
                moved = shifted_rows(dc, -back)
                dx = dx + moved * w[3 - back : 4 - back]
                rows[3 - back] = jnp.sum(moved * x, 0, keepdims=True)
            out[:, lane] = dx.astype(bf16)
            dtaps[:, lane] = jnp.concatenate(rows, 0)

    dnormed[...] += sum(nt(ref[...], w_ref[p]) for p, ref in enumerate((dq_ref, dk_ref, dv_ref)))


def mixer_back_end(beta_ref, rate_ref, u_ref, normed_ref, gain_in, w_beta, dy_ref, dbeta_ref, dnormed, g_ref, dgain_in, dw_beta):
    dlogits = dbeta_ref[...] * beta_ref[...] * (1.0 - rate_ref[...])
    high = dlogits.astype(bf16)
    low = (dlogits - high.astype(f32)).astype(bf16)
    dw_beta[...] = tn(high, normed_ref[...]) + tn(low, normed_ref[...])
    x = u_ref[...].astype(f32)
    scale = lax.rsqrt(jnp.mean(x * x, 1, keepdims=True) + 1e-6)
    hat = x * scale
    grad = dnormed[...] + nn(high, w_beta[...])
    dgain_in[...] = jnp.sum(grad * hat, 0, keepdims=True)
    grad = grad * gain_in[...]
    dx = scale * (grad - hat * jnp.mean(grad * hat, 1, keepdims=True))
    g_ref[...] = (dy_ref[...].astype(f32) + dx).astype(bf16)


def mixer_bwd_kernel(per, q_ref, k_ref, v_ref, beta_ref, taps_q, taps_k, taps_v, gain_ref, t_ref, n_ref, s_ref, o_ref, dm_ref,
                     u_ref, normed_ref, rate_ref, gain_in, w_ref, w_beta, dy_ref,
                     dq_ref, dk_ref, dv_ref, dtq_ref, dtk_ref, dtv_ref, dgain_ref, g_ref, dgain_in, dw_beta, dbeta_ref, dnormed):
    step = pl.program_id(0)
    mixer_back_step(per, step, q_ref, k_ref, v_ref, beta_ref, taps_q, taps_k, taps_v, gain_ref, t_ref, n_ref, s_ref, o_ref, dm_ref, w_ref,
                    dq_ref, dk_ref, dv_ref, dtq_ref, dtk_ref, dtv_ref, dgain_ref, dbeta_ref, dnormed)

    @pl.when(step == pl.num_programs(0) - 1)
    def _():
        mixer_back_end(beta_ref, rate_ref, u_ref, normed_ref, gain_in, w_beta, dy_ref, dbeta_ref, dnormed, g_ref, dgain_in, dw_beta)


def mixer_bwd(kept, w, dmixed, dy, per=4):
    u, normed, rate, beta, q, k, v, t, n, s, o = kept
    rows, width = u.shape
    heads = width // 128
    steps = heads // per
    wide = 128 * per
    part = pl.BlockSpec((rows, wide), lambda h: (0, h))
    tap = lambda p: pl.BlockSpec((None, 4, wide), lambda h, p=p: (p, 0, h))
    taps_out = pl.BlockSpec((4, wide), lambda h: (0, h))
    whole = lambda *shape: pl.BlockSpec(shape, lambda h: (0,) * len(shape))
    saved = pl.BlockSpec((per, rows, 128), lambda h: (h, 0, 0))
    shape = lambda kind, *dims: jax.ShapeDtypeStruct(dims, kind)
    stream = whole(rows, width)
    return pl.pallas_call(
        functools.partial(mixer_bwd_kernel, per),
        grid=(steps,),
        in_specs=[part, part, part, whole(rows, heads), tap(0), tap(1), tap(2), whole(1, 128), saved, saved, saved, part, part]
        + [stream, stream, whole(rows, heads), whole(1, width), pl.BlockSpec((3, width, wide), lambda h: (0, 0, h)), whole(heads, width), stream],
        out_specs=[part] * 3 + [taps_out] * 3 + [whole(1, 128), stream, whole(1, width), whole(heads, width)],
        out_shape=[shape(bf16, rows, width)] * 3 + [shape(f32, 4, width)] * 3
        + [shape(f32, 1, 128), shape(bf16, rows, width), shape(f32, 1, width), shape(f32, heads, width)],
        scratch_shapes=[pltpu.VMEM((rows, heads), f32), pltpu.VMEM((rows, width), f32)],
        compiler_params=pltpu.CompilerParams(vmem_limit_bytes=VMEM),
        name="mixer_backward",
    )(q, k, v, beta, w["conv"], w["conv"], w["conv"], w["head_gain"], t, n, s, o, dmixed, u, normed, rate, w["attn_gain"], w["qkv"], w["beta"], dy)


AHEAD = 2


def ff_blocks(ff):
    cuts = [0, 256]
    while cuts[-1] < ff:
        cuts.append(min(ff, cuts[-1] + 512))
    return list(zip(cuts, cuts[1:]))


def mlp_kernel(forward, keep, down, backward, *refs):
    refs = list(refs)
    take = lambda n: [refs.pop(0) for _ in range(n)]
    gain_ref, w_out_hbm, w_gate_hbm, w_up_hbm, w_down_hbm = take(5)
    if forward:
        u0_ref, mixed_ref = take(2)
    else:
        u1_ref, gate_hbm, up_hbm = take(3)
    if backward:
        (dy_ref,) = take(1)
    if forward:
        u1_ref, normed_ref = take(2)
    if keep:
        kept_hbm = take(3)
    if down:
        (u2_ref,) = take(1)
    if backward:
        if not forward:
            (grads_hbm,) = take(1)
        g1_ref, dm_ref, dgain_ref = take(3)
    w_out, w_gate, w_up, w_down, sems, out_sems, out_sem = take(7)
    if keep or not forward:
        gate_all, up_all = take(2)
    if keep:
        (hidden_all,) = take(1)
    if backward and not forward:
        dgate_all, dup_all = take(2)
    blocks = ff_blocks(w_down.shape[0])
    out_copy = pltpu.make_async_copy(w_out_hbm, w_out, out_sem)

    def loads(i):
        a, b = blocks[i]
        pairs = [(w_gate_hbm.at[:, a:b], w_gate.at[:, a:b]), (w_up_hbm.at[:, a:b], w_up.at[:, a:b]), (w_down_hbm.at[a:b], w_down.at[a:b])]
        if not forward:
            pairs += [(gate_hbm.at[:, a:b], gate_all.at[:, a:b]), (up_hbm.at[:, a:b], up_all.at[:, a:b])]
        return [pltpu.make_async_copy(s, d, sems.at[i, n]) for n, (s, d) in enumerate(pairs)]

    def stores(i):
        a, b = blocks[i]
        pairs = []
        if keep:
            pairs = list(zip((gate_all, up_all, hidden_all), kept_hbm))
        pairs = [(s.at[:, a:b], d.at[:, a:b]) for s, d in pairs]
        if backward and not forward:
            ff = blocks[-1][1]
            pairs = [(dgate_all.at[:, a:b], grads_hbm.at[:, a:b]), (dup_all.at[:, a:b], grads_hbm.at[:, ff + a : ff + b])]
        return [pltpu.make_async_copy(s, d, out_sems.at[i, n]) for n, (s, d) in enumerate(pairs)]

    if forward:
        out_copy.start()
    for i in range(AHEAD):
        for copy in loads(i):
            copy.start()
    if forward:
        out_copy.wait()
        u1 = (u0_ref[...].astype(f32) + nn(mixed_ref[...], w_out[...])).astype(bf16)
        u1_ref[...] = u1
        x = u1.astype(f32)
        normed = (x * lax.rsqrt(jnp.mean(x * x, 1, keepdims=True) + 1e-6) * gain_ref[...]).astype(bf16)
        normed_ref[...] = normed
    total = dnormed = None
    for i, (a, b) in enumerate(blocks):
        for copy in loads(i):
            copy.wait()
        if i + AHEAD < len(blocks):
            for copy in loads(i + AHEAD):
                copy.start()
        elif not forward and i + AHEAD == len(blocks):
            out_copy.start()
        if forward:
            gate, up = nn(normed_ref[...], w_gate[:, a:b]), nn(normed_ref[...], w_up[:, a:b])
        else:
            gate, up = gate_all[:, a:b], up_all[:, a:b]
        sig = jax.nn.sigmoid(gate)
        silu = gate * sig
        if forward:
            hidden = (silu * up).astype(bf16)
        if keep:
            gate_all[:, a:b], up_all[:, a:b], hidden_all[:, a:b] = gate, up, hidden
        if down:
            part = nn(hidden, w_down[a:b])
            total = part if total is None else total + part
        if backward:
            dhidden = nt(dy_ref[...], w_down[a:b])
            dgate = (dhidden * up * (sig + silu * (1.0 - sig))).astype(bf16)
            dup = (dhidden * silu).astype(bf16)
            if not forward:
                dgate_all[:, a:b], dup_all[:, a:b] = dgate, dup
            part = nt(jnp.concatenate([dgate, dup], 1), jnp.concatenate([w_gate[:, a:b], w_up[:, a:b]], 1))
            dnormed = part if dnormed is None else dnormed + part
        for copy in stores(i):
            copy.start()
    x = u1_ref[...].astype(f32)
    if down:
        u2_ref[...] = (x + total).astype(bf16)
    if backward:
        if not forward:
            out_copy.wait()
        scale = lax.rsqrt(jnp.mean(x * x, 1, keepdims=True) + 1e-6)
        hat = x * scale
        dgain_ref[...] = jnp.sum(dnormed * hat, 0, keepdims=True)
        grad = dnormed * gain_ref[...]
        dx = scale * (grad - hat * jnp.mean(grad * hat, 1, keepdims=True))
        g1 = (dy_ref[...].astype(f32) + dx).astype(bf16)
        g1_ref[...] = g1
        dm_ref[...] = nt(g1, w_out[...])
    for i in range(len(blocks)):
        for copy in stores(i):
            copy.wait()


def mlp_call(w, rows, forward=None, backward=None, keep=False, down=False):
    width, ff = w["gate"].shape
    going = len(forward) == 2
    here, there = pl.BlockSpec(memory_space=pltpu.VMEM), pl.BlockSpec(memory_space=pl.ANY)
    shape = lambda kind, n=width: jax.ShapeDtypeStruct((rows, n), kind)
    ins = [here] + [there] * 4
    ins += [here, here] if going else [here, there, there]
    args = [w["mlp_gain"], w["out"], w["gate"], w["up"], w["down"], *forward]
    outs, shapes = [], []
    count = len(ff_blocks(ff))
    scratch = [pltpu.VMEM((width, width), bf16), pltpu.VMEM((width, ff), bf16), pltpu.VMEM((width, ff), bf16), pltpu.VMEM((ff, width), bf16)]
    scratch += [pltpu.SemaphoreType.DMA((count, 5)), pltpu.SemaphoreType.DMA((count, 3)), pltpu.SemaphoreType.DMA]
    if backward is not None:
        ins.append(here)
        args.append(backward)
    if going:
        outs += [here, here]
        shapes += [shape(bf16), shape(bf16)]
    if keep or not going:
        scratch += [pltpu.VMEM((rows, ff), f32)] * 2
    if keep:
        outs += [there] * 3
        shapes += [shape(f32, ff), shape(f32, ff), shape(bf16, ff)]
        scratch.append(pltpu.VMEM((rows, ff), bf16))
    if down:
        outs.append(here)
        shapes.append(shape(bf16))
    if backward is not None:
        if not going:
            outs.append(there)
            shapes.append(shape(bf16, 2 * ff))
            scratch += [pltpu.VMEM((rows, ff), bf16)] * 2
        outs += [here, here, here]
        shapes += [shape(bf16), shape(f32), jax.ShapeDtypeStruct((1, width), f32)]
    return pl.pallas_call(
        functools.partial(mlp_kernel, going, keep, down, backward is not None),
        in_specs=ins,
        out_specs=outs,
        out_shape=shapes,
        scratch_shapes=scratch,
        compiler_params=pltpu.CompilerParams(vmem_limit_bytes=VMEM),
        name="feed_forward" + ("_keep" if keep else "") + ("_back" if backward is not None else ""),
    )(*args)


PIECE = (64, 256)
SLOTS = 4
LAGS = (1, 5, 9, 13, 14)
HELD = 24
PAIR = 2


def sum_kernel(total, n2_ref, n1_ref, m_ref, h_ref, dgu, dy, g1, beta_ref, rate_ref, conv_ref, head_ref, attn_ref, w_beta, u_ref, normed_ref, d_mlp_ref,
               q_hbm, k_hbm, v_hbm, o_hbm, dm_hbm, t_hbm, n_hbm, s_hbm, w_hbm, u1, u2,
               gu_out, down_out, out_out, qkv_out, small_out, u_out, g_out,
               q_blk, k_blk, v_blk, o_blk, dm_blk, t_blk, n_blk, s_blk, w_blk, load_sem, dqkv, dtaps, dhead, g0, dattn, dw_beta, dbeta, dnormed, small,
               fin, keep_sem, give_sem, take_sem, fin_sem, far_sem, own, send, rc, rx, ry, rz, send_sem, xs_sem, ys_sem, zs_sem, rc_sem, rx_sem, ry_sem, rz_sem):
    section, me = lax.axis_index("section"), lax.axis_index("dp")
    core, x, low, high = lax.rem(section, 2), lax.rem(me, 2), lax.rem(me // 2, 2), me // 4
    far_core = {"section": section + 1 - 2 * core}
    far_x, far_low, far_high = {"dp": me + 1 - 2 * x}, {"dp": me + 2 - 4 * low}, {"dp": me + 4 - 8 * high}
    barrier = pltpu.get_barrier_semaphore()
    for other in (far_core, far_x, far_low, far_high):
        pl.semaphore_signal(barrier, inc=1, device_id=other, device_id_type=MESH)
    pl.semaphore_wait(barrier, 4)

    def remote(src, dst, sent, got, other):
        return pltpu.make_async_remote_copy(src_ref=src, dst_ref=dst, send_sem=sent, recv_sem=got, device_id=other, device_id_type=MESH)

    def micro(which, mixer_side, mlp_side, into):
        return (
            pltpu.make_async_copy(mixer_side if which == 0 else mlp_side, into.at[core], keep_sem.at[0 if into is u_out else 1]),
            remote(mlp_side if which == 0 else mixer_side, into.at[core], give_sem.at[0 if into is u_out else 1], take_sem.at[0 if into is u_out else 1], far_core),
        )

    def each_core(act):
        for which in range(2):
            @pl.when(core == which)
            def _():
                act(which)

    def start_micro(*sides):
        def act(which):
            for copy in micro(which, *sides):
                copy.start()
        each_core(act)

    start_micro(u1, u2, u_out)

    def loads(s):
        cols = pl.ds(pl.multiple_of(s * PAIR * 128, PAIR * 128), PAIR * 128)
        pairs = [(src.at[:, cols], dst) for src, dst in ((q_hbm, q_blk), (k_hbm, k_blk), (v_hbm, v_blk), (o_hbm, o_blk), (dm_hbm, dm_blk))]
        pairs += [(src.at[pl.ds(s * PAIR, PAIR)], dst) for src, dst in ((t_hbm, t_blk), (n_hbm, n_blk), (s_hbm, s_blk))]
        pairs.append((w_hbm.at[:, :, cols], w_blk))
        return [pltpu.make_async_copy(src, dst, load_sem.at[i]) for i, (src, dst) in enumerate(pairs)]

    for copy in loads(0):
        copy.start()

    def mixer_step(s):
        for copy in loads(s):
            copy.wait()
        width = dattn.shape[1]
        cols = lambda p: pl.ds(pl.multiple_of(p * width + s * PAIR * 128, PAIR * 128), PAIR * 128)
        taps = [conv_ref.at[p, :, cols(0)] for p in range(3)]
        grads = [dqkv.at[:, cols(p)] for p in range(3)]
        dt = [dtaps.at[p, :, cols(0)] for p in range(3)]
        mixer_back_step(PAIR, s, q_blk, k_blk, v_blk, beta_ref, *taps, head_ref, t_blk, n_blk, s_blk, o_blk, dm_blk, w_blk, *grads, *dt, dhead, dbeta, dnormed)

        @pl.when(s + 1 < width // (PAIR * 128))
        def _():
            for copy in loads(s + 1):
                copy.start()

    def mixer_end():
        mixer_back_end(beta_ref, rate_ref, u_ref, normed_ref, attn_ref, w_beta, g1, dbeta, dnormed, g0, dattn, dw_beta)
        start_micro(g0, g1, g_out)
        zeros = lambda n: jnp.zeros((n, PIECE[1]), f32)
        for d in range(8):
            lane = slice(d * 128, (d + 1) * 128)
            wide = lambda a: jnp.concatenate([a, jnp.zeros_like(a)], 1)
            rows = [wide(dattn[:, lane]), zeros(7)]
            for p in range(3):
                rows += [wide(dtaps[p, :, lane])]
            rows += [zeros(4), wide(dhead[...]), zeros(7), wide(dw_beta[:, lane]), zeros(PIECE[0] - 40)]
            small[0, d // 4, d // 2 % 2, d % 2] = jnp.concatenate(rows, 0).astype(bf16)
            small[1, d // 4, d // 2 % 2, d % 2] = jnp.concatenate([wide(d_mlp_ref[:, lane]), zeros(PIECE[0] - 1)], 0).astype(bf16)

    def held(t):
        return lax.rem(t, HELD)

    def slot(t):
        return lax.rem(t, SLOTS)

    def core_copy(t):
        return remote(send.at[slot(t)], rc.at[held(t)], send_sem.at[slot(t)], rc_sem.at[t], far_core)

    def turned(t):
        return lax.rem(t, 4) // 3

    def first_copy(t, z_first):
        src = rc.at[held(t), :, 1 - low] if z_first else rc.at[held(t), :, :, 1 - x]
        return remote(src, rx.at[held(t)], xs_sem.at[slot(t)], rx_sem.at[t], far_low if z_first else far_x)

    def second_copy(t):
        way = turned(t)
        other = {"dp": me + way * (1 - 2 * x) + (1 - way) * (2 - 4 * low)}
        mine = way * x + (1 - way) * low
        return remote(rx.at[held(t), :, 1 - mine], ry.at[held(t)], ys_sem.at[slot(t)], ry_sem.at[t], other)

    def high_copy(t):
        return remote(ry.at[held(t), 1 - high], rz.at[held(t)], zs_sem.at[slot(t)], rz_sem.at[t], far_high)

    def free(copy, t):
        @pl.when(t >= SLOTS)
        def _():
            copy(t - SLOTS).wait_send()

    def either(t, act):
        for z_first in (False, True):
            @pl.when(turned(t) == int(z_first))
            def _():
                act(z_first)

    def after_core(t):
        core_copy(t).wait_recv()
        rc[held(t)] = rc[held(t)] + own[slot(t)]
        free(lambda u: first_copy(u, False), t)
        either(t, lambda z_first: first_copy(t, z_first).start())

    def after_first(t):
        first_copy(t, False).wait_recv()

        def add(z_first):
            rx[held(t)] = rx[held(t)] + (rc[held(t), :, low] if z_first else rc[held(t), :, :, x])

        either(t, add)
        free(second_copy, t)
        second_copy(t).start()

    def after_second(t):
        second_copy(t).wait_recv()
        way = turned(t)
        ry[held(t)] = ry[held(t)] + rx[held(t), :, way * x + (1 - way) * low]
        free(high_copy, t)
        high_copy(t).start()

    def rows_of(t, base, into):
        return into.at[pl.ds(pl.multiple_of(core * PIECE[0], PIECE[0]), PIECE[0]), span(t, base)]

    def slab_of(t, base, into):
        return into.at[core * (into.shape[0] // 2) + t - base]

    def part_of(t, base, into):
        per = into.shape[2] // PIECE[1]
        part = (t - base) // per
        return rows_of(t - part * per, base, into.at[part])

    def piece_here(t, where):
        return pltpu.make_async_copy(fin.at[slot(t)], where, fin_sem.at[slot(t)])

    def piece_there(t, where):
        return remote(fin.at[slot(t)], where, fin_sem.at[slot(t)], far_sem.at[t], far_core)

    def fin_wait(t):
        pltpu.make_async_copy(fin.at[slot(t)], fin.at[slot(t)], fin_sem.at[slot(t)]).wait()

    def after_high(t):
        high_copy(t).wait_recv()
        value = rz[held(t)].astype(f32) + ry[held(t), high].astype(f32)

        @pl.when(t == total - 1)
        def _():
            small_out[...] = value

        @pl.when(t < total - 1)
        def _():
            @pl.when(t >= SLOTS)
            def _():
                fin_wait(t)

            fin[slot(t)] = value
            for base, count, target, _, where, into in segments:
                @pl.when((t >= base) & (t < base + count))
                def _():
                    @pl.when(core == target)
                    def _():
                        piece_here(t, where(t, base, into)).start()

                    @pl.when(core != target)
                    def _():
                        piece_there(t, where(t, base, into)).start()

    def after_far(t):
        for base, count, target, _, where, into in segments:
            @pl.when((t >= base) & (t < base + count) & (core == target))
            def _():
                piece_there(t, where(t, base, into)).wait_recv()

    def later(t):
        for step, lag in zip((after_core, after_first, after_second, after_high, after_far), LAGS):
            @pl.when((t >= lag) & (t < total + lag))
            def _():
                step(t - lag)

    def span(t, base):
        return pl.ds(pl.multiple_of((t - base) * PIECE[1], PIECE[1]), PIECE[1])

    def by_columns(lhs, rhs, base):
        def fill(t):
            block = rhs[:, span(t, base)]
            for which, into in ((1 - core, send), (core, own)):
                part = nn(lhs[which], block).astype(bf16)
                into[slot(t)] = part.reshape(own.shape[1:])
        return fill

    def by_rows(base):
        def fill(t):
            for which, into in ((1 - core, send), (core, own)):
                part = nn(h_ref[t - base, which], dy[...]).astype(bf16)
                count = part.shape[0] // 8
                for d in range(8):
                    for c in range(PIECE[0] // count):
                        into[slot(t), d // 4, d // 2 % 2, d % 2, c * count : (c + 1) * count, :] = part[d * count : (d + 1) * count, c * PIECE[1] : (c + 1) * PIECE[1]]
        return fill

    def given(t):
        send[slot(t)] = small[1 - core]
        own[slot(t)] = small[core]

    segments, base = [], 0
    for target, columns, lhs, rhs, where, into in (
        (1, True, n2_ref, dgu, rows_of, gu_out),
        (1, False, h_ref, dy, slab_of, down_out),
        (0, True, m_ref, g1, rows_of, out_out),
        (0, True, n1_ref, dqkv, part_of, qkv_out),
    ):
        count = rhs.shape[1] // PIECE[1] if columns else lhs.shape[0]
        fill = by_columns(lhs, rhs, base) if columns else by_rows(base)
        segments.append((base, count, target, fill, where, into))
        base += count

    def block(t, fill):
        @pl.when(t >= SLOTS)
        def _():
            core_copy(t - SLOTS).wait_send()

        fill(t)
        core_copy(t).start()
        later(t)

    def run(begin, count, fill):
        def body(i, carry):
            block(begin + i, fill)
            return carry

        lax.fori_loop(0, count, body, 0)

    steps = dattn.shape[1] // (PAIR * 128)
    before = segments[0][1] // steps

    def mixer_turn(s, carry):
        run(s * before, before, segments[0][3])
        mixer_step(s)
        return carry

    lax.fori_loop(0, steps, mixer_turn, 0)
    mixer_end()
    done = steps * before
    for base, count, _, fill, _, _ in segments:
        run(max(base, done), base + count - max(base, done), fill)
    run(total - 1, 1, given)

    def drain(t, carry):
        later(t)
        return carry

    lax.fori_loop(total, total + LAGS[-1], drain, 0)
    for copy in (core_copy, lambda t: first_copy(t, False), second_copy, high_copy):
        for t in range(total - SLOTS, total):
            copy(jnp.int32(t)).wait_send()
    for t in range(SLOTS):
        fin_wait(jnp.int32(t))

    def end_micro(which):
        for keep, give in (micro(which, u1, u2, u_out), micro(which, g0, g1, g_out)):
            keep.wait()
            give.wait_send()
            give.wait_recv()

    each_core(end_micro)


def summed_gradients(n2, n1, m, h, dgu, dy, g1, kept, w, dm, d_mlp, u1, u2):
    u0, normed, rate, beta, q, k, v, t, n, s, o = kept
    rows, width = u0.shape
    ff = dgu.shape[1] // 2
    total = (2 * ff + 4 * width) // PIECE[1] + h.shape[0] + 1
    wide, heads = PAIR * 128, beta.shape[1]
    buffer = lambda *lead: pltpu.VMEM(lead + PIECE, bf16)
    dma = lambda n: pltpu.SemaphoreType.DMA((n,))
    vmem, anywhere = pl.BlockSpec(memory_space=pltpu.VMEM), pl.BlockSpec(memory_space=pl.ANY)
    near = (n2, n1, m, h, dgu, dy, g1, beta, rate, w["conv"], w["head_gain"], w["attn_gain"], w["beta"], u0, normed, d_mlp)
    far = (q, k, v, o, dm, t, n, s, w["qkv"], u1, u2)
    result = lambda *shape: jax.ShapeDtypeStruct(shape, f32)
    pair = jax.ShapeDtypeStruct((2,) + u1.shape, bf16)
    out_rows = 2 * PIECE[0]
    return pl.pallas_call(
        functools.partial(sum_kernel, total),
        out_shape=[result(out_rows, 2 * ff), result(2 * h.shape[0], *PIECE), result(out_rows, width), result(3, out_rows, width), result(*PIECE), pair, pair],
        in_specs=[vmem] * len(near) + [anywhere] * len(far),
        out_specs=[anywhere] * 4 + [vmem] + [anywhere] * 2,
        scratch_shapes=[pltpu.VMEM((rows, wide), f32)] * 5
        + [pltpu.VMEM((PAIR, rows, 128), bf16)] * 3
        + [pltpu.VMEM((3, width, wide), bf16), dma(9)]
        + [pltpu.VMEM((rows, 3 * width), bf16), pltpu.VMEM((3, 4, width), f32), pltpu.VMEM((1, 128), f32), pltpu.VMEM((rows, width), bf16)]
        + [pltpu.VMEM((1, width), f32), pltpu.VMEM((heads, width), f32), pltpu.VMEM((rows, heads), f32), pltpu.VMEM((rows, width), f32)]
        + [buffer(2, 2, 2, 2)]
        + [pltpu.VMEM((SLOTS,) + PIECE, f32), dma(2), dma(2), dma(2), dma(SLOTS), dma(total)]
        + [buffer(SLOTS, 2, 2, 2), buffer(SLOTS, 2, 2, 2), buffer(HELD, 2, 2, 2), buffer(HELD, 2, 2), buffer(HELD, 2), buffer(HELD)]
        + [dma(SLOTS)] * 4
        + [dma(total)] * 4,
        compiler_params=pltpu.CompilerParams(collective_id=0, has_side_effects=True, vmem_limit_bytes=VMEM),
        name="gradient_sums",
    )(*near, *far)


def matmul(a, b):
    return jnp.dot(a, b, preferred_element_type=f32)


def matmul_tn(a, b):
    return lax.dot_general(a, b, (((0,), (0,)), ((), ())), preferred_element_type=f32)


def pick(x, index, axis):
    return lax.dynamic_index_in_dim(x, index, axis, keepdims=False)


def shards(inputs, cotangent, lengths, attn_gain, qkv_weight, conv_weight, beta_weight, head_gain, out_weight, mlp_gain, gate_up_weight, down_weight):
    section, sections = lax.axis_index("section"), lax.axis_size("section")
    me, group = lax.axis_index("dp"), lax.axis_size("dp")
    core, stage = section % 2, section // 2
    swap = [(i, i ^ 1) for i in range(sections)]
    to_odd = [(i, i + 1) for i in range(0, sections, 2)]
    to_even = [(i + 1, i) for i in range(0, sections, 2)]
    rows = inputs.shape[2]
    width = inputs.shape[3]

    qkv, out_w, down, gate_w, first, seed, token_mask, conv, beta_w, attn, head, mlp, own_up = first_exchange(
        jnp.moveaxis(qkv_weight[0], 1, 0),
        out_weight[0],
        down_weight[0],
        inputs,
        cotangent,
        lengths,
        jnp.moveaxis(conv_weight[0], 1, 0),
        beta_weight[0].T,
        attn_gain,
        head_gain,
        mlp_gain,
        gate_up_weight[0],
    )
    w = {"attn_gain": attn, "conv": conv, "beta": beta_w, "head_gain": head, "qkv": qkv, "out": out_w, "mlp_gain": mlp, "down": down, "gate": gate_w}

    up_stage = [(i, i + 2) for i in range(sections - 2)]
    down_stage = [(i + 2, i) for i in range(sections - 2)]

    *passed, w["up"] = mixer_fwd(first, w, token_mask, (own_up,))
    mixed = passed[6]
    _, _, u2 = mlp_call(w, rows, (first, mixed), down=True)
    u0 = jnp.where(stage == 0, first, lax.ppermute(u2, "section", up_stage))
    normed1, rate, beta, q, k, v, mixed, *saved = mixer_fwd(u0, w, token_mask)
    kept = (u0, normed1, rate, beta, q, k, v, *saved)
    u1, normed2, gate, up, hidden, g1, dmixed, _ = mlp_call(w, rows, (u0, mixed), seed, keep=True)
    g0 = mixer_bwd(kept, w, dmixed, g1)[7]
    dy = jnp.where(stage == 1, seed, lax.ppermute(g0, "section", down_stage))
    u2 = (u1.astype(f32) + matmul(hidden, w["down"])).astype(bf16)
    ff = hidden.shape[1]
    fused = group == 8 and width == 1024 and ff % 256 == 0
    for_sums = ()
    if fused:
        by_owner = lambda a: a.reshape(rows, group, 2, 64).transpose(2, 1, 3, 0).reshape(2, group * 64, rows)
        down_rows = hidden.reshape(rows, group, 2, ff // 256, 16).transpose(3, 2, 1, 4, 0).reshape(ff // 256, 2, group * 16, rows)
        for_sums = (by_owner(normed2), by_owner(normed1), by_owner(mixed), down_rows)
    dy, u2, for_sums = lax.optimization_barrier((dy, u2, for_sums))
    dgate_up, g1, dmixed, d_mlp_gain = mlp_call(w, rows, (u1, gate, up), dy)

    if fused:
        sums = summed_gradients(*for_sums, dgate_up, dy, g1, kept, w, dmixed, d_mlp_gain, u1, u2)
        gate_up_sum, down_sum, out_sum, qkv_sum, attn_sum, conv_sum, head_sum, beta_sum, mlp_sum, sec_out, sec_grad = last_outputs(*sums, head_gain.shape[1] // group)
        return (
            sec_out[None, :, None],
            sec_grad[None, :, None],
            attn_sum,
            jnp.moveaxis(qkv_sum, 0, 1)[None],
            jnp.moveaxis(conv_sum, 0, 1)[None],
            beta_sum.T[None],
            head_sum,
            out_sum[None],
            mlp_sum,
            gate_up_sum[None],
            down_sum[None],
        )

    def halve(x):
        kept = pick(x, core, 1).astype(f32)
        x = (kept + lax.ppermute(pick(x, 1 - core, 1), "section", swap).astype(f32)).astype(bf16)
        return scatter(x)

    def scatter(x):
        kind = x.dtype
        bit = 1
        while bit < group:
            pairs = [(i, i ^ bit) for i in range(group)]
            mine = (me // bit) % 2
            x = x.reshape((x.shape[0] // 2, 2) + x.shape[1:])
            other = lax.ppermute(pick(x, 1 - mine, 1), "dp", pairs)
            x = pick(x, mine, 1).astype(f32) + other.astype(f32)
            bit *= 2
            if bit < group:
                x = x.astype(kind)
        return x[0]

    def share(grad):
        count, cols = grad.shape
        return halve(grad.astype(bf16).reshape(group, 2, count // group // 2, cols))

    *dproj, dtq, dtk, dtv, dhead, g0, d_attn_gain, dbeta = mixer_bwd(kept, w, dmixed, g1)
    dtaps = jnp.stack([dtq, dtk, dtv], 1)
    dbeta = dbeta.T
    taps_rows = jnp.moveaxis(dtaps.reshape(-1, 3, group, width // group), 2, 0).reshape(group, -1)
    small = [d_attn_gain.reshape(group, -1), taps_rows, dbeta.reshape(group, -1), dhead.reshape(group, -1), d_mlp_gain.reshape(group, -1)]
    sizes = [a.shape[1] for a in small]
    joined = jnp.concatenate(small, 1)
    down_share = share(matmul_tn(hidden, dy))
    gate_share = share(matmul_tn(normed2, dgate_up[:, :ff]))
    up_share = share(matmul_tn(normed2, dgate_up[:, ff:]))
    out_share = share(matmul_tn(mixed, g1))
    qkv_share = [share(matmul_tn(normed1, d)) for d in dproj]
    small = scatter(joined + lax.ppermute(joined, "section", swap))
    def to_core(x, target):
        other = lax.ppermute(x, "section", to_even if target == 0 else to_odd)
        both = jnp.concatenate([x, other] if target == 0 else [other, x], 0)
        return jnp.where(core == target, both, 0.0)

    grad_qkv = jnp.stack([to_core(x, 0) for x in qkv_share], 1)
    grad_out = to_core(out_share, 0)
    grad_gate_up = jnp.stack([to_core(gate_share, 1), to_core(up_share, 1)], 1)
    grad_down = to_core(down_share, 1)

    def both_micro(mixer_side, mlp_side):
        own = jnp.where(core == 0, mixer_side, mlp_side)
        other = lax.ppermute(jnp.where(core == 0, mlp_side, mixer_side), "section", swap)
        return jnp.where(core == 0, jnp.stack([own, other]), jnp.stack([other, own]))[None, :, None]

    on_even = lambda x: jnp.where(core == 0, x, 0.0)
    on_odd = lambda x: jnp.where(core == 1, x, 0.0)
    sec_out, sec_grad = both_micro(u1, u2), both_micro(g0, g1)
    offsets = [sum(sizes[:i]) for i in range(len(sizes) + 1)]
    s_attn, s_taps, s_beta, s_head, s_mlp = [small[a:b] for a, b in zip(offsets, offsets[1:])]

    return (
        sec_out,
        sec_grad,
        on_even(s_attn)[None],
        grad_qkv[None],
        on_even(s_taps).reshape(1, -1, 3, width // group),
        on_even(s_beta).reshape(1, -1, beta.shape[1]),
        on_even(s_head)[None],
        grad_out[None],
        on_odd(s_mlp)[None],
        grad_gate_up[None],
        grad_down[None],
    )


def solution(mesh):
    in_specs = (
        P(None, "dp", None, None),
        P(None, "dp", None, None),
        P(None, "dp"),
        P("section", None),
        P("section", None, None, None),
        P("section", None, None, None),
        P("section", None, None),
        P("section", None),
        P("section", None, None),
        P("section", None),
        P("section", None, None, None),
        P("section", None, None),
    )
    out_specs = (
        P("section", None, "dp", None, None),
        P("section", None, "dp", None, None),
        P("section", "dp"),
        P("section", "dp", None, None),
        P("section", None, None, "dp"),
        P("section", "dp", None),
        P("section", "dp"),
        P("section", "dp", None),
        P("section", "dp"),
        P("section", "dp", None, None),
        P("section", "dp", None),
    )
    return jax.shard_map(shards, mesh=mesh, in_specs=in_specs, out_specs=out_specs, check_vma=False)
```

```python
import functools

import jax, jax.numpy as jnp
from jax import lax
from jax.experimental import pallas as pl
from jax.experimental.pallas import tpu as pltpu
from jax.sharding import PartitionSpec as P

CHUNK = 128
VMEM = 63 * 1024 * 1024
MESH = pl.DeviceIdType.MESH
bf16, f32 = jnp.bfloat16, jnp.float32


def nn(a, b):
    return lax.dot_general(a.astype(bf16), b.astype(bf16), (((1,), (0,)), ((), ())), preferred_element_type=f32)


def nt(a, b):
    return lax.dot_general(a.astype(bf16), b.astype(bf16), (((1,), (1,)), ((), ())), preferred_element_type=f32)


def tn(a, b):
    return lax.dot_general(a.astype(bf16), b.astype(bf16), (((0,), (0,)), ((), ())), preferred_element_type=f32)


def shifted_rows(x, steps):
    count = x.shape[0]
    rows = lax.broadcasted_iota(jnp.int32, (8, x.shape[1]), 0)
    moved = pltpu.roll(x, steps % count, 0)
    if steps > 0:
        return jnp.concatenate([jnp.where(rows >= steps, moved[:8], 0.0), moved[8:]], 0)
    return jnp.concatenate([moved[:-8], jnp.where(rows < 8 + steps, moved[-8:], 0.0)], 0)


def convolved(x, taps):
    total = x * taps[3:4]
    for back in range(1, 4):
        total = total + shifted_rows(x, back) * taps[3 - back : 4 - back]
    return total


def chunk_masks():
    row = lax.broadcasted_iota(jnp.int32, (CHUNK, CHUNK), 0)
    col = lax.broadcasted_iota(jnp.int32, (CHUNK, CHUNK), 1)
    return row, col


def level_mask(row, col, size):
    shift = size.bit_length() - 1
    same = (row >> (shift + 1)) == (col >> (shift + 1))
    return same & (((row >> shift) & 1) == 1) & (((col >> shift) & 1) == 0)


def triangular_inverse(a_list, row, col):
    mask = level_mask(row, col, 1)
    xs = [jnp.where(mask, -a, 0.0) for a in a_list]
    size = 2
    while size < CHUNK:
        mask = level_mask(row, col, size)
        parts = [jnp.where(mask, a, 0.0) for a in a_list]
        ys = [p + nn(p, x) for p, x in zip(parts, xs)]
        xs = [x - (y + nn(x, y)) for x, y in zip(xs, ys)]
        size *= 2
    return xs


def head_column(block, head):
    lanes = lax.broadcasted_iota(jnp.int32, block.shape, 1)
    return jnp.sum(jnp.where(lanes == head, block, 0.0), axis=1, keepdims=True)


def greet_far_core(section):
    far = {"section": section + 1 - 2 * lax.rem(section, 2)}
    barrier = pltpu.get_barrier_semaphore()
    pl.semaphore_signal(barrier, inc=1, device_id=far, device_id_type=MESH)
    pl.semaphore_wait(barrier, 1)
    return far


def give_weights(step, steps, from_even, from_odd, send_sem, recv_sem):
    section = lax.axis_index("section")
    core = lax.rem(section, 2)
    far = {"section": section + 1 - 2 * core}
    pairs = [(0, *p) for p in from_even] + [(1, *p) for p in from_odd]

    def give(i):
        return pltpu.make_async_remote_copy(
            src_ref=pairs[i][1], dst_ref=pairs[i][2], send_sem=send_sem.at[i], recv_sem=recv_sem.at[i], device_id=far, device_id_type=MESH
        )

    @pl.when(step == 0)
    def _():
        greet_far_core(section)
        for i, (owner, _, _) in enumerate(pairs):
            @pl.when(core == owner)
            def _():
                give(i).start()

    @pl.when(step == steps - 1)
    def _():
        for i, (owner, _, _) in enumerate(pairs):
            @pl.when(core == owner)
            def _():
                give(i).wait_send()

            @pl.when(core != owner)
            def _():
                give(i).wait_recv()


def first_kernel(qkv, out, down, inputs, cotangent, lengths, conv, beta, attn_gain, head_gain, mlp_gain, both, qkv_part, out_part, down_part,
                 qkv_full, out_full, down_full, gate_full, first, seed, mask, conv_full, beta_full, attn_full, head_full, mlp_full, up,
                 gate, mine, theirs, local_sem, send_sem, recv_sem, small_sems, stream_sem, gate_local, gate_send, gate_recv):
    step, steps = pl.program_id(0), pl.num_programs(0)
    section = lax.axis_index("section")
    core = lax.rem(section, 2)
    far = {"section": section + 1 - 2 * core}
    give_weights(step, steps, [(qkv, qkv_full), (out, out_full)], [(down, down_full)], send_sem, recv_sem)
    small = pltpu.make_async_remote_copy(
        src_ref=mine, dst_ref=theirs, send_sem=small_sems.at[0], recv_sem=small_sems.at[1], device_id=far, device_id_type=MESH
    )
    streams = [
        pltpu.make_async_copy(inputs.at[core, 0], first, stream_sem.at[0]),
        pltpu.make_async_copy(cotangent.at[core, 0], seed, stream_sem.at[1]),
    ]

    @pl.when(step == 0)
    def _():
        for copy in streams:
            copy.start()
        mine[...] = jnp.zeros_like(mine)
        for p in range(3):
            mine[8 * p : 8 * p + 4, :] = conv[p].astype(f32)
        mine[4:5, :] = attn_gain[...].astype(f32)
        mine[5:6, : head_gain.shape[1]] = head_gain[...].astype(f32)
        mine[6:7, :] = mlp_gain[...].astype(f32)
        mine[24:32, :] = beta[...].astype(f32)
        small.start()
        length = jnp.where(core == 0, lengths[0:1, :], lengths[1:2, :])
        mask[...] = (lax.broadcasted_iota(jnp.int32, mask.shape, 0) < length).astype(f32)

    count, down_count = out_part.shape[0], down_part.shape[0]
    block, down_block = pl.ds(step * count, count), pl.ds(step * down_count, down_count)
    own = [
        (0, pltpu.make_async_copy(qkv_part, qkv_full.at[:, block], local_sem.at[0])),
        (0, pltpu.make_async_copy(out_part, out_full.at[block], local_sem.at[1])),
        (1, pltpu.make_async_copy(down_part, down_full.at[down_block], local_sem.at[2])),
    ]
    for owner, copy in own:
        @pl.when(core == owner)
        def _():
            copy.start()

    def gate_here(i):
        return pltpu.make_async_copy(gate.at[lax.rem(i, 2)], gate_full.at[pl.ds(i * count, count)], gate_local.at[i])

    def gate_there(i):
        return pltpu.make_async_remote_copy(
            src_ref=gate.at[lax.rem(i, 2)], dst_ref=gate_full.at[pl.ds(i * count, count)],
            send_sem=gate_send.at[i], recv_sem=gate_recv.at[i], device_id=far, device_id_type=MESH,
        )

    @pl.when((core == 1) & (step >= 2))
    def _():
        gate_here(step - 2).wait()
        gate_there(step - 2).wait_send()

    apart = jnp.swapaxes(both[...], 0, 1)
    gate[lax.rem(step, 2)] = apart[0]
    up[...] = apart[1]

    @pl.when(core == 1)
    def _():
        gate_here(step).start()
        gate_there(step).start()

    for owner, copy in own:
        @pl.when(core == owner)
        def _():
            copy.wait()

    @pl.when(step == steps - 1)
    def _():
        small.wait()
        mixer = jnp.where(core == 0, mine[...], theirs[...])
        for p in range(3):
            conv_full[p] = mixer[8 * p : 8 * p + 4]
        attn_full[...] = mixer[4:5]
        head_full[...] = mixer[5:6, : head_full.shape[1]]
        beta_full[...] = mixer[24:32].astype(bf16)
        mlp_full[...] = jnp.where(core == 1, mine[6:7, :], theirs[6:7, :])
        for copy in streams:
            copy.wait()

        @pl.when(core == 1)
        def _():
            for i in (step - 1, step):
                gate_here(i).wait()
                gate_there(i).wait_send()

        @pl.when(core == 0)
        def _():
            def arrived(i, carry):
                gate_there(i).wait_recv()
                return carry

            lax.fori_loop(0, steps, arrived, 0)


def first_exchange(qkv, out, down, inputs, cotangent, lengths, conv, beta, attn_gain, head_gain, mlp_gain, both):
    rows, _, ff = both.shape
    width = out.shape[1]
    length = inputs.shape[2]
    count = 128
    steps = rows // count
    anywhere = pl.BlockSpec(memory_space=pl.ANY)
    whole = lambda *shape: pl.BlockSpec(shape, lambda i: (0,) * len(shape))
    like = lambda a, kind: jax.ShapeDtypeStruct(a.shape, kind)
    shape = lambda kind, *dims: jax.ShapeDtypeStruct(dims, kind)
    smalls = (conv, beta, attn_gain, head_gain, mlp_gain)
    dma = lambda n: pltpu.SemaphoreType.DMA((n,))
    return pl.pallas_call(
        first_kernel,
        grid=(steps,),
        in_specs=[anywhere] * 5
        + [whole(*a.shape) for a in (lengths, *smalls)]
        + [
            pl.BlockSpec((count, 2, ff), lambda i: (i, 0, 0)),
            pl.BlockSpec((3, count, width), lambda i: (0, i, 0)),
            pl.BlockSpec((count, width), lambda i: (i, 0)),
            pl.BlockSpec((ff * count // rows, width), lambda i: (i, 0)),
        ],
        out_specs=[anywhere] * 4 + [whole(length, width)] * 2 + [whole(length, 1)] + [whole(*a.shape) for a in smalls] + [pl.BlockSpec((count, ff), lambda i: (i, 0))],
        out_shape=[like(qkv, bf16), like(out, bf16), like(down, bf16), shape(bf16, rows, ff), shape(bf16, length, width), shape(bf16, length, width), shape(f32, length, 1)]
        + [like(conv, f32), like(beta, bf16), like(attn_gain, f32), like(head_gain, f32), like(mlp_gain, f32), shape(bf16, rows, ff)],
        scratch_shapes=[pltpu.VMEM((2, count, ff), bf16)] + [pltpu.VMEM((32, width), f32)] * 2 + [dma(3)] * 3 + [dma(2)] * 2 + [dma(steps)] * 3,
        compiler_params=pltpu.CompilerParams(collective_id=1, has_side_effects=True, vmem_limit_bytes=VMEM),
        name="first_exchange",
    )(qkv, out, down, inputs, cotangent, lengths, *smalls, both, qkv, out, down)


def last_kernel(gate_up_in, down_in, out_in, qkv_in, small, sec_out_in, sec_grad_in, gate_up, down, out, qkv, attn, conv, head, beta, mlp, sec_out, sec_grad):
    core = lax.rem(lax.axis_index("section"), 2)
    me = lax.axis_index("dp")
    on = lambda which, x: jnp.where(core == which, x, 0.0)
    ff = gate_up.shape[2]
    both = on(1, gate_up_in[...])
    gate_up[...] = jnp.swapaxes(jnp.stack([both[:, :ff], both[:, ff:]], 0), 0, 1)
    count, wide = 16, small.shape[1]
    for j in range(down_in.shape[0]):
        for c in range(down.shape[1] // wide):
            down[j * count : (j + 1) * count, c * wide : (c + 1) * wide] = on(1, down_in[j, c * count : (c + 1) * count, :])
    out[...] = on(0, out_in[...])
    qkv[...] = on(0, qkv_in[...])
    sec_out[...] = sec_out_in[...]
    sec_grad[...] = sec_grad_in[...]
    lanes = attn.shape[1]
    attn[...] = on(0, small[0:1, :lanes])
    mlp[...] = on(1, small[0:1, :lanes])
    for p in range(3):
        conv[p] = on(0, small[8 + 4 * p : 12 + 4 * p, :lanes])
    beta[...] = on(0, small[32:40, :lanes])
    part = head.shape[1]
    turned = small[24:32, :lanes]
    shift = lax.rem(lanes - me * part, lanes)
    head[...] = on(0, pltpu.roll(turned, shift, 1)[0:1, :part])


def last_outputs(gate_up, down, out, qkv, small, sec_out, sec_grad, head_part):
    rows, width = out.shape
    ff = gate_up.shape[1] // 2
    half = rows // 2
    lanes = rows
    whole = lambda *shape: pl.BlockSpec(shape, lambda i: (0,) * len(shape))
    by_rows = lambda *shape: pl.BlockSpec(shape, lambda i: (i,) + (0,) * (len(shape) - 1))
    shape = lambda *dims: jax.ShapeDtypeStruct(dims, f32)
    qkv_spec = pl.BlockSpec((3, half, width), lambda i: (0, i, 0))
    stream = by_rows(1, *sec_out.shape[1:])
    tall = down.shape[0] // 2
    return pl.pallas_call(
        last_kernel,
        grid=(2,),
        in_specs=[by_rows(half, 2 * ff), by_rows(tall, *down.shape[1:]), by_rows(half, width), qkv_spec, whole(*small.shape), stream, stream],
        out_specs=[by_rows(half, 2, ff), by_rows(16 * tall, width), by_rows(half, width), qkv_spec]
        + [whole(1, lanes), whole(3, 4, lanes), whole(1, head_part), whole(8, lanes), whole(1, lanes), stream, stream],
        out_shape=[shape(rows, 2, ff), shape(32 * tall, width), shape(rows, width), shape(3, rows, width)]
        + [shape(1, lanes), shape(3, 4, lanes), shape(1, head_part), shape(8, lanes), shape(1, lanes)]
        + [jax.ShapeDtypeStruct(sec_out.shape, bf16)] * 2,
        compiler_params=pltpu.CompilerParams(vmem_limit_bytes=VMEM),
        name="last_outputs",
    )(gate_up, down, out, qkv, small, sec_out, sec_grad)


def mixer_fwd_kernel(per, trade, u_ref, gain_in, w_ref, w_beta, mask_ref, taps_q, taps_k, taps_v, gain_ref, *refs):
    own, refs = refs[:trade], refs[trade:]
    normed_ref, rate_ref, beta_ref, q_ref, k_ref, v_ref, mixed_ref, t_ref, n_ref, s_ref, o_ref = refs[:11]
    if trade:
        give_weights(pl.program_id(0), pl.num_programs(0), [], list(zip(own, refs[11 : 11 + trade])), *refs[11 + trade :])

    @pl.when(pl.program_id(0) == 0)
    def _():
        x = u_ref[...].astype(f32)
        normed = (x * lax.rsqrt(jnp.mean(x * x, 1, keepdims=True) + 1e-6) * gain_in[...]).astype(bf16)
        normed_ref[...] = normed
        rate = jax.nn.sigmoid(nt(normed, w_beta[...]))
        rate_ref[...] = rate
        beta_ref[...] = rate * mask_ref[...]

    for p, ref in enumerate((q_ref, k_ref, v_ref)):
        ref[...] = nn(normed_ref[...], w_ref[p])
    row, col = chunk_masks()
    strict, causal = row > col, row >= col
    chunks = q_ref.shape[0] // CHUNK
    beta_all = beta_ref[...]
    cut = lambda x: [x[i * CHUNK : (i + 1) * CHUNK] for i in range(chunks)]
    lanes = [slice(j * 128, (j + 1) * 128) for j in range(per)]
    qs, ks, vs, bs = [], [], [], []
    for j, lane in enumerate(lanes):

        def activated(ref, taps):
            c = convolved(ref[:, lane], taps[:, lane])
            return c * jax.nn.sigmoid(c)

        q, k, v = activated(q_ref, taps_q), activated(k_ref, taps_k), activated(v_ref, taps_v)
        q = q * lax.rsqrt(jnp.sum(q * q, 1, keepdims=True) + 1e-6)
        k = k * lax.rsqrt(jnp.sum(k * k, 1, keepdims=True) + 1e-6)
        qs.append(cut(q))
        ks.append(cut(k))
        vs.append(cut(v))
        bs.append(cut(head_column(beta_all, pl.program_id(0) * per + j)))
    each = [(j, i) for j in range(per) for i in range(chunks)]
    a_list = [jnp.where(strict, nt(ks[j][i], ks[j][i]) * bs[j][i], 0.0) for j, i in each]
    ps = {(j, i): jnp.where(causal, nt(qs[j][i], ks[j][i]), 0.0) for j, i in each}
    ts = dict(zip(each, triangular_inverse(a_list, row, col)))
    wu = {}
    for j, i in each:
        both = jnp.concatenate([ks[j][i] * bs[j][i], vs[j][i] * bs[j][i]], 1)
        wu[j, i] = both + nn(ts[j, i], both)
    states = [jnp.zeros((128, 128), f32)] * per
    for i in range(chunks):
        span = pl.ds(i * CHUNK, CHUNK)
        news = [wu[j, i][:, 128:] - nn(wu[j, i][:, :128], states[j]) for j in range(per)]
        outs = [nn(jnp.concatenate([qs[j][i], ps[j, i]], 1), jnp.concatenate([states[j], news[j]], 0)) for j in range(per)]
        for j, lane in enumerate(lanes):
            o = outs[j]
            s_ref[j, span, :] = states[j].astype(bf16)
            n_ref[j, span, :] = news[j].astype(bf16)
            t_ref[j, span, :] = ts[j, i].astype(bf16)
            o_ref[span, lane] = o
            mixed_ref[span, lane] = (o * lax.rsqrt(jnp.mean(o * o, 1, keepdims=True) + 1e-5) * gain_ref[...]).astype(bf16)
        if i + 1 < chunks:
            states = [states[j] + tn(ks[j][i], news[j]) for j in range(per)]


def mixer_fwd(u, w, mask, own=(), per=4):
    rows, width = u.shape
    heads = width // 128
    steps = heads // per
    wide = 128 * per
    part = pl.BlockSpec((rows, wide), lambda h: (0, h))
    tap = lambda p: pl.BlockSpec((None, 4, wide), lambda h, p=p: (p, 0, h))
    whole = lambda *shape: pl.BlockSpec(shape, lambda h: (0,) * len(shape))
    saved = pl.BlockSpec((per, rows, 128), lambda h: (h, 0, 0))
    anywhere = [pl.BlockSpec(memory_space=pl.ANY)] * len(own)
    dma = pltpu.SemaphoreType.DMA((max(1, len(own)),))
    shape = lambda kind, *dims: jax.ShapeDtypeStruct(dims, kind)
    return pl.pallas_call(
        functools.partial(mixer_fwd_kernel, per, len(own)),
        grid=(steps,),
        in_specs=[whole(rows, width), whole(1, width), pl.BlockSpec((3, width, wide), lambda h: (0, 0, h)), whole(heads, width), whole(rows, 1)]
        + [tap(0), tap(1), tap(2), whole(1, 128)] + anywhere,
        out_specs=[whole(rows, width), whole(rows, heads), whole(rows, heads), part, part, part, part, saved, saved, saved, part] + anywhere,
        out_shape=[shape(bf16, rows, width), shape(f32, rows, heads), shape(f32, rows, heads)]
        + [shape(f32, rows, width)] * 3
        + [shape(bf16, rows, width)]
        + [shape(bf16, heads, rows, 128)] * 3
        + [shape(f32, rows, width)]
        + [jax.ShapeDtypeStruct(a.shape, a.dtype) for a in own],
        scratch_shapes=[dma, dma] if own else [],
        input_output_aliases={9 + i: 11 + i for i in range(len(own))},
        compiler_params=pltpu.CompilerParams(vmem_limit_bytes=VMEM, **({"collective_id": 2, "has_side_effects": True} if own else {})),
        name="mixer_forward",
    )(u, w["attn_gain"], w["qkv"], w["beta"], mask, w["conv"], w["conv"], w["conv"], w["head_gain"], *own)


def mixer_back_step(per, step, q_ref, k_ref, v_ref, beta_ref, taps_q, taps_k, taps_v, gain_ref, t_ref, n_ref, s_ref, o_ref, dm_ref, w_ref,
                    dq_ref, dk_ref, dv_ref, dtq_ref, dtk_ref, dtv_ref, dgain_ref, dbeta_ref, dnormed):
    row, col = chunk_masks()
    strict, causal_t = row > col, row <= col
    causal = row >= col
    chunks = q_ref.shape[0] // CHUNK
    beta_all = beta_ref[...]

    @pl.when(step == 0)
    def _():
        dbeta_ref[...] = jnp.zeros_like(dbeta_ref)
        dgain_ref[...] = jnp.zeros_like(dgain_ref)
        dnormed[...] = jnp.zeros_like(dnormed)

    cut = lambda x: [x[i * CHUNK : (i + 1) * CHUNK] for i in range(chunks)]
    heads = range(per)
    lanes = [slice(j * 128, (j + 1) * 128) for j in heads]
    kept, qs, ks, vs, bs, dos = [], [], [], [], [], []
    for j, lane in enumerate(lanes):

        def activated(ref, taps):
            c = convolved(ref[:, lane], taps[:, lane])
            sig = jax.nn.sigmoid(c)
            return c * sig, sig * (1.0 + c * (1.0 - sig))

        q_act, q_slope = activated(q_ref, taps_q)
        k_act, k_slope = activated(k_ref, taps_k)
        v, v_slope = activated(v_ref, taps_v)
        q_scale = lax.rsqrt(jnp.sum(q_act * q_act, 1, keepdims=True) + 1e-6)
        k_scale = lax.rsqrt(jnp.sum(k_act * k_act, 1, keepdims=True) + 1e-6)
        q, k = q_act * q_scale, k_act * k_scale
        o, dm, gain = o_ref[:, lane], dm_ref[:, lane], gain_ref[...]
        o_scale = lax.rsqrt(jnp.mean(o * o, 1, keepdims=True) + 1e-5)
        o_hat = o * o_scale
        dgain_ref[...] += jnp.sum(dm * o_hat, 0, keepdims=True)
        dmg = dm * gain
        do = o_scale * (dmg - o_hat * jnp.mean(dmg * o_hat, 1, keepdims=True))
        kept.append((q, k, q_scale, k_scale, q_slope, k_slope, v_slope))
        qs.append(cut(q))
        ks.append(cut(k))
        vs.append(cut(v))
        bs.append(cut(head_column(beta_all, step * per + j)))
        dos.append(cut(do))
    dstates = [jnp.zeros((128, 128), f32)] * per
    dqs, dks, dvs, dbs = [[[] for _ in heads] for _ in range(4)]
    for i in reversed(range(chunks)):
        span = pl.ds(i * CHUNK, CHUNK)
        qc, kc, vc, bc, doc = [[x[j][i] for j in heads] for x in (qs, ks, vs, bs, dos)]
        n, s, t = [[ref[j, span, :] for j in heads] for ref in (n_ref, s_ref, t_ref)]
        gp = [nt(kc[j], jnp.concatenate([kc[j], qc[j]], 0)) for j in heads]
        p_t = [jnp.where(causal_t, gp[j][:, 128:], 0.0) for j in heads]
        dn = [nn(jnp.concatenate([p_t[j], kc[j]], 1), jnp.concatenate([doc[j], dstates[j]], 0)) for j in heads]
        dr = [dn[j] + tn(t[j], dn[j]) for j in heads]
        de = [dr[j] * bc[j] for j in heads]
        both = [nt(doc[j], jnp.concatenate([n[j], s[j]], 0)) for j in heads]
        e = [vc[j] - nn(kc[j], s[j]) for j in heads]
        da = [jnp.where(strict, -nt(dr[j], n[j]), 0.0) for j in heads]
        dp = [jnp.where(causal, both[j][:, :128], 0.0) for j in heads]
        dg = [da[j] * bc[j] for j in heads]
        for j in heads:
            dqs[j].append(both[j][:, 128:] + nn(dp[j], kc[j]))
            dbs[j].append(jnp.sum(dr[j] * e[j], 1, keepdims=True) + jnp.sum(da[j] * gp[j][:, :128], 1, keepdims=True))
            dks[j].append(
                tn(dp[j], qc[j])
                + nt(jnp.concatenate([n[j], -de[j].astype(bf16)], 1), jnp.concatenate([dstates[j].astype(bf16), s[j]], 1))
                + nn(dg[j], kc[j])
                + tn(dg[j], kc[j])
            )
            dvs[j].append(de[j])
        if i:
            dstates = [dstates[j] + tn(qc[j], doc[j]) - tn(kc[j], de[j]) for j in heads]
    join = lambda xs: jnp.concatenate(xs[::-1], 0)
    lane_ids = lax.broadcasted_iota(jnp.int32, dbeta_ref.shape, 1)
    for j, lane in enumerate(lanes):
        q, k, q_scale, k_scale, q_slope, k_slope, v_slope = kept[j]
        dq, dk, dv, db = join(dqs[j]), join(dks[j]), join(dvs[j]), join(dbs[j])
        dq = q_scale * (dq - q * jnp.sum(dq * q, 1, keepdims=True))
        dk = k_scale * (dk - k * jnp.sum(dk * k, 1, keepdims=True))
        dbeta_ref[...] += jnp.where(lane_ids == step * per + j, db, 0.0)
        for grad, slope, ref, taps, out, dtaps in (
            (dq, q_slope, q_ref, taps_q, dq_ref, dtq_ref),
            (dk, k_slope, k_ref, taps_k, dk_ref, dtk_ref),
            (dv, v_slope, v_ref, taps_v, dv_ref, dtv_ref),
        ):
            dc = grad * slope
            x = ref[:, lane]
            w = taps[:, lane]
            dx = dc * w[3:4]
            rows = [None] * 4
            rows[3] = jnp.sum(dc * x, 0, keepdims=True)
            for back in range(1, 4):
                moved = shifted_rows(dc, -back)
                dx = dx + moved * w[3 - back : 4 - back]
                rows[3 - back] = jnp.sum(moved * x, 0, keepdims=True)
            out[:, lane] = dx.astype(bf16)
            dtaps[:, lane] = jnp.concatenate(rows, 0)

    dnormed[...] += sum(nt(ref[...], w_ref[p]) for p, ref in enumerate((dq_ref, dk_ref, dv_ref)))


def norm_back(u, gain, grad, dy, dgain_ref):
    x = u.astype(f32)
    scale = lax.rsqrt(jnp.mean(x * x, 1, keepdims=True) + 1e-6)
    hat = x * scale
    dgain_ref[...] = jnp.sum(grad * hat, 0, keepdims=True)
    grad = grad * gain
    dx = scale * (grad - hat * jnp.mean(grad * hat, 1, keepdims=True))
    return (dy.astype(f32) + dx).astype(bf16)


def mixer_back_end(beta_ref, rate_ref, u_ref, normed_ref, gain_in, w_beta, dy_ref, dbeta_ref, dnormed, g_ref, dgain_in, dw_beta):
    dlogits = dbeta_ref[...] * beta_ref[...] * (1.0 - rate_ref[...])
    high = dlogits.astype(bf16)
    low = (dlogits - high.astype(f32)).astype(bf16)
    dw_beta[...] = tn(high, normed_ref[...]) + tn(low, normed_ref[...])
    g_ref[...] = norm_back(u_ref[...], gain_in[...], dnormed[...] + nn(high, w_beta[...]), dy_ref[...], dgain_in)


def mixer_bwd_kernel(per, q_ref, k_ref, v_ref, beta_ref, taps_q, taps_k, taps_v, gain_ref, t_ref, n_ref, s_ref, o_ref, dm_ref,
                     u_ref, normed_ref, rate_ref, gain_in, w_ref, w_beta, dy_ref,
                     dq_ref, dk_ref, dv_ref, dtq_ref, dtk_ref, dtv_ref, dgain_ref, g_ref, dgain_in, dw_beta, dbeta_ref, dnormed):
    step = pl.program_id(0)
    mixer_back_step(per, step, q_ref, k_ref, v_ref, beta_ref, taps_q, taps_k, taps_v, gain_ref, t_ref, n_ref, s_ref, o_ref, dm_ref, w_ref,
                    dq_ref, dk_ref, dv_ref, dtq_ref, dtk_ref, dtv_ref, dgain_ref, dbeta_ref, dnormed)

    @pl.when(step == pl.num_programs(0) - 1)
    def _():
        mixer_back_end(beta_ref, rate_ref, u_ref, normed_ref, gain_in, w_beta, dy_ref, dbeta_ref, dnormed, g_ref, dgain_in, dw_beta)


def mixer_bwd(kept, w, dmixed, dy, per=4):
    u, normed, rate, beta, q, k, v, t, n, s, o = kept
    rows, width = u.shape
    heads = width // 128
    steps = heads // per
    wide = 128 * per
    part = pl.BlockSpec((rows, wide), lambda h: (0, h))
    tap = lambda p: pl.BlockSpec((None, 4, wide), lambda h, p=p: (p, 0, h))
    taps_out = pl.BlockSpec((4, wide), lambda h: (0, h))
    whole = lambda *shape: pl.BlockSpec(shape, lambda h: (0,) * len(shape))
    saved = pl.BlockSpec((per, rows, 128), lambda h: (h, 0, 0))
    shape = lambda kind, *dims: jax.ShapeDtypeStruct(dims, kind)
    stream = whole(rows, width)
    return pl.pallas_call(
        functools.partial(mixer_bwd_kernel, per),
        grid=(steps,),
        in_specs=[part, part, part, whole(rows, heads), tap(0), tap(1), tap(2), whole(1, 128), saved, saved, saved, part, part]
        + [stream, stream, whole(rows, heads), whole(1, width), pl.BlockSpec((3, width, wide), lambda h: (0, 0, h)), whole(heads, width), stream],
        out_specs=[part] * 3 + [taps_out] * 3 + [whole(1, 128), stream, whole(1, width), whole(heads, width)],
        out_shape=[shape(bf16, rows, width)] * 3 + [shape(f32, 4, width)] * 3
        + [shape(f32, 1, 128), shape(bf16, rows, width), shape(f32, 1, width), shape(f32, heads, width)],
        scratch_shapes=[pltpu.VMEM((rows, heads), f32), pltpu.VMEM((rows, width), f32)],
        compiler_params=pltpu.CompilerParams(vmem_limit_bytes=VMEM),
        name="mixer_backward",
    )(q, k, v, beta, w["conv"], w["conv"], w["conv"], w["head_gain"], t, n, s, o, dmixed, u, normed, rate, w["attn_gain"], w["qkv"], w["beta"], dy)


AHEAD = 2


def ff_blocks(ff):
    cuts = [0, 256]
    while cuts[-1] < ff:
        cuts.append(min(ff, cuts[-1] + 512))
    return list(zip(cuts, cuts[1:]))


def mlp_kernel(forward, keep, down, backward, *refs):
    refs = list(refs)
    take = lambda n: [refs.pop(0) for _ in range(n)]
    gain_ref, w_out_hbm, w_gate_hbm, w_up_hbm, w_down_hbm = take(5)
    if forward:
        u0_ref, mixed_ref = take(2)
    else:
        u1_ref, gate_hbm, up_hbm = take(3)
    if backward:
        (dy_ref,) = take(1)
    if forward:
        u1_ref, normed_ref = take(2)
    if keep:
        kept_hbm = take(3)
    if down:
        (u2_ref,) = take(1)
    if backward:
        if not forward:
            (grads_hbm,) = take(1)
        g1_ref, dm_ref, dgain_ref = take(3)
    w_out, w_gate, w_up, w_down, sems, out_sems, out_sem = take(7)
    if keep or not forward:
        gate_all, up_all = take(2)
    if keep:
        (hidden_all,) = take(1)
    if backward and not forward:
        dgate_all, dup_all = take(2)
    blocks = ff_blocks(w_down.shape[0])
    out_copy = pltpu.make_async_copy(w_out_hbm, w_out, out_sem)

    def loads(i):
        a, b = blocks[i]
        pairs = [(w_gate_hbm.at[:, a:b], w_gate.at[:, a:b]), (w_up_hbm.at[:, a:b], w_up.at[:, a:b]), (w_down_hbm.at[a:b], w_down.at[a:b])]
        if not forward:
            pairs += [(gate_hbm.at[:, a:b], gate_all.at[:, a:b]), (up_hbm.at[:, a:b], up_all.at[:, a:b])]
        return [pltpu.make_async_copy(s, d, sems.at[i, n]) for n, (s, d) in enumerate(pairs)]

    def stores(i):
        a, b = blocks[i]
        pairs = []
        if keep:
            pairs = list(zip((gate_all, up_all, hidden_all), kept_hbm))
        pairs = [(s.at[:, a:b], d.at[:, a:b]) for s, d in pairs]
        if backward and not forward:
            ff = blocks[-1][1]
            pairs = [(dgate_all.at[:, a:b], grads_hbm.at[:, a:b]), (dup_all.at[:, a:b], grads_hbm.at[:, ff + a : ff + b])]
        return [pltpu.make_async_copy(s, d, out_sems.at[i, n]) for n, (s, d) in enumerate(pairs)]

    if forward:
        out_copy.start()
    for i in range(AHEAD):
        for copy in loads(i):
            copy.start()
    if forward:
        out_copy.wait()
        u1 = (u0_ref[...].astype(f32) + nn(mixed_ref[...], w_out[...])).astype(bf16)
        u1_ref[...] = u1
        x = u1.astype(f32)
        normed = (x * lax.rsqrt(jnp.mean(x * x, 1, keepdims=True) + 1e-6) * gain_ref[...]).astype(bf16)
        normed_ref[...] = normed
    total = dnormed = None
    for i, (a, b) in enumerate(blocks):
        for copy in loads(i):
            copy.wait()
        if i + AHEAD < len(blocks):
            for copy in loads(i + AHEAD):
                copy.start()
        elif not forward and i + AHEAD == len(blocks):
            out_copy.start()
        if forward:
            gate, up = nn(normed_ref[...], w_gate[:, a:b]), nn(normed_ref[...], w_up[:, a:b])
        else:
            gate, up = gate_all[:, a:b], up_all[:, a:b]
        sig = jax.nn.sigmoid(gate)
        silu = gate * sig
        if forward:
            hidden = (silu * up).astype(bf16)
        if keep:
            gate_all[:, a:b], up_all[:, a:b], hidden_all[:, a:b] = gate, up, hidden
        if down:
            part = nn(hidden, w_down[a:b])
            total = part if total is None else total + part
        if backward:
            dhidden = nt(dy_ref[...], w_down[a:b])
            dgate = (dhidden * up * (sig + silu * (1.0 - sig))).astype(bf16)
            dup = (dhidden * silu).astype(bf16)
            if not forward:
                dgate_all[:, a:b], dup_all[:, a:b] = dgate, dup
            part = nt(jnp.concatenate([dgate, dup], 1), jnp.concatenate([w_gate[:, a:b], w_up[:, a:b]], 1))
            dnormed = part if dnormed is None else dnormed + part
        for copy in stores(i):
            copy.start()
    x = u1_ref[...].astype(f32)
    if down:
        u2_ref[...] = (x + total).astype(bf16)
    if backward:
        if not forward:
            out_copy.wait()
        scale = lax.rsqrt(jnp.mean(x * x, 1, keepdims=True) + 1e-6)
        hat = x * scale
        dgain_ref[...] = jnp.sum(dnormed * hat, 0, keepdims=True)
        grad = dnormed * gain_ref[...]
        dx = scale * (grad - hat * jnp.mean(grad * hat, 1, keepdims=True))
        g1 = (dy_ref[...].astype(f32) + dx).astype(bf16)
        g1_ref[...] = g1
        dm_ref[...] = nt(g1, w_out[...])
    for i in range(len(blocks)):
        for copy in stores(i):
            copy.wait()


def mlp_call(w, rows, forward=None, backward=None, keep=False, down=False):
    width, ff = w["gate"].shape
    going = len(forward) == 2
    here, there = pl.BlockSpec(memory_space=pltpu.VMEM), pl.BlockSpec(memory_space=pl.ANY)
    shape = lambda kind, n=width: jax.ShapeDtypeStruct((rows, n), kind)
    ins = [here] + [there] * 4
    ins += [here, here] if going else [here, there, there]
    args = [w["mlp_gain"], w["out"], w["gate"], w["up"], w["down"], *forward]
    outs, shapes = [], []
    count = len(ff_blocks(ff))
    scratch = [pltpu.VMEM((width, width), bf16), pltpu.VMEM((width, ff), bf16), pltpu.VMEM((width, ff), bf16), pltpu.VMEM((ff, width), bf16)]
    scratch += [pltpu.SemaphoreType.DMA((count, 5)), pltpu.SemaphoreType.DMA((count, 3)), pltpu.SemaphoreType.DMA]
    if backward is not None:
        ins.append(here)
        args.append(backward)
    if going:
        outs += [here, here]
        shapes += [shape(bf16), shape(bf16)]
    if keep or not going:
        scratch += [pltpu.VMEM((rows, ff), f32)] * 2
    if keep:
        outs += [there] * 3
        shapes += [shape(f32, ff), shape(f32, ff), shape(bf16, ff)]
        scratch.append(pltpu.VMEM((rows, ff), bf16))
    if down:
        outs.append(here)
        shapes.append(shape(bf16))
    if backward is not None:
        if not going:
            outs.append(there)
            shapes.append(shape(bf16, 2 * ff))
            scratch += [pltpu.VMEM((rows, ff), bf16)] * 2
        outs += [here, here, here]
        shapes += [shape(bf16), shape(f32), jax.ShapeDtypeStruct((1, width), f32)]
    return pl.pallas_call(
        functools.partial(mlp_kernel, going, keep, down, backward is not None),
        in_specs=ins,
        out_specs=outs,
        out_shape=shapes,
        scratch_shapes=scratch,
        compiler_params=pltpu.CompilerParams(vmem_limit_bytes=VMEM),
        name="feed_forward" + ("_keep" if keep else "") + ("_back" if backward is not None else ""),
    )(*args)


SEND_ROWS = (0, 256, 512)


def mlp_send_kernel(cuts, gain_ref, w_out_hbm, w_gate_hbm, w_up_hbm, w_down_hbm, u0_ref, mixed_ref, next_ref,
                    w_out, w_gate, w_up, w_down, sems, out_sem, u2, arrived, send_sem, recv_sem):
    section = lax.axis_index("section")
    stage = section // 2
    far = {"section": section + 2 - 4 * stage}
    blocks = ff_blocks(w_down.shape[0])
    out_copy = pltpu.make_async_copy(w_out_hbm, w_out, out_sem)
    parts = list(zip(cuts, cuts[1:]))

    def loads(i):
        a, b = blocks[i]
        pairs = [(w_gate_hbm.at[:, a:b], w_gate.at[:, a:b]), (w_up_hbm.at[:, a:b], w_up.at[:, a:b]), (w_down_hbm.at[a:b], w_down.at[a:b])]
        return [pltpu.make_async_copy(s, d, sems.at[i, n]) for n, (s, d) in enumerate(pairs)]

    def send(p):
        a, b = parts[p]
        return pltpu.make_async_remote_copy(
            src_ref=u2.at[a:b], dst_ref=arrived.at[a:b], send_sem=send_sem.at[p], recv_sem=recv_sem.at[p], device_id=far, device_id_type=MESH
        )

    out_copy.start()
    for i in range(AHEAD):
        for copy in loads(i):
            copy.start()
    barrier = pltpu.get_barrier_semaphore()
    pl.semaphore_signal(barrier, inc=1, device_id=far, device_id_type=MESH)
    pl.semaphore_wait(barrier, 1)
    out_copy.wait()
    for p, (first, last) in enumerate(parts):
        u1 = (u0_ref[first:last].astype(f32) + nn(mixed_ref[first:last], w_out[...])).astype(bf16)
        x = u1.astype(f32)
        normed = (x * lax.rsqrt(jnp.mean(x * x, 1, keepdims=True) + 1e-6) * gain_ref[...]).astype(bf16)
        total = x
        for i, (a, b) in enumerate(blocks):
            if p == 0:
                for copy in loads(i):
                    copy.wait()
                if i + AHEAD < len(blocks):
                    for copy in loads(i + AHEAD):
                        copy.start()
            gate, up = nn(normed, w_gate[:, a:b]), nn(normed, w_up[:, a:b])
            total = total + nn((gate * jax.nn.sigmoid(gate) * up).astype(bf16), w_down[a:b])
        u2[first:last] = total.astype(bf16)

        @pl.when(stage == 0)
        def _():
            send(p).start()

    @pl.when(stage == 0)
    def _():
        next_ref[...] = u0_ref[...]
        for p in range(len(parts)):
            send(p).wait_send()

    @pl.when(stage == 1)
    def _():
        for p, (first, last) in enumerate(parts):
            send(p).wait_recv()
            next_ref[first:last] = arrived[first:last]


def mlp_send(w, u0, mixed):
    rows, width = u0.shape
    ff = w["gate"].shape[1]
    cuts = SEND_ROWS if SEND_ROWS[-1] == rows else (0, rows)
    here, there = pl.BlockSpec(memory_space=pltpu.VMEM), pl.BlockSpec(memory_space=pl.ANY)
    count, parts = len(ff_blocks(ff)), len(cuts) - 1
    vmem = lambda *shape: pltpu.VMEM(shape, bf16)
    dma = lambda *n: pltpu.SemaphoreType.DMA(n)
    return pl.pallas_call(
        functools.partial(mlp_send_kernel, cuts),
        in_specs=[here] + [there] * 4 + [here] * 2,
        out_specs=here,
        out_shape=jax.ShapeDtypeStruct((rows, width), bf16),
        scratch_shapes=[vmem(width, width), vmem(width, ff), vmem(width, ff), vmem(ff, width), dma(count, 3), pltpu.SemaphoreType.DMA]
        + [vmem(rows, width), vmem(rows, width), dma(parts), dma(parts)],
        compiler_params=pltpu.CompilerParams(collective_id=3, has_side_effects=True, vmem_limit_bytes=VMEM),
        name="feed_forward_send",
    )(w["mlp_gain"], w["out"], w["gate"], w["up"], w["down"], u0, mixed)


PIECE = (64, 256)
SLOTS = 4
LAGS = (1, 5, 9, 13, 14)
HELD = 24
PAIR = 2


def sum_kernel(total, n2_ref, n1_ref, m_ref, h_ref, dy, u1_ref, mlp_gain, beta_ref, rate_ref, conv_ref, head_ref, attn_ref, w_beta, u_ref, normed_ref,
               gate_hbm, up_hbm, w_gate_hbm, w_up_hbm, w_down_hbm, w_out_hbm, q_hbm, k_hbm, v_hbm, o_hbm, t_hbm, n_hbm, s_hbm, w_hbm, u1, u2,
               gu_out, down_out, out_out, qkv_out, small_out, u_out, g_out,
               gate_blk, up_blk, w_gate, w_up, w_down, w_out, feed_sem, out_sem, dgu, g1, dm, d_mlp,
               q_blk, k_blk, v_blk, o_blk, t_blk, n_blk, s_blk, w_blk, load_sem, dqkv, dtaps, dhead, g0, dattn, dw_beta, dbeta, dnormed, small,
               fin, keep_sem, give_sem, take_sem, fin_sem, far_sem, own, send, rc, rx, ry, rz, send_sem, xs_sem, ys_sem, zs_sem, rc_sem, rx_sem, ry_sem, rz_sem):
    section, me = lax.axis_index("section"), lax.axis_index("dp")
    core, x, low, high = lax.rem(section, 2), lax.rem(me, 2), lax.rem(me // 2, 2), me // 4
    far_core = {"section": section + 1 - 2 * core}
    far_x, far_low, far_high = {"dp": me + 1 - 2 * x}, {"dp": me + 2 - 4 * low}, {"dp": me + 4 - 8 * high}
    barrier = pltpu.get_barrier_semaphore()
    for other in (far_core, far_x, far_low, far_high):
        pl.semaphore_signal(barrier, inc=1, device_id=other, device_id_type=MESH)
    pl.semaphore_wait(barrier, 4)

    def remote(src, dst, sent, got, other):
        return pltpu.make_async_remote_copy(src_ref=src, dst_ref=dst, send_sem=sent, recv_sem=got, device_id=other, device_id_type=MESH)

    def micro(which, mixer_side, mlp_side, into):
        return (
            pltpu.make_async_copy(mixer_side if which == 0 else mlp_side, into.at[core], keep_sem.at[0 if into is u_out else 1]),
            remote(mlp_side if which == 0 else mixer_side, into.at[core], give_sem.at[0 if into is u_out else 1], take_sem.at[0 if into is u_out else 1], far_core),
        )

    def each_core(act):
        for which in range(2):
            @pl.when(core == which)
            def _():
                act(which)

    def start_micro(*sides):
        def act(which):
            for copy in micro(which, *sides):
                copy.start()
        each_core(act)

    start_micro(u1, u2, u_out)

    ff = gu_out.shape[1] // 2
    feeds = ff // PIECE[1]

    def feed_loads(b):
        at = lax.rem(b, 2)
        cols = pl.ds(pl.multiple_of(b * PIECE[1], PIECE[1]), PIECE[1])
        pairs = [(src.at[:, cols], dst.at[at]) for src, dst in ((gate_hbm, gate_blk), (up_hbm, up_blk), (w_gate_hbm, w_gate), (w_up_hbm, w_up))]
        pairs.append((w_down_hbm.at[cols], w_down.at[at]))
        return [pltpu.make_async_copy(src, dst, feed_sem.at[at, i]) for i, (src, dst) in enumerate(pairs)]

    for copy in feed_loads(0):
        copy.start()
    w_out_copy = pltpu.make_async_copy(w_out_hbm, w_out, out_sem)

    def feed_step(b):
        at = lax.rem(b, 2)
        for copy in feed_loads(b):
            copy.wait()

        @pl.when(b + 1 < feeds)
        def _():
            for copy in feed_loads(b + 1):
                copy.start()

        @pl.when(b == 0)
        def _():
            dnormed[...] = jnp.zeros_like(dnormed)
            w_out_copy.start()

        gate, up = gate_blk[at], up_blk[at]
        sig = jax.nn.sigmoid(gate)
        silu = gate * sig
        dhidden = nt(dy[...], w_down[at])
        dgate = (dhidden * up * (sig + silu * (1.0 - sig))).astype(bf16)
        dup = (dhidden * silu).astype(bf16)
        dgu[0], dgu[1] = dgate, dup
        dnormed[...] += nt(jnp.concatenate([dgate, dup], 1), jnp.concatenate([w_gate[at], w_up[at]], 1))

    def feed_end():
        w_out_copy.wait()
        g1[...] = norm_back(u1_ref[...], mlp_gain[...], dnormed[...], dy[...], d_mlp)
        dm[...] = nt(g1[...], w_out[...])

    def loads(s):
        cols = pl.ds(pl.multiple_of(s * PAIR * 128, PAIR * 128), PAIR * 128)
        pairs = [(src.at[:, cols], dst) for src, dst in ((q_hbm, q_blk), (k_hbm, k_blk), (v_hbm, v_blk), (o_hbm, o_blk))]
        pairs += [(src.at[pl.ds(s * PAIR, PAIR)], dst) for src, dst in ((t_hbm, t_blk), (n_hbm, n_blk), (s_hbm, s_blk))]
        pairs.append((w_hbm.at[:, :, cols], w_blk))
        return [pltpu.make_async_copy(src, dst, load_sem.at[i]) for i, (src, dst) in enumerate(pairs)]

    for copy in loads(0):
        copy.start()

    def mixer_step(s):
        for copy in loads(s):
            copy.wait()
        width = dattn.shape[1]
        cols = lambda p: pl.ds(pl.multiple_of(p * width + s * PAIR * 128, PAIR * 128), PAIR * 128)
        taps = [conv_ref.at[p, :, cols(0)] for p in range(3)]
        grads = [dqkv.at[:, cols(p)] for p in range(3)]
        dt = [dtaps.at[p, :, cols(0)] for p in range(3)]
        mixer_back_step(PAIR, s, q_blk, k_blk, v_blk, beta_ref, *taps, head_ref, t_blk, n_blk, s_blk, o_blk, dm.at[:, cols(0)], w_blk, *grads, *dt, dhead, dbeta, dnormed)

        @pl.when(s + 1 < width // (PAIR * 128))
        def _():
            for copy in loads(s + 1):
                copy.start()

    def mixer_end():
        mixer_back_end(beta_ref, rate_ref, u_ref, normed_ref, attn_ref, w_beta, g1, dbeta, dnormed, g0, dattn, dw_beta)
        start_micro(g0, g1, g_out)
        zeros = lambda n: jnp.zeros((n, PIECE[1]), f32)
        for d in range(8):
            lane = slice(d * 128, (d + 1) * 128)
            wide = lambda a: jnp.concatenate([a, jnp.zeros_like(a)], 1)
            rows = [wide(dattn[:, lane]), zeros(7)]
            for p in range(3):
                rows += [wide(dtaps[p, :, lane])]
            rows += [zeros(4), wide(dhead[...]), zeros(7), wide(dw_beta[:, lane]), zeros(PIECE[0] - 40)]
            small[0, d // 4, d // 2 % 2, d % 2] = jnp.concatenate(rows, 0).astype(bf16)
            small[1, d // 4, d // 2 % 2, d % 2] = jnp.concatenate([wide(d_mlp[:, lane]), zeros(PIECE[0] - 1)], 0).astype(bf16)

    def held(t):
        return lax.rem(t, HELD)

    def slot(t):
        return lax.rem(t, SLOTS)

    def core_copy(t):
        return remote(send.at[slot(t)], rc.at[held(t)], send_sem.at[slot(t)], rc_sem.at[t], far_core)

    def turned(t):
        return lax.rem(t, 4) // 3

    def first_copy(t, z_first):
        src = rc.at[held(t), :, 1 - low] if z_first else rc.at[held(t), :, :, 1 - x]
        return remote(src, rx.at[held(t)], xs_sem.at[slot(t)], rx_sem.at[t], far_low if z_first else far_x)

    def second_copy(t):
        way = turned(t)
        other = {"dp": me + way * (1 - 2 * x) + (1 - way) * (2 - 4 * low)}
        mine = way * x + (1 - way) * low
        return remote(rx.at[held(t), :, 1 - mine], ry.at[held(t)], ys_sem.at[slot(t)], ry_sem.at[t], other)

    def high_copy(t):
        return remote(ry.at[held(t), 1 - high], rz.at[held(t)], zs_sem.at[slot(t)], rz_sem.at[t], far_high)

    def free(copy, t):
        @pl.when(t >= SLOTS)
        def _():
            copy(t - SLOTS).wait_send()

    def either(t, act):
        for z_first in (False, True):
            @pl.when(turned(t) == int(z_first))
            def _():
                act(z_first)

    def after_core(t):
        core_copy(t).wait_recv()
        rc[held(t)] = rc[held(t)] + own[slot(t)]
        free(lambda u: first_copy(u, False), t)
        either(t, lambda z_first: first_copy(t, z_first).start())

    def after_first(t):
        first_copy(t, False).wait_recv()

        def add(z_first):
            rx[held(t)] = rx[held(t)] + (rc[held(t), :, low] if z_first else rc[held(t), :, :, x])

        either(t, add)
        free(second_copy, t)
        second_copy(t).start()

    def after_second(t):
        second_copy(t).wait_recv()
        way = turned(t)
        ry[held(t)] = ry[held(t)] + rx[held(t), :, way * x + (1 - way) * low]
        free(high_copy, t)
        high_copy(t).start()

    def cols_of(i):
        return pl.ds(pl.multiple_of(i * PIECE[1], PIECE[1]), PIECE[1])

    def rows_of(into, i):
        return into.at[pl.ds(pl.multiple_of(core * PIECE[0], PIECE[0]), PIECE[0]), cols_of(i)]

    def gate_up_at(i):
        return rows_of(gu_out, lax.rem(i, 2) * feeds + i // 2)

    def down_at(i):
        return down_out.at[core * (down_out.shape[0] // 2) + i]

    def qkv_at(i):
        per = qkv_out.shape[2] // PIECE[1]
        return rows_of(qkv_out.at[i // per], lax.rem(i, per))

    def piece_here(t, where):
        return pltpu.make_async_copy(fin.at[slot(t)], where, fin_sem.at[slot(t)])

    def piece_there(t, where):
        return remote(fin.at[slot(t)], where, fin_sem.at[slot(t)], far_sem.at[t], far_core)

    def fin_wait(t):
        pltpu.make_async_copy(fin.at[slot(t)], fin.at[slot(t)], fin_sem.at[slot(t)]).wait()

    def after_high(t):
        high_copy(t).wait_recv()
        value = rz[held(t)].astype(f32) + ry[held(t), high].astype(f32)

        @pl.when(t == total - 1)
        def _():
            small_out[...] = value

        @pl.when(t < total - 1)
        def _():
            @pl.when(t >= SLOTS)
            def _():
                fin_wait(t)

            fin[slot(t)] = value
            for target, inside, index, where in segments:
                @pl.when(inside(t) & (core == target))
                def _():
                    piece_here(t, where(index(t))).start()

                @pl.when(inside(t) & (core != target))
                def _():
                    piece_there(t, where(index(t))).start()

    def after_far(t):
        for target, inside, index, where in segments:
            @pl.when(inside(t) & (core == target))
            def _():
                piece_there(t, where(index(t))).wait_recv()

    def later(t):
        for step, lag in zip((after_core, after_first, after_second, after_high, after_far), LAGS):
            @pl.when((t >= lag) & (t < total + lag))
            def _():
                step(t - lag)

    def columns(t, lhs, block):
        for which, into in ((1 - core, send), (core, own)):
            into[slot(t)] = nn(lhs[which], block).astype(bf16).reshape(own.shape[1:])

    def fill_gate_up(t):
        columns(t, n2_ref, dgu[lax.rem(t, 2)])

    def fill_out(t):
        columns(t, m_ref, g1[:, cols_of(out_index(t))])

    def fill_qkv(t):
        columns(t, n1_ref, dqkv[:, cols_of(t - qkv_base)])

    def fill_down(t):
        for which, into in ((1 - core, send), (core, own)):
            part = nn(h_ref[down_index(t), which], dy[...]).astype(bf16)
            count = part.shape[0] // 8
            for d in range(8):
                for c in range(PIECE[0] // count):
                    into[slot(t), d // 4, d // 2 % 2, d % 2, c * count : (c + 1) * count, :] = part[d * count : (d + 1) * count, c * PIECE[1] : (c + 1) * PIECE[1]]

    def given(t):
        send[slot(t)] = small[1 - core]
        own[slot(t)] = small[core]

    turns, downs = out_out.shape[1] // PIECE[1], h_ref.shape[0]
    turn_base = 2 * feeds
    rest_base = turn_base + 3 * turns
    qkv_base = turn_base + downs + turns
    in_turns = lambda t: (t >= turn_base) & (t < rest_base)
    of_turn = lambda t: lax.rem(jnp.maximum(t - turn_base, 0), 3)
    out_index = lambda t: jnp.maximum(t - turn_base, 0) // 3
    down_index = lambda t: jnp.where(t < rest_base, 2 * out_index(t) + of_turn(t), t - turn_base - turns)
    segments = (
        (1, lambda t: t < turn_base, lambda t: t, gate_up_at),
        (1, lambda t: (in_turns(t) & (of_turn(t) < 2)) | ((t >= rest_base) & (t < qkv_base)), down_index, down_at),
        (0, lambda t: in_turns(t) & (of_turn(t) == 2), out_index, lambda i: rows_of(out_out, i)),
        (0, lambda t: (t >= qkv_base) & (t < total - 1), lambda t: t - qkv_base, qkv_at),
    )

    def block(t, fill):
        @pl.when(t >= SLOTS)
        def _():
            core_copy(t - SLOTS).wait_send()

        fill(t)
        core_copy(t).start()
        later(t)

    def run(begin, count, fill):
        def body(i, carry):
            block(begin + i, fill)
            return carry

        lax.fori_loop(0, count, body, 0)

    def feed_turn(b, carry):
        feed_step(b)
        run(2 * b, 2, fill_gate_up)
        return carry

    def mixer_turn(s, carry):
        begin = turn_base + 3 * s
        run(begin, 2, fill_down)
        block(begin + 2, fill_out)
        mixer_step(s)
        return carry

    lax.fori_loop(0, feeds, feed_turn, 0)
    feed_end()
    lax.fori_loop(0, turns, mixer_turn, 0)
    mixer_end()
    run(rest_base, qkv_base - rest_base, fill_down)
    run(qkv_base, total - 1 - qkv_base, fill_qkv)
    run(total - 1, 1, given)

    def drain(t, carry):
        later(t)
        return carry

    lax.fori_loop(total, total + LAGS[-1], drain, 0)
    for copy in (core_copy, lambda t: first_copy(t, False), second_copy, high_copy):
        for t in range(total - SLOTS, total):
            copy(jnp.int32(t)).wait_send()
    for t in range(SLOTS):
        fin_wait(jnp.int32(t))

    def end_micro(which):
        for keep, give in (micro(which, u1, u2, u_out), micro(which, g0, g1, g_out)):
            keep.wait()
            give.wait_send()
            give.wait_recv()

    each_core(end_micro)


def summed_gradients(n2, n1, m, h, dy, gate, up, kept, w, u1, u2):
    u0, normed, rate, beta, q, k, v, t, n, s, o = kept
    rows, width = u0.shape
    ff = gate.shape[1]
    total = (2 * ff + 4 * width) // PIECE[1] + h.shape[0] + 1
    wide, heads = PAIR * 128, beta.shape[1]
    buffer = lambda *lead: pltpu.VMEM(lead + PIECE, bf16)
    dma = lambda *n: pltpu.SemaphoreType.DMA(n)
    vmem, anywhere = pl.BlockSpec(memory_space=pltpu.VMEM), pl.BlockSpec(memory_space=pl.ANY)
    near = (n2, n1, m, h, dy, u1, w["mlp_gain"], beta, rate, w["conv"], w["head_gain"], w["attn_gain"], w["beta"], u0, normed)
    far = (gate, up, w["gate"], w["up"], w["down"], w["out"], q, k, v, o, t, n, s, w["qkv"], u1, u2)
    result = lambda *shape: jax.ShapeDtypeStruct(shape, f32)
    pair = jax.ShapeDtypeStruct((2,) + u1.shape, bf16)
    out_rows = 2 * PIECE[0]
    return pl.pallas_call(
        functools.partial(sum_kernel, total),
        out_shape=[result(out_rows, 2 * ff), result(2 * h.shape[0], *PIECE), result(out_rows, width), result(3, out_rows, width), result(*PIECE), pair, pair],
        in_specs=[vmem] * len(near) + [anywhere] * len(far),
        out_specs=[anywhere] * 4 + [vmem] + [anywhere] * 2,
        scratch_shapes=[pltpu.VMEM((2, rows, PIECE[1]), f32)] * 2
        + [pltpu.VMEM((2, width, PIECE[1]), bf16)] * 2
        + [pltpu.VMEM((2, PIECE[1], width), bf16), pltpu.VMEM((width, width), bf16), dma(2, 5), pltpu.SemaphoreType.DMA]
        + [pltpu.VMEM((2, rows, PIECE[1]), bf16), pltpu.VMEM((rows, width), bf16), pltpu.VMEM((rows, width), f32), pltpu.VMEM((1, width), f32)]
        + [pltpu.VMEM((rows, wide), f32)] * 4
        + [pltpu.VMEM((PAIR, rows, 128), bf16)] * 3
        + [pltpu.VMEM((3, width, wide), bf16), dma(8)]
        + [pltpu.VMEM((rows, 3 * width), bf16), pltpu.VMEM((3, 4, width), f32), pltpu.VMEM((1, 128), f32), pltpu.VMEM((rows, width), bf16)]
        + [pltpu.VMEM((1, width), f32), pltpu.VMEM((heads, width), f32), pltpu.VMEM((rows, heads), f32), pltpu.VMEM((rows, width), f32)]
        + [buffer(2, 2, 2, 2)]
        + [pltpu.VMEM((SLOTS,) + PIECE, f32), dma(2), dma(2), dma(2), dma(SLOTS), dma(total)]
        + [buffer(SLOTS, 2, 2, 2), buffer(SLOTS, 2, 2, 2), buffer(HELD, 2, 2, 2), buffer(HELD, 2, 2), buffer(HELD, 2), buffer(HELD)]
        + [dma(SLOTS)] * 4
        + [dma(total)] * 4,
        compiler_params=pltpu.CompilerParams(collective_id=0, has_side_effects=True, vmem_limit_bytes=VMEM),
        name="gradient_sums",
    )(*near, *far)


def matmul(a, b):
    return jnp.dot(a, b, preferred_element_type=f32)


def matmul_tn(a, b):
    return lax.dot_general(a, b, (((0,), (0,)), ((), ())), preferred_element_type=f32)


def pick(x, index, axis):
    return lax.dynamic_index_in_dim(x, index, axis, keepdims=False)


def shards(inputs, cotangent, lengths, attn_gain, qkv_weight, conv_weight, beta_weight, head_gain, out_weight, mlp_gain, gate_up_weight, down_weight):
    section, sections = lax.axis_index("section"), lax.axis_size("section")
    me, group = lax.axis_index("dp"), lax.axis_size("dp")
    core, stage = section % 2, section // 2
    swap = [(i, i ^ 1) for i in range(sections)]
    to_odd = [(i, i + 1) for i in range(0, sections, 2)]
    to_even = [(i + 1, i) for i in range(0, sections, 2)]
    rows = inputs.shape[2]
    width = inputs.shape[3]

    qkv, out_w, down, gate_w, first, seed, token_mask, conv, beta_w, attn, head, mlp, own_up = first_exchange(
        jnp.moveaxis(qkv_weight[0], 1, 0),
        out_weight[0],
        down_weight[0],
        inputs,
        cotangent,
        lengths,
        jnp.moveaxis(conv_weight[0], 1, 0),
        beta_weight[0].T,
        attn_gain,
        head_gain,
        mlp_gain,
        gate_up_weight[0],
    )
    w = {"attn_gain": attn, "conv": conv, "beta": beta_w, "head_gain": head, "qkv": qkv, "out": out_w, "mlp_gain": mlp, "down": down, "gate": gate_w}

    down_stage = [(i + 2, i) for i in range(sections - 2)]

    *passed, w["up"] = mixer_fwd(first, w, token_mask, (own_up,))
    u0 = mlp_send(w, first, passed[6])
    normed1, rate, beta, q, k, v, mixed, *saved = mixer_fwd(u0, w, token_mask)
    kept = (u0, normed1, rate, beta, q, k, v, *saved)
    u1, normed2, gate, up, hidden, g1, dmixed, _ = mlp_call(w, rows, (u0, mixed), seed, keep=True)
    g0 = mixer_bwd(kept, w, dmixed, g1)[7]
    dy = jnp.where(stage == 1, seed, lax.ppermute(g0, "section", down_stage))
    u2 = (u1.astype(f32) + matmul(hidden, w["down"])).astype(bf16)
    ff = hidden.shape[1]
    fused = group == 8 and width == 1024 and ff % 256 == 0
    for_sums = ()
    if fused:
        by_owner = lambda a: a.reshape(rows, group, 2, 64).transpose(2, 1, 3, 0).reshape(2, group * 64, rows)
        down_rows = hidden.reshape(rows, group, 2, ff // 256, 16).transpose(3, 2, 1, 4, 0).reshape(ff // 256, 2, group * 16, rows)
        for_sums = (by_owner(normed2), by_owner(normed1), by_owner(mixed), down_rows)
    dy, u2, for_sums = lax.optimization_barrier((dy, u2, for_sums))

    if fused:
        sums = summed_gradients(*for_sums, dy, gate, up, kept, w, u1, u2)
        gate_up_sum, down_sum, out_sum, qkv_sum, attn_sum, conv_sum, head_sum, beta_sum, mlp_sum, sec_out, sec_grad = last_outputs(*sums, head_gain.shape[1] // group)
        return (
            sec_out[None, :, None],
            sec_grad[None, :, None],
            attn_sum,
            jnp.moveaxis(qkv_sum, 0, 1)[None],
            jnp.moveaxis(conv_sum, 0, 1)[None],
            beta_sum.T[None],
            head_sum,
            out_sum[None],
            mlp_sum,
            gate_up_sum[None],
            down_sum[None],
        )

    def halve(x):
        kept = pick(x, core, 1).astype(f32)
        x = (kept + lax.ppermute(pick(x, 1 - core, 1), "section", swap).astype(f32)).astype(bf16)
        return scatter(x)

    def scatter(x):
        kind = x.dtype
        bit = 1
        while bit < group:
            pairs = [(i, i ^ bit) for i in range(group)]
            mine = (me // bit) % 2
            x = x.reshape((x.shape[0] // 2, 2) + x.shape[1:])
            other = lax.ppermute(pick(x, 1 - mine, 1), "dp", pairs)
            x = pick(x, mine, 1).astype(f32) + other.astype(f32)
            bit *= 2
            if bit < group:
                x = x.astype(kind)
        return x[0]

    def share(grad):
        count, cols = grad.shape
        return halve(grad.astype(bf16).reshape(group, 2, count // group // 2, cols))

    dgate_up, g1, dmixed, d_mlp_gain = mlp_call(w, rows, (u1, gate, up), dy)
    *dproj, dtq, dtk, dtv, dhead, g0, d_attn_gain, dbeta = mixer_bwd(kept, w, dmixed, g1)
    dtaps = jnp.stack([dtq, dtk, dtv], 1)
    dbeta = dbeta.T
    taps_rows = jnp.moveaxis(dtaps.reshape(-1, 3, group, width // group), 2, 0).reshape(group, -1)
    small = [d_attn_gain.reshape(group, -1), taps_rows, dbeta.reshape(group, -1), dhead.reshape(group, -1), d_mlp_gain.reshape(group, -1)]
    sizes = [a.shape[1] for a in small]
    joined = jnp.concatenate(small, 1)
    down_share = share(matmul_tn(hidden, dy))
    gate_share = share(matmul_tn(normed2, dgate_up[:, :ff]))
    up_share = share(matmul_tn(normed2, dgate_up[:, ff:]))
    out_share = share(matmul_tn(mixed, g1))
    qkv_share = [share(matmul_tn(normed1, d)) for d in dproj]
    small = scatter(joined + lax.ppermute(joined, "section", swap))
    def to_core(x, target):
        other = lax.ppermute(x, "section", to_even if target == 0 else to_odd)
        both = jnp.concatenate([x, other] if target == 0 else [other, x], 0)
        return jnp.where(core == target, both, 0.0)

    grad_qkv = jnp.stack([to_core(x, 0) for x in qkv_share], 1)
    grad_out = to_core(out_share, 0)
    grad_gate_up = jnp.stack([to_core(gate_share, 1), to_core(up_share, 1)], 1)
    grad_down = to_core(down_share, 1)

    def both_micro(mixer_side, mlp_side):
        own = jnp.where(core == 0, mixer_side, mlp_side)
        other = lax.ppermute(jnp.where(core == 0, mlp_side, mixer_side), "section", swap)
        return jnp.where(core == 0, jnp.stack([own, other]), jnp.stack([other, own]))[None, :, None]

    on_even = lambda x: jnp.where(core == 0, x, 0.0)
    on_odd = lambda x: jnp.where(core == 1, x, 0.0)
    sec_out, sec_grad = both_micro(u1, u2), both_micro(g0, g1)
    offsets = [sum(sizes[:i]) for i in range(len(sizes) + 1)]
    s_attn, s_taps, s_beta, s_head, s_mlp = [small[a:b] for a, b in zip(offsets, offsets[1:])]

    return (
        sec_out,
        sec_grad,
        on_even(s_attn)[None],
        grad_qkv[None],
        on_even(s_taps).reshape(1, -1, 3, width // group),
        on_even(s_beta).reshape(1, -1, beta.shape[1]),
        on_even(s_head)[None],
        grad_out[None],
        on_odd(s_mlp)[None],
        grad_gate_up[None],
        grad_down[None],
    )


def solution(mesh):
    in_specs = (
        P(None, "dp", None, None),
        P(None, "dp", None, None),
        P(None, "dp"),
        P("section", None),
        P("section", None, None, None),
        P("section", None, None, None),
        P("section", None, None),
        P("section", None),
        P("section", None, None),
        P("section", None),
        P("section", None, None, None),
        P("section", None, None),
    )
    out_specs = (
        P("section", None, "dp", None, None),
        P("section", None, "dp", None, None),
        P("section", "dp"),
        P("section", "dp", None, None),
        P("section", None, None, "dp"),
        P("section", "dp", None),
        P("section", "dp"),
        P("section", "dp", None),
        P("section", "dp"),
        P("section", "dp", None, None),
        P("section", "dp", None),
    )
    return jax.shard_map(shards, mesh=mesh, in_specs=in_specs, out_specs=out_specs, check_vma=False)
```

```python
import functools

import jax, jax.numpy as jnp
from jax import lax
from jax.experimental import pallas as pl
from jax.experimental.pallas import tpu as pltpu
from jax.sharding import PartitionSpec as P

CHUNK = 128
VMEM = 63 * 1024 * 1024
MESH = pl.DeviceIdType.MESH
bf16, f32 = jnp.bfloat16, jnp.float32


def nn(a, b):
    return lax.dot_general(a.astype(bf16), b.astype(bf16), (((1,), (0,)), ((), ())), preferred_element_type=f32)


def nt(a, b):
    return lax.dot_general(a.astype(bf16), b.astype(bf16), (((1,), (1,)), ((), ())), preferred_element_type=f32)


def tn(a, b):
    return lax.dot_general(a.astype(bf16), b.astype(bf16), (((0,), (0,)), ((), ())), preferred_element_type=f32)


def shifted_rows(x, steps):
    count = x.shape[0]
    rows = lax.broadcasted_iota(jnp.int32, (8, x.shape[1]), 0)
    moved = pltpu.roll(x, steps % count, 0)
    if steps > 0:
        return jnp.concatenate([jnp.where(rows >= steps, moved[:8], 0.0), moved[8:]], 0)
    return jnp.concatenate([moved[:-8], jnp.where(rows < 8 + steps, moved[-8:], 0.0)], 0)


def convolved(x, taps):
    total = x * taps[3:4]
    for back in range(1, 4):
        total = total + shifted_rows(x, back) * taps[3 - back : 4 - back]
    return total


def chunk_masks():
    row = lax.broadcasted_iota(jnp.int32, (CHUNK, CHUNK), 0)
    col = lax.broadcasted_iota(jnp.int32, (CHUNK, CHUNK), 1)
    return row, col


def level_mask(row, col, size):
    shift = size.bit_length() - 1
    same = (row >> (shift + 1)) == (col >> (shift + 1))
    return same & (((row >> shift) & 1) == 1) & (((col >> shift) & 1) == 0)


def triangular_inverse(a_list, row, col):
    mask = level_mask(row, col, 1)
    xs = [jnp.where(mask, -a, 0.0) for a in a_list]
    size = 2
    while size < CHUNK:
        mask = level_mask(row, col, size)
        parts = [jnp.where(mask, a, 0.0) for a in a_list]
        ys = [p + nn(p, x) for p, x in zip(parts, xs)]
        xs = [x - (y + nn(x, y)) for x, y in zip(xs, ys)]
        size *= 2
    return xs


def head_column(block, head):
    lanes = lax.broadcasted_iota(jnp.int32, block.shape, 1)
    return jnp.sum(jnp.where(lanes == head, block, 0.0), axis=1, keepdims=True)


def greet_far_core(section):
    far = {"section": section + 1 - 2 * lax.rem(section, 2)}
    barrier = pltpu.get_barrier_semaphore()
    pl.semaphore_signal(barrier, inc=1, device_id=far, device_id_type=MESH)
    pl.semaphore_wait(barrier, 1)
    return far


def give_weights(step, steps, from_even, from_odd, send_sem, recv_sem):
    section = lax.axis_index("section")
    core = lax.rem(section, 2)
    far = {"section": section + 1 - 2 * core}
    pairs = [(0, *p) for p in from_even] + [(1, *p) for p in from_odd]

    def give(i):
        return pltpu.make_async_remote_copy(
            src_ref=pairs[i][1], dst_ref=pairs[i][2], send_sem=send_sem.at[i], recv_sem=recv_sem.at[i], device_id=far, device_id_type=MESH
        )

    @pl.when(step == 0)
    def _():
        greet_far_core(section)
        for i, (owner, _, _) in enumerate(pairs):
            @pl.when(core == owner)
            def _():
                give(i).start()

    @pl.when(step == steps - 1)
    def _():
        for i, (owner, _, _) in enumerate(pairs):
            @pl.when(core == owner)
            def _():
                give(i).wait_send()

            @pl.when(core != owner)
            def _():
                give(i).wait_recv()


def first_kernel(qkv, out, down, inputs, cotangent, lengths, conv, beta, attn_gain, head_gain, mlp_gain, both, qkv_part, out_part, down_part,
                 qkv_full, out_full, down_full, gate_full, first, seed, mask, conv_full, beta_full, attn_full, head_full, mlp_full, up,
                 gate, mine, theirs, local_sem, send_sem, recv_sem, small_sems, stream_sem, gate_local, gate_send, gate_recv):
    step, steps = pl.program_id(0), pl.num_programs(0)
    section = lax.axis_index("section")
    core = lax.rem(section, 2)
    far = {"section": section + 1 - 2 * core}
    give_weights(step, steps, [(qkv, qkv_full), (out, out_full)], [(down, down_full)], send_sem, recv_sem)
    small = pltpu.make_async_remote_copy(
        src_ref=mine, dst_ref=theirs, send_sem=small_sems.at[0], recv_sem=small_sems.at[1], device_id=far, device_id_type=MESH
    )
    streams = [
        pltpu.make_async_copy(inputs.at[core, 0], first, stream_sem.at[0]),
        pltpu.make_async_copy(cotangent.at[core, 0], seed, stream_sem.at[1]),
    ]

    @pl.when(step == 0)
    def _():
        for copy in streams:
            copy.start()
        mine[...] = jnp.zeros_like(mine)
        for p in range(3):
            mine[8 * p : 8 * p + 4, :] = conv[p].astype(f32)
        mine[4:5, :] = attn_gain[...].astype(f32)
        mine[5:6, : head_gain.shape[1]] = head_gain[...].astype(f32)
        mine[6:7, :] = mlp_gain[...].astype(f32)
        mine[24:32, :] = beta[...].astype(f32)
        small.start()
        length = jnp.where(core == 0, lengths[:, 0:1], lengths[:, 1:2])
        mask[...] = (lax.broadcasted_iota(jnp.int32, mask.shape, 0) < length).astype(f32)

    count, down_count = out_part.shape[0], down_part.shape[0]
    block, down_block = pl.ds(step * count, count), pl.ds(step * down_count, down_count)
    own = [
        (0, pltpu.make_async_copy(qkv_part, qkv_full.at[:, block], local_sem.at[0])),
        (0, pltpu.make_async_copy(out_part, out_full.at[block], local_sem.at[1])),
        (1, pltpu.make_async_copy(down_part, down_full.at[down_block], local_sem.at[2])),
    ]
    for owner, copy in own:
        @pl.when(core == owner)
        def _():
            copy.start()

    now = gate_full.shape[0] // count * 3 // 4

    def gate_here(i):
        return pltpu.make_async_copy(gate.at[lax.rem(i, 2)], gate_full.at[pl.ds(i * count, count)], gate_local.at[i])

    def gate_there(i):
        return pltpu.make_async_remote_copy(
            src_ref=gate.at[lax.rem(i, 2)], dst_ref=gate_full.at[pl.ds(i * count, count)],
            send_sem=gate_send.at[i], recv_sem=gate_recv.at[i], device_id=far, device_id_type=MESH,
        )

    @pl.when((core == 1) & (step >= 2))
    def _():
        gate_here(step - 2).wait()

        @pl.when(step - 2 < now)
        def _():
            gate_there(step - 2).wait_send()

    apart = jnp.swapaxes(both[...], 0, 1)
    gate[lax.rem(step, 2)] = apart[0]
    up[...] = apart[1]

    @pl.when(core == 1)
    def _():
        gate_here(step).start()

        @pl.when(step < now)
        def _():
            gate_there(step).start()

    for owner, copy in own:
        @pl.when(core == owner)
        def _():
            copy.wait()

    @pl.when(step == steps - 1)
    def _():
        small.wait()
        mixer = jnp.where(core == 0, mine[...], theirs[...])
        for p in range(3):
            conv_full[p] = mixer[8 * p : 8 * p + 4]
        attn_full[...] = mixer[4:5]
        head_full[...] = mixer[5:6, : head_full.shape[1]]
        beta_full[...] = mixer[24:32].astype(bf16)
        mlp_full[...] = jnp.where(core == 1, mine[6:7, :], theirs[6:7, :])
        for copy in streams:
            copy.wait()

        @pl.when(core == 1)
        def _():
            for i in (step - 1, step):
                gate_here(i).wait()

        @pl.when(core == 0)
        def _():
            def arrived(i, carry):
                gate_there(i).wait_recv()
                return carry

            lax.fori_loop(0, now, arrived, 0)


def first_exchange(qkv, out, down, inputs, cotangent, lengths, conv, beta, attn_gain, head_gain, mlp_gain, both):
    rows, _, ff = both.shape
    width = out.shape[1]
    length = inputs.shape[2]
    count = 128
    steps = rows // count
    anywhere = pl.BlockSpec(memory_space=pl.ANY)
    whole = lambda *shape: pl.BlockSpec(shape, lambda i: (0,) * len(shape))
    like = lambda a, kind: jax.ShapeDtypeStruct(a.shape, kind)
    shape = lambda kind, *dims: jax.ShapeDtypeStruct(dims, kind)
    smalls = (conv, beta, attn_gain, head_gain, mlp_gain)
    dma = lambda n: pltpu.SemaphoreType.DMA((n,))
    return pl.pallas_call(
        first_kernel,
        grid=(steps,),
        in_specs=[anywhere] * 5
        + [whole(*a.shape) for a in (lengths, *smalls)]
        + [
            pl.BlockSpec((count, 2, ff), lambda i: (i, 0, 0)),
            pl.BlockSpec((3, count, width), lambda i: (0, i, 0)),
            pl.BlockSpec((count, width), lambda i: (i, 0)),
            pl.BlockSpec((ff * count // rows, width), lambda i: (i, 0)),
        ],
        out_specs=[anywhere] * 4 + [whole(length, width)] * 2 + [whole(length, 1)] + [whole(*a.shape) for a in smalls] + [pl.BlockSpec((count, ff), lambda i: (i, 0))],
        out_shape=[like(qkv, bf16), like(out, bf16), like(down, bf16), shape(bf16, rows, ff), shape(bf16, length, width), shape(bf16, length, width), shape(f32, length, 1)]
        + [like(conv, f32), like(beta, bf16), like(attn_gain, f32), like(head_gain, f32), like(mlp_gain, f32), shape(bf16, rows, ff)],
        scratch_shapes=[pltpu.VMEM((2, count, ff), bf16)] + [pltpu.VMEM((32, width), f32)] * 2 + [dma(3)] * 3 + [dma(2)] * 2 + [dma(steps)] * 3,
        compiler_params=pltpu.CompilerParams(collective_id=1, has_side_effects=True, vmem_limit_bytes=VMEM),
        name="first_exchange",
    )(qkv, out, down, inputs, cotangent, lengths, *smalls, both, qkv, out, down)


def last_kernel(gate_up_in, down_in, out_in, qkv_in, small, sec_out_in, sec_grad_in, gate_up, down, out, qkv, attn, conv, head, beta, mlp, sec_out, sec_grad):
    core = lax.rem(lax.axis_index("section"), 2)
    me = lax.axis_index("dp")
    on = lambda which, x: jnp.where(core == which, x, 0.0)
    ff = gate_up.shape[2]
    both = on(1, gate_up_in[...])
    gate_up[...] = jnp.swapaxes(jnp.stack([both[:, :ff], both[:, ff:]], 0), 0, 1)
    count, wide = 16, small.shape[1]
    for j in range(down_in.shape[0]):
        for c in range(down.shape[1] // wide):
            down[j * count : (j + 1) * count, c * wide : (c + 1) * wide] = on(1, down_in[j, c * count : (c + 1) * count, :])
    out[...] = on(0, out_in[...])
    qkv[...] = on(0, qkv_in[...])
    sec_out[...] = sec_out_in[...]
    sec_grad[...] = sec_grad_in[...]
    lanes = attn.shape[1]
    attn[...] = on(0, small[0:1, :lanes])
    mlp[...] = on(1, small[0:1, :lanes])
    for p in range(3):
        conv[p] = on(0, small[8 + 4 * p : 12 + 4 * p, :lanes])
    beta[...] = on(0, small[32:40, :lanes])
    part = head.shape[1]
    turned = small[24:32, :lanes]
    shift = lax.rem(lanes - me * part, lanes)
    head[...] = on(0, pltpu.roll(turned, shift, 1)[0:1, :part])


def last_outputs(gate_up, down, out, qkv, small, sec_out, sec_grad, head_part):
    rows, width = out.shape
    ff = gate_up.shape[1] // 2
    half = rows // 2
    lanes = rows
    whole = lambda *shape: pl.BlockSpec(shape, lambda i: (0,) * len(shape))
    by_rows = lambda *shape: pl.BlockSpec(shape, lambda i: (i,) + (0,) * (len(shape) - 1))
    shape = lambda *dims: jax.ShapeDtypeStruct(dims, f32)
    qkv_spec = pl.BlockSpec((3, half, width), lambda i: (0, i, 0))
    stream = by_rows(1, *sec_out.shape[1:])
    tall = down.shape[0] // 2
    return pl.pallas_call(
        last_kernel,
        grid=(2,),
        in_specs=[by_rows(half, 2 * ff), by_rows(tall, *down.shape[1:]), by_rows(half, width), qkv_spec, whole(*small.shape), stream, stream],
        out_specs=[by_rows(half, 2, ff), by_rows(16 * tall, width), by_rows(half, width), qkv_spec]
        + [whole(1, lanes), whole(3, 4, lanes), whole(1, head_part), whole(8, lanes), whole(1, lanes), stream, stream],
        out_shape=[shape(rows, 2, ff), shape(32 * tall, width), shape(rows, width), shape(3, rows, width)]
        + [shape(1, lanes), shape(3, 4, lanes), shape(1, head_part), shape(8, lanes), shape(1, lanes)]
        + [jax.ShapeDtypeStruct(sec_out.shape, bf16)] * 2,
        compiler_params=pltpu.CompilerParams(vmem_limit_bytes=VMEM),
        name="last_outputs",
    )(gate_up, down, out, qkv, small, sec_out, sec_grad)


def mixer_fwd_kernel(per, trade, u_ref, gain_in, w_ref, w_beta, mask_ref, taps_q, taps_k, taps_v, gain_ref, *refs):
    own, refs = refs[:trade], refs[trade:]
    normed_ref, rate_ref, beta_ref, q_ref, k_ref, v_ref, mixed_ref, t_ref, n_ref, s_ref, o_ref = refs[:11]
    if trade:
        pairs = []
        for src, dst, begin in zip(own, refs[11 : 11 + trade], (0, own[1].shape[0] * 3 // 4)):
            part = src.shape[0] // 8
            pairs += [(src.at[a : a + part], dst.at[a : a + part]) for a in range(begin, src.shape[0], part)]
        give_weights(pl.program_id(0), pl.num_programs(0), [], pairs, *refs[11 + trade :])

    @pl.when(pl.program_id(0) == 0)
    def _():
        x = u_ref[...].astype(f32)
        normed = (x * lax.rsqrt(jnp.mean(x * x, 1, keepdims=True) + 1e-6) * gain_in[...]).astype(bf16)
        normed_ref[...] = normed
        rate = jax.nn.sigmoid(nt(normed, w_beta[...]))
        rate_ref[...] = rate
        beta_ref[...] = rate * mask_ref[...]

    for p, ref in enumerate((q_ref, k_ref, v_ref)):
        ref[...] = nn(normed_ref[...], w_ref[p])
    row, col = chunk_masks()
    strict, causal = row > col, row >= col
    chunks = q_ref.shape[0] // CHUNK
    beta_all = beta_ref[...]
    cut = lambda x: [x[i * CHUNK : (i + 1) * CHUNK] for i in range(chunks)]
    lanes = [slice(j * 128, (j + 1) * 128) for j in range(per)]
    qs, ks, vs, bs = [], [], [], []
    for j, lane in enumerate(lanes):

        def activated(ref, taps):
            c = convolved(ref[:, lane], taps[:, lane])
            return c * jax.nn.sigmoid(c)

        q, k, v = activated(q_ref, taps_q), activated(k_ref, taps_k), activated(v_ref, taps_v)
        q = q * lax.rsqrt(jnp.sum(q * q, 1, keepdims=True) + 1e-6)
        k = k * lax.rsqrt(jnp.sum(k * k, 1, keepdims=True) + 1e-6)
        qs.append(cut(q))
        ks.append(cut(k))
        vs.append(cut(v))
        bs.append(cut(head_column(beta_all, pl.program_id(0) * per + j)))
    each = [(j, i) for j in range(per) for i in range(chunks)]
    a_list = [jnp.where(strict, nt(ks[j][i], ks[j][i]) * bs[j][i], 0.0) for j, i in each]
    ps = {(j, i): jnp.where(causal, nt(qs[j][i], ks[j][i]), 0.0) for j, i in each}
    ts = dict(zip(each, triangular_inverse(a_list, row, col)))
    wu = {}
    for j, i in each:
        both = jnp.concatenate([ks[j][i] * bs[j][i], vs[j][i] * bs[j][i]], 1)
        wu[j, i] = both + nn(ts[j, i], both)
    states = [jnp.zeros((128, 128), f32)] * per
    for i in range(chunks):
        span = pl.ds(i * CHUNK, CHUNK)
        news = [wu[j, i][:, 128:] - nn(wu[j, i][:, :128], states[j]) for j in range(per)]
        outs = [nn(jnp.concatenate([qs[j][i], ps[j, i]], 1), jnp.concatenate([states[j], news[j]], 0)) for j in range(per)]
        for j, lane in enumerate(lanes):
            o = outs[j]
            s_ref[j, span, :] = states[j].astype(bf16)
            n_ref[j, span, :] = news[j].astype(bf16)
            t_ref[j, span, :] = ts[j, i].astype(bf16)
            o_ref[span, lane] = o
            mixed_ref[span, lane] = (o * lax.rsqrt(jnp.mean(o * o, 1, keepdims=True) + 1e-5) * gain_ref[...]).astype(bf16)
        if i + 1 < chunks:
            states = [states[j] + tn(ks[j][i], news[j]) for j in range(per)]


def mixer_fwd(u, w, mask, own=(), per=4):
    rows, width = u.shape
    heads = width // 128
    steps = heads // per
    wide = 128 * per
    part = pl.BlockSpec((rows, wide), lambda h: (0, h))
    tap = lambda p: pl.BlockSpec((None, 4, wide), lambda h, p=p: (p, 0, h))
    whole = lambda *shape: pl.BlockSpec(shape, lambda h: (0,) * len(shape))
    saved = pl.BlockSpec((per, rows, 128), lambda h: (h, 0, 0))
    anywhere = [pl.BlockSpec(memory_space=pl.ANY)] * len(own)
    dma = pltpu.SemaphoreType.DMA((12,))
    shape = lambda kind, *dims: jax.ShapeDtypeStruct(dims, kind)
    return pl.pallas_call(
        functools.partial(mixer_fwd_kernel, per, len(own)),
        grid=(steps,),
        in_specs=[whole(rows, width), whole(1, width), pl.BlockSpec((3, width, wide), lambda h: (0, 0, h)), whole(heads, width), whole(rows, 1)]
        + [tap(0), tap(1), tap(2), whole(1, 128)] + anywhere,
        out_specs=[whole(rows, width), whole(rows, heads), whole(rows, heads), part, part, part, part, saved, saved, saved, part] + anywhere,
        out_shape=[shape(bf16, rows, width), shape(f32, rows, heads), shape(f32, rows, heads)]
        + [shape(f32, rows, width)] * 3
        + [shape(bf16, rows, width)]
        + [shape(bf16, heads, rows, 128)] * 3
        + [shape(f32, rows, width)]
        + [jax.ShapeDtypeStruct(a.shape, a.dtype) for a in own],
        scratch_shapes=[dma, dma] if own else [],
        input_output_aliases={9 + i: 11 + i for i in range(len(own))},
        compiler_params=pltpu.CompilerParams(vmem_limit_bytes=VMEM, **({"collective_id": 2, "has_side_effects": True} if own else {})),
        name="mixer_forward",
    )(u, w["attn_gain"], w["qkv"], w["beta"], mask, w["conv"], w["conv"], w["conv"], w["head_gain"], *own)


def mixer_back_step(per, step, q_ref, k_ref, v_ref, beta_ref, taps_q, taps_k, taps_v, gain_ref, t_ref, n_ref, s_ref, o_ref, dm_ref, w_ref,
                    dq_ref, dk_ref, dv_ref, dtq_ref, dtk_ref, dtv_ref, dgain_ref, dbeta_ref, dnormed, with_taps=True):
    row, col = chunk_masks()
    strict, causal_t = row > col, row <= col
    causal = row >= col
    chunks = q_ref.shape[0] // CHUNK
    beta_all = beta_ref[...]

    @pl.when(step == 0)
    def _():
        dbeta_ref[...] = jnp.zeros_like(dbeta_ref)
        dgain_ref[...] = jnp.zeros_like(dgain_ref)
        dnormed[...] = jnp.zeros_like(dnormed)

    cut = lambda x: [x[i * CHUNK : (i + 1) * CHUNK] for i in range(chunks)]
    heads = range(per)
    lanes = [slice(j * 128, (j + 1) * 128) for j in heads]
    kept, qs, ks, vs, bs, dos = [], [], [], [], [], []
    for j, lane in enumerate(lanes):

        def activated(ref, taps):
            c = convolved(ref[:, lane], taps[:, lane])
            sig = jax.nn.sigmoid(c)
            return c * sig, sig * (1.0 + c * (1.0 - sig))

        q_act, q_slope = activated(q_ref, taps_q)
        k_act, k_slope = activated(k_ref, taps_k)
        v, v_slope = activated(v_ref, taps_v)
        q_scale = lax.rsqrt(jnp.sum(q_act * q_act, 1, keepdims=True) + 1e-6)
        k_scale = lax.rsqrt(jnp.sum(k_act * k_act, 1, keepdims=True) + 1e-6)
        q, k = q_act * q_scale, k_act * k_scale
        o, dm, gain = o_ref[:, lane], dm_ref[:, lane], gain_ref[...]
        o_scale = lax.rsqrt(jnp.mean(o * o, 1, keepdims=True) + 1e-5)
        o_hat = o * o_scale
        dgain_ref[...] += jnp.sum(dm * o_hat, 0, keepdims=True)
        dmg = dm * gain
        do = o_scale * (dmg - o_hat * jnp.mean(dmg * o_hat, 1, keepdims=True))
        kept.append((q, k, q_scale, k_scale, q_slope, k_slope, v_slope))
        qs.append(cut(q))
        ks.append(cut(k))
        vs.append(cut(v))
        bs.append(cut(head_column(beta_all, step * per + j)))
        dos.append(cut(do))
    dstates = [jnp.zeros((128, 128), f32)] * per
    dqs, dks, dvs, dbs = [[[] for _ in heads] for _ in range(4)]
    for i in reversed(range(chunks)):
        span = pl.ds(i * CHUNK, CHUNK)
        qc, kc, vc, bc, doc = [[x[j][i] for j in heads] for x in (qs, ks, vs, bs, dos)]
        n, s, t = [[ref[j, span, :] for j in heads] for ref in (n_ref, s_ref, t_ref)]
        gp = [nt(kc[j], jnp.concatenate([kc[j], qc[j]], 0)) for j in heads]
        p_t = [jnp.where(causal_t, gp[j][:, 128:], 0.0) for j in heads]
        dn = [nn(jnp.concatenate([p_t[j], kc[j]], 1), jnp.concatenate([doc[j], dstates[j]], 0)) for j in heads]
        dr = [dn[j] + tn(t[j], dn[j]) for j in heads]
        de = [dr[j] * bc[j] for j in heads]
        both = [nt(doc[j], jnp.concatenate([n[j], s[j]], 0)) for j in heads]
        e = [vc[j] - nn(kc[j], s[j]) for j in heads]
        da = [jnp.where(strict, -nt(dr[j], n[j]), 0.0) for j in heads]
        dp = [jnp.where(causal, both[j][:, :128], 0.0) for j in heads]
        dg = [da[j] * bc[j] for j in heads]
        for j in heads:
            dqs[j].append(both[j][:, 128:] + nn(dp[j], kc[j]))
            dbs[j].append(jnp.sum(dr[j] * e[j], 1, keepdims=True) + jnp.sum(da[j] * gp[j][:, :128], 1, keepdims=True))
            dks[j].append(
                tn(dp[j], qc[j])
                + nt(jnp.concatenate([n[j], -de[j].astype(bf16)], 1), jnp.concatenate([dstates[j].astype(bf16), s[j]], 1))
                + nn(dg[j], kc[j])
                + tn(dg[j], kc[j])
            )
            dvs[j].append(de[j])
        if i:
            dstates = [dstates[j] + tn(qc[j], doc[j]) - tn(kc[j], de[j]) for j in heads]
    join = lambda xs: jnp.concatenate(xs[::-1], 0)
    lane_ids = lax.broadcasted_iota(jnp.int32, dbeta_ref.shape, 1)
    for j, lane in enumerate(lanes):
        q, k, q_scale, k_scale, q_slope, k_slope, v_slope = kept[j]
        dq, dk, dv, db = join(dqs[j]), join(dks[j]), join(dvs[j]), join(dbs[j])
        dq = q_scale * (dq - q * jnp.sum(dq * q, 1, keepdims=True))
        dk = k_scale * (dk - k * jnp.sum(dk * k, 1, keepdims=True))
        dbeta_ref[...] += jnp.where(lane_ids == step * per + j, db, 0.0)
        for grad, slope, ref, taps, out, dtaps in (
            (dq, q_slope, q_ref, taps_q, dq_ref, dtq_ref),
            (dk, k_slope, k_ref, taps_k, dk_ref, dtk_ref),
            (dv, v_slope, v_ref, taps_v, dv_ref, dtv_ref),
        ):
            dc = grad * slope
            x = ref[:, lane]
            w = taps[:, lane]
            dx = dc * w[3:4]
            rows = [None] * 4
            if with_taps:
                rows[3] = jnp.sum(dc * x, 0, keepdims=True)
            for back in range(1, 4):
                moved = shifted_rows(dc, -back)
                dx = dx + moved * w[3 - back : 4 - back]
                if with_taps:
                    rows[3 - back] = jnp.sum(moved * x, 0, keepdims=True)
            out[:, lane] = dx.astype(bf16)
            if with_taps:
                dtaps[:, lane] = jnp.concatenate(rows, 0)

    dnormed[...] += sum(nt(ref[...], w_ref[p]) for p, ref in enumerate((dq_ref, dk_ref, dv_ref)))


def norm_back(u, gain, grad, dy, dgain_ref):
    x = u.astype(f32)
    scale = lax.rsqrt(jnp.mean(x * x, 1, keepdims=True) + 1e-6)
    hat = x * scale
    dgain_ref[...] = jnp.sum(grad * hat, 0, keepdims=True)
    grad = grad * gain
    dx = scale * (grad - hat * jnp.mean(grad * hat, 1, keepdims=True))
    return (dy.astype(f32) + dx).astype(bf16)


def mixer_back_end(beta_ref, rate_ref, u_ref, normed_ref, gain_in, w_beta, dy_ref, dbeta_ref, dnormed, g_ref, dgain_in, dw_beta):
    dlogits = dbeta_ref[...] * beta_ref[...] * (1.0 - rate_ref[...])
    high = dlogits.astype(bf16)
    low = (dlogits - high.astype(f32)).astype(bf16)
    dw_beta[...] = tn(high, normed_ref[...]) + tn(low, normed_ref[...])
    g_ref[...] = norm_back(u_ref[...], gain_in[...], dnormed[...] + nn(high, w_beta[...]), dy_ref[...], dgain_in)


def mixer_bwd_kernel(per, with_taps, q_ref, k_ref, v_ref, beta_ref, taps_q, taps_k, taps_v, gain_ref, t_ref, n_ref, s_ref, o_ref, dm_ref,
                     u_ref, normed_ref, rate_ref, gain_in, w_ref, w_beta, dy_ref,
                     dq_ref, dk_ref, dv_ref, dtq_ref, dtk_ref, dtv_ref, dgain_ref, g_ref, dgain_in, dw_beta, dbeta_ref, dnormed):
    step = pl.program_id(0)
    mixer_back_step(per, step, q_ref, k_ref, v_ref, beta_ref, taps_q, taps_k, taps_v, gain_ref, t_ref, n_ref, s_ref, o_ref, dm_ref, w_ref,
                    dq_ref, dk_ref, dv_ref, dtq_ref, dtk_ref, dtv_ref, dgain_ref, dbeta_ref, dnormed, with_taps)

    if not with_taps:
        for ref in (dtq_ref, dtk_ref, dtv_ref):
            ref[...] = jnp.zeros_like(ref)

    @pl.when(step == pl.num_programs(0) - 1)
    def _():
        mixer_back_end(beta_ref, rate_ref, u_ref, normed_ref, gain_in, w_beta, dy_ref, dbeta_ref, dnormed, g_ref, dgain_in, dw_beta)


def mixer_bwd(kept, w, dmixed, dy, with_taps=True, per=4):
    u, normed, rate, beta, q, k, v, t, n, s, o = kept
    rows, width = u.shape
    heads = width // 128
    steps = heads // per
    wide = 128 * per
    part = pl.BlockSpec((rows, wide), lambda h: (0, h))
    tap = lambda p: pl.BlockSpec((None, 4, wide), lambda h, p=p: (p, 0, h))
    taps_out = pl.BlockSpec((4, wide), lambda h: (0, h))
    whole = lambda *shape: pl.BlockSpec(shape, lambda h: (0,) * len(shape))
    saved = pl.BlockSpec((per, rows, 128), lambda h: (h, 0, 0))
    shape = lambda kind, *dims: jax.ShapeDtypeStruct(dims, kind)
    stream = whole(rows, width)
    return pl.pallas_call(
        functools.partial(mixer_bwd_kernel, per, with_taps),
        grid=(steps,),
        in_specs=[part, part, part, whole(rows, heads), tap(0), tap(1), tap(2), whole(1, 128), saved, saved, saved, part, part]
        + [stream, stream, whole(rows, heads), whole(1, width), pl.BlockSpec((3, width, wide), lambda h: (0, 0, h)), whole(heads, width), stream],
        out_specs=[part] * 3 + [taps_out] * 3 + [whole(1, 128), stream, whole(1, width), whole(heads, width)],
        out_shape=[shape(bf16, rows, width)] * 3 + [shape(f32, 4, width)] * 3
        + [shape(f32, 1, 128), shape(bf16, rows, width), shape(f32, 1, width), shape(f32, heads, width)],
        scratch_shapes=[pltpu.VMEM((rows, heads), f32), pltpu.VMEM((rows, width), f32)],
        compiler_params=pltpu.CompilerParams(vmem_limit_bytes=VMEM),
        name="mixer_backward",
    )(q, k, v, beta, w["conv"], w["conv"], w["conv"], w["head_gain"], t, n, s, o, dmixed, u, normed, rate, w["attn_gain"], w["qkv"], w["beta"], dy)


AHEAD = 2


def ff_blocks(ff):
    cuts = [0, 256]
    while cuts[-1] < ff:
        cuts.append(min(ff, cuts[-1] + 512))
    return list(zip(cuts, cuts[1:]))


def mlp_kernel(forward, keep, down, backward, *refs):
    refs = list(refs)
    take = lambda n: [refs.pop(0) for _ in range(n)]
    gain_ref, w_out_hbm, w_gate_hbm, w_up_hbm, w_down_hbm = take(5)
    if forward:
        u0_ref, mixed_ref = take(2)
    else:
        u1_ref, gate_hbm, up_hbm = take(3)
    if backward:
        (dy_ref,) = take(1)
    if forward:
        u1_ref, normed_ref = take(2)
    if keep:
        kept_hbm = take(3)
    if down:
        (u2_ref,) = take(1)
    if backward:
        if not forward:
            (grads_hbm,) = take(1)
        g1_ref, dm_ref, dgain_ref = take(3)
    w_out, w_gate, w_up, w_down, sems, out_sems, out_sem = take(7)
    if keep or not forward:
        gate_all, up_all = take(2)
    if keep:
        (hidden_all,) = take(1)
    if backward and not forward:
        dgate_all, dup_all = take(2)
    blocks = ff_blocks(w_down.shape[0])
    out_copy = pltpu.make_async_copy(w_out_hbm, w_out, out_sem)

    def loads(i):
        a, b = blocks[i]
        pairs = [(w_gate_hbm.at[:, a:b], w_gate.at[:, a:b]), (w_up_hbm.at[:, a:b], w_up.at[:, a:b]), (w_down_hbm.at[a:b], w_down.at[a:b])]
        if not forward:
            pairs += [(gate_hbm.at[:, a:b], gate_all.at[:, a:b]), (up_hbm.at[:, a:b], up_all.at[:, a:b])]
        return [pltpu.make_async_copy(s, d, sems.at[i, n]) for n, (s, d) in enumerate(pairs)]

    def stores(i):
        a, b = blocks[i]
        pairs = []
        if keep:
            pairs = list(zip((gate_all, up_all, hidden_all), kept_hbm))
        pairs = [(s.at[:, a:b], d.at[:, a:b]) for s, d in pairs]
        if backward and not forward:
            ff = blocks[-1][1]
            pairs = [(dgate_all.at[:, a:b], grads_hbm.at[:, a:b]), (dup_all.at[:, a:b], grads_hbm.at[:, ff + a : ff + b])]
        return [pltpu.make_async_copy(s, d, out_sems.at[i, n]) for n, (s, d) in enumerate(pairs)]

    if forward:
        out_copy.start()
    for i in range(AHEAD):
        for copy in loads(i):
            copy.start()
    if forward:
        out_copy.wait()
        u1 = (u0_ref[...].astype(f32) + nn(mixed_ref[...], w_out[...])).astype(bf16)
        u1_ref[...] = u1
        x = u1.astype(f32)
        normed = (x * lax.rsqrt(jnp.mean(x * x, 1, keepdims=True) + 1e-6) * gain_ref[...]).astype(bf16)
        normed_ref[...] = normed
    total = dnormed = None
    for i, (a, b) in enumerate(blocks):
        for copy in loads(i):
            copy.wait()
        if i + AHEAD < len(blocks):
            for copy in loads(i + AHEAD):
                copy.start()
        elif not forward and i + AHEAD == len(blocks):
            out_copy.start()
        if forward:
            gate, up = nn(normed_ref[...], w_gate[:, a:b]), nn(normed_ref[...], w_up[:, a:b])
        else:
            gate, up = gate_all[:, a:b], up_all[:, a:b]
        sig = jax.nn.sigmoid(gate)
        silu = gate * sig
        if forward:
            hidden = (silu * up).astype(bf16)
        if keep:
            gate_all[:, a:b], up_all[:, a:b], hidden_all[:, a:b] = gate, up, hidden
        if down:
            part = nn(hidden, w_down[a:b])
            total = part if total is None else total + part
        if backward:
            dhidden = nt(dy_ref[...], w_down[a:b])
            dgate = (dhidden * up * (sig + silu * (1.0 - sig))).astype(bf16)
            dup = (dhidden * silu).astype(bf16)
            if not forward:
                dgate_all[:, a:b], dup_all[:, a:b] = dgate, dup
            part = nt(jnp.concatenate([dgate, dup], 1), jnp.concatenate([w_gate[:, a:b], w_up[:, a:b]], 1))
            dnormed = part if dnormed is None else dnormed + part
        for copy in stores(i):
            copy.start()
    x = u1_ref[...].astype(f32)
    if down:
        u2_ref[...] = (x + total).astype(bf16)
    if backward:
        if not forward:
            out_copy.wait()
        scale = lax.rsqrt(jnp.mean(x * x, 1, keepdims=True) + 1e-6)
        hat = x * scale
        dgain_ref[...] = jnp.sum(dnormed * hat, 0, keepdims=True)
        grad = dnormed * gain_ref[...]
        dx = scale * (grad - hat * jnp.mean(grad * hat, 1, keepdims=True))
        g1 = (dy_ref[...].astype(f32) + dx).astype(bf16)
        g1_ref[...] = g1
        dm_ref[...] = nt(g1, w_out[...])
    for i in range(len(blocks)):
        for copy in stores(i):
            copy.wait()


def mlp_call(w, rows, forward=None, backward=None, keep=False, down=False):
    width, ff = w["gate"].shape
    going = len(forward) == 2
    here, there = pl.BlockSpec(memory_space=pltpu.VMEM), pl.BlockSpec(memory_space=pl.ANY)
    shape = lambda kind, n=width: jax.ShapeDtypeStruct((rows, n), kind)
    ins = [here] + [there] * 4
    ins += [here, here] if going else [here, there, there]
    args = [w["mlp_gain"], w["out"], w["gate"], w["up"], w["down"], *forward]
    outs, shapes = [], []
    count = len(ff_blocks(ff))
    scratch = [pltpu.VMEM((width, width), bf16), pltpu.VMEM((width, ff), bf16), pltpu.VMEM((width, ff), bf16), pltpu.VMEM((ff, width), bf16)]
    scratch += [pltpu.SemaphoreType.DMA((count, 5)), pltpu.SemaphoreType.DMA((count, 3)), pltpu.SemaphoreType.DMA]
    if backward is not None:
        ins.append(here)
        args.append(backward)
    if going:
        outs += [here, here]
        shapes += [shape(bf16), shape(bf16)]
    if keep or not going:
        scratch += [pltpu.VMEM((rows, ff), f32)] * 2
    if keep:
        outs += [there] * 3
        shapes += [shape(f32, ff), shape(f32, ff), shape(bf16, ff)]
        scratch.append(pltpu.VMEM((rows, ff), bf16))
    if down:
        outs.append(here)
        shapes.append(shape(bf16))
    if backward is not None:
        if not going:
            outs.append(there)
            shapes.append(shape(bf16, 2 * ff))
            scratch += [pltpu.VMEM((rows, ff), bf16)] * 2
        outs += [here, here, here]
        shapes += [shape(bf16), shape(f32), jax.ShapeDtypeStruct((1, width), f32)]
    return pl.pallas_call(
        functools.partial(mlp_kernel, going, keep, down, backward is not None),
        in_specs=ins,
        out_specs=outs,
        out_shape=shapes,
        scratch_shapes=scratch,
        compiler_params=pltpu.CompilerParams(vmem_limit_bytes=VMEM),
        name="feed_forward" + ("_keep" if keep else "") + ("_back" if backward is not None else ""),
    )(*args)


SEND_ROWS = (0, 128, 320, 512)


def mlp_send_kernel(cuts, gain_ref, w_out_hbm, w_gate_hbm, w_up_hbm, w_down_hbm, u0_ref, mixed_ref, next_ref,
                    w_out, w_gate, w_up, w_down, sems, out_sem, u2, arrived, send_sem, recv_sem):
    section = lax.axis_index("section")
    stage = section // 2
    far = {"section": section + 2 - 4 * stage}
    blocks = ff_blocks(w_down.shape[0])
    out_copy = pltpu.make_async_copy(w_out_hbm, w_out, out_sem)
    parts = list(zip(cuts, cuts[1:]))

    def loads(i):
        a, b = blocks[i]
        pairs = [(w_gate_hbm.at[:, a:b], w_gate.at[:, a:b]), (w_up_hbm.at[:, a:b], w_up.at[:, a:b]), (w_down_hbm.at[a:b], w_down.at[a:b])]
        return [pltpu.make_async_copy(s, d, sems.at[i, n]) for n, (s, d) in enumerate(pairs)]

    def send(p):
        a, b = parts[p]
        return pltpu.make_async_remote_copy(
            src_ref=u2.at[a:b], dst_ref=arrived.at[a:b], send_sem=send_sem.at[p], recv_sem=recv_sem.at[p], device_id=far, device_id_type=MESH
        )

    out_copy.start()
    for i in range(AHEAD):
        for copy in loads(i):
            copy.start()
    barrier = pltpu.get_barrier_semaphore()
    pl.semaphore_signal(barrier, inc=1, device_id=far, device_id_type=MESH)
    pl.semaphore_wait(barrier, 1)
    out_copy.wait()
    for p, (first, last) in enumerate(parts):
        u1 = (u0_ref[first:last].astype(f32) + nn(mixed_ref[first:last], w_out[...])).astype(bf16)
        x = u1.astype(f32)
        normed = (x * lax.rsqrt(jnp.mean(x * x, 1, keepdims=True) + 1e-6) * gain_ref[...]).astype(bf16)
        total = x
        for i, (a, b) in enumerate(blocks):
            if p == 0:
                for copy in loads(i):
                    copy.wait()
                if i + AHEAD < len(blocks):
                    for copy in loads(i + AHEAD):
                        copy.start()
            gate, up = nn(normed, w_gate[:, a:b]), nn(normed, w_up[:, a:b])
            total = total + nn((gate * jax.nn.sigmoid(gate) * up).astype(bf16), w_down[a:b])
        u2[first:last] = total.astype(bf16)

        @pl.when(stage == 0)
        def _():
            send(p).start()

    @pl.when(stage == 0)
    def _():
        next_ref[...] = u0_ref[...]
        for p in range(len(parts)):
            send(p).wait_send()

    @pl.when(stage == 1)
    def _():
        for p, (first, last) in enumerate(parts):
            send(p).wait_recv()
            next_ref[first:last] = arrived[first:last]


def mlp_send(w, u0, mixed):
    rows, width = u0.shape
    ff = w["gate"].shape[1]
    cuts = SEND_ROWS if SEND_ROWS[-1] == rows else (0, rows)
    here, there = pl.BlockSpec(memory_space=pltpu.VMEM), pl.BlockSpec(memory_space=pl.ANY)
    count, parts = len(ff_blocks(ff)), len(cuts) - 1
    vmem = lambda *shape: pltpu.VMEM(shape, bf16)
    dma = lambda *n: pltpu.SemaphoreType.DMA(n)
    return pl.pallas_call(
        functools.partial(mlp_send_kernel, cuts),
        in_specs=[here] + [there] * 4 + [here] * 2,
        out_specs=here,
        out_shape=jax.ShapeDtypeStruct((rows, width), bf16),
        scratch_shapes=[vmem(width, width), vmem(width, ff), vmem(width, ff), vmem(ff, width), dma(count, 3), pltpu.SemaphoreType.DMA]
        + [vmem(rows, width), vmem(rows, width), dma(parts), dma(parts)],
        compiler_params=pltpu.CompilerParams(collective_id=3, has_side_effects=True, vmem_limit_bytes=VMEM),
        name="feed_forward_send",
    )(w["mlp_gain"], w["out"], w["gate"], w["up"], w["down"], u0, mixed)


PIECE = (64, 256)
SLOTS = 4
LAGS = (1, 5, 9, 13, 14)
HELD = 24
PAIR = 2


def sum_kernel(total, n2_ref, came, seed, mlp_gain, beta_ref, rate_ref, conv_ref, head_ref, attn_ref, w_beta,
               n1_hbm, m_hbm, h_hbm, u0_hbm, normed_hbm,
               gate_hbm, up_hbm, w_gate_hbm, w_up_hbm, w_down_hbm, w_out_hbm, q_hbm, k_hbm, v_hbm, o_hbm, t_hbm, n_hbm, s_hbm, w_hbm, u1, u2,
               gu_out, down_out, out_out, qkv_out, small_out, u_out, g_out,
               n1_ref, m_ref, h_ref, u_ref, normed_ref, u1_ref, late_sem,
               gate_blk, up_blk, w_gate, w_up, w_down, w_out, feed_sem, out_sem, dy, dgu, g1, dm, d_mlp,
               q_blk, k_blk, v_blk, o_blk, t_blk, n_blk, s_blk, w_blk, load_sem, dqkv, dtaps, dhead, g0, dattn, dw_beta, dbeta, dnormed, small,
               fin, keep_sem, give_sem, take_sem, fin_sem, far_sem, own, send, rc, rx, ry, rz, send_sem, xs_sem, ys_sem, zs_sem, rc_sem, rx_sem, ry_sem, rz_sem):
    section, me = lax.axis_index("section"), lax.axis_index("dp")
    core, x, low, high = lax.rem(section, 2), lax.rem(me, 2), lax.rem(me // 2, 2), me // 4
    far_core = {"section": section + 1 - 2 * core}
    far_x, far_low, far_high = {"dp": me + 1 - 2 * x}, {"dp": me + 2 - 4 * low}, {"dp": me + 4 - 8 * high}
    barrier = pltpu.get_barrier_semaphore()
    for other in (far_core, far_x, far_low, far_high):
        pl.semaphore_signal(barrier, inc=1, device_id=other, device_id_type=MESH)
    pl.semaphore_wait(barrier, 4)

    def remote(src, dst, sent, got, other):
        return pltpu.make_async_remote_copy(src_ref=src, dst_ref=dst, send_sem=sent, recv_sem=got, device_id=other, device_id_type=MESH)

    def micro(which, mixer_side, mlp_side, into):
        return (
            pltpu.make_async_copy(mixer_side if which == 0 else mlp_side, into.at[core], keep_sem.at[0 if into is u_out else 1]),
            remote(mlp_side if which == 0 else mixer_side, into.at[core], give_sem.at[0 if into is u_out else 1], take_sem.at[0 if into is u_out else 1], far_core),
        )

    def each_core(act):
        for which in range(2):
            @pl.when(core == which)
            def _():
                act(which)

    def start_micro(*sides):
        def act(which):
            for copy in micro(which, *sides):
                copy.start()
        each_core(act)

    start_micro(u1, u2, u_out)

    ff = gu_out.shape[1] // 2
    feeds = ff // PIECE[1]

    def feed_loads(b):
        at = lax.rem(b, 2)
        cols = pl.ds(pl.multiple_of(b * PIECE[1], PIECE[1]), PIECE[1])
        pairs = [(src.at[:, cols], dst.at[at]) for src, dst in ((gate_hbm, gate_blk), (up_hbm, up_blk), (w_gate_hbm, w_gate), (w_up_hbm, w_up))]
        pairs.append((w_down_hbm.at[cols], w_down.at[at]))
        return [pltpu.make_async_copy(src, dst, feed_sem.at[at, i]) for i, (src, dst) in enumerate(pairs)]

    for copy in feed_loads(0):
        copy.start()
    w_out_copy = pltpu.make_async_copy(w_out_hbm, w_out, out_sem)
    late = [
        pltpu.make_async_copy(src, dst, late_sem.at[i])
        for i, (src, dst) in enumerate(((u1, u1_ref), (h_hbm, h_ref), (m_hbm, m_ref), (n1_hbm, n1_ref), (u0_hbm, u_ref), (normed_hbm, normed_ref)))
    ]

    dy[...] = jnp.where(section >= 2, seed[...], came[...])

    def feed_step(b):
        at = lax.rem(b, 2)
        for copy in feed_loads(b):
            copy.wait()

        @pl.when(b + 1 < feeds)
        def _():
            for copy in feed_loads(b + 1):
                copy.start()

        @pl.when(b == 0)
        def _():
            dnormed[...] = jnp.zeros_like(dnormed)
            for copy in (w_out_copy, *late):
                copy.start()

        gate, up = gate_blk[at], up_blk[at]
        sig = jax.nn.sigmoid(gate)
        silu = gate * sig
        dhidden = nt(dy[...], w_down[at])
        dgate = (dhidden * up * (sig + silu * (1.0 - sig))).astype(bf16)
        dup = (dhidden * silu).astype(bf16)
        dgu[0], dgu[1] = dgate, dup
        dnormed[...] += nt(jnp.concatenate([dgate, dup], 1), jnp.concatenate([w_gate[at], w_up[at]], 1))

    def feed_end():
        for copy in (w_out_copy, *late):
            copy.wait()
        g1[...] = norm_back(u1_ref[...], mlp_gain[...], dnormed[...], dy[...], d_mlp)
        dm[...] = nt(g1[...], w_out[...])

    def mixer_begin():
        for copy in loads(0):
            copy.start()

    def loads(s):
        cols = pl.ds(pl.multiple_of(s * PAIR * 128, PAIR * 128), PAIR * 128)
        pairs = [(src.at[:, cols], dst) for src, dst in ((q_hbm, q_blk), (k_hbm, k_blk), (v_hbm, v_blk), (o_hbm, o_blk))]
        pairs += [(src.at[pl.ds(s * PAIR, PAIR)], dst) for src, dst in ((t_hbm, t_blk), (n_hbm, n_blk), (s_hbm, s_blk))]
        pairs.append((w_hbm.at[:, :, cols], w_blk))
        return [pltpu.make_async_copy(src, dst, load_sem.at[i]) for i, (src, dst) in enumerate(pairs)]

    def mixer_step(s):
        for copy in loads(s):
            copy.wait()
        width = dattn.shape[1]
        cols = lambda p: pl.ds(pl.multiple_of(p * width + s * PAIR * 128, PAIR * 128), PAIR * 128)
        taps = [conv_ref.at[p, :, cols(0)] for p in range(3)]
        grads = [dqkv.at[:, cols(p)] for p in range(3)]
        dt = [dtaps.at[p, :, cols(0)] for p in range(3)]
        mixer_back_step(PAIR, s, q_blk, k_blk, v_blk, beta_ref, *taps, head_ref, t_blk, n_blk, s_blk, o_blk, dm.at[:, cols(0)], w_blk, *grads, *dt, dhead, dbeta, dnormed)

        @pl.when(s + 1 < width // (PAIR * 128))
        def _():
            for copy in loads(s + 1):
                copy.start()

    def mixer_end():
        mixer_back_end(beta_ref, rate_ref, u_ref, normed_ref, attn_ref, w_beta, g1, dbeta, dnormed, g0, dattn, dw_beta)
        start_micro(g0, g1, g_out)
        zeros = lambda n: jnp.zeros((n, PIECE[1]), f32)
        for d in range(8):
            lane = slice(d * 128, (d + 1) * 128)
            wide = lambda a: jnp.concatenate([a, jnp.zeros_like(a)], 1)
            rows = [wide(dattn[:, lane]), zeros(7)]
            for p in range(3):
                rows += [wide(dtaps[p, :, lane])]
            rows += [zeros(4), wide(dhead[...]), zeros(7), wide(dw_beta[:, lane]), zeros(PIECE[0] - 40)]
            small[0, d // 4, d // 2 % 2, d % 2] = jnp.concatenate(rows, 0).astype(bf16)
            small[1, d // 4, d // 2 % 2, d % 2] = jnp.concatenate([wide(d_mlp[:, lane]), zeros(PIECE[0] - 1)], 0).astype(bf16)

    def held(t):
        return lax.rem(t, HELD)

    def slot(t):
        return lax.rem(t, SLOTS)

    def core_copy(t):
        return remote(send.at[slot(t)], rc.at[held(t)], send_sem.at[slot(t)], rc_sem.at[t], far_core)

    def turned(t):
        return lax.rem(t, 4) // 3

    def first_copy(t, z_first):
        src = rc.at[held(t), :, 1 - low] if z_first else rc.at[held(t), :, :, 1 - x]
        return remote(src, rx.at[held(t)], xs_sem.at[slot(t)], rx_sem.at[t], far_low if z_first else far_x)

    def second_copy(t):
        way = turned(t)
        other = {"dp": me + way * (1 - 2 * x) + (1 - way) * (2 - 4 * low)}
        mine = way * x + (1 - way) * low
        return remote(rx.at[held(t), :, 1 - mine], ry.at[held(t)], ys_sem.at[slot(t)], ry_sem.at[t], other)

    def high_copy(t):
        return remote(ry.at[held(t), 1 - high], rz.at[held(t)], zs_sem.at[slot(t)], rz_sem.at[t], far_high)

    def free(copy, t):
        @pl.when(t >= SLOTS)
        def _():
            copy(t - SLOTS).wait_send()

    def either(t, act):
        for z_first in (False, True):
            @pl.when(turned(t) == int(z_first))
            def _():
                act(z_first)

    def after_core(t):
        core_copy(t).wait_recv()
        rc[held(t)] = rc[held(t)] + own[slot(t)]
        free(lambda u: first_copy(u, False), t)
        either(t, lambda z_first: first_copy(t, z_first).start())

    def after_first(t):
        first_copy(t, False).wait_recv()

        def add(z_first):
            rx[held(t)] = rx[held(t)] + (rc[held(t), :, low] if z_first else rc[held(t), :, :, x])

        either(t, add)
        free(second_copy, t)
        second_copy(t).start()

    def after_second(t):
        second_copy(t).wait_recv()
        way = turned(t)
        ry[held(t)] = ry[held(t)] + rx[held(t), :, way * x + (1 - way) * low]
        free(high_copy, t)
        high_copy(t).start()

    def cols_of(i):
        return pl.ds(pl.multiple_of(i * PIECE[1], PIECE[1]), PIECE[1])

    def rows_of(into, i):
        return into.at[pl.ds(pl.multiple_of(core * PIECE[0], PIECE[0]), PIECE[0]), cols_of(i)]

    def gate_up_at(i):
        return rows_of(gu_out, lax.rem(i, 2) * feeds + i // 2)

    def down_at(i):
        return down_out.at[core * (down_out.shape[0] // 2) + i]

    def qkv_at(i):
        per = qkv_out.shape[2] // PIECE[1]
        return rows_of(qkv_out.at[i // per], lax.rem(i, per))

    def piece_here(t, where):
        return pltpu.make_async_copy(fin.at[slot(t)], where, fin_sem.at[slot(t)])

    def piece_there(t, where):
        return remote(fin.at[slot(t)], where, fin_sem.at[slot(t)], far_sem.at[t], far_core)

    def fin_wait(t):
        pltpu.make_async_copy(fin.at[slot(t)], fin.at[slot(t)], fin_sem.at[slot(t)]).wait()

    def after_high(t):
        high_copy(t).wait_recv()
        value = rz[held(t)].astype(f32) + ry[held(t), high].astype(f32)

        @pl.when(t == total - 1)
        def _():
            small_out[...] = value

        @pl.when(t < total - 1)
        def _():
            @pl.when(t >= SLOTS)
            def _():
                fin_wait(t)

            fin[slot(t)] = value
            for target, inside, index, where in segments:
                @pl.when(inside(t) & (core == target))
                def _():
                    piece_here(t, where(index(t))).start()

                @pl.when(inside(t) & (core != target))
                def _():
                    piece_there(t, where(index(t))).start()

    def after_far(t):
        for target, inside, index, where in segments:
            @pl.when(inside(t) & (core == target))
            def _():
                piece_there(t, where(index(t))).wait_recv()

    def later(t):
        for step, lag in zip((after_core, after_first, after_second, after_high, after_far), LAGS):
            @pl.when((t >= lag) & (t < total + lag))
            def _():
                step(t - lag)

    def columns(t, lhs, block):
        for which, into in ((1 - core, send), (core, own)):
            into[slot(t)] = nn(lhs[which], block).astype(bf16).reshape(own.shape[1:])

    def fill_gate_up(t):
        columns(t, n2_ref, dgu[lax.rem(t, 2)])

    def fill_out(t):
        columns(t, m_ref, g1[:, cols_of(out_index(t))])

    def fill_qkv(t):
        columns(t, n1_ref, dqkv[:, cols_of(t - qkv_base)])

    def fill_down(t):
        for which, into in ((1 - core, send), (core, own)):
            part = nn(h_ref[down_index(t), which], dy[...]).astype(bf16)
            count = part.shape[0] // 8
            for d in range(8):
                for c in range(PIECE[0] // count):
                    into[slot(t), d // 4, d // 2 % 2, d % 2, c * count : (c + 1) * count, :] = part[d * count : (d + 1) * count, c * PIECE[1] : (c + 1) * PIECE[1]]

    def given(t):
        send[slot(t)] = small[1 - core]
        own[slot(t)] = small[core]

    turns, downs = out_out.shape[1] // PIECE[1], h_ref.shape[0]
    turn_base = 2 * feeds
    rest_base = turn_base + 3 * turns
    qkv_base = turn_base + downs + turns
    in_turns = lambda t: (t >= turn_base) & (t < rest_base)
    of_turn = lambda t: lax.rem(jnp.maximum(t - turn_base, 0), 3)
    out_index = lambda t: jnp.maximum(t - turn_base, 0) // 3
    down_index = lambda t: jnp.where(t < rest_base, 2 * out_index(t) + of_turn(t), t - turn_base - turns)
    segments = (
        (1, lambda t: t < turn_base, lambda t: t, gate_up_at),
        (1, lambda t: (in_turns(t) & (of_turn(t) < 2)) | ((t >= rest_base) & (t < qkv_base)), down_index, down_at),
        (0, lambda t: in_turns(t) & (of_turn(t) == 2), out_index, lambda i: rows_of(out_out, i)),
        (0, lambda t: (t >= qkv_base) & (t < total - 1), lambda t: t - qkv_base, qkv_at),
    )

    def block(t, fill):
        @pl.when(t >= SLOTS)
        def _():
            core_copy(t - SLOTS).wait_send()

        fill(t)
        core_copy(t).start()
        later(t)

    def run(begin, count, fill):
        def body(i, carry):
            block(begin + i, fill)
            return carry

        lax.fori_loop(0, count, body, 0)

    def feed_turn(b, carry):
        feed_step(b)
        run(2 * b, 2, fill_gate_up)
        return carry

    def mixer_turn(s, carry):
        begin = turn_base + 3 * s
        run(begin, 2, fill_down)
        block(begin + 2, fill_out)
        mixer_step(s)
        return carry

    mixer_begin()
    lax.fori_loop(0, feeds, feed_turn, 0)
    feed_end()
    lax.fori_loop(0, turns, mixer_turn, 0)
    mixer_end()
    run(rest_base, qkv_base - rest_base, fill_down)
    run(qkv_base, total - 1 - qkv_base, fill_qkv)
    run(total - 1, 1, given)

    def drain(t, carry):
        later(t)
        return carry

    lax.fori_loop(total, total + LAGS[-1], drain, 0)
    for copy in (core_copy, lambda t: first_copy(t, False), second_copy, high_copy):
        for t in range(total - SLOTS, total):
            copy(jnp.int32(t)).wait_send()
    for t in range(SLOTS):
        fin_wait(jnp.int32(t))

    def end_micro(which):
        for keep, give in (micro(which, u1, u2, u_out), micro(which, g0, g1, g_out)):
            keep.wait()
            give.wait_send()
            give.wait_recv()

    each_core(end_micro)


def summed_gradients(n2, n1, m, h, dy, seed, gate, up, kept, w, u1, u2):
    u0, normed, rate, beta, q, k, v, t, n, s, o = kept
    rows, width = u0.shape
    ff = gate.shape[1]
    total = (2 * ff + 4 * width) // PIECE[1] + h.shape[0] + 1
    wide, heads = PAIR * 128, beta.shape[1]
    buffer = lambda *lead: pltpu.VMEM(lead + PIECE, bf16)
    dma = lambda *n: pltpu.SemaphoreType.DMA(n)
    vmem, anywhere = pl.BlockSpec(memory_space=pltpu.VMEM), pl.BlockSpec(memory_space=pl.ANY)
    near = (n2, dy, seed, w["mlp_gain"], beta, rate, w["conv"], w["head_gain"], w["attn_gain"], w["beta"])
    late = (n1, m, h, u0, normed)
    far = (*late, gate, up, w["gate"], w["up"], w["down"], w["out"], q, k, v, o, t, n, s, w["qkv"], u1, u2)
    result = lambda *shape: jax.ShapeDtypeStruct(shape, f32)
    pair = jax.ShapeDtypeStruct((2,) + u1.shape, bf16)
    out_rows = 2 * PIECE[0]
    return pl.pallas_call(
        functools.partial(sum_kernel, total),
        out_shape=[result(out_rows, 2 * ff), result(2 * h.shape[0], *PIECE), result(out_rows, width), result(3, out_rows, width), result(*PIECE), pair, pair],
        in_specs=[vmem] * len(near) + [anywhere] * len(far),
        out_specs=[anywhere] * 4 + [vmem] + [anywhere] * 2,
        scratch_shapes=[pltpu.VMEM(a.shape, a.dtype) for a in (*late, u1)]
        + [dma(6)]
        + [pltpu.VMEM((2, rows, PIECE[1]), f32)] * 2
        + [pltpu.VMEM((2, width, PIECE[1]), bf16)] * 2
        + [pltpu.VMEM((2, PIECE[1], width), bf16), pltpu.VMEM((width, width), bf16), dma(2, 5), pltpu.SemaphoreType.DMA]
        + [pltpu.VMEM((rows, width), bf16), pltpu.VMEM((2, rows, PIECE[1]), bf16), pltpu.VMEM((rows, width), bf16), pltpu.VMEM((rows, width), f32), pltpu.VMEM((1, width), f32)]
        + [pltpu.VMEM((rows, wide), f32)] * 4
        + [pltpu.VMEM((PAIR, rows, 128), bf16)] * 3
        + [pltpu.VMEM((3, width, wide), bf16), dma(8)]
        + [pltpu.VMEM((rows, 3 * width), bf16), pltpu.VMEM((3, 4, width), f32), pltpu.VMEM((1, 128), f32), pltpu.VMEM((rows, width), bf16)]
        + [pltpu.VMEM((1, width), f32), pltpu.VMEM((heads, width), f32), pltpu.VMEM((rows, heads), f32), pltpu.VMEM((rows, width), f32)]
        + [buffer(2, 2, 2, 2)]
        + [pltpu.VMEM((SLOTS,) + PIECE, f32), dma(2), dma(2), dma(2), dma(SLOTS), dma(total)]
        + [buffer(SLOTS, 2, 2, 2), buffer(SLOTS, 2, 2, 2), buffer(HELD, 2, 2, 2), buffer(HELD, 2, 2), buffer(HELD, 2), buffer(HELD)]
        + [dma(SLOTS)] * 4
        + [dma(total)] * 4,
        compiler_params=pltpu.CompilerParams(collective_id=0, has_side_effects=True, vmem_limit_bytes=VMEM),
        name="gradient_sums",
    )(*near, *far)


def matmul(a, b):
    return jnp.dot(a, b, preferred_element_type=f32)


def matmul_tn(a, b):
    return lax.dot_general(a, b, (((0,), (0,)), ((), ())), preferred_element_type=f32)


def pick(x, index, axis):
    return lax.dynamic_index_in_dim(x, index, axis, keepdims=False)


def shards(inputs, cotangent, lengths, attn_gain, qkv_weight, conv_weight, beta_weight, head_gain, out_weight, mlp_gain, gate_up_weight, down_weight):
    section, sections = lax.axis_index("section"), lax.axis_size("section")
    me, group = lax.axis_index("dp"), lax.axis_size("dp")
    core, stage = section % 2, section // 2
    swap = [(i, i ^ 1) for i in range(sections)]
    to_odd = [(i, i + 1) for i in range(0, sections, 2)]
    to_even = [(i + 1, i) for i in range(0, sections, 2)]
    rows = inputs.shape[2]
    width = inputs.shape[3]

    qkv, out_w, down, own_gate, first, seed, token_mask, conv, beta_w, attn, head, mlp, own_up = first_exchange(
        jnp.moveaxis(qkv_weight[0], 1, 0),
        out_weight[0],
        down_weight[0],
        inputs,
        cotangent,
        lengths.T,
        jnp.moveaxis(conv_weight[0], 1, 0),
        beta_weight[0].T,
        attn_gain,
        head_gain,
        mlp_gain,
        gate_up_weight[0],
    )
    w = {"attn_gain": attn, "conv": conv, "beta": beta_w, "head_gain": head, "qkv": qkv, "out": out_w, "mlp_gain": mlp, "down": down}

    down_stage = [(i + 2, i) for i in range(sections - 2)]

    *passed, w["up"], w["gate"] = mixer_fwd(first, w, token_mask, (own_up, own_gate))
    u0 = mlp_send(w, first, passed[6])
    normed1, rate, beta, q, k, v, mixed, *saved = mixer_fwd(u0, w, token_mask)
    kept = (u0, normed1, rate, beta, q, k, v, *saved)
    u1, normed2, gate, up, hidden, g1, dmixed, _ = mlp_call(w, rows, (u0, mixed), seed, keep=True)
    g0 = mixer_bwd(kept, w, dmixed, g1, with_taps=False)[7]
    dy = lax.ppermute(g0, "section", down_stage)
    u2 = (u1.astype(f32) + matmul(hidden, w["down"])).astype(bf16)
    ff = hidden.shape[1]
    fused = group == 8 and width == 1024 and ff % 256 == 0
    for_sums = ()
    if fused:
        by_owner = lambda a: a.reshape(rows, group, 2, 64).transpose(2, 1, 3, 0).reshape(2, group * 64, rows)
        down_rows = hidden.reshape(rows, group, 2, ff // 256, 16).transpose(3, 2, 1, 4, 0).reshape(ff // 256, 2, group * 16, rows)
        for_sums = (by_owner(normed2), by_owner(normed1), by_owner(mixed), down_rows)
    dy, u2, for_sums = lax.optimization_barrier((dy, u2, for_sums))

    if fused:
        sums = summed_gradients(*for_sums, dy, seed, gate, up, kept, w, u1, u2)
        gate_up_sum, down_sum, out_sum, qkv_sum, attn_sum, conv_sum, head_sum, beta_sum, mlp_sum, sec_out, sec_grad = last_outputs(*sums, head_gain.shape[1] // group)
        return (
            sec_out[None, :, None],
            sec_grad[None, :, None],
            attn_sum,
            jnp.moveaxis(qkv_sum, 0, 1)[None],
            jnp.moveaxis(conv_sum, 0, 1)[None],
            beta_sum.T[None],
            head_sum,
            out_sum[None],
            mlp_sum,
            gate_up_sum[None],
            down_sum[None],
        )

    dy = jnp.where(stage == 1, seed, dy)

    def halve(x):
        kept = pick(x, core, 1).astype(f32)
        x = (kept + lax.ppermute(pick(x, 1 - core, 1), "section", swap).astype(f32)).astype(bf16)
        return scatter(x)

    def scatter(x):
        kind = x.dtype
        bit = 1
        while bit < group:
            pairs = [(i, i ^ bit) for i in range(group)]
            mine = (me // bit) % 2
            x = x.reshape((x.shape[0] // 2, 2) + x.shape[1:])
            other = lax.ppermute(pick(x, 1 - mine, 1), "dp", pairs)
            x = pick(x, mine, 1).astype(f32) + other.astype(f32)
            bit *= 2
            if bit < group:
                x = x.astype(kind)
        return x[0]

    def share(grad):
        count, cols = grad.shape
        return halve(grad.astype(bf16).reshape(group, 2, count // group // 2, cols))

    dgate_up, g1, dmixed, d_mlp_gain = mlp_call(w, rows, (u1, gate, up), dy)
    *dproj, dtq, dtk, dtv, dhead, g0, d_attn_gain, dbeta = mixer_bwd(kept, w, dmixed, g1)
    dtaps = jnp.stack([dtq, dtk, dtv], 1)
    dbeta = dbeta.T
    taps_rows = jnp.moveaxis(dtaps.reshape(-1, 3, group, width // group), 2, 0).reshape(group, -1)
    small = [d_attn_gain.reshape(group, -1), taps_rows, dbeta.reshape(group, -1), dhead.reshape(group, -1), d_mlp_gain.reshape(group, -1)]
    sizes = [a.shape[1] for a in small]
    joined = jnp.concatenate(small, 1)
    down_share = share(matmul_tn(hidden, dy))
    gate_share = share(matmul_tn(normed2, dgate_up[:, :ff]))
    up_share = share(matmul_tn(normed2, dgate_up[:, ff:]))
    out_share = share(matmul_tn(mixed, g1))
    qkv_share = [share(matmul_tn(normed1, d)) for d in dproj]
    small = scatter(joined + lax.ppermute(joined, "section", swap))
    def to_core(x, target):
        other = lax.ppermute(x, "section", to_even if target == 0 else to_odd)
        both = jnp.concatenate([x, other] if target == 0 else [other, x], 0)
        return jnp.where(core == target, both, 0.0)

    grad_qkv = jnp.stack([to_core(x, 0) for x in qkv_share], 1)
    grad_out = to_core(out_share, 0)
    grad_gate_up = jnp.stack([to_core(gate_share, 1), to_core(up_share, 1)], 1)
    grad_down = to_core(down_share, 1)

    def both_micro(mixer_side, mlp_side):
        own = jnp.where(core == 0, mixer_side, mlp_side)
        other = lax.ppermute(jnp.where(core == 0, mlp_side, mixer_side), "section", swap)
        return jnp.where(core == 0, jnp.stack([own, other]), jnp.stack([other, own]))[None, :, None]

    on_even = lambda x: jnp.where(core == 0, x, 0.0)
    on_odd = lambda x: jnp.where(core == 1, x, 0.0)
    sec_out, sec_grad = both_micro(u1, u2), both_micro(g0, g1)
    offsets = [sum(sizes[:i]) for i in range(len(sizes) + 1)]
    s_attn, s_taps, s_beta, s_head, s_mlp = [small[a:b] for a, b in zip(offsets, offsets[1:])]

    return (
        sec_out,
        sec_grad,
        on_even(s_attn)[None],
        grad_qkv[None],
        on_even(s_taps).reshape(1, -1, 3, width // group),
        on_even(s_beta).reshape(1, -1, beta.shape[1]),
        on_even(s_head)[None],
        grad_out[None],
        on_odd(s_mlp)[None],
        grad_gate_up[None],
        grad_down[None],
    )


def solution(mesh):
    in_specs = (
        P(None, "dp", None, None),
        P(None, "dp", None, None),
        P(None, "dp"),
        P("section", None),
        P("section", None, None, None),
        P("section", None, None, None),
        P("section", None, None),
        P("section", None),
        P("section", None, None),
        P("section", None),
        P("section", None, None, None),
        P("section", None, None),
    )
    out_specs = (
        P("section", None, "dp", None, None),
        P("section", None, "dp", None, None),
        P("section", "dp"),
        P("section", "dp", None, None),
        P("section", None, None, "dp"),
        P("section", "dp", None),
        P("section", "dp"),
        P("section", "dp", None),
        P("section", "dp"),
        P("section", "dp", None, None),
        P("section", "dp", None),
    )
    return jax.shard_map(shards, mesh=mesh, in_specs=in_specs, out_specs=out_specs, check_vma=False)
```

```python
import functools

import jax, jax.numpy as jnp
from jax import lax
from jax.experimental import pallas as pl
from jax.experimental.pallas import tpu as pltpu
from jax.sharding import PartitionSpec as P

CHUNK = 128
VMEM = 63 * 1024 * 1024
MESH = pl.DeviceIdType.MESH
bf16, f32 = jnp.bfloat16, jnp.float32


def nn(a, b):
    return lax.dot_general(a.astype(bf16), b.astype(bf16), (((1,), (0,)), ((), ())), preferred_element_type=f32)


def nt(a, b):
    return lax.dot_general(a.astype(bf16), b.astype(bf16), (((1,), (1,)), ((), ())), preferred_element_type=f32)


def tn(a, b):
    return lax.dot_general(a.astype(bf16), b.astype(bf16), (((0,), (0,)), ((), ())), preferred_element_type=f32)


def fine(product, a, b):
    a_high, b_high = a.astype(bf16), b.astype(bf16)
    a_rest, b_rest = a - a_high.astype(f32), b - b_high.astype(f32)
    return product(a_high, b_high) + (product(a_rest, b_high) + product(a_high, b_rest))


def shifted_rows(x, steps):
    count = x.shape[0]
    rows = lax.broadcasted_iota(jnp.int32, (8, x.shape[1]), 0)
    moved = pltpu.roll(x, steps % count, 0)
    if steps > 0:
        return jnp.concatenate([jnp.where(rows >= steps, moved[:8], 0.0), moved[8:]], 0)
    return jnp.concatenate([moved[:-8], jnp.where(rows < 8 + steps, moved[-8:], 0.0)], 0)


def convolved(x, taps):
    total = x * taps[3:4]
    for back in range(1, 4):
        total = total + shifted_rows(x, back) * taps[3 - back : 4 - back]
    return total


def chunk_masks():
    row = lax.broadcasted_iota(jnp.int32, (CHUNK, CHUNK), 0)
    col = lax.broadcasted_iota(jnp.int32, (CHUNK, CHUNK), 1)
    return row, col


def level_mask(row, col, size):
    shift = size.bit_length() - 1
    same = (row >> (shift + 1)) == (col >> (shift + 1))
    return same & (((row >> shift) & 1) == 1) & (((col >> shift) & 1) == 0)


def triangular_inverse(a_list, row, col):
    mask = level_mask(row, col, 1)
    xs = [jnp.where(mask, -a, 0.0) for a in a_list]
    size = 2
    while size < CHUNK:
        mask = level_mask(row, col, size)
        parts = [jnp.where(mask, a, 0.0) for a in a_list]
        ys = [p + nn(p, x) for p, x in zip(parts, xs)]
        xs = [x - (y + nn(x, y)) for x, y in zip(xs, ys)]
        size *= 2
    rests = [x + a + fine(nn, a, x) for a, x in zip(a_list, xs)]
    return [x - (r + nn(x, r)) for x, r in zip(xs, rests)]


def head_column(block, head):
    lanes = lax.broadcasted_iota(jnp.int32, block.shape, 1)
    return jnp.sum(jnp.where(lanes == head, block, 0.0), axis=1, keepdims=True)


def greet_far_core(section):
    far = {"section": section + 1 - 2 * lax.rem(section, 2)}
    barrier = pltpu.get_barrier_semaphore()
    pl.semaphore_signal(barrier, inc=1, device_id=far, device_id_type=MESH)
    pl.semaphore_wait(barrier, 1)
    return far


def give_weights(step, steps, from_even, from_odd, send_sem, recv_sem):
    section = lax.axis_index("section")
    core = lax.rem(section, 2)
    far = {"section": section + 1 - 2 * core}
    pairs = [(0, *p) for p in from_even] + [(1, *p) for p in from_odd]

    def give(i):
        return pltpu.make_async_remote_copy(
            src_ref=pairs[i][1], dst_ref=pairs[i][2], send_sem=send_sem.at[i], recv_sem=recv_sem.at[i], device_id=far, device_id_type=MESH
        )

    @pl.when(step == 0)
    def _():
        greet_far_core(section)
        for i, (owner, _, _) in enumerate(pairs):
            @pl.when(core == owner)
            def _():
                give(i).start()

    @pl.when(step == steps - 1)
    def _():
        for i, (owner, _, _) in enumerate(pairs):
            @pl.when(core == owner)
            def _():
                give(i).wait_send()

            @pl.when(core != owner)
            def _():
                give(i).wait_recv()


def first_kernel(qkv, out, down, inputs, cotangent, lengths, conv, beta, attn_gain, head_gain, mlp_gain, both, qkv_part, out_part, down_part,
                 qkv_full, out_full, down_full, gate_full, first, seed, mask, conv_full, beta_full, attn_full, head_full, mlp_full, up,
                 gate, mine, theirs, local_sem, send_sem, recv_sem, small_sems, stream_sem, gate_local, gate_send, gate_recv):
    step, steps = pl.program_id(0), pl.num_programs(0)
    section = lax.axis_index("section")
    core = lax.rem(section, 2)
    far = {"section": section + 1 - 2 * core}
    give_weights(step, steps, [(qkv, qkv_full), (out, out_full)], [(down, down_full)], send_sem, recv_sem)
    small = pltpu.make_async_remote_copy(
        src_ref=mine, dst_ref=theirs, send_sem=small_sems.at[0], recv_sem=small_sems.at[1], device_id=far, device_id_type=MESH
    )
    streams = [
        pltpu.make_async_copy(inputs.at[core, 0], first, stream_sem.at[0]),
        pltpu.make_async_copy(cotangent.at[core, 0], seed, stream_sem.at[1]),
    ]

    @pl.when(step == 0)
    def _():
        for copy in streams:
            copy.start()
        mine[...] = jnp.zeros_like(mine)
        for p in range(3):
            mine[8 * p : 8 * p + 4, :] = conv[p].astype(f32)
        mine[4:5, :] = attn_gain[...].astype(f32)
        mine[5:6, : head_gain.shape[1]] = head_gain[...].astype(f32)
        mine[6:7, :] = mlp_gain[...].astype(f32)
        mine[24:32, :] = beta[...].astype(f32)
        small.start()
        length = jnp.where(core == 0, lengths[:, 0:1], lengths[:, 1:2])
        mask[...] = (lax.broadcasted_iota(jnp.int32, mask.shape, 0) < length).astype(f32)

    count, down_count = out_part.shape[0], down_part.shape[0]
    block, down_block = pl.ds(step * count, count), pl.ds(step * down_count, down_count)
    own = [
        (0, pltpu.make_async_copy(qkv_part, qkv_full.at[:, block], local_sem.at[0])),
        (0, pltpu.make_async_copy(out_part, out_full.at[block], local_sem.at[1])),
        (1, pltpu.make_async_copy(down_part, down_full.at[down_block], local_sem.at[2])),
    ]
    for owner, copy in own:
        @pl.when(core == owner)
        def _():
            copy.start()

    now = gate_full.shape[0] // count * 3 // 4

    def gate_here(i):
        return pltpu.make_async_copy(gate.at[lax.rem(i, 2)], gate_full.at[pl.ds(i * count, count)], gate_local.at[i])

    def gate_there(i):
        return pltpu.make_async_remote_copy(
            src_ref=gate.at[lax.rem(i, 2)], dst_ref=gate_full.at[pl.ds(i * count, count)],
            send_sem=gate_send.at[i], recv_sem=gate_recv.at[i], device_id=far, device_id_type=MESH,
        )

    @pl.when((core == 1) & (step >= 2))
    def _():
        gate_here(step - 2).wait()

        @pl.when(step - 2 < now)
        def _():
            gate_there(step - 2).wait_send()

    apart = jnp.swapaxes(both[...], 0, 1)
    gate[lax.rem(step, 2)] = apart[0]
    up[...] = apart[1]

    @pl.when(core == 1)
    def _():
        gate_here(step).start()

        @pl.when(step < now)
        def _():
            gate_there(step).start()

    for owner, copy in own:
        @pl.when(core == owner)
        def _():
            copy.wait()

    @pl.when(step == steps - 1)
    def _():
        small.wait()
        mixer = jnp.where(core == 0, mine[...], theirs[...])
        for p in range(3):
            conv_full[p] = mixer[8 * p : 8 * p + 4]
        attn_full[...] = mixer[4:5]
        head_full[...] = mixer[5:6, : head_full.shape[1]]
        beta_full[...] = mixer[24:32].astype(bf16)
        mlp_full[...] = jnp.where(core == 1, mine[6:7, :], theirs[6:7, :])
        for copy in streams:
            copy.wait()

        @pl.when(core == 1)
        def _():
            for i in (step - 1, step):
                gate_here(i).wait()

        @pl.when(core == 0)
        def _():
            def arrived(i, carry):
                gate_there(i).wait_recv()
                return carry

            lax.fori_loop(0, now, arrived, 0)


def first_exchange(qkv, out, down, inputs, cotangent, lengths, conv, beta, attn_gain, head_gain, mlp_gain, both):
    rows, _, ff = both.shape
    width = out.shape[1]
    length = inputs.shape[2]
    count = 128
    steps = rows // count
    anywhere = pl.BlockSpec(memory_space=pl.ANY)
    whole = lambda *shape: pl.BlockSpec(shape, lambda i: (0,) * len(shape))
    like = lambda a, kind: jax.ShapeDtypeStruct(a.shape, kind)
    shape = lambda kind, *dims: jax.ShapeDtypeStruct(dims, kind)
    smalls = (conv, beta, attn_gain, head_gain, mlp_gain)
    dma = lambda n: pltpu.SemaphoreType.DMA((n,))
    return pl.pallas_call(
        first_kernel,
        grid=(steps,),
        in_specs=[anywhere] * 5
        + [whole(*a.shape) for a in (lengths, *smalls)]
        + [
            pl.BlockSpec((count, 2, ff), lambda i: (i, 0, 0)),
            pl.BlockSpec((3, count, width), lambda i: (0, i, 0)),
            pl.BlockSpec((count, width), lambda i: (i, 0)),
            pl.BlockSpec((ff * count // rows, width), lambda i: (i, 0)),
        ],
        out_specs=[anywhere] * 4 + [whole(length, width)] * 2 + [whole(length, 1)] + [whole(*a.shape) for a in smalls] + [pl.BlockSpec((count, ff), lambda i: (i, 0))],
        out_shape=[like(qkv, bf16), like(out, bf16), like(down, bf16), shape(bf16, rows, ff), shape(bf16, length, width), shape(bf16, length, width), shape(f32, length, 1)]
        + [like(conv, f32), like(beta, bf16), like(attn_gain, f32), like(head_gain, f32), like(mlp_gain, f32), shape(bf16, rows, ff)],
        scratch_shapes=[pltpu.VMEM((2, count, ff), bf16)] + [pltpu.VMEM((32, width), f32)] * 2 + [dma(3)] * 3 + [dma(2)] * 2 + [dma(steps)] * 3,
        compiler_params=pltpu.CompilerParams(collective_id=1, has_side_effects=True, vmem_limit_bytes=VMEM),
        name="first_exchange",
    )(qkv, out, down, inputs, cotangent, lengths, *smalls, both, qkv, out, down)


def last_kernel(gate_up_in, down_in, out_in, qkv_in, small, sec_out_in, sec_grad_in, gate_up, down, out, qkv, attn, conv, head, beta, mlp, sec_out, sec_grad):
    core = lax.rem(lax.axis_index("section"), 2)
    me = lax.axis_index("dp")
    on = lambda which, x: jnp.where(core == which, x, 0.0)
    ff = gate_up.shape[2]
    both = on(1, gate_up_in[...])
    gate_up[...] = jnp.swapaxes(jnp.stack([both[:, :ff], both[:, ff:]], 0), 0, 1)
    count, wide = 16, small.shape[1]
    for j in range(down_in.shape[0]):
        for c in range(down.shape[1] // wide):
            down[j * count : (j + 1) * count, c * wide : (c + 1) * wide] = on(1, down_in[j, c * count : (c + 1) * count, :])
    out[...] = on(0, out_in[...])
    qkv[...] = on(0, qkv_in[...])
    sec_out[...] = sec_out_in[...]
    sec_grad[...] = sec_grad_in[...]
    lanes = attn.shape[1]
    attn[...] = on(0, small[0:1, :lanes])
    mlp[...] = on(1, small[0:1, :lanes])
    for p in range(3):
        conv[p] = on(0, small[8 + 4 * p : 12 + 4 * p, :lanes])
    beta[...] = on(0, small[32:40, :lanes])
    part = head.shape[1]
    turned = small[24:32, :lanes]
    shift = lax.rem(lanes - me * part, lanes)
    head[...] = on(0, pltpu.roll(turned, shift, 1)[0:1, :part])


def last_outputs(gate_up, down, out, qkv, small, sec_out, sec_grad, head_part):
    rows, width = out.shape
    ff = gate_up.shape[1] // 2
    half = rows // 2
    lanes = rows
    whole = lambda *shape: pl.BlockSpec(shape, lambda i: (0,) * len(shape))
    by_rows = lambda *shape: pl.BlockSpec(shape, lambda i: (i,) + (0,) * (len(shape) - 1))
    shape = lambda *dims: jax.ShapeDtypeStruct(dims, f32)
    qkv_spec = pl.BlockSpec((3, half, width), lambda i: (0, i, 0))
    stream = by_rows(1, *sec_out.shape[1:])
    tall = down.shape[0] // 2
    return pl.pallas_call(
        last_kernel,
        grid=(2,),
        in_specs=[by_rows(half, 2 * ff), by_rows(tall, *down.shape[1:]), by_rows(half, width), qkv_spec, whole(*small.shape), stream, stream],
        out_specs=[by_rows(half, 2, ff), by_rows(16 * tall, width), by_rows(half, width), qkv_spec]
        + [whole(1, lanes), whole(3, 4, lanes), whole(1, head_part), whole(8, lanes), whole(1, lanes), stream, stream],
        out_shape=[shape(rows, 2, ff), shape(32 * tall, width), shape(rows, width), shape(3, rows, width)]
        + [shape(1, lanes), shape(3, 4, lanes), shape(1, head_part), shape(8, lanes), shape(1, lanes)]
        + [jax.ShapeDtypeStruct(sec_out.shape, bf16)] * 2,
        compiler_params=pltpu.CompilerParams(vmem_limit_bytes=VMEM),
        name="last_outputs",
    )(gate_up, down, out, qkv, small, sec_out, sec_grad)


def mixer_fwd_kernel(per, trade, u_ref, gain_in, w_ref, w_beta, mask_ref, taps_q, taps_k, taps_v, gain_ref, *refs):
    own, refs = refs[:trade], refs[trade:]
    normed_ref, rate_ref, beta_ref, q_ref, k_ref, v_ref, mixed_ref, t_ref, n_ref, s_ref, o_ref = refs[:11]
    if trade:
        pairs = []
        for src, dst, begin in zip(own, refs[11 : 11 + trade], (0, own[1].shape[0] * 3 // 4)):
            part = src.shape[0] // 8
            pairs += [(src.at[a : a + part], dst.at[a : a + part]) for a in range(begin, src.shape[0], part)]
        give_weights(pl.program_id(0), pl.num_programs(0), [], pairs, *refs[11 + trade :])

    @pl.when(pl.program_id(0) == 0)
    def _():
        x = u_ref[...].astype(f32)
        normed = (x * lax.rsqrt(jnp.mean(x * x, 1, keepdims=True) + 1e-6) * gain_in[...]).astype(bf16)
        normed_ref[...] = normed
        rate = jax.nn.sigmoid(nt(normed, w_beta[...]))
        rate_ref[...] = rate
        beta_ref[...] = rate * mask_ref[...]

    for p, ref in enumerate((q_ref, k_ref, v_ref)):
        ref[...] = nn(normed_ref[...], w_ref[p])
    row, col = chunk_masks()
    strict, causal = row > col, row >= col
    chunks = q_ref.shape[0] // CHUNK
    beta_all = beta_ref[...]
    cut = lambda x: [x[i * CHUNK : (i + 1) * CHUNK] for i in range(chunks)]
    lanes = [slice(j * 128, (j + 1) * 128) for j in range(per)]
    qs, ks, vs, bs = [], [], [], []
    for j, lane in enumerate(lanes):

        def activated(ref, taps):
            c = convolved(ref[:, lane], taps[:, lane])
            return c * jax.nn.sigmoid(c)

        q, k, v = activated(q_ref, taps_q), activated(k_ref, taps_k), activated(v_ref, taps_v)
        q = q * lax.rsqrt(jnp.sum(q * q, 1, keepdims=True) + 1e-6)
        k = k * lax.rsqrt(jnp.sum(k * k, 1, keepdims=True) + 1e-6)
        qs.append(cut(q))
        ks.append(cut(k))
        vs.append(cut(v))
        bs.append(cut(head_column(beta_all, pl.program_id(0) * per + j)))
    each = [(j, i) for j in range(per) for i in range(chunks)]
    a_list = [jnp.where(strict, fine(nt, ks[j][i], ks[j][i]) * bs[j][i], 0.0) for j, i in each]
    ps = {(j, i): jnp.where(causal, fine(nt, qs[j][i], ks[j][i]), 0.0) for j, i in each}
    ts = dict(zip(each, triangular_inverse(a_list, row, col)))
    wu = {}
    for j, i in each:
        both = jnp.concatenate([ks[j][i] * bs[j][i], vs[j][i] * bs[j][i]], 1)
        wu[j, i] = both + fine(nn, ts[j, i], both)
    states = [jnp.zeros((128, 128), f32)] * per
    for i in range(chunks):
        span = pl.ds(i * CHUNK, CHUNK)
        news = [wu[j, i][:, 128:] - fine(nn, wu[j, i][:, :128], states[j]) for j in range(per)]
        outs = [fine(nn, jnp.concatenate([qs[j][i], ps[j, i]], 1), jnp.concatenate([states[j], news[j]], 0)) for j in range(per)]
        for j, lane in enumerate(lanes):
            o = outs[j]
            s_ref[j, span, :] = states[j].astype(bf16)
            n_ref[j, span, :] = news[j].astype(bf16)
            t_ref[j, span, :] = ts[j, i].astype(bf16)
            o_ref[span, lane] = o
            mixed_ref[span, lane] = (o * lax.rsqrt(jnp.mean(o * o, 1, keepdims=True) + 1e-5) * gain_ref[...]).astype(bf16)
        if i + 1 < chunks:
            states = [states[j] + fine(tn, ks[j][i], news[j]) for j in range(per)]


def mixer_fwd(u, w, mask, own=(), per=4):
    rows, width = u.shape
    heads = width // 128
    steps = heads // per
    wide = 128 * per
    part = pl.BlockSpec((rows, wide), lambda h: (0, h))
    tap = lambda p: pl.BlockSpec((None, 4, wide), lambda h, p=p: (p, 0, h))
    whole = lambda *shape: pl.BlockSpec(shape, lambda h: (0,) * len(shape))
    saved = pl.BlockSpec((per, rows, 128), lambda h: (h, 0, 0))
    anywhere = [pl.BlockSpec(memory_space=pl.ANY)] * len(own)
    dma = pltpu.SemaphoreType.DMA((12,))
    shape = lambda kind, *dims: jax.ShapeDtypeStruct(dims, kind)
    return pl.pallas_call(
        functools.partial(mixer_fwd_kernel, per, len(own)),
        grid=(steps,),
        in_specs=[whole(rows, width), whole(1, width), pl.BlockSpec((3, width, wide), lambda h: (0, 0, h)), whole(heads, width), whole(rows, 1)]
        + [tap(0), tap(1), tap(2), whole(1, 128)] + anywhere,
        out_specs=[whole(rows, width), whole(rows, heads), whole(rows, heads), part, part, part, part, saved, saved, saved, part] + anywhere,
        out_shape=[shape(bf16, rows, width), shape(f32, rows, heads), shape(f32, rows, heads)]
        + [shape(f32, rows, width)] * 3
        + [shape(bf16, rows, width)]
        + [shape(bf16, heads, rows, 128)] * 3
        + [shape(f32, rows, width)]
        + [jax.ShapeDtypeStruct(a.shape, a.dtype) for a in own],
        scratch_shapes=[dma, dma] if own else [],
        input_output_aliases={9 + i: 11 + i for i in range(len(own))},
        compiler_params=pltpu.CompilerParams(vmem_limit_bytes=VMEM, **({"collective_id": 2, "has_side_effects": True} if own else {})),
        name="mixer_forward",
    )(u, w["attn_gain"], w["qkv"], w["beta"], mask, w["conv"], w["conv"], w["conv"], w["head_gain"], *own)


def mixer_back_step(per, step, q_ref, k_ref, v_ref, beta_ref, taps_q, taps_k, taps_v, gain_ref, t_ref, n_ref, s_ref, o_ref, dm_ref, w_ref,
                    dq_ref, dk_ref, dv_ref, dtq_ref, dtk_ref, dtv_ref, dgain_ref, dbeta_ref, dnormed, with_taps=True):
    row, col = chunk_masks()
    strict, causal_t = row > col, row <= col
    causal = row >= col
    chunks = q_ref.shape[0] // CHUNK
    beta_all = beta_ref[...]

    @pl.when(step == 0)
    def _():
        dbeta_ref[...] = jnp.zeros_like(dbeta_ref)
        dgain_ref[...] = jnp.zeros_like(dgain_ref)
        dnormed[...] = jnp.zeros_like(dnormed)

    cut = lambda x: [x[i * CHUNK : (i + 1) * CHUNK] for i in range(chunks)]
    heads = range(per)
    lanes = [slice(j * 128, (j + 1) * 128) for j in heads]
    kept, qs, ks, vs, bs, dos = [], [], [], [], [], []
    for j, lane in enumerate(lanes):

        def activated(ref, taps):
            c = convolved(ref[:, lane], taps[:, lane])
            sig = jax.nn.sigmoid(c)
            return c * sig, sig * (1.0 + c * (1.0 - sig))

        q_act, q_slope = activated(q_ref, taps_q)
        k_act, k_slope = activated(k_ref, taps_k)
        v, v_slope = activated(v_ref, taps_v)
        q_scale = lax.rsqrt(jnp.sum(q_act * q_act, 1, keepdims=True) + 1e-6)
        k_scale = lax.rsqrt(jnp.sum(k_act * k_act, 1, keepdims=True) + 1e-6)
        q, k = q_act * q_scale, k_act * k_scale
        o, dm, gain = o_ref[:, lane], dm_ref[:, lane], gain_ref[...]
        o_scale = lax.rsqrt(jnp.mean(o * o, 1, keepdims=True) + 1e-5)
        o_hat = o * o_scale
        dgain_ref[...] += jnp.sum(dm * o_hat, 0, keepdims=True)
        dmg = dm * gain
        do = o_scale * (dmg - o_hat * jnp.mean(dmg * o_hat, 1, keepdims=True))
        kept.append((q, k, q_scale, k_scale, q_slope, k_slope, v_slope))
        qs.append(cut(q))
        ks.append(cut(k))
        vs.append(cut(v))
        bs.append(cut(head_column(beta_all, step * per + j)))
        dos.append(cut(do))
    dstates = [jnp.zeros((128, 128), f32)] * per
    dqs, dks, dvs, dbs = [[[] for _ in heads] for _ in range(4)]
    for i in reversed(range(chunks)):
        span = pl.ds(i * CHUNK, CHUNK)
        qc, kc, vc, bc, doc = [[x[j][i] for j in heads] for x in (qs, ks, vs, bs, dos)]
        n, s, t = [[ref[j, span, :] for j in heads] for ref in (n_ref, s_ref, t_ref)]
        gp = [nt(kc[j], jnp.concatenate([kc[j], qc[j]], 0)) for j in heads]
        p_t = [jnp.where(causal_t, gp[j][:, 128:], 0.0) for j in heads]
        dn = [nn(jnp.concatenate([p_t[j], kc[j]], 1), jnp.concatenate([doc[j], dstates[j]], 0)) for j in heads]
        dr = [dn[j] + tn(t[j], dn[j]) for j in heads]
        de = [dr[j] * bc[j] for j in heads]
        both = [nt(doc[j], jnp.concatenate([n[j], s[j]], 0)) for j in heads]
        e = [vc[j] - nn(kc[j], s[j]) for j in heads]
        da = [jnp.where(strict, -nt(dr[j], n[j]), 0.0) for j in heads]
        dp = [jnp.where(causal, both[j][:, :128], 0.0) for j in heads]
        dg = [da[j] * bc[j] for j in heads]
        for j in heads:
            dqs[j].append(both[j][:, 128:] + nn(dp[j], kc[j]))
            dbs[j].append(jnp.sum(dr[j] * e[j], 1, keepdims=True) + jnp.sum(da[j] * gp[j][:, :128], 1, keepdims=True))
            dks[j].append(
                tn(dp[j], qc[j])
                + nt(jnp.concatenate([n[j], -de[j].astype(bf16)], 1), jnp.concatenate([dstates[j].astype(bf16), s[j]], 1))
                + nn(dg[j], kc[j])
                + tn(dg[j], kc[j])
            )
            dvs[j].append(de[j])
        if i:
            dstates = [dstates[j] + tn(qc[j], doc[j]) - tn(kc[j], de[j]) for j in heads]
    join = lambda xs: jnp.concatenate(xs[::-1], 0)
    lane_ids = lax.broadcasted_iota(jnp.int32, dbeta_ref.shape, 1)
    for j, lane in enumerate(lanes):
        q, k, q_scale, k_scale, q_slope, k_slope, v_slope = kept[j]
        dq, dk, dv, db = join(dqs[j]), join(dks[j]), join(dvs[j]), join(dbs[j])
        dq = q_scale * (dq - q * jnp.sum(dq * q, 1, keepdims=True))
        dk = k_scale * (dk - k * jnp.sum(dk * k, 1, keepdims=True))
        dbeta_ref[...] += jnp.where(lane_ids == step * per + j, db, 0.0)
        for grad, slope, ref, taps, out, dtaps in (
            (dq, q_slope, q_ref, taps_q, dq_ref, dtq_ref),
            (dk, k_slope, k_ref, taps_k, dk_ref, dtk_ref),
            (dv, v_slope, v_ref, taps_v, dv_ref, dtv_ref),
        ):
            dc = grad * slope
            x = ref[:, lane]
            w = taps[:, lane]
            dx = dc * w[3:4]
            rows = [None] * 4
            if with_taps:
                rows[3] = jnp.sum(dc * x, 0, keepdims=True)
            for back in range(1, 4):
                moved = shifted_rows(dc, -back)
                dx = dx + moved * w[3 - back : 4 - back]
                if with_taps:
                    rows[3 - back] = jnp.sum(moved * x, 0, keepdims=True)
            out[:, lane] = dx.astype(bf16)
            if with_taps:
                dtaps[:, lane] = jnp.concatenate(rows, 0)

    dnormed[...] += sum(nt(ref[...], w_ref[p]) for p, ref in enumerate((dq_ref, dk_ref, dv_ref)))


def norm_back(u, gain, grad, dy, dgain_ref):
    x = u.astype(f32)
    scale = lax.rsqrt(jnp.mean(x * x, 1, keepdims=True) + 1e-6)
    hat = x * scale
    dgain_ref[...] = jnp.sum(grad * hat, 0, keepdims=True)
    grad = grad * gain
    dx = scale * (grad - hat * jnp.mean(grad * hat, 1, keepdims=True))
    return (dy.astype(f32) + dx).astype(bf16)


def mixer_back_end(beta_ref, rate_ref, u_ref, normed_ref, gain_in, w_beta, dy_ref, dbeta_ref, dnormed, g_ref, dgain_in, dw_beta):
    dlogits = dbeta_ref[...] * beta_ref[...] * (1.0 - rate_ref[...])
    high = dlogits.astype(bf16)
    low = (dlogits - high.astype(f32)).astype(bf16)
    dw_beta[...] = tn(high, normed_ref[...]) + tn(low, normed_ref[...])
    g_ref[...] = norm_back(u_ref[...], gain_in[...], dnormed[...] + nn(high, w_beta[...]), dy_ref[...], dgain_in)


def mixer_bwd_kernel(per, with_taps, q_ref, k_ref, v_ref, beta_ref, taps_q, taps_k, taps_v, gain_ref, t_ref, n_ref, s_ref, o_ref, dm_ref,
                     u_ref, normed_ref, rate_ref, gain_in, w_ref, w_beta, dy_ref,
                     dq_ref, dk_ref, dv_ref, dtq_ref, dtk_ref, dtv_ref, dgain_ref, g_ref, dgain_in, dw_beta, dbeta_ref, dnormed):
    step = pl.program_id(0)
    mixer_back_step(per, step, q_ref, k_ref, v_ref, beta_ref, taps_q, taps_k, taps_v, gain_ref, t_ref, n_ref, s_ref, o_ref, dm_ref, w_ref,
                    dq_ref, dk_ref, dv_ref, dtq_ref, dtk_ref, dtv_ref, dgain_ref, dbeta_ref, dnormed, with_taps)

    if not with_taps:
        for ref in (dtq_ref, dtk_ref, dtv_ref):
            ref[...] = jnp.zeros_like(ref)

    @pl.when(step == pl.num_programs(0) - 1)
    def _():
        mixer_back_end(beta_ref, rate_ref, u_ref, normed_ref, gain_in, w_beta, dy_ref, dbeta_ref, dnormed, g_ref, dgain_in, dw_beta)


def mixer_bwd(kept, w, dmixed, dy, with_taps=True, per=4):
    u, normed, rate, beta, q, k, v, t, n, s, o = kept
    rows, width = u.shape
    heads = width // 128
    steps = heads // per
    wide = 128 * per
    part = pl.BlockSpec((rows, wide), lambda h: (0, h))
    tap = lambda p: pl.BlockSpec((None, 4, wide), lambda h, p=p: (p, 0, h))
    taps_out = pl.BlockSpec((4, wide), lambda h: (0, h))
    whole = lambda *shape: pl.BlockSpec(shape, lambda h: (0,) * len(shape))
    saved = pl.BlockSpec((per, rows, 128), lambda h: (h, 0, 0))
    shape = lambda kind, *dims: jax.ShapeDtypeStruct(dims, kind)
    stream = whole(rows, width)
    return pl.pallas_call(
        functools.partial(mixer_bwd_kernel, per, with_taps),
        grid=(steps,),
        in_specs=[part, part, part, whole(rows, heads), tap(0), tap(1), tap(2), whole(1, 128), saved, saved, saved, part, part]
        + [stream, stream, whole(rows, heads), whole(1, width), pl.BlockSpec((3, width, wide), lambda h: (0, 0, h)), whole(heads, width), stream],
        out_specs=[part] * 3 + [taps_out] * 3 + [whole(1, 128), stream, whole(1, width), whole(heads, width)],
        out_shape=[shape(bf16, rows, width)] * 3 + [shape(f32, 4, width)] * 3
        + [shape(f32, 1, 128), shape(bf16, rows, width), shape(f32, 1, width), shape(f32, heads, width)],
        scratch_shapes=[pltpu.VMEM((rows, heads), f32), pltpu.VMEM((rows, width), f32)],
        compiler_params=pltpu.CompilerParams(vmem_limit_bytes=VMEM),
        name="mixer_backward",
    )(q, k, v, beta, w["conv"], w["conv"], w["conv"], w["head_gain"], t, n, s, o, dmixed, u, normed, rate, w["attn_gain"], w["qkv"], w["beta"], dy)


AHEAD = 2


def ff_blocks(ff):
    cuts = [0, 256]
    while cuts[-1] < ff:
        cuts.append(min(ff, cuts[-1] + 512))
    return list(zip(cuts, cuts[1:]))


def mlp_kernel(forward, keep, down, backward, *refs):
    refs = list(refs)
    take = lambda n: [refs.pop(0) for _ in range(n)]
    gain_ref, w_out_hbm, w_gate_hbm, w_up_hbm, w_down_hbm = take(5)
    if forward:
        u0_ref, mixed_ref = take(2)
    else:
        u1_ref, gate_hbm, up_hbm = take(3)
    if backward:
        (dy_ref,) = take(1)
    if forward:
        u1_ref, normed_ref = take(2)
    if keep:
        kept_hbm = take(3)
    if down:
        (u2_ref,) = take(1)
    if backward:
        if not forward:
            (grads_hbm,) = take(1)
        g1_ref, dm_ref, dgain_ref = take(3)
    w_out, w_gate, w_up, w_down, sems, out_sems, out_sem = take(7)
    if keep or not forward:
        gate_all, up_all = take(2)
    if keep:
        (hidden_all,) = take(1)
    if backward and not forward:
        dgate_all, dup_all = take(2)
    blocks = ff_blocks(w_down.shape[0])
    out_copy = pltpu.make_async_copy(w_out_hbm, w_out, out_sem)

    def loads(i):
        a, b = blocks[i]
        pairs = [(w_gate_hbm.at[:, a:b], w_gate.at[:, a:b]), (w_up_hbm.at[:, a:b], w_up.at[:, a:b]), (w_down_hbm.at[a:b], w_down.at[a:b])]
        if not forward:
            pairs += [(gate_hbm.at[:, a:b], gate_all.at[:, a:b]), (up_hbm.at[:, a:b], up_all.at[:, a:b])]
        return [pltpu.make_async_copy(s, d, sems.at[i, n]) for n, (s, d) in enumerate(pairs)]

    def stores(i):
        a, b = blocks[i]
        pairs = []
        if keep:
            pairs = list(zip((gate_all, up_all, hidden_all), kept_hbm))
        pairs = [(s.at[:, a:b], d.at[:, a:b]) for s, d in pairs]
        if backward and not forward:
            ff = blocks[-1][1]
            pairs = [(dgate_all.at[:, a:b], grads_hbm.at[:, a:b]), (dup_all.at[:, a:b], grads_hbm.at[:, ff + a : ff + b])]
        return [pltpu.make_async_copy(s, d, out_sems.at[i, n]) for n, (s, d) in enumerate(pairs)]

    if forward:
        out_copy.start()
    for i in range(AHEAD):
        for copy in loads(i):
            copy.start()
    if forward:
        out_copy.wait()
        u1 = (u0_ref[...].astype(f32) + nn(mixed_ref[...], w_out[...])).astype(bf16)
        u1_ref[...] = u1
        x = u1.astype(f32)
        normed = (x * lax.rsqrt(jnp.mean(x * x, 1, keepdims=True) + 1e-6) * gain_ref[...]).astype(bf16)
        normed_ref[...] = normed
    total = dnormed = None
    for i, (a, b) in enumerate(blocks):
        for copy in loads(i):
            copy.wait()
        if i + AHEAD < len(blocks):
            for copy in loads(i + AHEAD):
                copy.start()
        elif not forward and i + AHEAD == len(blocks):
            out_copy.start()
        if forward:
            gate, up = nn(normed_ref[...], w_gate[:, a:b]), nn(normed_ref[...], w_up[:, a:b])
        else:
            gate, up = gate_all[:, a:b], up_all[:, a:b]
        sig = jax.nn.sigmoid(gate)
        silu = gate * sig
        if forward:
            hidden = (silu * up).astype(bf16)
        if keep:
            gate_all[:, a:b], up_all[:, a:b], hidden_all[:, a:b] = gate, up, hidden
        if down:
            part = nn(hidden, w_down[a:b])
            total = part if total is None else total + part
        if backward:
            dhidden = nt(dy_ref[...], w_down[a:b])
            dgate = (dhidden * up * (sig + silu * (1.0 - sig))).astype(bf16)
            dup = (dhidden * silu).astype(bf16)
            if not forward:
                dgate_all[:, a:b], dup_all[:, a:b] = dgate, dup
            part = nt(jnp.concatenate([dgate, dup], 1), jnp.concatenate([w_gate[:, a:b], w_up[:, a:b]], 1))
            dnormed = part if dnormed is None else dnormed + part
        for copy in stores(i):
            copy.start()
    x = u1_ref[...].astype(f32)
    if down:
        u2_ref[...] = (x + total).astype(bf16)
    if backward:
        if not forward:
            out_copy.wait()
        scale = lax.rsqrt(jnp.mean(x * x, 1, keepdims=True) + 1e-6)
        hat = x * scale
        dgain_ref[...] = jnp.sum(dnormed * hat, 0, keepdims=True)
        grad = dnormed * gain_ref[...]
        dx = scale * (grad - hat * jnp.mean(grad * hat, 1, keepdims=True))
        g1 = (dy_ref[...].astype(f32) + dx).astype(bf16)
        g1_ref[...] = g1
        dm_ref[...] = nt(g1, w_out[...])
    for i in range(len(blocks)):
        for copy in stores(i):
            copy.wait()


def mlp_call(w, rows, forward=None, backward=None, keep=False, down=False):
    width, ff = w["gate"].shape
    going = len(forward) == 2
    here, there = pl.BlockSpec(memory_space=pltpu.VMEM), pl.BlockSpec(memory_space=pl.ANY)
    shape = lambda kind, n=width: jax.ShapeDtypeStruct((rows, n), kind)
    ins = [here] + [there] * 4
    ins += [here, here] if going else [here, there, there]
    args = [w["mlp_gain"], w["out"], w["gate"], w["up"], w["down"], *forward]
    outs, shapes = [], []
    count = len(ff_blocks(ff))
    scratch = [pltpu.VMEM((width, width), bf16), pltpu.VMEM((width, ff), bf16), pltpu.VMEM((width, ff), bf16), pltpu.VMEM((ff, width), bf16)]
    scratch += [pltpu.SemaphoreType.DMA((count, 5)), pltpu.SemaphoreType.DMA((count, 3)), pltpu.SemaphoreType.DMA]
    if backward is not None:
        ins.append(here)
        args.append(backward)
    if going:
        outs += [here, here]
        shapes += [shape(bf16), shape(bf16)]
    if keep or not going:
        scratch += [pltpu.VMEM((rows, ff), f32)] * 2
    if keep:
        outs += [there] * 3
        shapes += [shape(f32, ff), shape(f32, ff), shape(bf16, ff)]
        scratch.append(pltpu.VMEM((rows, ff), bf16))
    if down:
        outs.append(here)
        shapes.append(shape(bf16))
    if backward is not None:
        if not going:
            outs.append(there)
            shapes.append(shape(bf16, 2 * ff))
            scratch += [pltpu.VMEM((rows, ff), bf16)] * 2
        outs += [here, here, here]
        shapes += [shape(bf16), shape(f32), jax.ShapeDtypeStruct((1, width), f32)]
    return pl.pallas_call(
        functools.partial(mlp_kernel, going, keep, down, backward is not None),
        in_specs=ins,
        out_specs=outs,
        out_shape=shapes,
        scratch_shapes=scratch,
        compiler_params=pltpu.CompilerParams(vmem_limit_bytes=VMEM),
        name="feed_forward" + ("_keep" if keep else "") + ("_back" if backward is not None else ""),
    )(*args)


SEND_ROWS = (0, 128, 320, 512)


def mlp_send_kernel(cuts, gain_ref, w_out_hbm, w_gate_hbm, w_up_hbm, w_down_hbm, u0_ref, mixed_ref, next_ref,
                    w_out, w_gate, w_up, w_down, sems, out_sem, u2, arrived, send_sem, recv_sem):
    section = lax.axis_index("section")
    stage = section // 2
    far = {"section": section + 2 - 4 * stage}
    blocks = ff_blocks(w_down.shape[0])
    out_copy = pltpu.make_async_copy(w_out_hbm, w_out, out_sem)
    parts = list(zip(cuts, cuts[1:]))

    def loads(i):
        a, b = blocks[i]
        pairs = [(w_gate_hbm.at[:, a:b], w_gate.at[:, a:b]), (w_up_hbm.at[:, a:b], w_up.at[:, a:b]), (w_down_hbm.at[a:b], w_down.at[a:b])]
        return [pltpu.make_async_copy(s, d, sems.at[i, n]) for n, (s, d) in enumerate(pairs)]

    def send(p):
        a, b = parts[p]
        return pltpu.make_async_remote_copy(
            src_ref=u2.at[a:b], dst_ref=arrived.at[a:b], send_sem=send_sem.at[p], recv_sem=recv_sem.at[p], device_id=far, device_id_type=MESH
        )

    out_copy.start()
    for i in range(AHEAD):
        for copy in loads(i):
            copy.start()
    barrier = pltpu.get_barrier_semaphore()
    pl.semaphore_signal(barrier, inc=1, device_id=far, device_id_type=MESH)
    pl.semaphore_wait(barrier, 1)
    out_copy.wait()
    for p, (first, last) in enumerate(parts):
        u1 = (u0_ref[first:last].astype(f32) + nn(mixed_ref[first:last], w_out[...])).astype(bf16)
        x = u1.astype(f32)
        normed = (x * lax.rsqrt(jnp.mean(x * x, 1, keepdims=True) + 1e-6) * gain_ref[...]).astype(bf16)
        total = x
        for i, (a, b) in enumerate(blocks):
            if p == 0:
                for copy in loads(i):
                    copy.wait()
                if i + AHEAD < len(blocks):
                    for copy in loads(i + AHEAD):
                        copy.start()
            gate, up = nn(normed, w_gate[:, a:b]), nn(normed, w_up[:, a:b])
            total = total + nn((gate * jax.nn.sigmoid(gate) * up).astype(bf16), w_down[a:b])
        u2[first:last] = total.astype(bf16)

        @pl.when(stage == 0)
        def _():
            send(p).start()

    @pl.when(stage == 0)
    def _():
        next_ref[...] = u0_ref[...]
        for p in range(len(parts)):
            send(p).wait_send()

    @pl.when(stage == 1)
    def _():
        for p, (first, last) in enumerate(parts):
            send(p).wait_recv()
            next_ref[first:last] = arrived[first:last]


def mlp_send(w, u0, mixed):
    rows, width = u0.shape
    ff = w["gate"].shape[1]
    cuts = SEND_ROWS if SEND_ROWS[-1] == rows else (0, rows)
    here, there = pl.BlockSpec(memory_space=pltpu.VMEM), pl.BlockSpec(memory_space=pl.ANY)
    count, parts = len(ff_blocks(ff)), len(cuts) - 1
    vmem = lambda *shape: pltpu.VMEM(shape, bf16)
    dma = lambda *n: pltpu.SemaphoreType.DMA(n)
    return pl.pallas_call(
        functools.partial(mlp_send_kernel, cuts),
        in_specs=[here] + [there] * 4 + [here] * 2,
        out_specs=here,
        out_shape=jax.ShapeDtypeStruct((rows, width), bf16),
        scratch_shapes=[vmem(width, width), vmem(width, ff), vmem(width, ff), vmem(ff, width), dma(count, 3), pltpu.SemaphoreType.DMA]
        + [vmem(rows, width), vmem(rows, width), dma(parts), dma(parts)],
        compiler_params=pltpu.CompilerParams(collective_id=3, has_side_effects=True, vmem_limit_bytes=VMEM),
        name="feed_forward_send",
    )(w["mlp_gain"], w["out"], w["gate"], w["up"], w["down"], u0, mixed)


PIECE = (64, 256)
SLOTS = 4
LAGS = (1, 5, 9, 13, 14)
HELD = 24
PAIR = 2


def sum_kernel(total, n2_ref, came, seed, mlp_gain, beta_ref, rate_ref, conv_ref, head_ref, attn_ref, w_beta,
               n1_hbm, m_hbm, h_hbm, u0_hbm, normed_hbm,
               gate_hbm, up_hbm, w_gate_hbm, w_up_hbm, w_down_hbm, w_out_hbm, q_hbm, k_hbm, v_hbm, o_hbm, t_hbm, n_hbm, s_hbm, w_hbm, u1, u2,
               gu_out, down_out, out_out, qkv_out, small_out, u_out, g_out,
               n1_ref, m_ref, h_ref, u_ref, normed_ref, u1_ref, late_sem,
               gate_blk, up_blk, w_gate, w_up, w_down, w_out, feed_sem, out_sem, dy, dgu, g1, dm, d_mlp,
               q_blk, k_blk, v_blk, o_blk, t_blk, n_blk, s_blk, w_blk, load_sem, dqkv, dtaps, dhead, g0, dattn, dw_beta, dbeta, dnormed, small,
               fin, keep_sem, give_sem, take_sem, fin_sem, far_sem, own, send, rc, rx, ry, rz, send_sem, xs_sem, ys_sem, zs_sem, rc_sem, rx_sem, ry_sem, rz_sem):
    section, me = lax.axis_index("section"), lax.axis_index("dp")
    core, x, low, high = lax.rem(section, 2), lax.rem(me, 2), lax.rem(me // 2, 2), me // 4
    far_core = {"section": section + 1 - 2 * core}
    far_x, far_low, far_high = {"dp": me + 1 - 2 * x}, {"dp": me + 2 - 4 * low}, {"dp": me + 4 - 8 * high}
    barrier = pltpu.get_barrier_semaphore()
    for other in (far_core, far_x, far_low, far_high):
        pl.semaphore_signal(barrier, inc=1, device_id=other, device_id_type=MESH)
    pl.semaphore_wait(barrier, 4)

    def remote(src, dst, sent, got, other):
        return pltpu.make_async_remote_copy(src_ref=src, dst_ref=dst, send_sem=sent, recv_sem=got, device_id=other, device_id_type=MESH)

    def micro(which, mixer_side, mlp_side, into):
        return (
            pltpu.make_async_copy(mixer_side if which == 0 else mlp_side, into.at[core], keep_sem.at[0 if into is u_out else 1]),
            remote(mlp_side if which == 0 else mixer_side, into.at[core], give_sem.at[0 if into is u_out else 1], take_sem.at[0 if into is u_out else 1], far_core),
        )

    def each_core(act):
        for which in range(2):
            @pl.when(core == which)
            def _():
                act(which)

    def start_micro(*sides):
        def act(which):
            for copy in micro(which, *sides):
                copy.start()
        each_core(act)

    start_micro(u1, u2, u_out)

    ff = gu_out.shape[1] // 2
    feeds = ff // PIECE[1]

    def feed_loads(b):
        at = lax.rem(b, 2)
        cols = pl.ds(pl.multiple_of(b * PIECE[1], PIECE[1]), PIECE[1])
        pairs = [(src.at[:, cols], dst.at[at]) for src, dst in ((gate_hbm, gate_blk), (up_hbm, up_blk), (w_gate_hbm, w_gate), (w_up_hbm, w_up))]
        pairs.append((w_down_hbm.at[cols], w_down.at[at]))
        return [pltpu.make_async_copy(src, dst, feed_sem.at[at, i]) for i, (src, dst) in enumerate(pairs)]

    for copy in feed_loads(0):
        copy.start()
    w_out_copy = pltpu.make_async_copy(w_out_hbm, w_out, out_sem)
    late = [
        pltpu.make_async_copy(src, dst, late_sem.at[i])
        for i, (src, dst) in enumerate(((u1, u1_ref), (h_hbm, h_ref), (m_hbm, m_ref), (n1_hbm, n1_ref), (u0_hbm, u_ref), (normed_hbm, normed_ref)))
    ]

    dy[...] = jnp.where(section >= 2, seed[...], came[...])

    def feed_step(b):
        at = lax.rem(b, 2)
        for copy in feed_loads(b):
            copy.wait()

        @pl.when(b + 1 < feeds)
        def _():
            for copy in feed_loads(b + 1):
                copy.start()

        @pl.when(b == 0)
        def _():
            dnormed[...] = jnp.zeros_like(dnormed)
            for copy in (w_out_copy, *late):
                copy.start()

        gate, up = gate_blk[at], up_blk[at]
        sig = jax.nn.sigmoid(gate)
        silu = gate * sig
        dhidden = nt(dy[...], w_down[at])
        dgate = (dhidden * up * (sig + silu * (1.0 - sig))).astype(bf16)
        dup = (dhidden * silu).astype(bf16)
        dgu[0], dgu[1] = dgate, dup
        dnormed[...] += nt(jnp.concatenate([dgate, dup], 1), jnp.concatenate([w_gate[at], w_up[at]], 1))

    def feed_end():
        for copy in (w_out_copy, *late):
            copy.wait()
        g1[...] = norm_back(u1_ref[...], mlp_gain[...], dnormed[...], dy[...], d_mlp)
        dm[...] = nt(g1[...], w_out[...])

    def mixer_begin():
        for copy in loads(0):
            copy.start()

    def loads(s):
        cols = pl.ds(pl.multiple_of(s * PAIR * 128, PAIR * 128), PAIR * 128)
        pairs = [(src.at[:, cols], dst) for src, dst in ((q_hbm, q_blk), (k_hbm, k_blk), (v_hbm, v_blk), (o_hbm, o_blk))]
        pairs += [(src.at[pl.ds(s * PAIR, PAIR)], dst) for src, dst in ((t_hbm, t_blk), (n_hbm, n_blk), (s_hbm, s_blk))]
        pairs.append((w_hbm.at[:, :, cols], w_blk))
        return [pltpu.make_async_copy(src, dst, load_sem.at[i]) for i, (src, dst) in enumerate(pairs)]

    def mixer_step(s):
        for copy in loads(s):
            copy.wait()
        width = dattn.shape[1]
        cols = lambda p: pl.ds(pl.multiple_of(p * width + s * PAIR * 128, PAIR * 128), PAIR * 128)
        taps = [conv_ref.at[p, :, cols(0)] for p in range(3)]
        grads = [dqkv.at[:, cols(p)] for p in range(3)]
        dt = [dtaps.at[p, :, cols(0)] for p in range(3)]
        mixer_back_step(PAIR, s, q_blk, k_blk, v_blk, beta_ref, *taps, head_ref, t_blk, n_blk, s_blk, o_blk, dm.at[:, cols(0)], w_blk, *grads, *dt, dhead, dbeta, dnormed)

        @pl.when(s + 1 < width // (PAIR * 128))
        def _():
            for copy in loads(s + 1):
                copy.start()

    def mixer_end():
        mixer_back_end(beta_ref, rate_ref, u_ref, normed_ref, attn_ref, w_beta, g1, dbeta, dnormed, g0, dattn, dw_beta)
        start_micro(g0, g1, g_out)
        zeros = lambda n: jnp.zeros((n, PIECE[1]), f32)
        for d in range(8):
            lane = slice(d * 128, (d + 1) * 128)
            wide = lambda a: jnp.concatenate([a, jnp.zeros_like(a)], 1)
            rows = [wide(dattn[:, lane]), zeros(7)]
            for p in range(3):
                rows += [wide(dtaps[p, :, lane])]
            rows += [zeros(4), wide(dhead[...]), zeros(7), wide(dw_beta[:, lane]), zeros(PIECE[0] - 40)]
            small[0, d // 4, d // 2 % 2, d % 2] = jnp.concatenate(rows, 0).astype(bf16)
            small[1, d // 4, d // 2 % 2, d % 2] = jnp.concatenate([wide(d_mlp[:, lane]), zeros(PIECE[0] - 1)], 0).astype(bf16)

    def held(t):
        return lax.rem(t, HELD)

    def slot(t):
        return lax.rem(t, SLOTS)

    def core_copy(t):
        return remote(send.at[slot(t)], rc.at[held(t)], send_sem.at[slot(t)], rc_sem.at[t], far_core)

    def turned(t):
        return lax.rem(t, 4) // 3

    def first_copy(t, z_first):
        src = rc.at[held(t), :, 1 - low] if z_first else rc.at[held(t), :, :, 1 - x]
        return remote(src, rx.at[held(t)], xs_sem.at[slot(t)], rx_sem.at[t], far_low if z_first else far_x)

    def second_copy(t):
        way = turned(t)
        other = {"dp": me + way * (1 - 2 * x) + (1 - way) * (2 - 4 * low)}
        mine = way * x + (1 - way) * low
        return remote(rx.at[held(t), :, 1 - mine], ry.at[held(t)], ys_sem.at[slot(t)], ry_sem.at[t], other)

    def high_copy(t):
        return remote(ry.at[held(t), 1 - high], rz.at[held(t)], zs_sem.at[slot(t)], rz_sem.at[t], far_high)

    def free(copy, t):
        @pl.when(t >= SLOTS)
        def _():
            copy(t - SLOTS).wait_send()

    def either(t, act):
        for z_first in (False, True):
            @pl.when(turned(t) == int(z_first))
            def _():
                act(z_first)

    def after_core(t):
        core_copy(t).wait_recv()
        rc[held(t)] = rc[held(t)] + own[slot(t)]
        free(lambda u: first_copy(u, False), t)
        either(t, lambda z_first: first_copy(t, z_first).start())

    def after_first(t):
        first_copy(t, False).wait_recv()

        def add(z_first):
            rx[held(t)] = rx[held(t)] + (rc[held(t), :, low] if z_first else rc[held(t), :, :, x])

        either(t, add)
        free(second_copy, t)
        second_copy(t).start()

    def after_second(t):
        second_copy(t).wait_recv()
        way = turned(t)
        ry[held(t)] = ry[held(t)] + rx[held(t), :, way * x + (1 - way) * low]
        free(high_copy, t)
        high_copy(t).start()

    def cols_of(i):
        return pl.ds(pl.multiple_of(i * PIECE[1], PIECE[1]), PIECE[1])

    def rows_of(into, i):
        return into.at[pl.ds(pl.multiple_of(core * PIECE[0], PIECE[0]), PIECE[0]), cols_of(i)]

    def gate_up_at(i):
        return rows_of(gu_out, lax.rem(i, 2) * feeds + i // 2)

    def down_at(i):
        return down_out.at[core * (down_out.shape[0] // 2) + i]

    def qkv_at(i):
        per = qkv_out.shape[2] // PIECE[1]
        return rows_of(qkv_out.at[i // per], lax.rem(i, per))

    def piece_here(t, where):
        return pltpu.make_async_copy(fin.at[slot(t)], where, fin_sem.at[slot(t)])

    def piece_there(t, where):
        return remote(fin.at[slot(t)], where, fin_sem.at[slot(t)], far_sem.at[t], far_core)

    def fin_wait(t):
        pltpu.make_async_copy(fin.at[slot(t)], fin.at[slot(t)], fin_sem.at[slot(t)]).wait()

    def after_high(t):
        high_copy(t).wait_recv()
        value = rz[held(t)].astype(f32) + ry[held(t), high].astype(f32)

        @pl.when(t == total - 1)
        def _():
            small_out[...] = value

        @pl.when(t < total - 1)
        def _():
            @pl.when(t >= SLOTS)
            def _():
                fin_wait(t)

            fin[slot(t)] = value
            for target, inside, index, where in segments:
                @pl.when(inside(t) & (core == target))
                def _():
                    piece_here(t, where(index(t))).start()

                @pl.when(inside(t) & (core != target))
                def _():
                    piece_there(t, where(index(t))).start()

    def after_far(t):
        for target, inside, index, where in segments:
            @pl.when(inside(t) & (core == target))
            def _():
                piece_there(t, where(index(t))).wait_recv()

    def later(t):
        for step, lag in zip((after_core, after_first, after_second, after_high, after_far), LAGS):
            @pl.when((t >= lag) & (t < total + lag))
            def _():
                step(t - lag)

    def columns(t, lhs, block):
        for which, into in ((1 - core, send), (core, own)):
            into[slot(t)] = nn(lhs[which], block).astype(bf16).reshape(own.shape[1:])

    def fill_gate_up(t):
        columns(t, n2_ref, dgu[lax.rem(t, 2)])

    def fill_out(t):
        columns(t, m_ref, g1[:, cols_of(out_index(t))])

    def fill_qkv(t):
        columns(t, n1_ref, dqkv[:, cols_of(t - qkv_base)])

    def fill_down(t):
        for which, into in ((1 - core, send), (core, own)):
            part = nn(h_ref[down_index(t), which], dy[...]).astype(bf16)
            count = part.shape[0] // 8
            for d in range(8):
                for c in range(PIECE[0] // count):
                    into[slot(t), d // 4, d // 2 % 2, d % 2, c * count : (c + 1) * count, :] = part[d * count : (d + 1) * count, c * PIECE[1] : (c + 1) * PIECE[1]]

    def given(t):
        send[slot(t)] = small[1 - core]
        own[slot(t)] = small[core]

    turns, downs = out_out.shape[1] // PIECE[1], h_ref.shape[0]
    turn_base = 2 * feeds
    rest_base = turn_base + 3 * turns
    qkv_base = turn_base + downs + turns
    in_turns = lambda t: (t >= turn_base) & (t < rest_base)
    of_turn = lambda t: lax.rem(jnp.maximum(t - turn_base, 0), 3)
    out_index = lambda t: jnp.maximum(t - turn_base, 0) // 3
    down_index = lambda t: jnp.where(t < rest_base, 2 * out_index(t) + of_turn(t), t - turn_base - turns)
    segments = (
        (1, lambda t: t < turn_base, lambda t: t, gate_up_at),
        (1, lambda t: (in_turns(t) & (of_turn(t) < 2)) | ((t >= rest_base) & (t < qkv_base)), down_index, down_at),
        (0, lambda t: in_turns(t) & (of_turn(t) == 2), out_index, lambda i: rows_of(out_out, i)),
        (0, lambda t: (t >= qkv_base) & (t < total - 1), lambda t: t - qkv_base, qkv_at),
    )

    def block(t, fill):
        @pl.when(t >= SLOTS)
        def _():
            core_copy(t - SLOTS).wait_send()

        fill(t)
        core_copy(t).start()
        later(t)

    def run(begin, count, fill):
        def body(i, carry):
            block(begin + i, fill)
            return carry

        lax.fori_loop(0, count, body, 0)

    def feed_turn(b, carry):
        feed_step(b)
        run(2 * b, 2, fill_gate_up)
        return carry

    def mixer_turn(s, carry):
        begin = turn_base + 3 * s
        run(begin, 2, fill_down)
        block(begin + 2, fill_out)
        mixer_step(s)
        return carry

    mixer_begin()
    lax.fori_loop(0, feeds, feed_turn, 0)
    feed_end()
    lax.fori_loop(0, turns, mixer_turn, 0)
    mixer_end()
    run(rest_base, qkv_base - rest_base, fill_down)
    run(qkv_base, total - 1 - qkv_base, fill_qkv)
    run(total - 1, 1, given)

    def drain(t, carry):
        later(t)
        return carry

    lax.fori_loop(total, total + LAGS[-1], drain, 0)
    for copy in (core_copy, lambda t: first_copy(t, False), second_copy, high_copy):
        for t in range(total - SLOTS, total):
            copy(jnp.int32(t)).wait_send()
    for t in range(SLOTS):
        fin_wait(jnp.int32(t))

    def end_micro(which):
        for keep, give in (micro(which, u1, u2, u_out), micro(which, g0, g1, g_out)):
            keep.wait()
            give.wait_send()
            give.wait_recv()

    each_core(end_micro)


def summed_gradients(n2, n1, m, h, dy, seed, gate, up, kept, w, u1, u2):
    u0, normed, rate, beta, q, k, v, t, n, s, o = kept
    rows, width = u0.shape
    ff = gate.shape[1]
    total = (2 * ff + 4 * width) // PIECE[1] + h.shape[0] + 1
    wide, heads = PAIR * 128, beta.shape[1]
    buffer = lambda *lead: pltpu.VMEM(lead + PIECE, bf16)
    dma = lambda *n: pltpu.SemaphoreType.DMA(n)
    vmem, anywhere = pl.BlockSpec(memory_space=pltpu.VMEM), pl.BlockSpec(memory_space=pl.ANY)
    near = (n2, dy, seed, w["mlp_gain"], beta, rate, w["conv"], w["head_gain"], w["attn_gain"], w["beta"])
    late = (n1, m, h, u0, normed)
    far = (*late, gate, up, w["gate"], w["up"], w["down"], w["out"], q, k, v, o, t, n, s, w["qkv"], u1, u2)
    result = lambda *shape: jax.ShapeDtypeStruct(shape, f32)
    pair = jax.ShapeDtypeStruct((2,) + u1.shape, bf16)
    out_rows = 2 * PIECE[0]
    return pl.pallas_call(
        functools.partial(sum_kernel, total),
        out_shape=[result(out_rows, 2 * ff), result(2 * h.shape[0], *PIECE), result(out_rows, width), result(3, out_rows, width), result(*PIECE), pair, pair],
        in_specs=[vmem] * len(near) + [anywhere] * len(far),
        out_specs=[anywhere] * 4 + [vmem] + [anywhere] * 2,
        scratch_shapes=[pltpu.VMEM(a.shape, a.dtype) for a in (*late, u1)]
        + [dma(6)]
        + [pltpu.VMEM((2, rows, PIECE[1]), f32)] * 2
        + [pltpu.VMEM((2, width, PIECE[1]), bf16)] * 2
        + [pltpu.VMEM((2, PIECE[1], width), bf16), pltpu.VMEM((width, width), bf16), dma(2, 5), pltpu.SemaphoreType.DMA]
        + [pltpu.VMEM((rows, width), bf16), pltpu.VMEM((2, rows, PIECE[1]), bf16), pltpu.VMEM((rows, width), bf16), pltpu.VMEM((rows, width), f32), pltpu.VMEM((1, width), f32)]
        + [pltpu.VMEM((rows, wide), f32)] * 4
        + [pltpu.VMEM((PAIR, rows, 128), bf16)] * 3
        + [pltpu.VMEM((3, width, wide), bf16), dma(8)]
        + [pltpu.VMEM((rows, 3 * width), bf16), pltpu.VMEM((3, 4, width), f32), pltpu.VMEM((1, 128), f32), pltpu.VMEM((rows, width), bf16)]
        + [pltpu.VMEM((1, width), f32), pltpu.VMEM((heads, width), f32), pltpu.VMEM((rows, heads), f32), pltpu.VMEM((rows, width), f32)]
        + [buffer(2, 2, 2, 2)]
        + [pltpu.VMEM((SLOTS,) + PIECE, f32), dma(2), dma(2), dma(2), dma(SLOTS), dma(total)]
        + [buffer(SLOTS, 2, 2, 2), buffer(SLOTS, 2, 2, 2), buffer(HELD, 2, 2, 2), buffer(HELD, 2, 2), buffer(HELD, 2), buffer(HELD)]
        + [dma(SLOTS)] * 4
        + [dma(total)] * 4,
        compiler_params=pltpu.CompilerParams(collective_id=0, has_side_effects=True, vmem_limit_bytes=VMEM),
        name="gradient_sums",
    )(*near, *far)


def matmul(a, b):
    return jnp.dot(a, b, preferred_element_type=f32)


def matmul_tn(a, b):
    return lax.dot_general(a, b, (((0,), (0,)), ((), ())), preferred_element_type=f32)


def pick(x, index, axis):
    return lax.dynamic_index_in_dim(x, index, axis, keepdims=False)


def shards(inputs, cotangent, lengths, attn_gain, qkv_weight, conv_weight, beta_weight, head_gain, out_weight, mlp_gain, gate_up_weight, down_weight):
    section, sections = lax.axis_index("section"), lax.axis_size("section")
    me, group = lax.axis_index("dp"), lax.axis_size("dp")
    core, stage = section % 2, section // 2
    swap = [(i, i ^ 1) for i in range(sections)]
    to_odd = [(i, i + 1) for i in range(0, sections, 2)]
    to_even = [(i + 1, i) for i in range(0, sections, 2)]
    rows = inputs.shape[2]
    width = inputs.shape[3]

    qkv, out_w, down, own_gate, first, seed, token_mask, conv, beta_w, attn, head, mlp, own_up = first_exchange(
        jnp.moveaxis(qkv_weight[0], 1, 0),
        out_weight[0],
        down_weight[0],
        inputs,
        cotangent,
        lengths.T,
        jnp.moveaxis(conv_weight[0], 1, 0),
        beta_weight[0].T,
        attn_gain,
        head_gain,
        mlp_gain,
        gate_up_weight[0],
    )
    w = {"attn_gain": attn, "conv": conv, "beta": beta_w, "head_gain": head, "qkv": qkv, "out": out_w, "mlp_gain": mlp, "down": down}

    down_stage = [(i + 2, i) for i in range(sections - 2)]

    *passed, w["up"], w["gate"] = mixer_fwd(first, w, token_mask, (own_up, own_gate))
    u0 = mlp_send(w, first, passed[6])
    normed1, rate, beta, q, k, v, mixed, *saved = mixer_fwd(u0, w, token_mask)
    kept = (u0, normed1, rate, beta, q, k, v, *saved)
    u1, normed2, gate, up, hidden, g1, dmixed, _ = mlp_call(w, rows, (u0, mixed), seed, keep=True)
    g0 = mixer_bwd(kept, w, dmixed, g1, with_taps=False)[7]
    dy = lax.ppermute(g0, "section", down_stage)
    u2 = (u1.astype(f32) + matmul(hidden, w["down"])).astype(bf16)
    ff = hidden.shape[1]
    fused = group == 8 and width == 1024 and ff % 256 == 0
    for_sums = ()
    if fused:
        by_owner = lambda a: a.reshape(rows, group, 2, 64).transpose(2, 1, 3, 0).reshape(2, group * 64, rows)
        down_rows = hidden.reshape(rows, group, 2, ff // 256, 16).transpose(3, 2, 1, 4, 0).reshape(ff // 256, 2, group * 16, rows)
        for_sums = (by_owner(normed2), by_owner(normed1), by_owner(mixed), down_rows)
    dy, u2, for_sums = lax.optimization_barrier((dy, u2, for_sums))

    if fused:
        sums = summed_gradients(*for_sums, dy, seed, gate, up, kept, w, u1, u2)
        gate_up_sum, down_sum, out_sum, qkv_sum, attn_sum, conv_sum, head_sum, beta_sum, mlp_sum, sec_out, sec_grad = last_outputs(*sums, head_gain.shape[1] // group)
        return (
            sec_out[None, :, None],
            sec_grad[None, :, None],
            attn_sum,
            jnp.moveaxis(qkv_sum, 0, 1)[None],
            jnp.moveaxis(conv_sum, 0, 1)[None],
            beta_sum.T[None],
            head_sum,
            out_sum[None],
            mlp_sum,
            gate_up_sum[None],
            down_sum[None],
        )

    dy = jnp.where(stage == 1, seed, dy)

    def halve(x):
        kept = pick(x, core, 1).astype(f32)
        x = (kept + lax.ppermute(pick(x, 1 - core, 1), "section", swap).astype(f32)).astype(bf16)
        return scatter(x)

    def scatter(x):
        kind = x.dtype
        bit = 1
        while bit < group:
            pairs = [(i, i ^ bit) for i in range(group)]
            mine = (me // bit) % 2
            x = x.reshape((x.shape[0] // 2, 2) + x.shape[1:])
            other = lax.ppermute(pick(x, 1 - mine, 1), "dp", pairs)
            x = pick(x, mine, 1).astype(f32) + other.astype(f32)
            bit *= 2
            if bit < group:
                x = x.astype(kind)
        return x[0]

    def share(grad):
        count, cols = grad.shape
        return halve(grad.astype(bf16).reshape(group, 2, count // group // 2, cols))

    dgate_up, g1, dmixed, d_mlp_gain = mlp_call(w, rows, (u1, gate, up), dy)
    *dproj, dtq, dtk, dtv, dhead, g0, d_attn_gain, dbeta = mixer_bwd(kept, w, dmixed, g1)
    dtaps = jnp.stack([dtq, dtk, dtv], 1)
    dbeta = dbeta.T
    taps_rows = jnp.moveaxis(dtaps.reshape(-1, 3, group, width // group), 2, 0).reshape(group, -1)
    small = [d_attn_gain.reshape(group, -1), taps_rows, dbeta.reshape(group, -1), dhead.reshape(group, -1), d_mlp_gain.reshape(group, -1)]
    sizes = [a.shape[1] for a in small]
    joined = jnp.concatenate(small, 1)
    down_share = share(matmul_tn(hidden, dy))
    gate_share = share(matmul_tn(normed2, dgate_up[:, :ff]))
    up_share = share(matmul_tn(normed2, dgate_up[:, ff:]))
    out_share = share(matmul_tn(mixed, g1))
    qkv_share = [share(matmul_tn(normed1, d)) for d in dproj]
    small = scatter(joined + lax.ppermute(joined, "section", swap))
    def to_core(x, target):
        other = lax.ppermute(x, "section", to_even if target == 0 else to_odd)
        both = jnp.concatenate([x, other] if target == 0 else [other, x], 0)
        return jnp.where(core == target, both, 0.0)

    grad_qkv = jnp.stack([to_core(x, 0) for x in qkv_share], 1)
    grad_out = to_core(out_share, 0)
    grad_gate_up = jnp.stack([to_core(gate_share, 1), to_core(up_share, 1)], 1)
    grad_down = to_core(down_share, 1)

    def both_micro(mixer_side, mlp_side):
        own = jnp.where(core == 0, mixer_side, mlp_side)
        other = lax.ppermute(jnp.where(core == 0, mlp_side, mixer_side), "section", swap)
        return jnp.where(core == 0, jnp.stack([own, other]), jnp.stack([other, own]))[None, :, None]

    on_even = lambda x: jnp.where(core == 0, x, 0.0)
    on_odd = lambda x: jnp.where(core == 1, x, 0.0)
    sec_out, sec_grad = both_micro(u1, u2), both_micro(g0, g1)
    offsets = [sum(sizes[:i]) for i in range(len(sizes) + 1)]
    s_attn, s_taps, s_beta, s_head, s_mlp = [small[a:b] for a, b in zip(offsets, offsets[1:])]

    return (
        sec_out,
        sec_grad,
        on_even(s_attn)[None],
        grad_qkv[None],
        on_even(s_taps).reshape(1, -1, 3, width // group),
        on_even(s_beta).reshape(1, -1, beta.shape[1]),
        on_even(s_head)[None],
        grad_out[None],
        on_odd(s_mlp)[None],
        grad_gate_up[None],
        grad_down[None],
    )


def solution(mesh):
    in_specs = (
        P(None, "dp", None, None),
        P(None, "dp", None, None),
        P(None, "dp"),
        P("section", None),
        P("section", None, None, None),
        P("section", None, None, None),
        P("section", None, None),
        P("section", None),
        P("section", None, None),
        P("section", None),
        P("section", None, None, None),
        P("section", None, None),
    )
    out_specs = (
        P("section", None, "dp", None, None),
        P("section", None, "dp", None, None),
        P("section", "dp"),
        P("section", "dp", None, None),
        P("section", None, None, "dp"),
        P("section", "dp", None),
        P("section", "dp"),
        P("section", "dp", None),
        P("section", "dp"),
        P("section", "dp", None, None),
        P("section", "dp", None),
    )
    return jax.shard_map(shards, mesh=mesh, in_specs=in_specs, out_specs=out_specs, check_vma=False)
```
